32 devices in a mesh: rep: 4 (over y, x), shard: 8 (over z, core).
Axes of the slice: x: 2, y: 2, z: 4, core: 2. Of those that a mesh axis runs over, the one named last changes fastest.
Arguments:
- tokens: bfloat16 [8192, 1536], P(('rep', 'shard')), may hold values from -6 to 6
- cotangent: bfloat16 [8192, 1536], P(('rep', 'shard')), may hold values from -6 to 6
- dealt_to: int32 [32], P(('rep', 'shard')), may hold values from 0 to 7, as said below
- lengths: int32 [32, 3], P(('rep', 'shard')), may hold values from 1 to 192, 256 in all within a row
- routes: int32 [8192, 6], P(('rep', 'shard')), may hold values from 0 to 15, as said below
- slot_index: int32 [8192, 6], P(('rep', 'shard')), may hold values from 0 to 127, as said below
- in_norm: bfloat16 [1536], P('shard'), may hold values from 0.5 to 1.5
- in_proj: bfloat16 [1536, 6448], P('shard'), may hold values from -0.15625 to 0.15625
- conv_weight: bfloat16 [4, 3328], P(None, 'shard'), may hold values from -3 to 3
- conv_bias: bfloat16 [3328], P('shard'), may hold values from -3 to 3
- dt_bias: bfloat16 [48], P('shard'), may hold values from -5 to -2
- decay_log: bfloat16 [48], P('shard'), may hold values from -1 to 2.5
- skip_gain: bfloat16 [48], P('shard'), may hold values from 0.5 to 1.5
- mixer_norm: bfloat16 [3072], P('shard'), may hold values from 0.5 to 1.5
- out_proj: bfloat16 [3072, 1536], P('shard'), may hold values from -0.109375 to 0.109375
- post_norm: bfloat16 [1536], P('shard'), may hold values from 0.5 to 1.5
- router: bfloat16 [1536, 16], P('shard'), may hold values from -0.078125 to 0.078125
- shared_in: bfloat16 [1536, 2048], P('shard'), may hold values from -0.15625 to 0.15625
- shared_out: bfloat16 [1024, 1536], P('shard'), may hold values from -0.1875 to 0.1875
- expert_in: bfloat16 [16, 1536, 1024], P('shard'), may hold values from -0.15625 to 0.15625
- expert_out: bfloat16 [16, 512, 1536], P('shard'), may hold values from -0.5 to 0.5
Outputs:
- layer_out: bfloat16 [8192, 1536], P(('rep', 'shard'))
- grad_tokens: bfloat16 [8192, 1536], P(('rep', 'shard'))
- grad_in_norm: float32 [1536], P('shard')
- grad_in_proj: float32 [1536, 6448], P('shard')
- grad_conv_weight: float32 [4, 3328], P(None, 'shard')
- grad_conv_bias: float32 [3328], P('shard')
- grad_dt_bias: float32 [48], P('shard')
- grad_decay_log: float32 [48], P('shard')
- grad_skip_gain: float32 [48], P('shard')
- grad_mixer_norm: float32 [3072], P('shard')
- grad_out_proj: float32 [3072, 1536], P('shard')
- grad_post_norm: float32 [1536], P('shard')
- grad_router: float32 [1536, 16], P('shard')
- grad_shared_in: float32 [1536, 2048], P('shard')
- grad_shared_out: float32 [1024, 1536], P('shard')
- grad_expert_in: float32 [16, 1536, 1024], P('shard')
- grad_expert_out: float32 [16, 512, 1536], P('shard')
The draws below stay inside these ranges and needn't reach their ends.
Inputs may be any that keep to these rules, and one draw needn't show every extreme that they name: `dealt_to`: the blocks come in groups of 8 consecutive ones; in each group, with q the block's place in it, the entry is q XOR m for one m of that group. `routes`: each row names 6 different experts in rising order. In the rows of one block no expert is named more than 128 times and some expert exactly 128 times; in each group of 8 consecutive blocks one expert is named exactly 128 times in every block. `slot_index`: in one block, the entries of the places that name expert e are 0 to n - 1, once each, where n is how often the block names e.
All inputs are finite; a program needn't handle non-finite values.
Results may differ from the reference program's by a relative error of at most 0.012.
Values may be sent and summed in bfloat16 or wider, within the bound.
A program may use at most 384 MiB of HBM per device.

```python
import math
import jax
import jax.numpy as jnp
import numpy as np
from jax import lax

D = 1536
HEADS = 48
CONV = 4
FF = 512
SHARED = 1024
TOP = 6
TOK_DEV = 256
SEQ_DEV = 3
INNER = 3072
XBC = 3328
PROJ = 6448
EXPERTS = 16
CAP = 128
LEN_MOST = 192
TOKENS = 8192
N_SHARD = 8
DEVICES = 32


def one_block(block_key, full_expert):
    key_order, key_shift, key_tokens = jax.random.split(block_key, 3)
    expert_order = jax.random.permutation(key_order, EXPERTS).astype(jnp.int32)
    where_full = jnp.argmax(expert_order == full_expert)
    first_expert = expert_order[0]
    expert_order = expert_order.at[where_full].set(first_expert).at[0].set(full_expert)
    mean_load = TOK_DEV * TOP // EXPERTS
    spare_load = CAP - mean_load
    load_shift = jax.random.randint(key_shift, (EXPERTS // 2,), 0, spare_load + 1).astype(jnp.int32)
    load_shift = load_shift.at[0].set(spare_load)
    paired = jnp.stack([mean_load + load_shift, mean_load - load_shift], axis=1).reshape(EXPERTS)
    counts = jnp.zeros((EXPERTS,), jnp.int32).at[expert_order].set(paired.astype(jnp.int32))
    load_ends = jnp.cumsum(counts).astype(jnp.int32)
    load_starts = load_ends - counts
    entry_index = jnp.arange(TOK_DEV * TOP, dtype=jnp.int32)
    expert_of = jnp.sum((entry_index[:, None] >= load_ends[None, :]).astype(jnp.int32), axis=1).astype(jnp.int32)
    slot_of = entry_index - load_starts[expert_of]
    token_order = jax.random.permutation(key_tokens, TOK_DEV)
    route_block = jnp.zeros((TOK_DEV, TOP), jnp.int32).at[token_order].set(expert_of.reshape(TOP, TOK_DEV).T)
    slot_block = jnp.zeros((TOK_DEV, TOP), jnp.int32).at[token_order].set(slot_of.reshape(TOP, TOK_DEV).T)
    return (route_block, slot_block)


def route_tables(key):
    group_full = jax.random.randint(jax.random.fold_in(key, 5), (DEVICES // N_SHARD,), 0, EXPERTS).astype(jnp.int32)
    block_keys = jax.random.split(jax.random.fold_in(key, 6), DEVICES)
    block_full = jnp.repeat(group_full, N_SHARD)
    route_blocks, slot_blocks = jax.vmap(one_block)(block_keys, block_full)
    return (route_blocks.reshape(DEVICES * TOK_DEV, TOP), slot_blocks.reshape(DEVICES * TOK_DEV, TOP))


def draw_routes(key, part):
    tables = route_tables(key)
    return tables[0]


def draw_slot_index(key, part):
    tables = route_tables(key)
    return tables[1]


def draw_dealt_to(key, part):
    key = jax.random.fold_in(key, 3)
    masks = jax.random.randint(key, (DEVICES // N_SHARD,), 0, N_SHARD).astype(jnp.int32)
    position = jnp.arange(DEVICES, dtype=jnp.int32) % N_SHARD
    return (position ^ jnp.repeat(masks, N_SHARD)).astype(jnp.int32)


def levels(own_key, extent, cuts, least, top_value):
    loudness = 1.0
    for axis_at, parts in cuts:
        draws = jax.random.uniform(jax.random.fold_in(jax.random.fold_in(own_key, 6), axis_at), (parts,), jnp.float32, least / len(cuts), top_value / len(cuts))
        loudness = loudness * jnp.repeat(jnp.exp(draws), extent[axis_at] // parts).reshape((-1,) + (1,) * (len(extent) - 1 - axis_at))
    return loudness


def length_profile(amount, total, most, lean):
    loads = [(1 << 20) // math.isqrt(grade ** lean) + 1 for grade in range(2, amount + 1)]
    surplus, holding = total - most - (amount - 1), [1] * (amount - 1)
    while surplus > 0:
        free = [i for i in range(amount - 1) if holding[i] < most]
        whole, left = sum([loads[i] for i in free]), surplus
        for i in free:
            addition = min(most - holding[i], max(1, left * loads[i] // whole), surplus)
            holding[i] = holding[i] + addition
            surplus = surplus - addition
    return np.array([most] + holding)


def uneven(stream_key, count, total, bound, lean):
    if count == 2:
        one = jax.random.randint(stream_key, (), max(1, total - bound), min(bound, total - 1) + 1)
        return jnp.stack([one, total - one])
    sizes = jnp.asarray(length_profile(count, total, bound, lean), jnp.int32)
    twos = (count - 1) // 2
    giver, taker = sizes[1:1 + 2 * twos:2], sizes[2:2 + 2 * twos:2]
    slack = jnp.minimum(giver - 1, bound - taker)
    shifted = jax.random.randint(jax.random.fold_in(stream_key, 1), (twos,), 0, 1 << 20) % (slack + 1)
    sizes = sizes.at[1:1 + 2 * twos:2].set(giver - shifted).at[2:2 + 2 * twos:2].set(taker + shifted)
    return sizes[jax.random.permutation(jax.random.fold_in(stream_key, 2), count)]


def normal_values(stream_key, dims, width, limit, cuts=(), held_as=jnp.bfloat16):
    gain = levels(stream_key, dims, cuts, -0.22, 0.18) if cuts else 1.0
    values = jax.random.normal(stream_key, dims, jnp.float32) * width * gain
    return jnp.minimum(jnp.maximum(values, -limit), limit).astype(held_as)


def setup_inputs(seed: int = 0) -> dict:
    splits = jax.random.split(jax.random.key(seed), 22)
    tokens = normal_values(splits[0], (TOKENS, D), 1.0, 6.0, ((0, 32),))
    cotangent = normal_values(splits[1], (TOKENS, D), 1.0, 6.0, ((0, 32),))
    dealt_to = draw_dealt_to(jax.random.fold_in(splits[21], 71), 0)
    lengths = jax.vmap(lambda own: uneven(own, SEQ_DEV, TOK_DEV, LEN_MOST, 2))(jax.random.split(splits[3], DEVICES)).reshape((DEVICES, SEQ_DEV)).astype(jnp.int32)
    routes = draw_routes(jax.random.fold_in(splits[21], 71), 0)
    slot_index = draw_slot_index(jax.random.fold_in(splits[21], 71), 0)
    in_norm = jnp.clip(1.0 + 0.1 * jax.random.normal(splits[6], (D,), jnp.float32), 0.5, 1.5).astype(jnp.bfloat16)
    in_proj = normal_values(splits[7], (D, PROJ), D ** -0.5, 0.15625, ((0, 8),))
    conv_weight = normal_values(splits[8], (CONV, XBC), CONV ** -0.5, 3.0, ((1, 8),))
    conv_bias = normal_values(splits[9], (XBC,), 0.5, 3.0, ((0, 8),))
    dt_bias = jnp.clip(-5.0 + 3.0 * jax.random.uniform(splits[10], (HEADS,), jnp.float32) ** levels(splits[10], (HEADS,), ((0, 8),), -0.2, 0.2), -5.0, -2.0).astype(jnp.bfloat16)
    decay_log = jnp.clip(-1.0 + 3.5 * jax.random.uniform(splits[11], (HEADS,), jnp.float32) ** levels(splits[11], (HEADS,), ((0, 8),), -0.2, 0.2), -1.0, 2.5).astype(jnp.bfloat16)
    skip_gain = jnp.clip(0.5 + 1.0 * jax.random.uniform(splits[12], (HEADS,), jnp.float32) ** levels(splits[12], (HEADS,), ((0, 8),), -0.2, 0.2), 0.5, 1.5).astype(jnp.bfloat16)
    mixer_norm = jnp.clip(1.0 + 0.1 * jax.random.normal(splits[13], (INNER,), jnp.float32), 0.5, 1.5).astype(jnp.bfloat16)
    out_proj = normal_values(splits[14], (INNER, D), INNER ** -0.5, 0.109375, ((0, 8),))
    post_norm = jnp.clip(1.0 + 0.1 * jax.random.normal(splits[15], (D,), jnp.float32), 0.5, 1.5).astype(jnp.bfloat16)
    router = normal_values(splits[16], (D, EXPERTS), (4 * D) ** -0.5, 0.078125, ((0, 8),))
    shared_in = normal_values(splits[17], (D, 2 * SHARED), D ** -0.5, 0.15625, ((0, 8),))
    shared_out = normal_values(splits[18], (SHARED, D), SHARED ** -0.5, 0.1875, ((0, 8),))
    expert_in = normal_values(splits[19], (EXPERTS, D, 2 * FF), D ** -0.5, 0.15625, ((0, 8),))
    expert_out = normal_values(splits[20], (EXPERTS, FF, D), (FF // 4) ** -0.5, 0.5, ((0, 8),))
    return dict(tokens=tokens, cotangent=cotangent, dealt_to=dealt_to, lengths=lengths, routes=routes, slot_index=slot_index, in_norm=in_norm, in_proj=in_proj, conv_weight=conv_weight, conv_bias=conv_bias, dt_bias=dt_bias, decay_log=decay_log, skip_gain=skip_gain, mixer_norm=mixer_norm, out_proj=out_proj, post_norm=post_norm, router=router, shared_in=shared_in, shared_out=shared_out, expert_in=expert_in, expert_out=expert_out)


EPS = 1e-05
HIGH = lax.Precision.HIGHEST
block_limit = 128

@jax.custom_vjp
def low(v):
    return lax.optimization_barrier(v.astype(jnp.bfloat16)).astype(jnp.float32)

@jax.custom_vjp
def low_back(v):
    return v

def low_keep(v):
    return (low(v), None)

def low_pass(kept, grad):
    return (grad,)

def back_keep(v):
    return (v, None)

def back_low(kept, grad):
    return (low(grad),)
low.defvjp(low_keep, low_pass)
low_back.defvjp(back_keep, back_low)

def product(left, right):
    return jnp.dot(left, right, precision=HIGH, preferred_element_type=jnp.float32)

def rms_scale(values, scale_gain):
    return values * lax.rsqrt(lax.optimization_barrier(jnp.mean(values * values, axis=-1, keepdims=True)) + EPS) * scale_gain

def segment_ids(lengths_row, row_count):
    length_ends = jnp.cumsum(lengths_row)
    position = jnp.arange(row_count, dtype=jnp.int32)
    return lax.optimization_barrier(jnp.sum((position[:, None] >= length_ends[None, :]).astype(jnp.int32), axis=1)).astype(jnp.int32)

def conv_mix(channels, conv_weight, conv_bias, seg_ids):
    row_count = channels.shape[0]
    tap_count = conv_weight.shape[0]
    result = jnp.zeros_like(channels) + conv_bias[None, :]
    for tap_index in range(tap_count):
        offset = tap_count - 1 - tap_index
        earlier = jnp.pad(channels, ((offset, 0), (0, 0)))[:row_count]
        earlier_seg = jnp.pad(seg_ids, (offset, 0), constant_values=-1)[:row_count]
        same_segment = (earlier_seg == seg_ids).astype(channels.dtype)
        result = result + conv_weight[tap_index][None, :] * earlier * same_segment[:, None]
    return result

def state_scan(inputs, step_sizes, decay_log, write_rows, read_rows, seg_ids):
    row_count, head_count, head_width = inputs.shape
    block_size = min(block_limit, row_count)
    block_count = row_count // block_size
    state_width = write_rows.shape[1]
    log_decay = -step_sizes * jnp.exp(decay_log)[None, :]
    scaled = inputs * step_sizes[:, :, None]
    causal_mask = jnp.arange(block_size)[:, None] >= jnp.arange(block_size)[None, :]

    def advance(carry_in, pieces):
        carried_state, last_seg = carry_in
        block_log, block_input, block_write, block_read, block_seg = pieces
        cumulative = jnp.cumsum(block_log, axis=0)
        keep_mask = causal_mask & (block_seg[:, None] == block_seg[None, :])
        log_gaps = jnp.where(keep_mask[:, :, None], cumulative[:, None, :] - cumulative[None, :, :], 0.0)
        weights = jnp.exp(log_gaps) * keep_mask[:, :, None].astype(log_gaps.dtype)
        scores = jnp.dot(block_read, block_write.T, precision=HIGH)
        inner_part = jnp.einsum('tsh,shp->thp', scores[:, :, None] * weights, block_input, precision=HIGH)
        carried_flag = (block_seg == last_seg).astype(cumulative.dtype)
        entry_decay = jnp.exp(cumulative) * carried_flag[:, None]
        outer_part = jnp.einsum('tn,hnp->thp', block_read, carried_state, precision=HIGH) * entry_decay[:, :, None]
        end_seg = block_seg[-1]
        tail_weights = jnp.exp(cumulative[-1][None, :] - cumulative) * (block_seg == end_seg).astype(cumulative.dtype)[:, None]
        fresh_state = jnp.einsum('sn,sh,shp->hnp', block_write, tail_weights, block_input, precision=HIGH)
        through = jnp.exp(cumulative[-1]) * (end_seg == last_seg).astype(cumulative.dtype)
        carried_state = carried_state * through[:, None, None] + fresh_state
        return ((carried_state, end_seg), inner_part + outer_part)
    start_carry = (jnp.zeros((head_count, state_width, head_width), inputs.dtype), jnp.array(-1, jnp.int32))
    pieces = (log_decay.reshape(block_count, block_size, head_count), scaled.reshape(block_count, block_size, head_count, head_width), write_rows.reshape(block_count, block_size, state_width), read_rows.reshape(block_count, block_size, state_width), seg_ids.reshape(block_count, block_size))
    final_carry, outputs = lax.scan(advance, start_carry, pieces)
    return outputs.reshape(row_count, head_count, head_width)

def mixer_middle(projected, conv_weight, conv_bias, dt_shift, decay_log, skip_gain, norm_gain, seg_ids):
    inner_width = norm_gain.shape[0]
    xbc_width = conv_bias.shape[0]
    row_count = projected.shape[0]
    head_count = decay_log.shape[0]
    head_width = inner_width // head_count
    state_width = (xbc_width - inner_width) // 2
    gate_side = projected[:, :inner_width]
    channels = projected[:, inner_width:inner_width + xbc_width]
    dt_raw = projected[:, inner_width + xbc_width:]
    activated = jax.nn.silu(conv_mix(channels, conv_weight, conv_bias, seg_ids))
    values_in = activated[:, :inner_width].reshape(row_count, head_count, head_width)
    write_rows = activated[:, inner_width:inner_width + state_width]
    read_rows = activated[:, inner_width + state_width:]
    step_sizes = jax.nn.softplus(dt_raw + dt_shift[None, :])
    scanned = state_scan(values_in, step_sizes, decay_log, write_rows, read_rows, seg_ids)
    scanned = scanned + skip_gain[None, :, None] * values_in
    gated = scanned.reshape(row_count, inner_width) * jax.nn.silu(gate_side)
    return rms_scale(gated, norm_gain)

def pack_forward(params, rows_in, seg_ids, route_rows, slot_rows):
    in_norm, in_proj, conv_weight, conv_bias, dt_bias, decay_log, skip_gain, mixer_norm, out_proj, post_norm, router, shared_in, shared_out, expert_in, expert_out = params
    first_low = low(rms_scale(rows_in, in_norm))
    projected = low_back(product(first_low, in_proj))
    normed = mixer_middle(projected, conv_weight, conv_bias, dt_bias, decay_log, skip_gain, mixer_norm, seg_ids)
    mixer_result = low_back(product(low(normed), out_proj))
    after_mixer = rows_in + mixer_result
    second = low(rms_scale(after_mixer, post_norm))
    logits = low_back(product(second, router))
    picked = jnp.take_along_axis(logits, route_rows, axis=1)
    gate_weights = jax.nn.softmax(picked, axis=1)
    shared_pre = low_back(product(second, shared_in))
    shared_half = shared_pre.shape[1] // 2
    shared_hidden = low(jax.nn.silu(shared_pre[:, :shared_half]) * shared_pre[:, shared_half:])
    shared_result = low_back(product(shared_hidden, shared_out))
    flat_slot = (route_rows * CAP + slot_rows).reshape(-1)
    buffer = jnp.zeros((EXPERTS * CAP, D), rows_in.dtype).at[flat_slot].set(jnp.repeat(second, TOP, axis=0))
    buffer = low_back(buffer).reshape(EXPERTS, CAP, D)
    expert_pre = low_back(jnp.einsum('ecd,edf->ecf', buffer, expert_in, precision=HIGH))
    expert_half = expert_pre.shape[2] // 2
    expert_hidden = low(jax.nn.silu(expert_pre[:, :, :expert_half]) * expert_pre[:, :, expert_half:])
    expert_result = low_back(low(jnp.einsum('ecf,efd->ecd', expert_hidden, expert_out, precision=HIGH)))
    returned = expert_result.reshape(EXPERTS * CAP, D)[flat_slot].reshape(TOK_DEV, TOP, D)
    routed = lax.optimization_barrier(jnp.sum(gate_weights[:, :, None] * returned, axis=1))
    return after_mixer + shared_result + routed

def reference(tokens, cotangent, dealt_to, lengths, routes, slot_index, in_norm, in_proj, conv_weight, conv_bias, dt_bias, decay_log, skip_gain, mixer_norm, out_proj, post_norm, router, shared_in, shared_out, expert_in, expert_out):
    params = (in_norm.astype(jnp.float32), in_proj.astype(jnp.float32), conv_weight.astype(jnp.float32), conv_bias.astype(jnp.float32), dt_bias.astype(jnp.float32), decay_log.astype(jnp.float32), skip_gain.astype(jnp.float32), mixer_norm.astype(jnp.float32), out_proj.astype(jnp.float32), post_norm.astype(jnp.float32), router.astype(jnp.float32), shared_in.astype(jnp.float32), shared_out.astype(jnp.float32), expert_in.astype(jnp.float32), expert_out.astype(jnp.float32))
    blocks_in = tokens.astype(jnp.float32).reshape(DEVICES, TOK_DEV, D)
    group_start = jnp.arange(DEVICES, dtype=jnp.int32) // N_SHARD * N_SHARD
    source = (group_start + dealt_to.astype(jnp.int32)).astype(jnp.int32)

    def block_segments(lengths_row):
        return segment_ids(lengths_row, TOK_DEV)
    seg_all = jax.vmap(block_segments)(lengths)[source]
    route_all = routes.reshape(DEVICES, TOK_DEV, TOP)[source]
    slot_all = slot_index.reshape(DEVICES, TOK_DEV, TOP)[source]
    one_pack = jax.checkpoint(pack_forward)

    def forward(weights, blocks):

        def visit_block(carry_in, pieces):
            return (carry_in, one_pack(weights, pieces[0], pieces[1], pieces[2], pieces[3]))
        final_carry, outputs = lax.scan(visit_block, jnp.zeros((), jnp.float32), (blocks, seg_all, route_all, slot_all))
        return outputs
    outputs, pullback = jax.vjp(forward, params, blocks_in)
    grad_weights, grad_blocks = pullback(cotangent.astype(jnp.float32).reshape(DEVICES, TOK_DEV, D))
    return (outputs.reshape(TOKENS, D).astype(jnp.bfloat16), grad_blocks.reshape(TOKENS, D).astype(jnp.bfloat16), grad_weights[0], grad_weights[1], grad_weights[2], grad_weights[3], grad_weights[4], grad_weights[5], grad_weights[6], grad_weights[7], grad_weights[8], grad_weights[9], grad_weights[10], grad_weights[11], grad_weights[12], grad_weights[13], grad_weights[14])
```

```python
import functools

import jax
import jax.numpy as jnp
from jax import lax
from jax.experimental import pallas as pl
from jax.experimental.pallas import tpu as pltpu
from jax.sharding import Mesh
from jax.sharding import PartitionSpec as P

EPS = 1e-05
HIGH = lax.Precision.HIGHEST
F32 = jnp.float32
BF16 = jnp.bfloat16
ALL = ("rep", "z", "core")
COLUMN = ("z", "core")
PLANE = ("rep", "core")
LANES = 128


def rms_rows(values):
    return lax.rsqrt(jnp.mean(values * values, axis=-1, keepdims=True) + EPS)


def mm(left, right):
    return jnp.dot(left, right, preferred_element_type=F32)


def mm_nt(left, right):
    return lax.dot_general(left, right, (((1,), (1,)), ((), ())), preferred_element_type=F32)


def mm_tn(left, right):
    return lax.dot_general(left, right, (((0,), (0,)), ((), ())), preferred_element_type=F32)


def silu_slope(values, sig):
    return sig * (1.0 + values * (1.0 - sig))


def split_two(values):
    high = values.astype(BF16)
    return high, (values - high.astype(F32)).astype(BF16)


class Block:
    def __init__(self, proj, seg_col, seg_row, taps, heads, channels, width, state):
        rows = proj.shape[0]
        self.rows, self.channels, self.width, self.state = rows, channels, width, state
        self.gate = proj[:, :channels]
        self.xbc = proj[:, channels : 2 * channels + 2 * state]
        self.turn = lax.axis_index("core") * (LANES // 2)
        dt_raw = pltpu.roll(proj[:, 2 * channels + 2 * state :], self.turn, 1)
        position = lax.broadcasted_iota(jnp.int32, (rows, 1), 0)
        seg_wide = jnp.broadcast_to(seg_col, (rows, LANES))
        self.masks = []
        conv = taps[4:5, :] + taps[3:4, :] * self.xbc
        for offset in (1, 2, 3):
            before = pltpu.roll(seg_wide, offset, 0)[:, :1]
            mask = jnp.where((before == seg_col) & (position >= offset), 1.0, 0.0)
            self.masks.append(mask)
            conv = conv + taps[3 - offset : 4 - offset, :] * (mask * pltpu.roll(self.xbc, offset, 0))
        self.conv = conv
        self.conv_sig = jax.nn.sigmoid(conv)
        act = conv * self.conv_sig
        self.xin = act[:, :channels]
        self.write = act[:, channels : channels + state].astype(BF16)
        self.read = act[:, channels + state :].astype(BF16)
        shifted = dt_raw + heads[0:1, :]
        self.step = jnp.maximum(shifted, 0.0) + jnp.log1p(jnp.exp(-jnp.abs(shifted)))
        self.step_sig = jax.nn.sigmoid(shifted)
        self.speed = heads[1:2, :]
        self.rate = -self.step * self.speed
        row_at = lax.broadcasted_iota(jnp.int32, (rows, rows), 0)
        col_at = lax.broadcasted_iota(jnp.int32, (rows, rows), 1)
        self.causal = row_at >= col_at
        self.keep = self.causal & (seg_col == seg_row)
        self.cum = jnp.dot(self.causal.astype(F32), self.rate, precision=HIGH, preferred_element_type=F32)
        self.cum_t = self.cum.T
        self.scores = jnp.where(self.keep, mm_nt(self.read, self.write), 0.0)

    def groups(self):
        for start in range(0, self.channels, LANES):
            stop = min(start + LANES, self.channels)
            yield start, stop, list(range(start // self.width, (stop - 1) // self.width + 1))

    def spread(self, columns, start, stop, heads):
        lane = lax.broadcasted_iota(jnp.int32, (self.rows, stop - start), 1) + start
        result = jnp.broadcast_to(columns[:, heads[0] : heads[0] + 1], (self.rows, stop - start))
        for head in heads[1:]:
            result = jnp.where(lane >= head * self.width, columns[:, head : head + 1], result)
        return result

    def inside(self, start, stop, head):
        lane = lax.broadcasted_iota(jnp.int32, (self.rows, stop - start), 1) + start
        return (lane >= head * self.width) & (lane < (head + 1) * self.width)

    def decay(self, head):
        gaps = self.cum[:, head : head + 1] - self.cum_t[head : head + 1, :]
        return jnp.exp(jnp.where(self.keep, gaps, 0.0))


def mixer_forward_kernel(
    channels, width, state,
    x_ref, gain_ref, weight_ref, seg_col_ref, seg_row_ref, taps_ref, heads_ref, skip_ref, norm_ref, out_ref,
    part_ref, square_ref, proj_ref,
):
    x = x_ref[...].astype(F32)
    first = (x * rms_rows(x) * gain_ref[...]).astype(BF16)
    proj = mm(first, weight_ref[...])
    proj_ref[...] = proj
    block = Block(proj, seg_col_ref[...], seg_row_ref[...], taps_ref[...], heads_ref[...], channels, width, state)
    rows = block.rows
    mixed = []
    for start, stop, heads in block.groups():
        xin = block.xin[:, start:stop]
        scaled = (xin * block.spread(block.step, start, stop, heads)).astype(BF16)
        y = None
        for head in heads:
            weights = (block.scores * block.decay(head)).astype(BF16)
            term = mm(weights, scaled)
            y = term if y is None else jnp.where(block.inside(start, stop, head), term, y)
        gate = block.gate[:, start:stop]
        mixed.append((y + skip_ref[:, start:stop] * xin) * gate * jax.nn.sigmoid(gate))
    mixed = jnp.concatenate(mixed, axis=1)
    square_ref[...] = row_of(jnp.sum(mixed * mixed, axis=1, keepdims=True), rows)
    part_ref[...] = mm((mixed * norm_ref[...]).astype(BF16), out_ref[...]).astype(BF16)


def mixer_backward_kernel(
    channels, width, state,
    x_ref, gain_ref, weight_ref, seg_col_ref, seg_row_ref, taps_ref, heads_ref, skip_ref, norm_ref, out_ref,
    proj_ref, low_ref, scale_ref,
    back_ref, in_grad_ref, out_grad_ref, taps_grad_ref, heads_grad_ref, wide_grad_ref,
):
    block_at = pl.program_id(0)

    @pl.when(block_at == 0)
    def _():
        in_grad_ref[...] = jnp.zeros_like(in_grad_ref)
        out_grad_ref[...] = jnp.zeros_like(out_grad_ref)
        taps_grad_ref[...] = jnp.zeros_like(taps_grad_ref)
        heads_grad_ref[...] = jnp.zeros_like(heads_grad_ref)
        wide_grad_ref[...] = jnp.zeros_like(wide_grad_ref)

    block = Block(
        proj_ref[...], seg_col_ref[...], seg_row_ref[...], taps_ref[...], heads_ref[...], channels, width, state
    )
    rows = block.rows
    low = low_ref[...]
    scale = column_of(scale_ref[0, 0:1, :], rows)
    pull = column_of(scale_ref[1, 0:1, :], rows)
    normed_grad = mm_nt(low, out_ref[...])
    taps = taps_ref[...]
    gate_grads, x_grads, mixed_all, norm_grads, skip_grads = [], [], [], [], []
    step_grad = jnp.zeros((rows, LANES), F32)
    cum_grad = jnp.zeros((rows, LANES), F32)
    cum_grad_t = jnp.zeros((LANES, rows), F32)
    score_grad = jnp.zeros((rows, rows), F32)
    lane_all = lax.broadcasted_iota(jnp.int32, (rows, LANES), 1)
    sub_all = lax.broadcasted_iota(jnp.int32, (LANES, rows), 0)
    for start, stop, heads in block.groups():
        xin = block.xin[:, start:stop]
        spread = block.spread(block.step, start, stop, heads)
        scaled = (xin * spread).astype(BF16)
        weights, decays = [], []
        y = None
        for head in heads:
            decays.append(block.decay(head))
            weights.append(block.scores * decays[-1])
            term = mm(weights[-1].astype(BF16), scaled)
            y = term if y is None else jnp.where(block.inside(start, stop, head), term, y)
        skip = skip_ref[:, start:stop]
        y = y + skip * xin
        gate = block.gate[:, start:stop]
        gate_sig = jax.nn.sigmoid(gate)
        gate_act = gate * gate_sig
        mixed = y * gate_act
        mixed_all.append(mixed)
        q = normed_grad[:, start:stop]
        norm_grads.append(jnp.sum(mixed * scale * q, axis=0, keepdims=True))
        mixed_grad = scale * norm_ref[:, start:stop] * q - mixed * pull
        gate_grads.append(mixed_grad * y * silu_slope(gate, gate_sig))
        y_grad = mixed_grad * gate_act
        skip_grads.append(jnp.sum(y_grad * xin, axis=0, keepdims=True))
        y_low = y_grad.astype(BF16)
        scaled_grad = None
        for at, head in enumerate(heads):
            inside = block.inside(start, stop, head)
            term = mm_tn(weights[at].astype(BF16), y_low)
            scaled_grad = term if scaled_grad is None else jnp.where(inside, term, scaled_grad)
            pair_grad = mm_nt(jnp.where(inside, y_low, jnp.zeros_like(y_low)), scaled)
            score_grad = score_grad + pair_grad * decays[at]
            exponent_grad = pair_grad * weights[at]
            cum_grad = jnp.where(lane_all == head, jnp.sum(exponent_grad, axis=1, keepdims=True), cum_grad)
            cum_grad_t = jnp.where(sub_all == head, jnp.sum(exponent_grad, axis=0, keepdims=True), cum_grad_t)
        for head in heads:
            inside = block.inside(start, stop, head)
            per_row = jnp.sum(jnp.where(inside, scaled_grad * xin, 0.0), axis=1, keepdims=True)
            step_grad = jnp.where(lane_all == head, per_row, step_grad)
        x_grads.append(scaled_grad * spread + skip * y_grad)
    score_grad = jnp.where(block.keep, score_grad, 0.0).astype(BF16)
    read_grad = mm(score_grad, block.write)
    write_grad = mm_tn(score_grad, block.read)
    cum_grad = cum_grad - cum_grad_t.T
    rate_grad = lax.dot_general(
        block.causal.astype(F32), cum_grad, (((0,), (0,)), ((), ())), precision=HIGH, preferred_element_type=F32
    )
    step_grad = step_grad - block.speed * rate_grad
    dt_grad = step_grad * block.step_sig
    heads_grad_ref[0:1, :] += jnp.sum(dt_grad, axis=0, keepdims=True)
    heads_grad_ref[1:2, :] += jnp.sum(rate_grad * block.rate, axis=0, keepdims=True)
    act_grad = jnp.concatenate(x_grads + [write_grad, read_grad], axis=1)
    conv_grad = act_grad * silu_slope(block.conv, block.conv_sig)
    taps_grad_ref[4:5, :] += jnp.sum(conv_grad, axis=0, keepdims=True)
    taps_grad_ref[3:4, :] += jnp.sum(conv_grad * block.xbc, axis=0, keepdims=True)
    xbc_grad = taps[3:4, :] * conv_grad
    for offset in (1, 2, 3):
        masked = conv_grad * block.masks[offset - 1]
        taps_grad_ref[3 - offset : 4 - offset, :] += jnp.sum(
            masked * pltpu.roll(block.xbc, offset, 0), axis=0, keepdims=True
        )
        xbc_grad = xbc_grad + taps[3 - offset : 4 - offset, :] * pltpu.roll(masked, rows - offset, 0)
    wide_grad_ref[0:1, :] += jnp.concatenate(norm_grads, axis=1)
    wide_grad_ref[1:2, :] += jnp.concatenate(skip_grads, axis=1)
    proj_grad = jnp.concatenate(gate_grads + [xbc_grad, pltpu.roll(dt_grad, block.turn, 1)], axis=1).astype(BF16)
    back_ref[...] = mm_nt(proj_grad, weight_ref[...]).astype(BF16)
    x = x_ref[...].astype(F32)
    first = (x * rms_rows(x) * gain_ref[...]).astype(BF16)
    in_grad_ref[...] += mm_tn(first, proj_grad)
    normed = (jnp.concatenate(mixed_all, axis=1) * scale * norm_ref[...]).astype(BF16)
    out_grad_ref[...] += mm_tn(normed, low)


def whole(shape):
    return pl.BlockSpec(shape, lambda i: (0,) * len(shape))


def by_rows(shape):
    return pl.BlockSpec(shape, lambda i: (i,) + (0,) * (len(shape) - 1))


def mixer_specs(rows, model, channels, state):
    wide = 2 * channels + 2 * state + LANES
    return [
        by_rows((rows, model)),
        whole((1, model)),
        whole((model, wide)),
        by_rows((rows, 1)),
        pl.BlockSpec((None, 1, rows), lambda i: (i, 0, 0)),
        whole((8, channels + 2 * state)),
        whole((8, LANES)),
        whole((1, channels)),
        whole((1, channels)),
        whole((channels, model)),
    ]


def mixer_forward(args, rows, channels, width, state):
    total, model = args[0].shape
    wide = 2 * channels + 2 * state + LANES
    return pl.pallas_call(
        functools.partial(mixer_forward_kernel, channels, width, state),
        grid=(total // rows,),
        in_specs=mixer_specs(rows, model, channels, state),
        out_specs=[
            by_rows((rows, model)),
            pl.BlockSpec((None, 8, rows), lambda i: (i, 0, 0)),
            by_rows((rows, wide)),
        ],
        out_shape=[
            jax.ShapeDtypeStruct((total, model), BF16),
            jax.ShapeDtypeStruct((total // rows, 8, rows), F32),
            jax.ShapeDtypeStruct((total, wide), F32),
        ],
        compiler_params=pltpu.CompilerParams(vmem_limit_bytes=56 * 2**20),
        name="mixer_forward",
    )(*args)


def mixer_backward(args, proj, low, scale, rows, channels, width, state):
    total, model = args[0].shape
    wide = 2 * channels + 2 * state + LANES
    return pl.pallas_call(
        functools.partial(mixer_backward_kernel, channels, width, state),
        grid=(total // rows,),
        in_specs=mixer_specs(rows, model, channels, state)
        + [
            by_rows((rows, wide)),
            by_rows((rows, model)),
            pl.BlockSpec((None, 2, 8, rows), lambda i: (i, 0, 0, 0)),
        ],
        out_specs=[
            by_rows((rows, model)),
            whole((model, wide)),
            whole((channels, model)),
            whole((8, channels + 2 * state)),
            whole((8, LANES)),
            whole((8, channels)),
        ],
        out_shape=[
            jax.ShapeDtypeStruct((total, model), BF16),
            jax.ShapeDtypeStruct((model, wide), F32),
            jax.ShapeDtypeStruct((channels, model), F32),
            jax.ShapeDtypeStruct((8, channels + 2 * state), F32),
            jax.ShapeDtypeStruct((8, LANES), F32),
            jax.ShapeDtypeStruct((8, channels), F32),
        ],
        compiler_params=pltpu.CompilerParams(vmem_limit_bytes=60 * 2**20),
        name="mixer_backward",
    )(*args, proj, low, scale)


MESH_ID = pl.DeviceIdType.MESH


def when(condition, action):
    if condition is True:
        action()
    elif condition is not False:
        pl.when(condition)(action)


class Place:
    def __init__(self, reps, depth):
        self.reps, self.depth = reps, depth
        self.rep, self.z, self.core = lax.axis_index("rep"), lax.axis_index("z"), lax.axis_index("core")
        self.here = {"rep": self.rep, "z": self.z, "core": self.core}
        self.pending = []

    def device(self, **changes):
        return {**self.here, **changes}

    def sibling(self):
        return self.device(core=1 - self.core)

    def rep_at(self, distance):
        return lax.rem(self.rep + distance, self.reps)

    def barrier(self, plane=False, column=False, everyone=False):
        semaphore = pltpu.get_barrier_semaphore()

        def greet(device):
            pl.semaphore_signal(semaphore, inc=1, device_id=device, device_id_type=MESH_ID)

        if everyone:
            count = self.reps * self.depth * 2
            mine = (self.rep * self.depth + self.z) * 2 + self.core

            def step(distance, carry):
                other = lax.rem(mine + distance, count)
                greet({"rep": other // (2 * self.depth), "z": lax.rem(other // 2, self.depth), "core": lax.rem(other, 2)})
                return carry

            lax.fori_loop(1, count, step, 0)
            pl.semaphore_wait(semaphore, count - 1)
            return
        amount = 1
        greet(self.sibling())
        if plane:
            for distance in range(1, self.reps):
                greet(self.device(rep=self.rep_at(distance)))
            amount = amount + self.reps - 1
        if column:
            above, below = self.z < self.depth - 1, self.z > 0
            when(above, lambda: greet(self.device(z=self.z + 1)))
            when(below, lambda: greet(self.device(z=self.z - 1)))
            amount = amount + jnp.where(above, 1, 0) + jnp.where(below, 1, 0)
        pl.semaphore_wait(semaphore, amount)

    def send(self, source, target, send_sem, recv_sem, device, condition=True):
        copy = pltpu.make_async_remote_copy(
            src_ref=source, dst_ref=target, send_sem=send_sem, recv_sem=recv_sem, device_id=device,
            device_id_type=MESH_ID,
        )
        when(condition, copy.start)
        self.pending.append((condition, copy))

    def local(self, source, target, sem):
        copy = pltpu.make_async_copy(source, target, sem)
        copy.start()
        return copy

    def arrived(self, target, recv_sem, condition=True):
        copy = pltpu.make_async_remote_copy(
            src_ref=target, dst_ref=target, send_sem=recv_sem, recv_sem=recv_sem, device_id=self.sibling(),
            device_id_type=MESH_ID,
        )
        when(condition, copy.wait_recv)

    def finish(self):
        for condition, copy in self.pending:
            when(condition, copy.wait_send)
        self.pending = []


class PlaneGather:
    @staticmethod
    def scratch(reps):
        return [pltpu.SemaphoreType.DMA((4, reps)), pltpu.SemaphoreType.DMA((1,))]

    def __init__(self, place, own, out, sems, local_sem):
        self.place, self.out, self.sems = place, out, sems
        p = place
        self.keep = p.local(own, out.at[p.rep, p.core], local_sem.at[0])
        for distance in range(1, p.reps):
            p.send(own, out.at[p.rep, p.core], sems.at[0, distance], sems.at[1, distance],
                   p.device(rep=p.rep_at(distance)))
        p.send(own, out.at[p.rep, p.core], sems.at[2, 0], sems.at[3, 0], p.sibling())

    def relay(self):
        p = self.place
        for distance in range(1, p.reps):
            source = self.out.at[p.rep_at(p.reps - distance), p.core]
            p.arrived(source, self.sems.at[1, distance])
            p.send(source, source, self.sems.at[2, distance], self.sems.at[3, distance], p.sibling())

    def finish(self):
        p = self.place
        self.keep.wait()
        for distance in range(p.reps):
            source = p.rep_at(p.reps - distance) if distance else p.rep
            p.arrived(self.out.at[source, 1 - p.core], self.sems.at[3, distance])


class ColumnGather:
    @staticmethod
    def scratch(depth):
        return [pltpu.SemaphoreType.DMA((8, depth)), pltpu.SemaphoreType.DMA((1,))]

    def __init__(self, place, own, slot, sems, local_sem, shared=None, keep=True):
        self.place, self.slot, self.sems, self.shared = place, slot, sems, shared
        p = place
        self.keep = p.local(own, slot(p.z), local_sem.at[0]) if keep else None
        self.onward(own, slot(p.z), 0, True, True)
        if shared is not None:
            p.send(own, slot(p.z), sems.at[4, 0], sems.at[5, 0], p.sibling())

    def onward(self, source, target, distance, up, down):
        p = self.place
        if up is not False:
            p.send(source, target, self.sems.at[0, distance], self.sems.at[1, distance], p.device(z=p.z + 1),
                   (p.z < p.depth - 1) if up is True else up & (p.z < p.depth - 1))
        if down is not False:
            p.send(source, target, self.sems.at[2, distance], self.sems.at[3, distance], p.device(z=p.z - 1),
                   (p.z > 0) if down is True else down & (p.z > 0))

    def hop(self, distance):
        p = self.place
        below, above = p.z >= distance, p.z + distance < p.depth
        low, high = self.slot(jnp.maximum(p.z - distance, 0)), self.slot(jnp.minimum(p.z + distance, p.depth - 1))
        p.arrived(low, self.sems.at[1, distance - 1], below)
        self.onward(low, low, distance, below, False)
        if self.shared is not None:
            p.send(low, low, self.sems.at[4, distance], self.sems.at[5, distance], p.sibling(), below)
        p.arrived(high, self.sems.at[3, distance - 1], above)
        self.onward(high, high, distance, False, above)
        if self.shared is not None:
            p.send(high, high, self.sems.at[6, distance], self.sems.at[7, distance], p.sibling(), above)

    def finish(self):
        p = self.place
        if self.keep is not None:
            self.keep.wait()
        if self.shared is None:
            return
        p.arrived(self.shared(p.z), self.sems.at[5, 0])
        for distance in range(1, p.depth):
            below, above = p.z >= distance, p.z + distance < p.depth
            p.arrived(self.shared(jnp.maximum(p.z - distance, 0)), self.sems.at[5, distance], below)
            p.arrived(self.shared(jnp.minimum(p.z + distance, p.depth - 1)), self.sems.at[7, distance], above)


def add_up(*terms):
    total = terms[0].astype(F32)
    for term in terms[1:]:
        total = total + term.astype(F32)
    return total


class PlaneSum:
    @staticmethod
    def scratch(reps, shape, dtype):
        return [
            pltpu.VMEM((reps,) + shape, dtype), pltpu.VMEM((reps,) + shape, dtype), pltpu.VMEM((reps,) + shape, dtype),
            pltpu.SemaphoreType.DMA((4, reps)),
        ]

    def __init__(self, place, parts, pair, out, into, sems):
        self.place, self.parts, self.pair, self.out, self.into, self.sems = place, parts, pair, out, into, sems
        p = place
        for distance in list(range(1, p.reps)) + [0]:
            rep = p.rep_at(distance) if distance else p.rep
            p.send(parts.at[rep, 1 - p.core], pair.at[distance], sems.at[0, distance], sems.at[1, distance], p.sibling())

    def relay(self):
        p = self.place
        for distance in range(1, p.reps):
            rep = p.rep_at(distance)
            p.arrived(self.pair.at[distance], self.sems.at[1, distance])
            self.out[distance] = add_up(self.parts[rep, p.core], self.pair[distance]).astype(self.out.dtype)
            p.send(self.out.at[distance], self.into.at[distance], self.sems.at[2, distance], self.sems.at[3, distance],
                   p.device(rep=rep))

    def total(self):
        p = self.place
        p.arrived(self.pair.at[0], self.sems.at[1, 0])
        terms = [self.parts[p.rep, p.core], self.pair[0]]
        for distance in range(1, p.reps):
            p.arrived(self.into.at[distance], self.sems.at[3, distance])
            terms.append(self.into[distance])
        return add_up(*terms)


class ColumnSum:
    @staticmethod
    def scratch(depth, shape, dtype):
        return [
            pltpu.VMEM((depth,) + shape, dtype), pltpu.VMEM((2, depth) + shape, dtype),
            pltpu.VMEM((2, depth) + shape, dtype), pltpu.SemaphoreType.DMA((2, depth)),
            pltpu.SemaphoreType.DMA((4, depth)),
        ]

    def __init__(self, place, parts, pair, out, into, pair_sems, sems):
        self.place, self.parts, self.pair, self.out, self.into = place, parts, pair, out, into
        self.pair_sems, self.sems = pair_sems, sems
        p = place
        for distance in list(range(p.depth - 1, 0, -1)) + [0]:
            at = lax.rem(p.z + distance, p.depth)
            p.send(parts.at[at, 1 - p.core], pair.at[at], pair_sems.at[0, at], pair_sems.at[1, at], p.sibling())
        for distance in list(range(p.depth - 1, 0, -1)) + [0]:
            at = lax.rem(p.z + distance, p.depth)
            p.arrived(pair.at[at], pair_sems.at[1, at])

    def step(self, at):
        p = self.place
        last = p.depth - 1
        for way, towards, goal, first, valid in (
            (0, p.z + 1, last - (at - p.z), p.z == 0, (at >= p.z) & (last - (at - p.z) > p.z)),
            (1, p.z - 1, at - (last - p.z), p.z == last, (at >= last - p.z) & (at - (last - p.z) < p.z)),
        ):
            goal = jnp.clip(goal, 0, last)
            p.arrived(self.into.at[way, goal], self.sems.at[2 * way + 1, goal], valid & jnp.logical_not(first))

            def start(goal=goal, way=way):
                self.out[way, goal] = add_up(self.parts[goal, p.core], self.pair[goal]).astype(self.out.dtype)

            def follow(goal=goal, way=way):
                self.out[way, goal] = add_up(
                    self.parts[goal, p.core], self.pair[goal], self.into[way, goal]
                ).astype(self.out.dtype)

            when(valid & first, start)
            when(valid & jnp.logical_not(first), follow)
            p.send(self.out.at[way, goal], self.into.at[way, goal], self.sems.at[2 * way, goal],
                   self.sems.at[2 * way + 1, goal], p.device(z=towards), valid)

    def total(self, result):
        p = self.place
        result[...] = add_up(self.parts[p.z, p.core], self.pair[p.z])
        for way, condition in ((0, p.z > 0), (1, p.z < p.depth - 1)):
            p.arrived(self.into.at[way, p.z], self.sems.at[2 * way + 1, p.z], condition)

            def add(way=way):
                result[...] += self.into[way, p.z].astype(F32)

            when(condition, add)


def anywhere(count):
    return [pl.BlockSpec(memory_space=pl.ANY)] * count


def in_vmem(count):
    return [pl.BlockSpec(memory_space=pltpu.VMEM)] * count


def remote_params(identity, mebibytes=60):
    return pltpu.CompilerParams(
        collective_id=identity, has_side_effects=True, vmem_limit_bytes=mebibytes * 2**20
    )


def start_gather(tokens, own_pair, other_pair, common, pack, numbers, out_quarters, reps, depth):
    rows, model = tokens.shape
    part, side = own_pair.shape
    wide = side + common.shape[1]

    def kernel(x_ref, own_ref, other_ref, common_ref, pack_ref, numbers_ref, quarters_ref,
               x_out, weight_out, pack_out, numbers_out, out_out, mid_out,
               x_sems, x_local, a_sems, a_local, b_sems, b_local, c_sems, c_local, p_sems, p_local,
               n_sems, n_local, o_sems, o_local, e_sems, swap_sems):
        p = Place(reps, depth)
        p.barrier(everyone=True)

        def left(core):
            return lambda z: weight_out.at[z, core, :, pl.ds(0, side)]

        def right(core):
            return lambda z: weight_out.at[z, core, :, pl.ds(side, wide - side)]

        slot = left(p.core)
        p.send(other_ref, slot(p.z), swap_sems.at[0], swap_sems.at[1], p.sibling())
        pack_job = ColumnGather(p, pack_ref, lambda z: pack_out.at[z, p.core], p_sems, p_local,
                                shared=lambda z: pack_out.at[z, 1 - p.core])
        count = reps * depth * 2
        mine = (p.rep * depth + p.z) * 2 + p.core
        number_keep = p.local(numbers_ref, numbers_out.at[mine], n_local.at[0])

        def number_copy(distance, other):
            return pltpu.make_async_remote_copy(
                src_ref=numbers_ref, dst_ref=numbers_out.at[mine], send_sem=n_sems.at[0, distance],
                recv_sem=n_sems.at[1, distance],
                device_id={"rep": other // (2 * depth), "z": lax.rem(other // 2, depth), "core": lax.rem(other, 2)},
                device_id_type=MESH_ID,
            )

        def number_send(distance, carry):
            number_copy(distance, lax.rem(mine + distance, count)).start()
            return carry

        lax.fori_loop(1, count, number_send, 0)
        job_a = ColumnGather(p, own_ref, slot, a_sems, a_local)
        job_c = ColumnGather(p, common_ref, right(p.core), c_sems, c_local, shared=right(1 - p.core))
        x_job = PlaneGather(p, x_ref, x_out, x_sems, x_local)
        other = left(1 - p.core)
        p.arrived(other(p.z), swap_sems.at[1])
        job_b = ColumnGather(p, other(p.z), other, b_sems, b_local, keep=False)
        job_o = ColumnGather(p, quarters_ref.at[p.rep], lambda z: mid_out.at[z], o_sems, o_local)
        for distance in range(1, depth):
            pack_job.hop(distance)
            job_a.hop(distance)
            job_c.hop(distance)
            job_b.hop(distance)
            if distance == 1:
                x_job.relay()
            job_o.hop(distance)
        job_o.finish()
        for distance in range(1, reps):
            rep = p.rep_at(distance)
            p.send(mid_out.at[rep], out_out.at[p.rep], e_sems.at[0, distance], e_sems.at[1, distance], p.device(rep=rep))
        out_keep = p.local(mid_out.at[p.rep], out_out.at[p.rep], o_local.at[0])
        for job in (x_job, pack_job, job_a, job_b, job_c):
            job.finish()
        number_keep.wait()

        def number_wait(distance, carry):
            copy = number_copy(distance, lax.rem(mine + distance, count))
            copy.wait_send()
            copy.wait_recv()
            return carry

        lax.fori_loop(1, count, number_wait, 0)
        out_keep.wait()
        for distance in range(1, reps):
            p.arrived(out_out.at[p.rep_at(reps - distance)], e_sems.at[1, distance])
        p.finish()

    quarter = out_quarters.shape[1]
    return pl.pallas_call(
        kernel,
        in_specs=anywhere(7),
        out_specs=anywhere(6),
        out_shape=[
            jax.ShapeDtypeStruct((reps, 2, rows, model), BF16),
            jax.ShapeDtypeStruct((depth, 2, part, wide), BF16),
            jax.ShapeDtypeStruct((depth, 2) + pack.shape, BF16),
            jax.ShapeDtypeStruct((reps * depth * 2,) + numbers.shape, jnp.int32),
            jax.ShapeDtypeStruct((reps, quarter, model), BF16),
            jax.ShapeDtypeStruct((depth, quarter, model), BF16),
        ],
        scratch_shapes=PlaneGather.scratch(reps)
        + ColumnGather.scratch(depth) * 4
        + [pltpu.SemaphoreType.DMA((2, reps * depth * 2)), pltpu.SemaphoreType.DMA((1,))]
        + ColumnGather.scratch(depth)
        + [pltpu.SemaphoreType.DMA((2, reps)), pltpu.SemaphoreType.DMA((2,))],
        compiler_params=remote_params(0, 16),
        name="start_gather",
    )(tokens, own_pair, other_pair, common, pack, numbers, out_quarters)


def column_of(row_values, rows):
    return jnp.broadcast_to(row_values, (LANES, rows)).T[:, 0:1]


def row_of(column_values, rows):
    return jnp.broadcast_to(column_values, (rows, LANES)).T[0:8, :]


def join_mixer(parts, squares, tokens, post_gain, inner, reps, depth):
    rows, model = tokens.shape

    def kernel(parts_ref, squares_ref, x_ref, gain_ref, after_ref, mixed_ref, scale_ref, rows_out,
               pair, out, into, sems, s_pair, s_out, s_into, s_sems, second, g_sems, g_local):
        p = Place(reps, depth)
        p.barrier(plane=True, column=True)
        squares_job = PlaneSum(p, squares_ref, s_pair, s_out, s_into, s_sems)
        parts_job = PlaneSum(p, parts_ref, pair, out, into, sems)
        squares_job.relay()
        parts_job.relay()
        square = squares_job.total()
        scale_row = lax.rsqrt(square / inner + EPS)
        scale_ref[...] = scale_row
        mixed = column_of(scale_row[0:1, :], rows) * parts_job.total()
        mixed_ref[...] = mixed
        after = x_ref[...].astype(F32) + mixed
        after_ref[...] = after
        second[...] = (after * rms_rows(after) * gain_ref[...]).astype(BF16)
        job = ColumnGather(p, second, lambda z: rows_out.at[z, p.core], g_sems, g_local,
                           shared=lambda z: rows_out.at[z, 1 - p.core])
        for distance in range(1, depth):
            job.hop(distance)
        job.finish()
        p.finish()

    return pl.pallas_call(
        kernel,
        in_specs=in_vmem(4),
        out_specs=in_vmem(3) + anywhere(1),
        out_shape=[
            jax.ShapeDtypeStruct((rows, model), F32),
            jax.ShapeDtypeStruct((rows, model), F32),
            jax.ShapeDtypeStruct((8, rows), F32),
            jax.ShapeDtypeStruct((depth, 2, rows, model), BF16),
        ],
        scratch_shapes=PlaneSum.scratch(reps, (rows, model), BF16)
        + PlaneSum.scratch(reps, (8, rows), F32)
        + [pltpu.VMEM((rows, model), BF16)]
        + ColumnGather.scratch(depth),
        compiler_params=remote_params(1),
        name="join_mixer",
    )(parts, squares, tokens, post_gain)


def join_experts(parts, cotangent, after, mixed, scale, post_gain, inner, reps, depth):
    rows, model = cotangent.shape

    def kernel(parts_ref, g_ref, after_ref, mixed_ref, scale_ref, gain_ref,
               grad_ref, gain_grad_ref, low_out, scale_out,
               pair, out, into, pair_sems, sems, low, scales, l_sems, l_local, s_sems, s_local):
        p = Place(reps, depth)
        p.barrier(plane=True, column=True)
        job = ColumnSum(p, parts_ref, pair, out, into, pair_sems, sems)
        for at in range(depth - 1):
            job.step(at)
        job.total(grad_ref)
        second_grad = grad_ref[...]
        after_rows = after_ref[...]
        after_scale = rms_rows(after_rows)
        gain_grad_ref[...] = jnp.sum(after_rows * second_grad * after_scale, axis=0, keepdims=True)
        weighted = second_grad * gain_ref[...]
        after_grad = (
            g_ref[...].astype(F32)
            + after_scale * weighted
            - after_rows * after_scale**3 * jnp.mean(after_rows * weighted, axis=1, keepdims=True)
        )
        grad_ref[...] = after_grad
        after_low = after_grad.astype(BF16)
        low[...] = after_low
        scale_row = scale_ref[...]
        dot_row = row_of(jnp.sum(after_low.astype(F32) * mixed_ref[...], axis=1, keepdims=True), rows)
        scales[0] = scale_row
        scales[1] = scale_row**2 * dot_row / inner
        s_job = PlaneGather(p, scales, scale_out, s_sems, s_local)
        l_job = PlaneGather(p, low, low_out, l_sems, l_local)
        s_job.relay()
        l_job.relay()
        s_job.finish()
        l_job.finish()
        p.finish()

    return pl.pallas_call(
        kernel,
        in_specs=in_vmem(6),
        out_specs=in_vmem(2) + anywhere(2),
        out_shape=[
            jax.ShapeDtypeStruct((rows, model), F32),
            jax.ShapeDtypeStruct((1, model), F32),
            jax.ShapeDtypeStruct((reps, 2, rows, model), BF16),
            jax.ShapeDtypeStruct((reps, 2, 2, 8, rows), F32),
        ],
        scratch_shapes=ColumnSum.scratch(depth, (rows, model), BF16)
        + [pltpu.VMEM((rows, model), BF16), pltpu.VMEM((2, 8, rows), F32)]
        + PlaneGather.scratch(reps) * 2,
        compiler_params=remote_params(2),
        name="join_experts",
    )(parts, cotangent, after, mixed, scale, post_gain)


def join_input(parts, tokens, after_grad, in_gain, reps, depth):
    rows, model = tokens.shape

    def kernel(parts_ref, x_ref, grad_ref, gain_ref, tokens_grad_ref, gain_grad_ref, pair, out, into, sems):
        p = Place(reps, depth)
        p.barrier(plane=True)
        job = PlaneSum(p, parts_ref, pair, out, into, sems)
        job.relay()
        first_grad = job.total()
        x = x_ref[...].astype(F32)
        x_scale = rms_rows(x)
        gain_grad_ref[...] = jnp.sum(x * first_grad * x_scale, axis=0, keepdims=True)
        weighted = first_grad * gain_ref[...]
        tokens_grad_ref[...] = (
            grad_ref[...]
            + x_scale * weighted
            - x * x_scale**3 * jnp.mean(x * weighted, axis=1, keepdims=True)
        ).astype(BF16)
        p.finish()

    return pl.pallas_call(
        kernel,
        in_specs=in_vmem(4),
        out_specs=in_vmem(2),
        out_shape=[jax.ShapeDtypeStruct((rows, model), BF16), jax.ShapeDtypeStruct((1, model), F32)],
        scratch_shapes=PlaneSum.scratch(reps, (rows, model), BF16),
        compiler_params=remote_params(3),
        name="join_input",
    )(parts, tokens, after_grad, in_gain)


def gather(values, axes, axis=0):
    return lax.all_gather(values, axes, axis=axis, tiled=True)


def scatter_sum(values, axes, axis=0):
    return lax.psum_scatter(values, axes, scatter_dimension=axis, tiled=True)


def columns_of(values, start, size, axis=1):
    return lax.dynamic_slice_in_dim(values, start, size, axis=axis)


def shards(
    tokens,
    cotangent,
    dealt_to,
    lengths,
    routes,
    slot_index,
    in_norm,
    in_proj,
    conv_weight,
    conv_bias,
    dt_bias,
    decay_log,
    skip_gain,
    mixer_norm,
    out_proj,
    post_norm,
    router,
    shared_in,
    shared_out,
    expert_in,
    expert_out,
):
    reps, depth = lax.axis_size("rep"), lax.axis_size("z")
    group = 2 * depth
    rep, z, core = lax.axis_index("rep"), lax.axis_index("z"), lax.axis_index("core")
    shard = 2 * z + core
    team = 2 * rep + core
    members = 2 * reps
    rows, model = tokens.shape
    top = routes.shape[1]
    local = expert_in.shape[0]
    experts = local * group
    capacity = rows * top * 4 // (3 * experts)
    inner = mixer_norm.shape[0] * group
    convolved = conv_bias.shape[0] * group
    head_count = dt_bias.shape[0] * group
    width = inner // head_count
    state = (convolved - inner) // 2
    channels = inner // members
    heads = head_count // members
    shared = shared_out.shape[0]
    part = in_norm.shape[0]

    expert_ids = jnp.arange(experts, dtype=jnp.int32)
    table = jnp.sum(
        jnp.where(routes[:, None, :] == expert_ids[None, :, None], slot_index[:, None, :] + 1, 0), axis=2
    ).astype(BF16)
    numbers = jnp.pad(jnp.concatenate([lengths[0], dealt_to])[None, :], ((0, 7), (0, LANES - lengths.shape[1] - 1)))
    pieces = [
        table.T.reshape(-1), in_norm, conv_weight.reshape(-1), conv_bias, dt_bias, decay_log, skip_gain,
        mixer_norm, post_norm, router.reshape(-1),
    ]
    sizes = [piece.shape[0] for piece in pieces]
    pack = jnp.concatenate(pieces)
    pack_wide = -(-pack.shape[0] // (16 * LANES)) * LANES
    pack = jnp.pad(pack, (0, 16 * pack_wide - pack.shape[0])).reshape(16, pack_wide)
    pair_heads = 2 * heads
    dt_pair = columns_of(in_proj, inner + convolved + pair_heads * rep, pair_heads)
    blank = jnp.zeros((part, LANES // 2 - heads), BF16)
    common = jnp.concatenate(
        [in_proj[:, 2 * inner : 2 * inner + 2 * state], dt_pair[:, :heads], blank, dt_pair[:, heads:], blank], axis=1
    )

    def pair_of(member):
        return jnp.concatenate(
            [columns_of(in_proj, channels * member, channels), columns_of(in_proj, inner + channels * member, channels)],
            axis=1,
        )

    x_plane, weight, packed, numbers_all, out_own, _ = start_gather(
        tokens, pair_of(team), pair_of(2 * rep + 1 - core), common, pack, numbers,
        out_proj.reshape(reps, channels // reps, model), reps, depth,
    )
    x_plane = x_plane.reshape(members * rows, model)
    weight = weight.reshape(model, -1)
    out_own = out_own.reshape(channels, model)
    numbers_all = numbers_all[:, 0, :4].reshape(reps, group, 4)
    packed = packed.reshape(group, -1)
    unpacked, offset = [], 0
    for size in sizes:
        unpacked.append(packed[:, offset : offset + size])
        offset += size
    table_all = unpacked[0].reshape(group, experts, rows)
    in_gain = unpacked[1].reshape(1, model).astype(F32)
    taps_full = unpacked[2].reshape(group, -1, convolved // group).transpose(1, 0, 2).reshape(-1, convolved)
    taps_full = jnp.concatenate(
        [taps_full, unpacked[3].reshape(1, convolved), jnp.zeros((3, convolved), BF16)], axis=0
    ).astype(F32)
    dt_full, decay_full, skip_full = [unpacked[at].reshape(head_count).astype(F32) for at in (4, 5, 6)]
    mixer_gain = unpacked[7].reshape(1, inner).astype(F32)
    post_gain = unpacked[8].reshape(1, model).astype(F32)
    router_full = unpacked[9].reshape(model, experts)

    g_column = gather(cotangent, COLUMN)
    shared_in_own = lax.all_to_all(
        shared_in.reshape(part, 2, group, shared).transpose(2, 0, 1, 3).reshape(group * part, 2 * shared),
        COLUMN, split_axis=0, concat_axis=0, tiled=True,
    )

    blocks = numbers_all[:, :, 3].reshape(reps, depth, 2)
    dealt_plane = lax.dynamic_index_in_dim(blocks, z, axis=1, keepdims=False)
    lengths_plane = jnp.take_along_axis(numbers_all[:, :, :3], dealt_plane[:, :, None], axis=1).reshape(members, 3)
    ends = jnp.cumsum(lengths_plane, axis=1)
    position = jnp.arange(rows, dtype=jnp.int32)
    seg = jnp.sum((position[None, :, None] >= ends[:, None, :]).astype(jnp.int32), axis=2)

    taps_own = jnp.concatenate(
        [columns_of(taps_full, channels * team, channels), taps_full[:, inner:]], axis=1
    )
    own_heads = [lax.dynamic_slice_in_dim(v, heads * team, heads) for v in (dt_full, decay_full, skip_full)]
    head_rows = jnp.pad(jnp.stack([own_heads[0], jnp.exp(own_heads[1])]), ((0, 6), (0, LANES - heads)))
    skip_own = jnp.repeat(own_heads[2], width)[None, :]
    norm_own = columns_of(mixer_gain, channels * team, channels)
    mixer_args = (
        x_plane, in_gain, weight, seg.reshape(members * rows, 1), seg[:, None, :], taps_own, head_rows, skip_own,
        norm_own, out_own,
    )
    parts, squares, projected = mixer_forward(mixer_args, rows, channels, width, state)
    after, mixer_result, scale, second_column = join_mixer(
        parts.reshape(reps, 2, rows, model), squares.reshape(reps, 2, 8, rows), tokens, post_gain, inner, reps, depth
    )
    second_column = second_column.reshape(group * rows, model)

    second_blocks = second_column.reshape(group, rows, model)
    g_blocks = g_column.reshape(group, rows, model)
    dealt_column = lax.dynamic_index_in_dim(numbers_all[:, :, 3], rep, axis=0, keepdims=False)
    table_dealt = jnp.take(table_all, dealt_column, axis=0)
    logits = mm(second_column, router_full).reshape(group, rows, experts)
    used = table_dealt.transpose(0, 2, 1) > 0
    top_logit = jnp.max(jnp.where(used, logits, -jnp.inf), axis=2, keepdims=True)
    raw = jnp.where(used, jnp.exp(jnp.where(used, logits - top_logit, 0.0)), 0.0)
    gates = raw / jnp.sum(raw, axis=2, keepdims=True)
    slots = columns_of(table_dealt, local * shard, local).astype(jnp.int32) - 1
    onehot_mask = slots[:, :, None, :] == jnp.arange(capacity, dtype=jnp.int32)[None, None, :, None]
    onehot = onehot_mask.astype(BF16)
    gates_own = columns_of(gates, local * shard, local, axis=2).transpose(0, 2, 1)
    gate_slot = jnp.sum(jnp.where(onehot_mask, gates_own[:, :, None, :], 0.0), axis=3)
    gate_slot = gate_slot.transpose(1, 0, 2).reshape(local, group * capacity, 1)

    def to_slots(values):
        return jnp.einsum("qict,qtd->iqcd", onehot, values, preferred_element_type=F32).astype(BF16).reshape(
            local, group * capacity, model
        )

    def to_rows(values):
        return jnp.einsum(
            "qict,iqcd->qtd", onehot, values.reshape(local, group, capacity, model), preferred_element_type=F32
        ).reshape(group * rows, model)

    buffer = to_slots(second_blocks)
    slot_g = to_slots(g_blocks)
    expert_pre = jnp.einsum("ind,idf->inf", buffer, expert_in, preferred_element_type=F32)
    half = expert_pre.shape[2] // 2
    pre_a, pre_b = expert_pre[:, :, :half], expert_pre[:, :, half:]
    sig_a = jax.nn.sigmoid(pre_a)
    hidden = (pre_a * sig_a * pre_b).astype(BF16)
    result = jnp.einsum("inf,ifd->ind", hidden, expert_out, preferred_element_type=F32).astype(BF16)
    shared_pre = mm(second_column, shared_in_own)
    shared_a, shared_b = shared_pre[:, :shared], shared_pre[:, shared:]
    shared_sig = jax.nn.sigmoid(shared_a)
    shared_hidden = (shared_a * shared_sig * shared_b).astype(BF16)

    result_grad = (gate_slot * slot_g.astype(F32)).astype(BF16)
    hidden_grad = jnp.einsum("ind,ifd->inf", result_grad, expert_out, preferred_element_type=F32)
    pre_grad = jnp.concatenate(
        [hidden_grad * pre_b * silu_slope(pre_a, sig_a), hidden_grad * pre_a * sig_a], axis=2
    ).astype(BF16)
    buffer_grad = jnp.einsum("inf,idf->ind", pre_grad, expert_in, preferred_element_type=F32).astype(BF16)
    shared_back = mm_nt(g_column, shared_out)
    shared_grad = jnp.concatenate(
        [shared_back * shared_b * silu_slope(shared_a, shared_sig), shared_back * shared_a * shared_sig], axis=1
    ).astype(BF16)
    slot_dot = jnp.sum(slot_g.astype(F32) * result.astype(F32), axis=2).reshape(local, group, capacity)
    gate_grad = jnp.sum(jnp.where(onehot_mask, slot_dot.transpose(1, 0, 2)[:, :, :, None], 0.0), axis=2)
    gate_sum = jnp.sum(gates_own * gate_grad, axis=1)
    own_expert = (expert_ids[None, :] == (local * shard + jnp.arange(local, dtype=jnp.int32))[:, None]).astype(F32)
    gate_full = jnp.sum(gate_grad[:, :, :, None] * own_expert[None, :, None, :], axis=1)
    logit_grad = (gates * (gate_full - gate_sum[:, :, None])).reshape(group * rows, experts)
    logit_pair = jnp.concatenate(split_two(logit_grad), axis=1)
    second_part = (
        to_rows(buffer_grad)
        + mm_nt(logit_pair, jnp.concatenate([router_full, router_full], axis=1))
        + mm_nt(shared_grad, shared_in_own)
    )

    layer_part = to_rows((gate_slot * result.astype(F32)).astype(BF16)) + mm(shared_hidden, shared_out)
    layer_sum = scatter_sum(layer_part.astype(BF16), COLUMN).astype(F32)
    layer_out = (after + layer_sum).astype(BF16)

    grad_expert_out = jnp.einsum("inf,ind->ifd", hidden, result_grad, preferred_element_type=F32)
    grad_expert_in = jnp.einsum("ind,inf->idf", buffer, pre_grad, preferred_element_type=F32)
    grad_expert_out = lax.psum(grad_expert_out.astype(BF16), "rep").astype(F32)
    grad_expert_in = lax.psum(grad_expert_in.astype(BF16), "rep").astype(F32)
    grad_shared_out = lax.psum(mm_tn(shared_hidden, g_column).astype(BF16), "rep").astype(F32)
    shared_in_columns = mm_tn(second_column, shared_grad).astype(BF16)
    shared_in_rows = lax.all_to_all(shared_in_columns, COLUMN, split_axis=0, concat_axis=0, tiled=True)
    shared_in_rows = shared_in_rows.reshape(group, part, 2, shared).transpose(1, 2, 0, 3).reshape(part, -1)
    grad_shared_in = lax.psum(shared_in_rows, "rep").astype(F32)
    router_pair = mm_tn(second_column, logit_pair)
    router_grad = router_pair[:, :experts] + router_pair[:, experts:]

    after_grad, post_grad, low_plane, scales = join_experts(
        second_part.astype(BF16).reshape(depth, 2, rows, model), cotangent, after, mixer_result, scale, post_gain,
        inner, reps, depth,
    )
    back_parts, in_grad, out_grad, taps_grad, heads_grad, wide_grad = mixer_backward(
        mixer_args, projected, low_plane.reshape(members * rows, model), scales.reshape(members, 2, 8, rows),
        rows, channels, width, state,
    )
    grad_tokens, in_norm_grad = join_input(
        back_parts.reshape(reps, 2, rows, model), tokens, after_grad, in_gain, reps, depth
    )

    in_low = in_grad.astype(BF16)
    first_core = core == 0
    pair = 2 * channels

    def paired(values):
        empty = jnp.zeros_like(values)
        return [jnp.where(first_core, values, empty), jnp.where(first_core, empty, values)]

    in_pair = jnp.concatenate(
        paired(in_low[:, :channels]) + paired(in_low[:, channels:pair]) + [in_low[:, pair:]], axis=1
    )
    in_rows = gather(scatter_sum(in_pair, COLUMN), "rep").reshape(reps, part, -1).transpose(1, 0, 2)
    dt_rows = in_rows[:, :, 2 * pair + 2 * state :].reshape(part, reps, 2, LANES // 2)[:, :, :, :heads]
    grad_in_proj = jnp.concatenate(
        [
            in_rows[:, :, :pair].reshape(part, inner).astype(F32),
            in_rows[:, :, pair : 2 * pair].reshape(part, inner).astype(F32),
            jnp.sum(in_rows[:, :, 2 * pair : 2 * pair + 2 * state].astype(F32), axis=1),
            dt_rows.reshape(part, head_count).astype(F32),
        ],
        axis=1,
    )
    out_chunk = scatter_sum(out_grad.astype(BF16), "z")
    out_chunks = gather(out_chunk[None], "rep")
    out_rows = lax.all_to_all(out_chunks, "z", split_axis=0, concat_axis=0, tiled=True)
    grad_out_proj = out_rows.reshape(channels, model).astype(F32)

    def placed(values, size, start):
        blank_row = jnp.zeros(values.shape[:-1] + (size,), F32)
        return lax.dynamic_update_slice_in_dim(blank_row, values, start, axis=values.ndim - 1)

    taps_full_grad = jnp.concatenate(
        [placed(taps_grad[:5, :channels], inner, channels * team), taps_grad[:5, channels:]], axis=1
    )
    skip_head_grad = jnp.sum(wide_grad[1].reshape(heads, width), axis=1)
    small = [
        in_norm_grad.reshape(group, -1),
        taps_full_grad.reshape(5, group, -1).transpose(1, 0, 2).reshape(group, -1),
        placed(heads_grad[0, :heads], head_count, heads * team).reshape(group, -1),
        placed(heads_grad[1, :heads], head_count, heads * team).reshape(group, -1),
        placed(skip_head_grad, head_count, heads * team).reshape(group, -1),
        placed(wide_grad[0], inner, channels * team).reshape(group, -1),
        post_grad.reshape(group, -1),
        router_grad.reshape(group, -1),
    ]
    small_sizes = [piece.shape[1] for piece in small]
    small_sum = lax.psum(scatter_sum(jnp.concatenate(small, axis=1), COLUMN), "rep")[0]
    small_out, offset = [], 0
    for size in small_sizes:
        small_out.append(small_sum[offset : offset + size])
        offset += size
    taps_out = small_out[1].reshape(5, -1)
    return (
        layer_out,
        grad_tokens,
        small_out[0],
        grad_in_proj,
        taps_out[:4],
        taps_out[4],
        small_out[2],
        small_out[3],
        small_out[4],
        small_out[5],
        grad_out_proj,
        small_out[6],
        small_out[7].reshape(part, experts),
        grad_shared_in,
        grad_shared_out,
        grad_expert_in,
        grad_expert_out,
    )


def solution(mesh):
    reps, group = mesh.shape["rep"], mesh.shape["shard"]
    split = Mesh(mesh.devices.reshape(reps, group // 2, 2), ALL)
    one, row = P(COLUMN), P(COLUMN, None)
    token = P(ALL, None)
    return jax.shard_map(
        shards,
        mesh=split,
        in_specs=(
            token, token, P(ALL), token, token, token, one, row, P(None, COLUMN), one, one, one, one, one, row,
            one, row, row, row, P(COLUMN, None, None), P(COLUMN, None, None),
        ),
        out_specs=(
            token, token, one, row, P(None, COLUMN), one, one, one, one, one, row, one, row, row, row,
            P(COLUMN, None, None), P(COLUMN, None, None),
        ),
        check_vma=False,
    )
```

```python
import functools

import jax
import jax.numpy as jnp
from jax import lax
from jax.experimental import pallas as pl
from jax.experimental.pallas import tpu as pltpu
from jax.sharding import Mesh
from jax.sharding import PartitionSpec as P

EPS = 1e-05
HIGH = lax.Precision.HIGHEST
F32 = jnp.float32
BF16 = jnp.bfloat16
ALL = ("rep", "z", "core")
COLUMN = ("z", "core")
PLANE = ("rep", "core")
LANES = 128


def rms_rows(values):
    return lax.rsqrt(jnp.mean(values * values, axis=-1, keepdims=True) + EPS)


def mm(left, right):
    return jnp.dot(left, right, preferred_element_type=F32)


def mm_nt(left, right):
    return lax.dot_general(left, right, (((1,), (1,)), ((), ())), preferred_element_type=F32)


def mm_tn(left, right):
    return lax.dot_general(left, right, (((0,), (0,)), ((), ())), preferred_element_type=F32)


def silu_slope(values, sig):
    return sig * (1.0 + values * (1.0 - sig))


def split_two(values):
    high = values.astype(BF16)
    return high, (values - high.astype(F32)).astype(BF16)


class Block:
    def __init__(self, proj, seg_col, seg_row, taps, heads, channels, width, state):
        rows = proj.shape[0]
        self.rows, self.channels, self.width, self.state = rows, channels, width, state
        self.gate = proj[:, :channels]
        self.xbc = proj[:, channels : 2 * channels + 2 * state]
        self.turn = lax.axis_index("core") * (LANES // 2)
        dt_raw = pltpu.roll(proj[:, 2 * channels + 2 * state :], self.turn, 1)
        position = lax.broadcasted_iota(jnp.int32, (rows, 1), 0)
        seg_wide = jnp.broadcast_to(seg_col, (rows, LANES))
        self.masks = []
        conv = taps[4:5, :] + taps[3:4, :] * self.xbc
        for offset in (1, 2, 3):
            before = pltpu.roll(seg_wide, offset, 0)[:, :1]
            mask = jnp.where((before == seg_col) & (position >= offset), 1.0, 0.0)
            self.masks.append(mask)
            conv = conv + taps[3 - offset : 4 - offset, :] * (mask * pltpu.roll(self.xbc, offset, 0))
        self.conv = conv
        self.conv_sig = jax.nn.sigmoid(conv)
        act = conv * self.conv_sig
        self.xin = act[:, :channels]
        self.write = act[:, channels : channels + state]
        self.read = act[:, channels + state :]
        shifted = dt_raw + heads[0:1, :]
        self.step = jnp.maximum(shifted, 0.0) + jnp.log1p(jnp.exp(-jnp.abs(shifted)))
        self.step_sig = jax.nn.sigmoid(shifted)
        self.speed = heads[1:2, :]
        self.rate = -self.step * self.speed
        row_at = lax.broadcasted_iota(jnp.int32, (rows, rows), 0)
        col_at = lax.broadcasted_iota(jnp.int32, (rows, rows), 1)
        self.causal = row_at >= col_at
        self.keep = self.causal & (seg_col == seg_row)
        self.cum = jnp.dot(self.causal.astype(F32), self.rate, precision=HIGH, preferred_element_type=F32)
        self.cum_t = self.cum.T
        scores = lax.dot_general(
            self.read, self.write, (((1,), (1,)), ((), ())), precision=HIGH, preferred_element_type=F32
        )
        self.scores = jnp.where(self.keep, scores, 0.0)

    def groups(self):
        for start in range(0, self.channels, LANES):
            stop = min(start + LANES, self.channels)
            yield start, stop, list(range(start // self.width, (stop - 1) // self.width + 1))

    def spread(self, columns, start, stop, heads):
        lane = lax.broadcasted_iota(jnp.int32, (self.rows, stop - start), 1) + start
        result = jnp.broadcast_to(columns[:, heads[0] : heads[0] + 1], (self.rows, stop - start))
        for head in heads[1:]:
            result = jnp.where(lane >= head * self.width, columns[:, head : head + 1], result)
        return result

    def inside(self, start, stop, head):
        lane = lax.broadcasted_iota(jnp.int32, (self.rows, stop - start), 1) + start
        return (lane >= head * self.width) & (lane < (head + 1) * self.width)

    def decay(self, head):
        gaps = self.cum[:, head : head + 1] - self.cum_t[head : head + 1, :]
        return jnp.exp(jnp.where(self.keep, gaps, 0.0))


def mixer_forward_kernel(
    channels, width, state,
    x_ref, gain_ref, weight_ref, seg_col_ref, seg_row_ref, taps_ref, heads_ref, skip_ref, norm_ref, out_ref,
    part_ref, square_ref, proj_ref,
):
    x = x_ref[...].astype(F32)
    first = (x * rms_rows(x) * gain_ref[...]).astype(BF16)
    proj = mm(first, weight_ref[...])
    proj_ref[...] = proj
    block = Block(proj, seg_col_ref[...], seg_row_ref[...], taps_ref[...], heads_ref[...], channels, width, state)
    rows = block.rows
    mixed = []
    for start, stop, heads in block.groups():
        xin = block.xin[:, start:stop]
        scaled = (xin * block.spread(block.step, start, stop, heads)).astype(BF16)
        y = None
        for head in heads:
            weights = (block.scores * block.decay(head)).astype(BF16)
            term = mm(weights, scaled)
            y = term if y is None else jnp.where(block.inside(start, stop, head), term, y)
        gate = block.gate[:, start:stop]
        mixed.append((y + skip_ref[:, start:stop] * xin) * gate * jax.nn.sigmoid(gate))
    mixed = jnp.concatenate(mixed, axis=1)
    square_ref[...] = row_of(jnp.sum(mixed * mixed, axis=1, keepdims=True), rows)
    part_ref[...] = mm((mixed * norm_ref[...]).astype(BF16), out_ref[...]).astype(BF16)


def mixer_backward_kernel(
    channels, width, state,
    x_ref, gain_ref, weight_ref, seg_col_ref, seg_row_ref, taps_ref, heads_ref, skip_ref, norm_ref, out_ref,
    proj_ref, low_ref, scale_ref,
    back_ref, in_grad_ref, out_grad_ref, taps_grad_ref, heads_grad_ref, wide_grad_ref,
):
    block_at = pl.program_id(0)

    @pl.when(block_at == 0)
    def _():
        in_grad_ref[...] = jnp.zeros_like(in_grad_ref)
        out_grad_ref[...] = jnp.zeros_like(out_grad_ref)
        taps_grad_ref[...] = jnp.zeros_like(taps_grad_ref)
        heads_grad_ref[...] = jnp.zeros_like(heads_grad_ref)
        wide_grad_ref[...] = jnp.zeros_like(wide_grad_ref)

    block = Block(
        proj_ref[...], seg_col_ref[...], seg_row_ref[...], taps_ref[...], heads_ref[...], channels, width, state
    )
    rows = block.rows
    low = low_ref[...]
    scale = column_of(scale_ref[0, 0:1, :], rows)
    pull = column_of(scale_ref[1, 0:1, :], rows)
    normed_grad = mm_nt(low, out_ref[...])
    taps = taps_ref[...]
    gate_grads, x_grads, mixed_all, norm_grads, skip_grads = [], [], [], [], []
    step_grad = jnp.zeros((rows, LANES), F32)
    cum_grad = jnp.zeros((rows, LANES), F32)
    cum_grad_t = jnp.zeros((LANES, rows), F32)
    score_grad = jnp.zeros((rows, rows), F32)
    lane_all = lax.broadcasted_iota(jnp.int32, (rows, LANES), 1)
    sub_all = lax.broadcasted_iota(jnp.int32, (LANES, rows), 0)
    for start, stop, heads in block.groups():
        xin = block.xin[:, start:stop]
        spread = block.spread(block.step, start, stop, heads)
        scaled, scaled_rest = split_two(xin * spread)
        scaled_wide = jnp.concatenate([scaled, scaled, scaled_rest], axis=1)
        weights, decays = [], []
        y = None
        for head in heads:
            decays.append(block.decay(head))
            weights.append(block.scores * decays[-1])
            term = mm(weights[-1].astype(BF16), scaled)
            y = term if y is None else jnp.where(block.inside(start, stop, head), term, y)
        skip = skip_ref[:, start:stop]
        y = y + skip * xin
        gate = block.gate[:, start:stop]
        gate_sig = jax.nn.sigmoid(gate)
        gate_act = gate * gate_sig
        mixed = y * gate_act
        mixed_all.append(mixed)
        q = normed_grad[:, start:stop]
        norm_grads.append(jnp.sum(mixed * scale * q, axis=0, keepdims=True))
        mixed_grad = scale * norm_ref[:, start:stop] * q - mixed * pull
        gate_grads.append(mixed_grad * y * silu_slope(gate, gate_sig))
        y_grad = mixed_grad * gate_act
        skip_grads.append(jnp.sum(y_grad * xin, axis=0, keepdims=True))
        y_low, y_rest = split_two(y_grad)
        scaled_grad = None
        for at, head in enumerate(heads):
            inside = block.inside(start, stop, head)
            term = mm_tn(weights[at].astype(BF16), y_low)
            scaled_grad = term if scaled_grad is None else jnp.where(inside, term, scaled_grad)
            blank = jnp.zeros_like(y_low)
            y_own = jnp.where(inside, y_low, blank)
            pair_grad = mm_nt(
                jnp.concatenate([y_own, jnp.where(inside, y_rest, blank), y_own], axis=1), scaled_wide
            )
            score_grad = score_grad + pair_grad * decays[at]
            exponent_grad = pair_grad * weights[at]
            cum_grad = jnp.where(lane_all == head, jnp.sum(exponent_grad, axis=1, keepdims=True), cum_grad)
            cum_grad_t = jnp.where(sub_all == head, jnp.sum(exponent_grad, axis=0, keepdims=True), cum_grad_t)
        for head in heads:
            inside = block.inside(start, stop, head)
            per_row = jnp.sum(jnp.where(inside, scaled_grad * xin, 0.0), axis=1, keepdims=True)
            step_grad = jnp.where(lane_all == head, per_row, step_grad)
        x_grads.append(scaled_grad * spread + skip * y_grad)
    score_grad = jnp.where(block.keep, score_grad, 0.0).astype(BF16)
    read_grad = mm(score_grad, block.write.astype(BF16))
    write_grad = mm_tn(score_grad, block.read.astype(BF16))
    cum_grad = cum_grad - cum_grad_t.T
    rate_grad = lax.dot_general(
        block.causal.astype(F32), cum_grad, (((0,), (0,)), ((), ())), precision=HIGH, preferred_element_type=F32
    )
    step_grad = step_grad - block.speed * rate_grad
    dt_grad = step_grad * block.step_sig
    heads_grad_ref[0:1, :] += jnp.sum(dt_grad, axis=0, keepdims=True)
    heads_grad_ref[1:2, :] += jnp.sum(rate_grad * block.rate, axis=0, keepdims=True)
    act_grad = jnp.concatenate(x_grads + [write_grad, read_grad], axis=1)
    conv_grad = act_grad * silu_slope(block.conv, block.conv_sig)
    taps_grad_ref[4:5, :] += jnp.sum(conv_grad, axis=0, keepdims=True)
    taps_grad_ref[3:4, :] += jnp.sum(conv_grad * block.xbc, axis=0, keepdims=True)
    xbc_grad = taps[3:4, :] * conv_grad
    for offset in (1, 2, 3):
        masked = conv_grad * block.masks[offset - 1]
        taps_grad_ref[3 - offset : 4 - offset, :] += jnp.sum(
            masked * pltpu.roll(block.xbc, offset, 0), axis=0, keepdims=True
        )
        xbc_grad = xbc_grad + taps[3 - offset : 4 - offset, :] * pltpu.roll(masked, rows - offset, 0)
    wide_grad_ref[0:1, :] += jnp.concatenate(norm_grads, axis=1)
    wide_grad_ref[1:2, :] += jnp.concatenate(skip_grads, axis=1)
    proj_grad = jnp.concatenate(gate_grads + [xbc_grad, pltpu.roll(dt_grad, block.turn, 1)], axis=1).astype(BF16)
    back_ref[...] = mm_nt(proj_grad, weight_ref[...]).astype(BF16)
    x = x_ref[...].astype(F32)
    first = (x * rms_rows(x) * gain_ref[...]).astype(BF16)
    in_grad_ref[...] += mm_tn(first, proj_grad)
    normed = (jnp.concatenate(mixed_all, axis=1) * scale * norm_ref[...]).astype(BF16)
    out_grad_ref[...] += mm_tn(normed, low)


def whole(shape):
    return pl.BlockSpec(shape, lambda i: (0,) * len(shape))


def by_rows(shape):
    return pl.BlockSpec(shape, lambda i: (i,) + (0,) * (len(shape) - 1))


def mixer_specs(rows, model, channels, state):
    wide = 2 * channels + 2 * state + LANES
    return [
        by_rows((rows, model)),
        whole((1, model)),
        whole((model, wide)),
        by_rows((rows, 1)),
        pl.BlockSpec((None, 1, rows), lambda i: (i, 0, 0)),
        whole((8, channels + 2 * state)),
        whole((8, LANES)),
        whole((1, channels)),
        whole((1, channels)),
        whole((channels, model)),
    ]


def mixer_forward(args, rows, channels, width, state):
    total, model = args[0].shape
    wide = 2 * channels + 2 * state + LANES
    return pl.pallas_call(
        functools.partial(mixer_forward_kernel, channels, width, state),
        grid=(total // rows,),
        in_specs=mixer_specs(rows, model, channels, state),
        out_specs=[
            by_rows((rows, model)),
            pl.BlockSpec((None, 8, rows), lambda i: (i, 0, 0)),
            by_rows((rows, wide)),
        ],
        out_shape=[
            jax.ShapeDtypeStruct((total, model), BF16),
            jax.ShapeDtypeStruct((total // rows, 8, rows), F32),
            jax.ShapeDtypeStruct((total, wide), F32),
        ],
        compiler_params=pltpu.CompilerParams(vmem_limit_bytes=56 * 2**20),
        name="mixer_forward",
    )(*args)


def mixer_backward(args, proj, low, scale, rows, channels, width, state):
    total, model = args[0].shape
    wide = 2 * channels + 2 * state + LANES
    return pl.pallas_call(
        functools.partial(mixer_backward_kernel, channels, width, state),
        grid=(total // rows,),
        in_specs=mixer_specs(rows, model, channels, state)
        + [
            by_rows((rows, wide)),
            by_rows((rows, model)),
            pl.BlockSpec((None, 2, 8, rows), lambda i: (i, 0, 0, 0)),
        ],
        out_specs=[
            by_rows((rows, model)),
            whole((model, wide)),
            whole((channels, model)),
            whole((8, channels + 2 * state)),
            whole((8, LANES)),
            whole((8, channels)),
        ],
        out_shape=[
            jax.ShapeDtypeStruct((total, model), BF16),
            jax.ShapeDtypeStruct((model, wide), F32),
            jax.ShapeDtypeStruct((channels, model), F32),
            jax.ShapeDtypeStruct((8, channels + 2 * state), F32),
            jax.ShapeDtypeStruct((8, LANES), F32),
            jax.ShapeDtypeStruct((8, channels), F32),
        ],
        compiler_params=pltpu.CompilerParams(vmem_limit_bytes=60 * 2**20),
        name="mixer_backward",
    )(*args, proj, low, scale)


MESH_ID = pl.DeviceIdType.MESH


def when(condition, action):
    if condition is True:
        action()
    elif condition is not False:
        pl.when(condition)(action)


class Place:
    def __init__(self, reps, depth):
        self.reps, self.depth = reps, depth
        self.rep, self.z, self.core = lax.axis_index("rep"), lax.axis_index("z"), lax.axis_index("core")
        self.here = {"rep": self.rep, "z": self.z, "core": self.core}
        self.pending = []

    def device(self, **changes):
        return {**self.here, **changes}

    def sibling(self):
        return self.device(core=1 - self.core)

    def rep_at(self, distance):
        return lax.rem(self.rep + distance, self.reps)

    def barrier(self, plane=False, column=False, everyone=False):
        semaphore = pltpu.get_barrier_semaphore()

        def greet(device):
            pl.semaphore_signal(semaphore, inc=1, device_id=device, device_id_type=MESH_ID)

        if everyone:
            count = self.reps * self.depth * 2
            mine = (self.rep * self.depth + self.z) * 2 + self.core

            def step(distance, carry):
                other = lax.rem(mine + distance, count)
                greet({"rep": other // (2 * self.depth), "z": lax.rem(other // 2, self.depth), "core": lax.rem(other, 2)})
                return carry

            lax.fori_loop(1, count, step, 0)
            pl.semaphore_wait(semaphore, count - 1)
            return
        amount = 1
        greet(self.sibling())
        if plane:
            for distance in range(1, self.reps):
                greet(self.device(rep=self.rep_at(distance)))
            amount = amount + self.reps - 1
        if column:
            above, below = self.z < self.depth - 1, self.z > 0
            when(above, lambda: greet(self.device(z=self.z + 1)))
            when(below, lambda: greet(self.device(z=self.z - 1)))
            amount = amount + jnp.where(above, 1, 0) + jnp.where(below, 1, 0)
        pl.semaphore_wait(semaphore, amount)

    def send(self, source, target, send_sem, recv_sem, device, condition=True):
        copy = pltpu.make_async_remote_copy(
            src_ref=source, dst_ref=target, send_sem=send_sem, recv_sem=recv_sem, device_id=device,
            device_id_type=MESH_ID,
        )
        when(condition, copy.start)
        self.pending.append((condition, copy))

    def local(self, source, target, sem):
        copy = pltpu.make_async_copy(source, target, sem)
        copy.start()
        return copy

    def arrived(self, target, recv_sem, condition=True):
        copy = pltpu.make_async_remote_copy(
            src_ref=target, dst_ref=target, send_sem=recv_sem, recv_sem=recv_sem, device_id=self.sibling(),
            device_id_type=MESH_ID,
        )
        when(condition, copy.wait_recv)

    def finish(self):
        for condition, copy in self.pending:
            when(condition, copy.wait_send)
        self.pending = []


class PlaneGather:
    @staticmethod
    def scratch(reps):
        return [pltpu.SemaphoreType.DMA((4, reps)), pltpu.SemaphoreType.DMA((1,))]

    def __init__(self, place, own, out, sems, local_sem):
        self.place, self.out, self.sems = place, out, sems
        p = place
        self.keep = p.local(own, out.at[p.rep, p.core], local_sem.at[0])
        for distance in range(1, p.reps):
            p.send(own, out.at[p.rep, p.core], sems.at[0, distance], sems.at[1, distance],
                   p.device(rep=p.rep_at(distance)))
        p.send(own, out.at[p.rep, p.core], sems.at[2, 0], sems.at[3, 0], p.sibling())

    def relay(self):
        p = self.place
        for distance in range(1, p.reps):
            source = self.out.at[p.rep_at(p.reps - distance), p.core]
            p.arrived(source, self.sems.at[1, distance])
            p.send(source, source, self.sems.at[2, distance], self.sems.at[3, distance], p.sibling())

    def finish(self):
        p = self.place
        self.keep.wait()
        for distance in range(p.reps):
            source = p.rep_at(p.reps - distance) if distance else p.rep
            p.arrived(self.out.at[source, 1 - p.core], self.sems.at[3, distance])


class ColumnGather:
    @staticmethod
    def scratch(depth):
        return [pltpu.SemaphoreType.DMA((8, depth)), pltpu.SemaphoreType.DMA((1,))]

    def __init__(self, place, own, slot, sems, local_sem, shared=None, keep=True):
        self.place, self.slot, self.sems, self.shared = place, slot, sems, shared
        p = place
        self.keep = p.local(own, slot(p.z), local_sem.at[0]) if keep else None
        self.onward(own, slot(p.z), 0, True, True)
        if shared is not None:
            p.send(own, slot(p.z), sems.at[4, 0], sems.at[5, 0], p.sibling())

    def onward(self, source, target, distance, up, down):
        p = self.place
        if up is not False:
            p.send(source, target, self.sems.at[0, distance], self.sems.at[1, distance], p.device(z=p.z + 1),
                   (p.z < p.depth - 1) if up is True else up & (p.z < p.depth - 1))
        if down is not False:
            p.send(source, target, self.sems.at[2, distance], self.sems.at[3, distance], p.device(z=p.z - 1),
                   (p.z > 0) if down is True else down & (p.z > 0))

    def hop(self, distance):
        p = self.place
        below, above = p.z >= distance, p.z + distance < p.depth
        low, high = self.slot(jnp.maximum(p.z - distance, 0)), self.slot(jnp.minimum(p.z + distance, p.depth - 1))
        p.arrived(low, self.sems.at[1, distance - 1], below)
        self.onward(low, low, distance, below, False)
        if self.shared is not None:
            p.send(low, low, self.sems.at[4, distance], self.sems.at[5, distance], p.sibling(), below)
        p.arrived(high, self.sems.at[3, distance - 1], above)
        self.onward(high, high, distance, False, above)
        if self.shared is not None:
            p.send(high, high, self.sems.at[6, distance], self.sems.at[7, distance], p.sibling(), above)

    def finish(self):
        p = self.place
        if self.keep is not None:
            self.keep.wait()
        if self.shared is None:
            return
        p.arrived(self.shared(p.z), self.sems.at[5, 0])
        for distance in range(1, p.depth):
            below, above = p.z >= distance, p.z + distance < p.depth
            p.arrived(self.shared(jnp.maximum(p.z - distance, 0)), self.sems.at[5, distance], below)
            p.arrived(self.shared(jnp.minimum(p.z + distance, p.depth - 1)), self.sems.at[7, distance], above)


def add_up(*terms):
    total = terms[0].astype(F32)
    for term in terms[1:]:
        total = total + term.astype(F32)
    return total


class PairSwap:
    @staticmethod
    def scratch(count, shape, dtype):
        return [pltpu.VMEM((count,) + shape, dtype), pltpu.SemaphoreType.DMA((2, count))]

    def __init__(self, place, parts, pair, sems, order):
        self.place, self.parts, self.pair, self.sems = place, parts, pair, sems
        for at in order:
            place.send(parts.at[at, 1 - place.core], pair.at[at], sems.at[0, at], sems.at[1, at], place.sibling())

    def wait(self, at):
        self.place.arrived(self.pair.at[at], self.sems.at[1, at])

    def terms(self, at):
        return [self.parts[at, self.place.core], self.pair[at]]


class PlaneSum:
    @staticmethod
    def scratch(reps, shape, dtype):
        return PairSwap.scratch(reps, shape, dtype) + [
            pltpu.VMEM((reps,) + shape, dtype), pltpu.SemaphoreType.DMA((2, reps)),
        ]

    def __init__(self, place, parts, pair, pair_sems, into, sems):
        self.place, self.pair, self.into, self.sems = place, pair, into, sems
        order = [place.rep_at(distance) for distance in range(1, place.reps)] + [place.rep]
        self.swap = PairSwap(place, parts, pair, pair_sems, order)

    def relay(self):
        p = self.place
        for distance in range(1, p.reps):
            rep = p.rep_at(distance)
            self.swap.wait(rep)
            self.pair[rep] = add_up(*self.swap.terms(rep)).astype(self.pair.dtype)
            p.send(self.pair.at[rep], self.into.at[distance], self.sems.at[0, distance], self.sems.at[1, distance],
                   p.device(rep=rep))

    def total(self):
        p = self.place
        self.swap.wait(p.rep)
        terms = self.swap.terms(p.rep)
        for distance in range(1, p.reps):
            p.arrived(self.into.at[distance], self.sems.at[1, distance])
            terms.append(self.into[distance])
        return add_up(*terms)


class LineSum:
    @staticmethod
    def scratch(depth, shape, dtype):
        return [pltpu.VMEM((depth + 1,) + shape, dtype), pltpu.SemaphoreType.DMA((4, depth))]

    def __init__(self, place, terms, out, into, sems):
        self.place, self.terms, self.out, self.into, self.sems = place, terms, out, into, sems

    def step(self, at):
        p = self.place
        last = p.depth - 1
        for way, towards, goal, first, valid in (
            (0, p.z + 1, last - (at - p.z), p.z == 0, (at >= p.z) & (last - (at - p.z) > p.z)),
            (1, p.z - 1, at - (last - p.z), p.z == last, (at >= last - p.z) & (at - (last - p.z) < p.z)),
        ):
            goal = jnp.clip(goal, 0, last)
            inner = valid & jnp.logical_not(first)
            p.arrived(self.into.at[goal], self.sems.at[2 * way + 1, goal], inner)

            def start(goal=goal):
                self.out[goal] = add_up(*self.terms(goal)).astype(self.out.dtype)

            def follow(goal=goal):
                self.out[goal] = add_up(*self.terms(goal), self.into[goal]).astype(self.out.dtype)

            when(valid & first, start)
            when(inner, follow)
            target = self.into.at[goal]
            if way:
                target = self.into.at[jnp.where(goal == towards, p.depth, goal)]
            p.send(self.out.at[goal], target, self.sems.at[2 * way, goal], self.sems.at[2 * way + 1, goal],
                   p.device(z=towards), valid)

    def total(self, result):
        p = self.place
        result[...] = add_up(*self.terms(p.z))
        for way, slot, condition in ((0, p.z, p.z > 0), (1, p.depth, p.z < p.depth - 1)):
            p.arrived(self.into.at[slot], self.sems.at[2 * way + 1, p.z], condition)

            def add(slot=slot):
                result[...] += self.into[slot].astype(F32)

            when(condition, add)


class ColumnSum:
    @staticmethod
    def scratch(depth, shape, dtype):
        return PairSwap.scratch(depth, shape, dtype) + LineSum.scratch(depth, shape, dtype)

    def __init__(self, place, parts, pair, pair_sems, into, sems):
        self.place = place
        order = [lax.rem(place.z + distance, place.depth) for distance in list(range(place.depth - 1, 0, -1)) + [0]]
        self.order = order
        self.swap = PairSwap(place, parts, pair, pair_sems, order)
        self.line = LineSum(place, self.swap.terms, pair, into, sems)

    def ready(self):
        for at in self.order:
            self.swap.wait(at)

    def step(self, at):
        self.line.step(at)

    def total(self, result):
        self.line.total(result)


def anywhere(count):
    return [pl.BlockSpec(memory_space=pl.ANY)] * count


def in_vmem(count):
    return [pl.BlockSpec(memory_space=pltpu.VMEM)] * count


def remote_params(identity, mebibytes=60):
    return pltpu.CompilerParams(
        collective_id=identity, has_side_effects=True, vmem_limit_bytes=mebibytes * 2**20
    )


def start_gather(tokens, own_pair, other_pair, common, pack, numbers, out_quarters, reps, depth):
    rows, model = tokens.shape
    part, side = own_pair.shape
    wide = side + common.shape[1]

    def kernel(x_ref, own_ref, other_ref, common_ref, pack_ref, numbers_ref, quarters_ref,
               x_out, weight_out, pack_out, numbers_out, out_out, mid_out,
               x_sems, x_local, a_sems, a_local, b_sems, b_local, c_sems, c_local, p_sems, p_local,
               n_sems, n_local, o_sems, o_local, e_sems, swap_sems):
        p = Place(reps, depth)
        p.barrier(everyone=True)

        def left(core):
            return lambda z: weight_out.at[z, core, :, pl.ds(0, side)]

        def right(core):
            return lambda z: weight_out.at[z, core, :, pl.ds(side, wide - side)]

        slot = left(p.core)
        p.send(other_ref, slot(p.z), swap_sems.at[0], swap_sems.at[1], p.sibling())
        pack_job = ColumnGather(p, pack_ref, lambda z: pack_out.at[z, p.core], p_sems, p_local,
                                shared=lambda z: pack_out.at[z, 1 - p.core])
        count = reps * depth * 2
        mine = (p.rep * depth + p.z) * 2 + p.core
        number_keep = p.local(numbers_ref, numbers_out.at[mine], n_local.at[0])

        def number_copy(distance, other):
            return pltpu.make_async_remote_copy(
                src_ref=numbers_ref, dst_ref=numbers_out.at[mine], send_sem=n_sems.at[0, distance],
                recv_sem=n_sems.at[1, distance],
                device_id={"rep": other // (2 * depth), "z": lax.rem(other // 2, depth), "core": lax.rem(other, 2)},
                device_id_type=MESH_ID,
            )

        def number_send(distance, carry):
            number_copy(distance, lax.rem(mine + distance, count)).start()
            return carry

        lax.fori_loop(1, count, number_send, 0)
        job_a = ColumnGather(p, own_ref, slot, a_sems, a_local)
        job_c = ColumnGather(p, common_ref, right(p.core), c_sems, c_local, shared=right(1 - p.core))
        x_job = PlaneGather(p, x_ref, x_out, x_sems, x_local)
        other = left(1 - p.core)
        p.arrived(other(p.z), swap_sems.at[1])
        job_b = ColumnGather(p, other(p.z), other, b_sems, b_local, keep=False)
        job_o = ColumnGather(p, quarters_ref.at[p.rep], lambda z: mid_out.at[z], o_sems, o_local)
        for distance in range(1, depth):
            pack_job.hop(distance)
            job_a.hop(distance)
            job_c.hop(distance)
            job_b.hop(distance)
            if distance == 1:
                x_job.relay()
            job_o.hop(distance)
        job_o.finish()
        for distance in range(1, reps):
            rep = p.rep_at(distance)
            p.send(mid_out.at[rep], out_out.at[p.rep], e_sems.at[0, distance], e_sems.at[1, distance], p.device(rep=rep))
        out_keep = p.local(mid_out.at[p.rep], out_out.at[p.rep], o_local.at[0])
        for job in (x_job, pack_job, job_a, job_b, job_c):
            job.finish()
        number_keep.wait()

        def number_wait(distance, carry):
            copy = number_copy(distance, lax.rem(mine + distance, count))
            copy.wait_send()
            copy.wait_recv()
            return carry

        lax.fori_loop(1, count, number_wait, 0)
        out_keep.wait()
        for distance in range(1, reps):
            p.arrived(out_out.at[p.rep_at(reps - distance)], e_sems.at[1, distance])
        p.finish()

    quarter = out_quarters.shape[1]
    return pl.pallas_call(
        kernel,
        in_specs=anywhere(7),
        out_specs=anywhere(6),
        out_shape=[
            jax.ShapeDtypeStruct((reps, 2, rows, model), BF16),
            jax.ShapeDtypeStruct((depth, 2, part, wide), BF16),
            jax.ShapeDtypeStruct((depth, 2) + pack.shape, BF16),
            jax.ShapeDtypeStruct((reps * depth * 2,) + numbers.shape, jnp.int32),
            jax.ShapeDtypeStruct((reps, quarter, model), BF16),
            jax.ShapeDtypeStruct((depth, quarter, model), BF16),
        ],
        scratch_shapes=PlaneGather.scratch(reps)
        + ColumnGather.scratch(depth) * 4
        + [pltpu.SemaphoreType.DMA((2, reps * depth * 2)), pltpu.SemaphoreType.DMA((1,))]
        + ColumnGather.scratch(depth)
        + [pltpu.SemaphoreType.DMA((2, reps)), pltpu.SemaphoreType.DMA((2,))],
        compiler_params=remote_params(0, 16),
        name="start_gather",
    )(tokens, own_pair, other_pair, common, pack, numbers, out_quarters)


def column_of(row_values, rows):
    return jnp.broadcast_to(row_values, (LANES, rows)).T[:, 0:1]


def row_of(column_values, rows):
    return jnp.broadcast_to(column_values, (rows, LANES)).T[0:8, :]


def join_mixer(parts, squares, tokens, post_gain, inner, reps, depth):
    rows, model = tokens.shape

    def kernel(parts_ref, squares_ref, x_ref, gain_ref, after_ref, mixed_ref, scale_ref, rows_out,
               *scratch):
        p = Place(reps, depth)
        p.barrier(plane=True, column=True)
        second, g_sems, g_local = scratch[8:]
        squares_job = PlaneSum(p, squares_ref, *scratch[4:8])
        parts_job = PlaneSum(p, parts_ref, *scratch[:4])
        squares_job.relay()
        parts_job.relay()
        square = squares_job.total()
        scale_row = lax.rsqrt(square / inner + EPS)
        scale_ref[...] = scale_row
        mixed = column_of(scale_row[0:1, :], rows) * parts_job.total()
        mixed_ref[...] = mixed.astype(BF16)
        after = x_ref[...].astype(F32) + mixed
        after_ref[...] = after
        second[...] = (after * rms_rows(after) * gain_ref[...]).astype(BF16)
        job = ColumnGather(p, second, lambda z: rows_out.at[z, p.core], g_sems, g_local,
                           shared=lambda z: rows_out.at[z, 1 - p.core])
        for distance in range(1, depth):
            job.hop(distance)
        job.finish()
        p.finish()

    return pl.pallas_call(
        kernel,
        in_specs=in_vmem(4),
        out_specs=in_vmem(3) + anywhere(1),
        out_shape=[
            jax.ShapeDtypeStruct((rows, model), F32),
            jax.ShapeDtypeStruct((rows, model), BF16),
            jax.ShapeDtypeStruct((8, rows), F32),
            jax.ShapeDtypeStruct((depth, 2, rows, model), BF16),
        ],
        scratch_shapes=PlaneSum.scratch(reps, (rows, model), BF16)
        + PlaneSum.scratch(reps, (8, rows), F32)
        + [pltpu.VMEM((rows, model), BF16)]
        + ColumnGather.scratch(depth),
        compiler_params=remote_params(1),
        name="join_mixer",
    )(parts, squares, tokens, post_gain)


def join_experts(parts, layer_parts, cotangent, after, mixed, scale, post_gain, inner, reps, depth):
    rows, model = cotangent.shape

    def kernel(parts_ref, layer_ref, g_ref, after_ref, mixed_ref, scale_ref, gain_ref,
               grad_ref, gain_grad_ref, layer_out_ref, low_out, scale_out, *scratch):
        scales, total, l_sems, l_local, s_sems, s_local = scratch[8:]
        p = Place(reps, depth)
        p.barrier(plane=True, column=True)
        job = ColumnSum(p, parts_ref, *scratch[:4])
        layer_job = ColumnSum(p, layer_ref, *scratch[4:8])
        job.ready()
        for at in range(depth - 1):
            job.step(at)
        layer_job.ready()
        job.total(grad_ref)
        layer_job.step(0)
        second_grad = grad_ref[...]
        after_rows = after_ref[...]
        after_scale = rms_rows(after_rows)
        gain_grad_ref[...] = jnp.sum(after_rows * second_grad * after_scale, axis=0, keepdims=True)
        weighted = second_grad * gain_ref[...]
        after_grad = (
            g_ref[...].astype(F32)
            + after_scale * weighted
            - after_rows * after_scale**3 * jnp.mean(after_rows * weighted, axis=1, keepdims=True)
        )
        grad_ref[...] = after_grad
        after_low = after_grad.astype(BF16)
        pair = scratch[0]
        pair[p.z] = after_low
        l_job = PlaneGather(p, pair.at[p.z], low_out, l_sems, l_local)
        scale_row = scale_ref[...]
        dot_row = row_of(jnp.sum(after_low.astype(F32) * mixed_ref[...].astype(F32), axis=1, keepdims=True), rows)
        scales[0] = scale_row
        scales[1] = scale_row**2 * dot_row / inner
        s_job = PlaneGather(p, scales, scale_out, s_sems, s_local)
        for at in range(1, depth - 1):
            layer_job.step(at)
        s_job.relay()
        l_job.relay()
        layer_job.total(total)
        layer_out_ref[...] = (total[...] + after_ref[...]).astype(BF16)
        s_job.finish()
        l_job.finish()
        p.finish()

    return pl.pallas_call(
        kernel,
        in_specs=in_vmem(7),
        out_specs=in_vmem(3) + anywhere(2),
        out_shape=[
            jax.ShapeDtypeStruct((rows, model), F32),
            jax.ShapeDtypeStruct((1, model), F32),
            jax.ShapeDtypeStruct((rows, model), BF16),
            jax.ShapeDtypeStruct((reps, 2, rows, model), BF16),
            jax.ShapeDtypeStruct((reps, 2, 2, 8, rows), F32),
        ],
        scratch_shapes=ColumnSum.scratch(depth, (rows, model), BF16) * 2
        + [pltpu.VMEM((2, 8, rows), F32), pltpu.VMEM((rows, model), F32)]
        + PlaneGather.scratch(reps) * 2,
        compiler_params=remote_params(2),
        name="join_experts",
    )(parts, layer_parts, cotangent, after, mixed, scale, post_gain)


def finish_input(parts, tokens, after_grad, in_gain, side, common, out_grad, small, reps, depth):
    rows, model = tokens.shape
    part, width = side.shape[2:]
    common_width = common.shape[3]
    quarter = out_grad.shape[1]
    small_width = small.shape[3]
    gain_width = -(-part // LANES) * LANES
    x_scratch = PlaneSum.scratch(reps, (rows, model), BF16)
    c_scratch = ColumnSum.scratch(depth, (part, common_width), BF16)
    s_scratch = ColumnSum.scratch(depth, small.shape[2:], F32)
    n_scratch = ColumnSum.scratch(depth, (8, gain_width), F32)
    a_scratch = [pltpu.VMEM((depth, 2, part, width), BF16)] + LineSum.scratch(depth, (2, part, width), BF16)
    o_scratch = [
        pltpu.VMEM((reps, quarter, model), BF16), pltpu.SemaphoreType.DMA((2, reps)),
        pltpu.VMEM((depth, quarter, model), BF16),
    ] + LineSum.scratch(depth, (quarter, model), BF16)

    def kernel(parts_ref, x_ref, grad_ref, gain_ref, side_ref, common_ref, out_ref, small_ref,
               tokens_grad_ref, side_out, common_out, out_out, small_out, gain_out, *scratch):
        x_work, c_work, s_work, n_work, a_work, o_work = (
            scratch[:4], scratch[4:8], scratch[8:12], scratch[12:16], scratch[16:19], scratch[19:24]
        )
        (side_total, side_pair, swap_sems, common_total, common_low, out_total, out_low, small_total, small_all,
         gain_parts, gain_total, gain_all, end_sems, local_sems) = scratch[24:]
        p = Place(reps, depth)
        p.barrier(plane=True, column=True)
        side_job = LineSum(p, lambda at: [side_ref[at]], *a_work)
        side_job.step(0)
        common_job = ColumnSum(p, common_ref, *c_work)
        small_job = ColumnSum(p, small_ref, *s_work)
        x_job = PlaneSum(p, parts_ref, *x_work)
        out_mid, o_sems = o_work[:2]
        for distance in range(1, reps):
            rep = p.rep_at(distance)
            p.send(out_ref.at[rep], out_mid.at[p.rep], o_sems.at[0, distance], o_sems.at[1, distance], p.device(rep=rep))
        out_mid[p.rep] = out_ref[p.rep]
        common_job.ready()
        small_job.ready()
        common_job.step(0)
        small_job.step(0)
        x_job.relay()
        for distance in range(1, reps):
            p.arrived(out_mid.at[p.rep_at(reps - distance)], o_sems.at[1, distance])
        out_job = LineSum(p, lambda at: [out_mid[at]], *o_work[2:])
        out_job.step(0)
        for at in range(1, depth - 1):
            for job in (side_job, common_job, small_job, out_job):
                job.step(at)

        def to_reps(source, target, at):
            for distance in range(1, reps):
                p.send(source, target.at[p.rep], end_sems.at[0, at, distance], end_sems.at[1, at, distance],
                       p.device(rep=p.rep_at(distance)))

        def from_reps(target, at):
            for distance in range(1, reps):
                p.arrived(target.at[p.rep_at(reps - distance)], end_sems.at[1, at, distance])

        side_job.total(side_total)
        side_pair[p.core] = side_total[p.core].astype(BF16)
        side_low = a_work[0].at[p.z, 1 - p.core]
        a_work[0][p.z, 1 - p.core] = side_total[1 - p.core].astype(BF16)
        p.send(side_low, side_pair.at[p.core], swap_sems.at[0], swap_sems.at[1], p.sibling())
        out_job.total(out_total)
        out_low[...] = out_total[...].astype(BF16)
        to_reps(out_low, out_out, 0)
        out_keep = p.local(out_low, out_out.at[p.rep], local_sems.at[0])
        p.arrived(side_pair.at[1 - p.core], swap_sems.at[1])
        to_reps(side_pair, side_out, 1)
        side_keep = p.local(side_pair, side_out.at[p.rep], local_sems.at[1])
        common_job.total(common_total)
        common_low[...] = common_total[...].astype(BF16)
        to_reps(common_low, common_out, 2)
        common_keep = p.local(common_low, common_out.at[p.rep], local_sems.at[2])
        small_job.total(small_total)
        small_all[p.rep] = small_total[...]
        to_reps(small_total, small_all, 3)

        first_grad = x_job.total()
        x = x_ref[...].astype(F32)
        x_scale = rms_rows(x)
        gain_grad = jnp.sum(x * first_grad * x_scale, axis=0, keepdims=True)
        gain_parts[...] = jnp.zeros_like(gain_parts)
        for z in range(depth):
            for core in range(2):
                at = (2 * z + core) * part
                gain_parts[z, core, 0:1, 0:part] = gain_grad[:, at : at + part]
        gain_job = ColumnSum(p, gain_parts, *n_work)
        weighted = first_grad * gain_ref[...]
        tokens_grad_ref[...] = (
            grad_ref[...]
            + x_scale * weighted
            - x * x_scale**3 * jnp.mean(x * weighted, axis=1, keepdims=True)
        ).astype(BF16)
        gain_job.ready()
        for at in range(depth - 1):
            gain_job.step(at)
        gain_job.total(gain_total)
        gain_all[p.rep] = gain_total[...]
        to_reps(gain_total, gain_all, 4)
        from_reps(small_all, 3)
        small_out[...] = add_up(*[small_all[at] for at in range(reps)])
        from_reps(gain_all, 4)
        gain_out[...] = add_up(*[gain_all[at] for at in range(reps)])
        for at, target, keep in ((0, out_out, out_keep), (1, side_out, side_keep), (2, common_out, common_keep)):
            from_reps(target, at)
            keep.wait()
        p.finish()

    return pl.pallas_call(
        kernel,
        in_specs=in_vmem(8),
        out_specs=in_vmem(1) + anywhere(3) + in_vmem(2),
        out_shape=[
            jax.ShapeDtypeStruct((rows, model), BF16),
            jax.ShapeDtypeStruct((reps, 2, part, width), BF16),
            jax.ShapeDtypeStruct((reps, part, common_width), BF16),
            jax.ShapeDtypeStruct((reps, quarter, model), BF16),
            jax.ShapeDtypeStruct(small.shape[2:], F32),
            jax.ShapeDtypeStruct((8, gain_width), F32),
        ],
        scratch_shapes=x_scratch + c_scratch + s_scratch + n_scratch + a_scratch + o_scratch
        + [
            pltpu.VMEM((2, part, width), F32), pltpu.VMEM((2, part, width), BF16), pltpu.SemaphoreType.DMA((2,)),
            pltpu.VMEM((part, common_width), F32), pltpu.VMEM((part, common_width), BF16),
            pltpu.VMEM((quarter, model), F32), pltpu.VMEM((quarter, model), BF16),
            pltpu.VMEM(small.shape[2:], F32), pltpu.VMEM((reps,) + small.shape[2:], F32),
            pltpu.VMEM((depth, 2, 8, gain_width), F32), pltpu.VMEM((8, gain_width), F32),
            pltpu.VMEM((reps, 8, gain_width), F32),
            pltpu.SemaphoreType.DMA((2, 5, reps)), pltpu.SemaphoreType.DMA((3,)),
        ],
        compiler_params=remote_params(3),
        name="finish_input",
    )(parts, tokens, after_grad, in_gain, side, common, out_grad, small)


def slot_match(table_row, capacity, rows):
    slot = lax.broadcasted_iota(jnp.int32, (capacity, rows), 0).astype(F32) + 1.0
    return table_row == slot


def dispatch_kernel(
    local, capacity, half,
    table_ref, own_ref, second_ref, g_ref, router_ref, in_ref, out_ref,
    buffer_ref, slot_g_ref, gate_slot_ref, gates_ref, hidden_ref, grad_ref, in_grad_ref, out_grad_ref,
    in_total, out_total,
):
    at = pl.program_id(0)
    second, g = second_ref[...], g_ref[...]
    rows = second.shape[0]
    table = table_ref[...].astype(F32)
    used = table > 0.0
    logits = mm_nt(router_ref[...], second)
    top = jnp.max(jnp.where(used, logits, -jnp.inf), axis=0, keepdims=True)
    raw = jnp.where(used, jnp.exp(jnp.where(used, logits - top, 0.0)), 0.0)
    gates = raw / jnp.sum(raw, axis=0, keepdims=True)
    gates_ref[...] = gates
    expert = lax.broadcasted_iota(jnp.int32, gates.shape, 0)
    shard = 2 * lax.axis_index("z") + lax.axis_index("core")
    for i in range(local):
        match = slot_match(own_ref[i : i + 1, :].astype(F32), capacity, rows)
        onehot = match.astype(BF16)
        buffer_ref[i] = mm(onehot, second).astype(BF16)
        slot_g_ref[i] = mm(onehot, g).astype(BF16)
        gate_row = jnp.sum(jnp.where(expert == local * shard + i, gates, 0.0), axis=0, keepdims=True)
        gate_slot = jnp.sum(jnp.where(match, gate_row, 0.0), axis=1, keepdims=True)
        gate_slot_ref[i] = jnp.broadcast_to(gate_slot, (capacity, LANES))
    pre = mm(second, in_ref[...])
    a, b = pre[:, :half], pre[:, half:]
    sig = jax.nn.sigmoid(a)
    hidden = (a * sig * b).astype(BF16)
    hidden_ref[...] = hidden
    back = mm_nt(g, out_ref[...])
    grad = jnp.concatenate([back * b * silu_slope(a, sig), back * a * sig], axis=1).astype(BF16)
    grad_ref[...] = grad

    @pl.when(at == 0)
    def _():
        in_total[...] = jnp.zeros_like(in_total)
        out_total[...] = jnp.zeros_like(out_total)

    in_total[...] += mm_tn(second, grad)
    out_total[...] += mm_tn(hidden, g)

    @pl.when(at == pl.num_programs(0) - 1)
    def _():
        in_grad_ref[...] = in_total[...].astype(BF16)
        out_grad_ref[...] = out_total[...].astype(BF16)


def dispatch(table, own, second, g, router_t, shared_in, shared_out, capacity):
    group, experts, rows = table.shape
    local = own.shape[1]
    model = second.shape[1]
    half = shared_out.shape[0]
    slots = group * capacity

    def by_block(*shape):
        return pl.BlockSpec((None,) + shape, lambda q: (q,) + (0,) * len(shape))

    def by_slots(width):
        return pl.BlockSpec((local, capacity, width), lambda q: (0, q, 0))

    return pl.pallas_call(
        functools.partial(dispatch_kernel, local, capacity, half),
        grid=(group,),
        in_specs=[
            by_block(experts, rows), by_block(local, rows), by_rows((rows, model)), by_rows((rows, model)),
            whole((experts, model)), whole((model, 2 * half)), whole((half, model)),
        ],
        out_specs=[
            by_slots(model), by_slots(model), by_slots(LANES), by_block(experts, rows), by_rows((rows, half)),
            by_rows((rows, 2 * half)), whole((model, 2 * half)), whole((half, model)),
        ],
        out_shape=[
            jax.ShapeDtypeStruct((local, slots, model), BF16),
            jax.ShapeDtypeStruct((local, slots, model), BF16),
            jax.ShapeDtypeStruct((local, slots, LANES), F32),
            jax.ShapeDtypeStruct((group, experts, rows), F32),
            jax.ShapeDtypeStruct((group * rows, half), BF16),
            jax.ShapeDtypeStruct((group * rows, 2 * half), BF16),
            jax.ShapeDtypeStruct((model, 2 * half), BF16),
            jax.ShapeDtypeStruct((half, model), BF16),
        ],
        scratch_shapes=[pltpu.VMEM((model, 2 * half), F32), pltpu.VMEM((half, model), F32)],
        compiler_params=pltpu.CompilerParams(vmem_limit_bytes=56 * 2**20),
        name="dispatch",
    )(table, own, second, g, router_t, shared_in, shared_out)


def experts_kernel(
    buffer_ref, slot_g_ref, gate_ref, in_ref, out_ref,
    weighted_ref, back_ref, dot_ref, in_grad_ref, out_grad_ref, in_total, out_total,
):
    at = pl.program_id(1)
    buffer, weight_in, weight_out = buffer_ref[...], in_ref[...], out_ref[...]
    half = weight_out.shape[0]
    pre = mm(buffer, weight_in)
    a, b = pre[:, :half], pre[:, half:]
    sig = jax.nn.sigmoid(a)
    act = a * sig
    hidden = (act * b).astype(BF16)
    gate = gate_ref[:, 0:1]
    slot_g = slot_g_ref[...].astype(F32)
    result = mm(hidden, weight_out).astype(BF16).astype(F32)
    weighted_ref[...] = (gate * result).astype(BF16)
    dot_ref[...] = jnp.broadcast_to(jnp.sum(slot_g * result, axis=1, keepdims=True), dot_ref.shape)
    result_grad = (gate * slot_g).astype(BF16)
    hidden_grad = mm_nt(result_grad, weight_out)
    pre_grad = jnp.concatenate([hidden_grad * b * silu_slope(a, sig), hidden_grad * act], axis=1).astype(BF16)
    back_ref[...] = mm_nt(pre_grad, weight_in).astype(BF16)

    @pl.when(at == 0)
    def _():
        in_total[...] = jnp.zeros_like(in_total)
        out_total[...] = jnp.zeros_like(out_total)

    in_total[...] += mm_tn(buffer, pre_grad)
    out_total[...] += mm_tn(hidden, result_grad)

    @pl.when(at == pl.num_programs(1) - 1)
    def _():
        in_grad_ref[...] = in_total[...].astype(BF16)
        out_grad_ref[...] = out_total[...].astype(BF16)


def run_experts(buffer, slot_g, gate_slot, expert_in, expert_out, step):
    local, slots, model = buffer.shape
    half = expert_out.shape[1]

    def by_step(width):
        return pl.BlockSpec((None, step, width), lambda i, m: (i, m, 0))

    def by_expert(*shape):
        return pl.BlockSpec((None,) + shape, lambda i, m: (i, 0, 0))

    return pl.pallas_call(
        experts_kernel,
        grid=(local, slots // step),
        in_specs=[
            by_step(model), by_step(model), by_step(LANES), by_expert(model, 2 * half), by_expert(half, model),
        ],
        out_specs=[
            by_step(model), by_step(model), by_step(LANES), by_expert(model, 2 * half), by_expert(half, model),
        ],
        out_shape=[
            jax.ShapeDtypeStruct((local, slots, model), BF16),
            jax.ShapeDtypeStruct((local, slots, model), BF16),
            jax.ShapeDtypeStruct((local, slots, LANES), F32),
            jax.ShapeDtypeStruct((local, model, 2 * half), BF16),
            jax.ShapeDtypeStruct((local, half, model), BF16),
        ],
        scratch_shapes=[pltpu.VMEM((model, 2 * half), F32), pltpu.VMEM((half, model), F32)],
        compiler_params=pltpu.CompilerParams(vmem_limit_bytes=62 * 2**20),
        name="run_experts",
    )(buffer, slot_g, gate_slot, expert_in, expert_out)


def combine_kernel(
    local, capacity,
    own_ref, gates_ref, dot_ref, weighted_ref, back_ref, second_ref, hidden_ref, grad_ref, router_ref, in_ref, out_ref,
    second_part_ref, layer_part_ref, router_grad_ref,
):
    gates = gates_ref[...]
    rows = gates.shape[1]
    expert = lax.broadcasted_iota(jnp.int32, gates.shape, 0)
    shard = 2 * lax.axis_index("z") + lax.axis_index("core")
    gate_grad = jnp.zeros_like(gates)
    second_part = mm_nt(grad_ref[...], in_ref[...])
    layer_part = mm(hidden_ref[...], out_ref[...])
    for i in range(local):
        match = slot_match(own_ref[i : i + 1, :].astype(F32), capacity, rows)
        onehot = match.astype(BF16)
        second_part = second_part + mm_tn(onehot, back_ref[i])
        layer_part = layer_part + mm_tn(onehot, weighted_ref[i])
        row = jnp.sum(jnp.where(match, dot_ref[i, :, 0:1], 0.0), axis=0, keepdims=True)
        gate_grad = jnp.where(expert == local * shard + i, row, gate_grad)
    logit_grad = gates * (gate_grad - jnp.sum(gates * gate_grad, axis=0, keepdims=True))
    high, low = split_two(logit_grad)
    router = router_ref[...]
    second_part = second_part + mm_tn(high, router) + mm_tn(low, router)
    second_part_ref[...] = second_part.astype(BF16)
    layer_part_ref[...] = layer_part.astype(BF16)
    second = second_ref[...]

    @pl.when(pl.program_id(0) == 0)
    def _():
        router_grad_ref[...] = jnp.zeros_like(router_grad_ref)

    router_grad_ref[...] += mm(high, second) + mm(low, second)


def combine(own, gates, dots, weighted, back, second, hidden, grad, router_t, shared_in, shared_out, capacity):
    group, experts, rows = gates.shape
    local = own.shape[1]
    model = second.shape[1]
    half = shared_out.shape[0]

    def by_block(*shape):
        return pl.BlockSpec((None,) + shape, lambda q: (q,) + (0,) * len(shape))

    def by_slots(width):
        return pl.BlockSpec((local, capacity, width), lambda q: (0, q, 0))

    return pl.pallas_call(
        functools.partial(combine_kernel, local, capacity),
        grid=(group,),
        in_specs=[
            by_block(local, rows), by_block(experts, rows), by_slots(LANES), by_slots(model), by_slots(model),
            by_rows((rows, model)), by_rows((rows, half)), by_rows((rows, 2 * half)),
            whole((experts, model)), whole((model, 2 * half)), whole((half, model)),
        ],
        out_specs=[by_rows((rows, model)), by_rows((rows, model)), whole((experts, model))],
        out_shape=[
            jax.ShapeDtypeStruct((group * rows, model), BF16),
            jax.ShapeDtypeStruct((group * rows, model), BF16),
            jax.ShapeDtypeStruct((experts, model), F32),
        ],
        compiler_params=pltpu.CompilerParams(vmem_limit_bytes=56 * 2**20),
        name="combine",
    )(own, gates, dots, weighted, back, second, hidden, grad, router_t, shared_in, shared_out)


def gather(values, axes, axis=0):
    return lax.all_gather(values, axes, axis=axis, tiled=True)


def scatter_sum(values, axes, axis=0):
    return lax.psum_scatter(values, axes, scatter_dimension=axis, tiled=True)


def columns_of(values, start, size, axis=1):
    return lax.dynamic_slice_in_dim(values, start, size, axis=axis)


def shards(
    tokens,
    cotangent,
    dealt_to,
    lengths,
    routes,
    slot_index,
    in_norm,
    in_proj,
    conv_weight,
    conv_bias,
    dt_bias,
    decay_log,
    skip_gain,
    mixer_norm,
    out_proj,
    post_norm,
    router,
    shared_in,
    shared_out,
    expert_in,
    expert_out,
):
    reps, depth = lax.axis_size("rep"), lax.axis_size("z")
    group = 2 * depth
    rep, z, core = lax.axis_index("rep"), lax.axis_index("z"), lax.axis_index("core")
    shard = 2 * z + core
    team = 2 * rep + core
    members = 2 * reps
    rows, model = tokens.shape
    top = routes.shape[1]
    local = expert_in.shape[0]
    experts = local * group
    capacity = rows * top * 4 // (3 * experts)
    inner = mixer_norm.shape[0] * group
    convolved = conv_bias.shape[0] * group
    head_count = dt_bias.shape[0] * group
    width = inner // head_count
    state = (convolved - inner) // 2
    channels = inner // members
    heads = head_count // members
    shared = shared_out.shape[0]
    part = in_norm.shape[0]

    expert_ids = jnp.arange(experts, dtype=jnp.int32)
    table = jnp.sum(
        jnp.where(routes[:, None, :] == expert_ids[None, :, None], slot_index[:, None, :] + 1, 0), axis=2
    ).astype(BF16)
    numbers = jnp.pad(jnp.concatenate([lengths[0], dealt_to])[None, :], ((0, 7), (0, LANES - lengths.shape[1] - 1)))
    pieces = [
        table.T.reshape(-1), in_norm, conv_weight.reshape(-1), conv_bias, dt_bias, decay_log, skip_gain,
        mixer_norm, post_norm, router.reshape(-1),
    ]
    sizes = [piece.shape[0] for piece in pieces]
    pack = jnp.concatenate(pieces)
    pack_wide = -(-pack.shape[0] // (16 * LANES)) * LANES
    pack = jnp.pad(pack, (0, 16 * pack_wide - pack.shape[0])).reshape(16, pack_wide)
    pair_heads = 2 * heads
    dt_pair = columns_of(in_proj, inner + convolved + pair_heads * rep, pair_heads)
    blank = jnp.zeros((part, LANES // 2 - heads), BF16)
    common = jnp.concatenate(
        [in_proj[:, 2 * inner : 2 * inner + 2 * state], dt_pair[:, :heads], blank, dt_pair[:, heads:], blank], axis=1
    )

    def pair_of(member):
        return jnp.concatenate(
            [columns_of(in_proj, channels * member, channels), columns_of(in_proj, inner + channels * member, channels)],
            axis=1,
        )

    x_plane, weight, packed, numbers_all, out_own, _ = start_gather(
        tokens, pair_of(team), pair_of(2 * rep + 1 - core), common, pack, numbers,
        out_proj.reshape(reps, channels // reps, model), reps, depth,
    )
    x_plane = x_plane.reshape(members * rows, model)
    weight = weight.reshape(model, -1)
    out_own = out_own.reshape(channels, model)
    numbers_all = numbers_all[:, 0, :4].reshape(reps, group, 4)
    packed = packed.reshape(group, -1)
    unpacked, offset = [], 0
    for size in sizes:
        unpacked.append(packed[:, offset : offset + size])
        offset += size
    table_all = unpacked[0].reshape(group, experts, rows)
    in_gain = unpacked[1].reshape(1, model).astype(F32)
    taps_full = unpacked[2].reshape(group, -1, convolved // group).transpose(1, 0, 2).reshape(-1, convolved)
    taps_full = jnp.concatenate(
        [taps_full, unpacked[3].reshape(1, convolved), jnp.zeros((3, convolved), BF16)], axis=0
    ).astype(F32)
    dt_full, decay_full, skip_full = [unpacked[at].reshape(head_count).astype(F32) for at in (4, 5, 6)]
    mixer_gain = unpacked[7].reshape(1, inner).astype(F32)
    post_gain = unpacked[8].reshape(1, model).astype(F32)
    router_full = unpacked[9].reshape(model, experts)

    g_column = gather(lax.optimization_barrier((cotangent, x_plane))[0], COLUMN)
    shared_in_own = lax.all_to_all(
        shared_in.reshape(part, 2, group, shared).transpose(2, 0, 1, 3).reshape(group * part, 2 * shared),
        COLUMN, split_axis=0, concat_axis=0, tiled=True,
    )

    dealt_column = lax.dynamic_index_in_dim(numbers_all[:, :, 3], rep, axis=0, keepdims=False)
    table_dealt = jnp.take(table_all, dealt_column, axis=0)
    table_own = columns_of(table_dealt, local * shard, local)

    blocks = numbers_all[:, :, 3].reshape(reps, depth, 2)
    dealt_plane = lax.dynamic_index_in_dim(blocks, z, axis=1, keepdims=False)
    lengths_plane = jnp.take_along_axis(numbers_all[:, :, :3], dealt_plane[:, :, None], axis=1).reshape(members, 3)
    ends = jnp.cumsum(lengths_plane, axis=1)
    position = jnp.arange(rows, dtype=jnp.int32)
    seg = jnp.sum((position[None, :, None] >= ends[:, None, :]).astype(jnp.int32), axis=2)

    taps_own = jnp.concatenate(
        [columns_of(taps_full, channels * team, channels), taps_full[:, inner:]], axis=1
    )
    own_heads = [lax.dynamic_slice_in_dim(v, heads * team, heads) for v in (dt_full, decay_full, skip_full)]
    head_rows = jnp.pad(jnp.stack([own_heads[0], jnp.exp(own_heads[1])]), ((0, 6), (0, LANES - heads)))
    skip_own = jnp.repeat(own_heads[2], width)[None, :]
    norm_own = columns_of(mixer_gain, channels * team, channels)
    mixer_args = (
        x_plane, in_gain, weight, seg.reshape(members * rows, 1), seg[:, None, :], taps_own, head_rows, skip_own,
        norm_own, out_own,
    )
    parts, squares, projected = mixer_forward(mixer_args, rows, channels, width, state)
    after, mixer_result, scale, second_column = join_mixer(
        parts.reshape(reps, 2, rows, model), squares.reshape(reps, 2, 8, rows), tokens, post_gain, inner, reps, depth
    )
    second_column = second_column.reshape(group * rows, model)

    router_t = router_full.T
    buffer, slot_g, gate_slot, gates, shared_hidden, shared_grad, shared_in_grad, shared_out_grad = dispatch(
        table_dealt, table_own, second_column, g_column, router_t, shared_in_own, shared_out, capacity
    )
    weighted, buffer_grad, dots, grad_expert_in, grad_expert_out = run_experts(
        buffer, slot_g, gate_slot, expert_in, expert_out, group * capacity // 2
    )
    second_part, layer_part, router_grad = combine(
        table_own, gates, dots, weighted, buffer_grad, second_column, shared_hidden, shared_grad, router_t,
        shared_in_own, shared_out, capacity,
    )
    shared_in_rows = lax.all_to_all(shared_in_grad, COLUMN, split_axis=0, concat_axis=0, tiled=True)
    shared_in_rows = shared_in_rows.reshape(group, part, 2, shared).transpose(1, 2, 0, 3).reshape(part, -1)
    grad_expert_in, grad_expert_out, grad_shared_out, grad_shared_in = [
        values.astype(F32)
        for values in lax.psum((grad_expert_in, grad_expert_out, shared_out_grad, shared_in_rows), "rep")
    ]
    router_grad = router_grad.T

    after_grad, post_grad, layer_out, low_plane, scales = join_experts(
        second_part.reshape(depth, 2, rows, model), layer_part.reshape(depth, 2, rows, model), cotangent, after,
        mixer_result, scale, post_gain, inner, reps, depth,
    )
    back_parts, in_grad, out_grad, taps_grad, heads_grad, wide_grad = mixer_backward(
        mixer_args, projected, low_plane.reshape(members * rows, model), scales.reshape(members, 2, 8, rows),
        rows, channels, width, state,
    )
    def placed(values, size, start):
        blank_row = jnp.zeros(values.shape[:-1] + (size,), F32)
        return lax.dynamic_update_slice_in_dim(blank_row, values, start, axis=values.ndim - 1)

    taps_full_grad = jnp.concatenate(
        [placed(taps_grad[:5, :channels], inner, channels * team), taps_grad[:5, channels:]], axis=1
    )
    skip_head_grad = jnp.sum(wide_grad[1].reshape(heads, width), axis=1)
    small = [
        taps_full_grad.reshape(5, group, -1).transpose(1, 0, 2).reshape(group, -1),
        placed(heads_grad[0, :heads], head_count, heads * team).reshape(group, -1),
        placed(heads_grad[1, :heads], head_count, heads * team).reshape(group, -1),
        placed(skip_head_grad, head_count, heads * team).reshape(group, -1),
        placed(wide_grad[0], inner, channels * team).reshape(group, -1),
        post_grad.reshape(group, -1),
        router_grad.reshape(group, -1),
    ]
    small_sizes = [piece.shape[1] for piece in small]
    small = jnp.concatenate(small, axis=1)
    small_wide = -(-small.shape[1] // (8 * LANES)) * LANES
    small = jnp.pad(small, ((0, 0), (0, 8 * small_wide - small.shape[1]))).reshape(depth, 2, 8, small_wide)
    pair = 2 * channels
    in_low = in_grad.astype(BF16).reshape(depth, 2, part, -1)
    grad_tokens, side_rows, common_rows, out_rows, small_sum, gain_sum = finish_input(
        back_parts.reshape(reps, 2, rows, model), tokens, after_grad, in_gain, in_low[:, :, :, :pair],
        in_low[:, :, :, pair:], out_grad.astype(BF16).reshape(reps, channels // reps, model), small, reps, depth,
    )
    small_sum = small_sum.reshape(-1)
    dt_rows = common_rows[:, :, 2 * state :].reshape(reps, part, 2, LANES // 2)[:, :, :, :heads]
    grad_in_proj = jnp.concatenate(
        [
            side_rows[:, :, :, :channels].transpose(2, 0, 1, 3).reshape(part, inner).astype(F32),
            side_rows[:, :, :, channels:].transpose(2, 0, 1, 3).reshape(part, inner).astype(F32),
            jnp.sum(common_rows[:, :, : 2 * state].astype(F32), axis=0),
            dt_rows.transpose(1, 0, 2, 3).reshape(part, head_count).astype(F32),
        ],
        axis=1,
    )
    grad_out_proj = out_rows.reshape(channels, model).astype(F32)
    small_out, offset = [], 0
    for size in small_sizes:
        small_out.append(small_sum[offset : offset + size])
        offset += size
    taps_out = small_out[0].reshape(5, -1)
    return (
        layer_out,
        grad_tokens,
        gain_sum[0, :part],
        grad_in_proj,
        taps_out[:4],
        taps_out[4],
        small_out[1],
        small_out[2],
        small_out[3],
        small_out[4],
        grad_out_proj,
        small_out[5],
        small_out[6].reshape(part, experts),
        grad_shared_in,
        grad_shared_out,
        grad_expert_in,
        grad_expert_out,
    )


def solution(mesh):
    reps, group = mesh.shape["rep"], mesh.shape["shard"]
    split = Mesh(mesh.devices.reshape(reps, group // 2, 2), ALL)
    one, row = P(COLUMN), P(COLUMN, None)
    token = P(ALL, None)
    return jax.shard_map(
        shards,
        mesh=split,
        in_specs=(
            token, token, P(ALL), token, token, token, one, row, P(None, COLUMN), one, one, one, one, one, row,
            one, row, row, row, P(COLUMN, None, None), P(COLUMN, None, None),
        ),
        out_specs=(
            token, token, one, row, P(None, COLUMN), one, one, one, one, one, row, one, row, row, row,
            P(COLUMN, None, None), P(COLUMN, None, None),
        ),
        check_vma=False,
    )
```

```python
import functools

import jax
import jax.numpy as jnp
from jax import lax
from jax.experimental import pallas as pl
from jax.experimental.pallas import tpu as pltpu
from jax.sharding import Mesh
from jax.sharding import PartitionSpec as P

EPS = 1e-05
HIGH = lax.Precision.HIGHEST
F32 = jnp.float32
BF16 = jnp.bfloat16
ALL = ("rep", "z", "core")
COLUMN = ("z", "core")
PLANE = ("rep", "core")
LANES = 128


def rms_rows(values):
    return lax.rsqrt(jnp.mean(values * values, axis=-1, keepdims=True) + EPS)


def mm(left, right):
    return jnp.dot(left, right, preferred_element_type=F32)


def mm_nt(left, right):
    return lax.dot_general(left, right, (((1,), (1,)), ((), ())), preferred_element_type=F32)


def mm_tn(left, right):
    return lax.dot_general(left, right, (((0,), (0,)), ((), ())), preferred_element_type=F32)


def silu_slope(values, sig):
    return sig * (1.0 + values * (1.0 - sig))


def split_two(values):
    high = values.astype(BF16)
    return high, (values - high.astype(F32)).astype(BF16)


def segments(lengths_row, sequences, rows):
    column = lax.broadcasted_iota(jnp.int32, (rows, 1), 0).astype(F32)
    line = lax.broadcasted_iota(jnp.int32, (1, rows), 1).astype(F32)
    end = jnp.zeros((1, 1), F32)
    seg_column, seg_line = jnp.zeros_like(column), jnp.zeros_like(line)
    for at in range(sequences):
        end = end + lengths_row[:, at : at + 1]
        seg_column = seg_column + jnp.where(column >= end, 1.0, 0.0)
        seg_line = seg_line + jnp.where(line >= end, 1.0, 0.0)
    return seg_column, seg_line


class Block:
    def __init__(self, proj, seg_col, seg_row, taps, heads, channels, width, state):
        rows = proj.shape[0]
        self.rows, self.channels, self.width, self.state = rows, channels, width, state
        self.gate = proj[:, :channels]
        self.xbc = proj[:, channels : 2 * channels + 2 * state]
        self.turn = lax.axis_index("core") * (LANES // 2)
        dt_raw = pltpu.roll(proj[:, 2 * channels + 2 * state :], self.turn, 1)
        position = lax.broadcasted_iota(jnp.int32, (rows, 1), 0)
        seg_wide = jnp.broadcast_to(seg_col, (rows, LANES))
        self.masks = []
        conv = taps[4:5, :] + taps[3:4, :] * self.xbc
        for offset in (1, 2, 3):
            before = pltpu.roll(seg_wide, offset, 0)[:, :1]
            mask = jnp.where((before == seg_col) & (position >= offset), 1.0, 0.0)
            self.masks.append(mask)
            conv = conv + taps[3 - offset : 4 - offset, :] * (mask * pltpu.roll(self.xbc, offset, 0))
        self.conv = conv
        self.conv_sig = jax.nn.sigmoid(conv)
        act = conv * self.conv_sig
        self.xin = act[:, :channels]
        self.write = act[:, channels : channels + state]
        self.read = act[:, channels + state :]
        shifted = dt_raw + heads[0:1, :]
        self.step = jnp.maximum(shifted, 0.0) + jnp.log1p(jnp.exp(-jnp.abs(shifted)))
        self.step_sig = jax.nn.sigmoid(shifted)
        self.speed = heads[1:2, :]
        self.rate = -self.step * self.speed
        row_at = lax.broadcasted_iota(jnp.int32, (rows, rows), 0)
        col_at = lax.broadcasted_iota(jnp.int32, (rows, rows), 1)
        self.causal = row_at >= col_at
        self.keep = self.causal & (seg_col == seg_row)
        self.cum = jnp.dot(self.causal.astype(F32), self.rate, precision=HIGH, preferred_element_type=F32)
        self.cum_t = self.cum.T
        scores = lax.dot_general(
            self.read, self.write, (((1,), (1,)), ((), ())), precision=HIGH, preferred_element_type=F32
        )
        self.scores = jnp.where(self.keep, scores, 0.0)

    def groups(self):
        for start in range(0, self.channels, LANES):
            stop = min(start + LANES, self.channels)
            yield start, stop, list(range(start // self.width, (stop - 1) // self.width + 1))

    def spread(self, columns, start, stop, heads):
        lane = lax.broadcasted_iota(jnp.int32, (self.rows, stop - start), 1) + start
        result = jnp.broadcast_to(columns[:, heads[0] : heads[0] + 1], (self.rows, stop - start))
        for head in heads[1:]:
            result = jnp.where(lane >= head * self.width, columns[:, head : head + 1], result)
        return result

    def inside(self, start, stop, head):
        lane = lax.broadcasted_iota(jnp.int32, (self.rows, stop - start), 1) + start
        return (lane >= head * self.width) & (lane < (head + 1) * self.width)

    def decay(self, head):
        gaps = self.cum[:, head : head + 1] - self.cum_t[head : head + 1, :]
        return jnp.exp(jnp.where(self.keep, gaps, 0.0))


def block_back(block, low, scale, pull, taps_ref, skip_ref, norm_ref, weight, out_weight):
    rows, channels = block.rows, block.channels
    normed_grad = mm_nt(low, out_weight)
    taps = taps_ref[...]
    gate_grads, x_grads, norm_grads, skip_grads = [], [], [], []
    step_grad = jnp.zeros((rows, LANES), F32)
    cum_grad = jnp.zeros((rows, LANES), F32)
    cum_grad_t = jnp.zeros((LANES, rows), F32)
    score_grad = jnp.zeros((rows, rows), F32)
    lane_all = lax.broadcasted_iota(jnp.int32, (rows, LANES), 1)
    sub_all = lax.broadcasted_iota(jnp.int32, (LANES, rows), 0)
    for start, stop, heads in block.groups():
        xin = block.xin[:, start:stop]
        spread = block.spread(block.step, start, stop, heads)
        scaled, scaled_rest = split_two(xin * spread)
        scaled_wide = jnp.concatenate([scaled, scaled, scaled_rest], axis=1)
        weights, decays = [], []
        y = None
        for head in heads:
            decays.append(block.decay(head))
            weights.append(block.scores * decays[-1])
            term = mm(weights[-1].astype(BF16), scaled)
            y = term if y is None else jnp.where(block.inside(start, stop, head), term, y)
        skip = skip_ref[:, start:stop]
        y = y + skip * xin
        gate = block.gate[:, start:stop]
        gate_sig = jax.nn.sigmoid(gate)
        gate_act = gate * gate_sig
        mixed = y * gate_act
        q = normed_grad[:, start:stop]
        norm_grads.append(jnp.sum(mixed * scale * q, axis=0, keepdims=True))
        mixed_grad = scale * norm_ref[:, start:stop] * q - mixed * pull
        gate_grads.append(mixed_grad * y * silu_slope(gate, gate_sig))
        y_grad = mixed_grad * gate_act
        skip_grads.append(jnp.sum(y_grad * xin, axis=0, keepdims=True))
        y_low, y_rest = split_two(y_grad)
        scaled_grad = None
        for at, head in enumerate(heads):
            inside = block.inside(start, stop, head)
            term = mm_tn(weights[at].astype(BF16), y_low)
            scaled_grad = term if scaled_grad is None else jnp.where(inside, term, scaled_grad)
            blank = jnp.zeros_like(y_low)
            y_own = jnp.where(inside, y_low, blank)
            pair_grad = mm_nt(
                jnp.concatenate([y_own, jnp.where(inside, y_rest, blank), y_own], axis=1), scaled_wide
            )
            score_grad = score_grad + pair_grad * decays[at]
            exponent_grad = pair_grad * weights[at]
            cum_grad = jnp.where(lane_all == head, jnp.sum(exponent_grad, axis=1, keepdims=True), cum_grad)
            cum_grad_t = jnp.where(sub_all == head, jnp.sum(exponent_grad, axis=0, keepdims=True), cum_grad_t)
        for head in heads:
            inside = block.inside(start, stop, head)
            per_row = jnp.sum(jnp.where(inside, scaled_grad * xin, 0.0), axis=1, keepdims=True)
            step_grad = jnp.where(lane_all == head, per_row, step_grad)
        x_grads.append(scaled_grad * spread + skip * y_grad)
    score_grad = jnp.where(block.keep, score_grad, 0.0).astype(BF16)
    read_grad = mm(score_grad, block.write.astype(BF16))
    write_grad = mm_tn(score_grad, block.read.astype(BF16))
    cum_grad = cum_grad - cum_grad_t.T
    rate_grad = lax.dot_general(
        block.causal.astype(F32), cum_grad, (((0,), (0,)), ((), ())), precision=HIGH, preferred_element_type=F32
    )
    dt_grad = (step_grad - block.speed * rate_grad) * block.step_sig
    head_rows = [jnp.sum(dt_grad, axis=0, keepdims=True), jnp.sum(rate_grad * block.rate, axis=0, keepdims=True)]
    act_grad = jnp.concatenate(x_grads + [write_grad, read_grad], axis=1)
    conv_grad = act_grad * silu_slope(block.conv, block.conv_sig)
    tap_rows = {4: jnp.sum(conv_grad, axis=0, keepdims=True), 3: jnp.sum(conv_grad * block.xbc, axis=0, keepdims=True)}
    xbc_grad = taps[3:4, :] * conv_grad
    for offset in (1, 2, 3):
        masked = conv_grad * block.masks[offset - 1]
        tap_rows[3 - offset] = jnp.sum(masked * pltpu.roll(block.xbc, offset, 0), axis=0, keepdims=True)
        xbc_grad = xbc_grad + taps[3 - offset : 4 - offset, :] * pltpu.roll(masked, rows - offset, 0)
    proj_grad = jnp.concatenate(gate_grads + [xbc_grad, pltpu.roll(dt_grad, block.turn, 1)], axis=1).astype(BF16)
    tap_grads = jnp.concatenate([tap_rows[at] for at in range(5)], axis=0)
    wide_grads = jnp.concatenate(
        [jnp.concatenate(norm_grads, axis=1), jnp.concatenate(skip_grads, axis=1)], axis=0
    )
    return proj_grad, tap_grads, head_rows, wide_grads


def whole(shape):
    return pl.BlockSpec(shape, lambda i: (0,) * len(shape))


def by_rows(shape):
    return pl.BlockSpec(shape, lambda i: (i,) + (0,) * (len(shape) - 1))


MESH_ID = pl.DeviceIdType.MESH


def when(condition, action):
    if condition is True:
        action()
    elif condition is not False:
        pl.when(condition)(action)


class Place:
    def __init__(self, reps, depth):
        self.reps, self.depth = reps, depth
        self.rep, self.z, self.core = lax.axis_index("rep"), lax.axis_index("z"), lax.axis_index("core")
        self.here = {"rep": self.rep, "z": self.z, "core": self.core}
        self.pending = []

    def device(self, **changes):
        return {**self.here, **changes}

    def sibling(self):
        return self.device(core=1 - self.core)

    def rep_at(self, distance):
        result, place = 0, 1
        while place < self.reps:
            mine, other = lax.rem(self.rep // place, 2), lax.rem(distance // place, 2)
            result = result + place * (mine + other - 2 * mine * other)
            place *= 2
        return result

    def barrier(self, plane=False, column=False, everyone=False):
        semaphore = pltpu.get_barrier_semaphore()

        def greet(device):
            pl.semaphore_signal(semaphore, inc=1, device_id=device, device_id_type=MESH_ID)

        if everyone:
            count = self.reps * self.depth * 2
            mine = (self.rep * self.depth + self.z) * 2 + self.core

            def step(distance, carry):
                other = lax.rem(mine + distance, count)
                greet({"rep": other // (2 * self.depth), "z": lax.rem(other // 2, self.depth), "core": lax.rem(other, 2)})
                return carry

            lax.fori_loop(1, count, step, 0)
            pl.semaphore_wait(semaphore, count - 1)
            return
        amount = 1
        greet(self.sibling())
        if plane:
            for distance in range(1, self.reps):
                greet(self.device(rep=self.rep_at(distance)))
            amount = amount + self.reps - 1
        if column:
            above, below = self.z < self.depth - 1, self.z > 0
            when(above, lambda: greet(self.device(z=self.z + 1)))
            when(below, lambda: greet(self.device(z=self.z - 1)))
            amount = amount + jnp.where(above, 1, 0) + jnp.where(below, 1, 0)
        pl.semaphore_wait(semaphore, amount)

    def send(self, source, target, send_sem, recv_sem, device, condition=True):
        copy = pltpu.make_async_remote_copy(
            src_ref=source, dst_ref=target, send_sem=send_sem, recv_sem=recv_sem, device_id=device,
            device_id_type=MESH_ID,
        )
        when(condition, copy.start)
        self.pending.append((condition, copy))

    def local(self, source, target, sem):
        copy = pltpu.make_async_copy(source, target, sem)
        copy.start()
        return copy

    def arrived(self, target, recv_sem, condition=True):
        copy = pltpu.make_async_remote_copy(
            src_ref=target, dst_ref=target, send_sem=recv_sem, recv_sem=recv_sem, device_id=self.sibling(),
            device_id_type=MESH_ID,
        )
        when(condition, copy.wait_recv)

    def finish(self):
        for condition, copy in self.pending:
            when(condition, copy.wait_send)
        self.pending = []


class PlaneGather:
    @staticmethod
    def scratch(reps):
        return [pltpu.SemaphoreType.DMA((4, reps)), pltpu.SemaphoreType.DMA((1,))]

    def __init__(self, place, own, out, sems, local_sem):
        self.place, self.out, self.sems = place, out, sems
        p = place
        self.keep = p.local(own, out.at[p.rep, p.core], local_sem.at[0])
        for distance in range(1, p.reps):
            p.send(own, out.at[p.rep, p.core], sems.at[0, distance], sems.at[1, distance],
                   p.device(rep=p.rep_at(distance)))
        p.send(own, out.at[p.rep, p.core], sems.at[2, 0], sems.at[3, 0], p.sibling())

    def relay(self):
        p = self.place
        for distance in range(1, p.reps):
            source = self.out.at[p.rep_at(distance), p.core]
            p.arrived(source, self.sems.at[1, distance])
            p.send(source, source, self.sems.at[2, distance], self.sems.at[3, distance], p.sibling())

    def finish(self):
        p = self.place
        self.keep.wait()
        for distance in range(p.reps):
            source = p.rep_at(distance) if distance else p.rep
            p.arrived(self.out.at[source, 1 - p.core], self.sems.at[3, distance])


class ColumnGather:
    @staticmethod
    def scratch(depth):
        return [pltpu.SemaphoreType.DMA((8, depth)), pltpu.SemaphoreType.DMA((1,))]

    def __init__(self, place, own, slot, sems, local_sem, shared=None, keep=True):
        self.place, self.slot, self.sems, self.shared = place, slot, sems, shared
        p = place
        self.keep = p.local(own, slot(p.z), local_sem.at[0]) if keep else None
        self.onward(own, slot(p.z), 0, True, True)
        if shared is not None:
            p.send(own, slot(p.z), sems.at[4, 0], sems.at[5, 0], p.sibling())

    def onward(self, source, target, distance, up, down):
        p = self.place
        if up is not False:
            p.send(source, target, self.sems.at[0, distance], self.sems.at[1, distance], p.device(z=p.z + 1),
                   (p.z < p.depth - 1) if up is True else up & (p.z < p.depth - 1))
        if down is not False:
            p.send(source, target, self.sems.at[2, distance], self.sems.at[3, distance], p.device(z=p.z - 1),
                   (p.z > 0) if down is True else down & (p.z > 0))

    def hop(self, distance):
        p = self.place
        below, above = p.z >= distance, p.z + distance < p.depth
        low, high = self.slot(jnp.maximum(p.z - distance, 0)), self.slot(jnp.minimum(p.z + distance, p.depth - 1))
        p.arrived(low, self.sems.at[1, distance - 1], below)
        self.onward(low, low, distance, below, False)
        if self.shared is not None:
            p.send(low, low, self.sems.at[4, distance], self.sems.at[5, distance], p.sibling(), below)
        p.arrived(high, self.sems.at[3, distance - 1], above)
        self.onward(high, high, distance, False, above)
        if self.shared is not None:
            p.send(high, high, self.sems.at[6, distance], self.sems.at[7, distance], p.sibling(), above)

    def finish(self):
        p = self.place
        if self.keep is not None:
            self.keep.wait()
        if self.shared is None:
            return
        p.arrived(self.shared(p.z), self.sems.at[5, 0])
        for distance in range(1, p.depth):
            below, above = p.z >= distance, p.z + distance < p.depth
            p.arrived(self.shared(jnp.maximum(p.z - distance, 0)), self.sems.at[5, distance], below)
            p.arrived(self.shared(jnp.minimum(p.z + distance, p.depth - 1)), self.sems.at[7, distance], above)


def add_up(*terms):
    total = terms[0].astype(F32)
    for term in terms[1:]:
        total = total + term.astype(F32)
    return total


class PairSwap:
    @staticmethod
    def scratch(count, shape, dtype):
        return [pltpu.VMEM((count,) + shape, dtype), pltpu.SemaphoreType.DMA((2, count))]

    def __init__(self, place, parts, pair, sems, order, own=None):
        self.place, self.parts, self.pair, self.sems, self.own = place, parts, pair, sems, own
        for at in order:
            place.send(parts.at[at, 1 - place.core], pair.at[at], sems.at[0, at], sems.at[1, at], place.sibling())

    def wait(self, at):
        self.place.arrived(self.pair.at[at], self.sems.at[1, at])

    def terms(self, at):
        if self.own is None:
            return [self.parts[at, self.place.core], self.pair[at]]
        slot, sem = self.own
        self.place.local(self.parts.at[at, self.place.core], slot, sem.at[0]).wait()
        return [slot[...], self.pair[at]]


class PlaneSum:
    @staticmethod
    def scratch(reps, shape, dtype):
        return PairSwap.scratch(reps, shape, dtype) + [
            pltpu.VMEM((reps,) + shape, dtype), pltpu.SemaphoreType.DMA((2, reps)),
        ]

    def __init__(self, place, parts, pair, pair_sems, into, sems):
        self.place, self.pair, self.into, self.sems = place, pair, into, sems
        order = [place.rep_at(distance) for distance in range(1, place.reps)] + [place.rep]
        self.swap = PairSwap(place, parts, pair, pair_sems, order)

    def relay(self):
        p = self.place
        for distance in range(1, p.reps):
            rep = p.rep_at(distance)
            self.swap.wait(rep)
            self.pair[rep] = add_up(*self.swap.terms(rep)).astype(self.pair.dtype)
            p.send(self.pair.at[rep], self.into.at[distance], self.sems.at[0, distance], self.sems.at[1, distance],
                   p.device(rep=rep))

    def total(self):
        p = self.place
        self.swap.wait(p.rep)
        terms = self.swap.terms(p.rep)
        for distance in range(1, p.reps):
            p.arrived(self.into.at[distance], self.sems.at[1, distance])
            terms.append(self.into[distance])
        return add_up(*terms)


class LineSum:
    @staticmethod
    def scratch(depth, shape, dtype):
        return [pltpu.VMEM((depth + 1,) + shape, dtype), pltpu.SemaphoreType.DMA((4, depth))]

    def __init__(self, place, terms, out, into, sems):
        self.place, self.terms, self.out, self.into, self.sems = place, terms, out, into, sems

    def moves(self, at):
        p = self.place
        last = p.depth - 1
        for way, towards, goal, first, valid in (
            (0, p.z + 1, last - (at - p.z), p.z == 0, (at >= p.z) & (last - (at - p.z) > p.z)),
            (1, p.z - 1, at - (last - p.z), p.z == last, (at >= last - p.z) & (at - (last - p.z) < p.z)),
        ):
            goal = jnp.clip(goal, 0, last)
            slot = jnp.where(goal == towards, p.depth, goal) if way else goal
            copy = pltpu.make_async_remote_copy(
                src_ref=self.out.at[goal], dst_ref=self.into.at[slot], send_sem=self.sems.at[2 * way, goal],
                recv_sem=self.sems.at[2 * way + 1, goal], device_id=p.device(z=towards), device_id_type=MESH_ID,
            )
            yield way, goal, first, valid, copy

    def step(self, at):
        p = self.place
        for way, goal, first, valid, copy in self.moves(at):
            inner = valid & jnp.logical_not(first)
            p.arrived(self.into.at[goal], self.sems.at[2 * way + 1, goal], inner)

            def start(goal=goal):
                self.out[goal] = add_up(*self.terms(goal)).astype(self.out.dtype)

            def follow(goal=goal):
                self.out[goal] = add_up(*self.terms(goal), self.into[goal]).astype(self.out.dtype)

            when(valid & first, start)
            when(inner, follow)
            when(valid, copy.start)

    def finish(self):
        for at in range(self.place.depth - 1):
            for _, _, _, valid, copy in self.moves(at):
                when(valid, copy.wait_send)

    def total(self, result):
        result[...] = add_up(*self.terms(self.place.z))
        self.gather(result)
        self.finish()

    def gather(self, result):
        p = self.place
        for way, slot, condition in ((0, p.z, p.z > 0), (1, p.depth, p.z < p.depth - 1)):
            p.arrived(self.into.at[slot], self.sems.at[2 * way + 1, p.z], condition)

            def add(slot=slot):
                result[...] += self.into[slot].astype(F32)

            when(condition, add)


class ColumnSum:
    @staticmethod
    def scratch(depth, shape, dtype):
        return PairSwap.scratch(depth, shape, dtype) + LineSum.scratch(depth, shape, dtype)

    def __init__(self, place, parts, pair, pair_sems, into, sems, own=None):
        self.place = place
        order = [lax.rem(place.z + distance, place.depth) for distance in list(range(place.depth - 1, 0, -1)) + [0]]
        self.order = order
        self.swap = PairSwap(place, parts, pair, pair_sems, order, own)
        self.line = LineSum(place, self.swap.terms, pair, into, sems)

    def ready(self):
        for at in self.order:
            self.swap.wait(at)

    def step(self, at):
        self.line.step(at)

    def total(self, result):
        self.line.total(result)


def anywhere(count):
    return [pl.BlockSpec(memory_space=pl.ANY)] * count


def in_vmem(count):
    return [pl.BlockSpec(memory_space=pltpu.VMEM)] * count


def remote_params(identity, mebibytes=60):
    return pltpu.CompilerParams(
        collective_id=identity, has_side_effects=True, vmem_limit_bytes=mebibytes * 2**20
    )


def column_of(row_values, rows):
    return jnp.broadcast_to(row_values, (LANES, rows)).T[:, 0:1]


def row_of(column_values, rows):
    return jnp.broadcast_to(column_values, (rows, LANES)).T[0:8, :]


def forward_mixer(tokens, cotangent, own_pair, other_pair, common, vectors, table, out_quarters, sizes):
    reps, depth, channels, width, state, sequences, inner, convolved = sizes
    rows, model = tokens.shape
    part, side = own_pair.shape
    wide = side + common.shape[1]
    quarter = out_quarters.shape[1]
    vector_width = vectors.shape[1]
    heads = channels // width
    per_shard = convolved // (2 * depth)

    x_scratch = [pltpu.VMEM((reps, 2, rows, model), BF16)] + PlaneGather.scratch(reps)
    w_scratch = [pltpu.VMEM((depth, 2, part, wide), BF16)] + ColumnGather.scratch(depth) * 3
    v_scratch = [pltpu.VMEM((depth, 2) + vectors.shape, BF16)] + ColumnGather.scratch(depth) * 2
    o_scratch = [
        pltpu.VMEM((depth, quarter, model), BF16), pltpu.VMEM((reps, quarter, model), BF16),
    ] + ColumnGather.scratch(depth) + [pltpu.SemaphoreType.DMA((2, reps)), pltpu.SemaphoreType.DMA((2,))]
    n_scratch = [pltpu.VMEM((8, LANES), F32)] + PlaneGather.scratch(reps)
    sum_scratch = [
        pltpu.VMEM((reps, rows, model), BF16), pltpu.VMEM((reps, 2, 8, rows), F32),
    ] + PlaneSum.scratch(reps, (rows, model), BF16) + PlaneSum.scratch(reps, (8, rows), F32)
    groups = [x_scratch, w_scratch, v_scratch, o_scratch, n_scratch, sum_scratch]

    def kernel(x_ref, g_ref, own_ref, other_ref, common_ref, vectors_ref, table_ref, quarters_ref,
               after_ref, mixed_ref, scale_ref, lengths_ref, in_gain_ref, post_gain_ref, taps_ref, heads_ref, skip_ref,
               norm_ref, table_out, second_out, g_out, first_out, weight_out, out_out, proj_out, mixed_out, *scratch):
        cut = [0]
        for group in groups:
            cut.append(cut[-1] + len(group))
        x_work, w_work, v_work, o_work, n_work, sum_work = [scratch[i:j] for i, j in zip(cut, cut[1:])]
        (second, second_sems, second_local, g_sems, g_local, proj_buffer, proj_sems, keep_sems,
         own_part, mixed_buffer, mixed_sems) = scratch[cut[-1]:]
        p = Place(reps, depth)
        p.barrier(plane=True, column=True)

        x_all, weight_all, vectors_all = x_work[0], w_work[0], v_work[0]

        def left(core):
            return lambda z: weight_all.at[z, core, :, pl.ds(0, side)]

        def right(core):
            return lambda z: weight_all.at[z, core, :, pl.ds(side, wide - side)]

        vector_job = ColumnGather(p, vectors_ref, lambda z: vectors_all.at[z, p.core], v_work[1], v_work[2],
                                  shared=lambda z: vectors_all.at[z, 1 - p.core])
        own_slot, other_slot = left(p.core), left(1 - p.core)
        p.send(other_ref, own_slot(p.z), keep_sems.at[0], keep_sems.at[1], p.sibling())
        job_a = ColumnGather(p, own_ref, own_slot, w_work[1], w_work[2])
        job_c = ColumnGather(p, common_ref, right(p.core), w_work[3], w_work[4], shared=right(1 - p.core))
        x_job = PlaneGather(p, x_ref, x_all, x_work[1], x_work[2])
        p.arrived(other_slot(p.z), keep_sems.at[1])
        job_b = ColumnGather(p, other_slot(p.z), other_slot, w_work[5], w_work[6], keep=False)
        mid, out_all = o_work[0], o_work[1]
        job_o = ColumnGather(p, quarters_ref.at[p.rep], lambda z: mid.at[z], o_work[2], o_work[3])
        table_job = ColumnGather(p, table_ref, lambda z: table_out.at[z, p.core], v_work[3], v_work[4],
                                 shared=lambda z: table_out.at[z, 1 - p.core])
        for distance in range(1, depth):
            vector_job.hop(distance)
        vector_job.finish()

        own_row = vectors_all[p.z, p.core].astype(F32)[11:12, :LANES]
        dealt = own_row[:, sequences : sequences + 1]
        lengths_row = jnp.zeros((1, LANES), F32)
        for z in range(depth):
            for core in range(2):
                row = vectors_all[z, core].astype(F32)[11:12, :LANES]
                lengths_row = jnp.where(dealt == float(2 * z + core), row, lengths_row)
        n_work[0][...] = jnp.broadcast_to(lengths_row, (8, LANES))
        n_job = PlaneGather(p, n_work[0], lengths_ref, n_work[1], n_work[2])

        pieces = [vectors_all[z, core].astype(F32) for z in range(depth) for core in range(2)]
        in_gain_ref[...] = jnp.concatenate([piece[0:1, :part] for piece in pieces], axis=1)
        post_gain_ref[...] = jnp.concatenate([piece[10:11, :part] for piece in pieces], axis=1)
        taps_full = jnp.concatenate([piece[0:8, :per_shard] for piece in pieces], axis=1)
        taps_full = jnp.concatenate([taps_full[1:6, :], jnp.zeros((3, convolved), F32)], axis=0)
        team = 2 * p.rep + p.core
        taps_own = taps_full[:, :channels]
        for member in range(1, 2 * reps):
            taps_own = jnp.where(team == member, taps_full[:, channels * member : channels * (member + 1)], taps_own)
        taps_ref[...] = jnp.concatenate([taps_own, taps_full[:, inner:]], axis=1)
        own = vectors_all[p.rep, p.core].astype(F32)
        lane = lax.broadcasted_iota(jnp.int32, (1, LANES), 1)
        speed = jnp.where(lane < heads, jnp.exp(jnp.where(lane < heads, own[7:8, :LANES], 0.0)), 0.0)
        heads_ref[...] = jnp.concatenate([own[6:7, :LANES], speed, jnp.zeros((6, LANES), F32)], axis=0)
        norm_ref[...] = own[9:10, :channels]
        wide_lane = lax.broadcasted_iota(jnp.int32, (1, channels), 1)
        skip = jnp.broadcast_to(own[8:9, 0:1], (1, channels))
        for head in range(1, heads):
            skip = jnp.where(wide_lane >= head * width, own[8:9, head : head + 1], skip)
        skip_ref[...] = skip

        n_job.relay()
        for distance in range(1, depth):
            for job in (job_a, job_c, job_b, job_o, table_job):
                job.hop(distance)
            if distance == 1:
                x_job.relay()
        for job in (n_job, x_job, job_a, job_b, job_c, job_o, table_job):
            job.finish()
        e_sems, e_local = o_work[4], o_work[5]
        for distance in range(1, reps):
            rep = p.rep_at(distance)
            p.send(mid.at[rep], out_all.at[p.rep], e_sems.at[0, distance], e_sems.at[1, distance], p.device(rep=rep))
        out_all[p.rep] = mid[p.rep]
        g_job = ColumnGather(p, g_ref, lambda z: g_out.at[z, p.core], g_sems, g_local,
                             shared=lambda z: g_out.at[z, 1 - p.core])
        for distance in range(1, reps):
            p.arrived(out_all.at[p.rep_at(distance)], e_sems.at[1, distance])
        weight_keep = p.local(weight_all, weight_out, e_local.at[0])
        out_keep = p.local(out_all, out_out, e_local.at[1])

        p.finish()
        parts, squares = sum_work[0], sum_work[1]
        pair, pair_sems, into, into_sems = sum_work[2:6]
        s_pair, s_pair_sems, s_into, s_into_sems = sum_work[6:10]

        def swap(rep, start):
            for source, target, sems in (
                (parts.at[rep], pair, pair_sems), (squares.at[rep, 1 - p.core], s_pair, s_pair_sems)
            ):
                copy = pltpu.make_async_remote_copy(
                    src_ref=source, dst_ref=target.at[rep], send_sem=sems.at[0, rep],
                    recv_sem=sems.at[1, rep], device_id=p.sibling(), device_id_type=MESH_ID,
                )
                if start:
                    copy.start()
                else:
                    copy.wait_send()

        def onward(distance, rep, start):
            for values, target, sems in ((pair, into, into_sems), (s_pair, s_into, s_into_sems)):
                copy = pltpu.make_async_remote_copy(
                    src_ref=values.at[rep], dst_ref=target.at[distance], send_sem=sems.at[0, distance],
                    recv_sem=sems.at[1, distance], device_id=p.device(rep=rep), device_id_type=MESH_ID,
                )
                if start:
                    copy.start()
                else:
                    copy.wait_send()

        def proj_copy(slot, rep, core):
            return pltpu.make_async_copy(proj_buffer.at[slot], proj_out.at[rep, core], proj_sems.at[slot])

        def mixed_copy(slot, rep, core):
            return pltpu.make_async_copy(mixed_buffer.at[slot], mixed_out.at[rep, core], mixed_sems.at[slot])

        def visit(at, carry):
            distance = lax.rem(at // 2 + 1, reps)
            rep = p.rep_at(distance)
            turn = lax.rem(at, 2)
            core = jnp.where(turn == 0, 1 - p.core, p.core)
            x = x_all[rep, core].astype(F32)
            first = (x * rms_rows(x) * in_gain_ref[...]).astype(BF16)
            x_all[rep, core] = first
            proj = mm(first, weight_all[...].reshape(model, wide))

            @pl.when(at >= 2)
            def _():
                proj_copy(turn, rep, core).wait()

            proj_buffer[turn] = proj
            proj_copy(turn, rep, core).start()
            seg_column, seg_line = segments(lengths_ref[rep, core][0:1, :], sequences, rows)
            block = Block(proj, seg_column, seg_line, taps_ref[...], heads_ref[...], channels, width, state)
            mixed = []
            for start, stop, inside in block.groups():
                xin = block.xin[:, start:stop]
                scaled, rest = split_two(xin * block.spread(block.step, start, stop, inside))
                scaled = jnp.concatenate([scaled, scaled, rest], axis=0)
                y = None
                for head in inside:
                    weights, weights_rest = split_two(block.scores * block.decay(head))
                    term = mm(jnp.concatenate([weights, weights_rest, weights], axis=1), scaled)
                    y = term if y is None else jnp.where(block.inside(start, stop, head), term, y)
                gate = block.gate[:, start:stop]
                mixed.append((y + skip_ref[:, start:stop] * xin) * gate * jax.nn.sigmoid(gate))
            mixed = jnp.concatenate(mixed, axis=1)
            squares[rep, core] = row_of(jnp.sum(mixed * mixed, axis=1, keepdims=True), rows)
            mixed = mixed * norm_ref[...]

            @pl.when(at >= 2)
            def _():
                mixed_copy(turn, rep, core).wait()

            mixed_buffer[turn] = mixed
            mixed_copy(turn, rep, core).start()
            mixed, mixed_rest = split_two(mixed)
            out_weight = out_all[...].reshape(channels, model)
            part_rows = mm(mixed, out_weight) + mm(mixed_rest, out_weight)

            @pl.when(turn == 0)
            def _():
                parts[rep] = part_rows.astype(BF16)
                swap(rep, True)

            @pl.when((turn == 1) & (distance == 0))
            def _():
                own_part[...] = part_rows

            @pl.when((turn == 1) & (distance > 0))
            def _():
                p.arrived(pair.at[rep], pair_sems.at[1, rep])
                pair[rep] = add_up(part_rows, pair[rep]).astype(BF16)
                p.arrived(s_pair.at[rep], s_pair_sems.at[1, rep])
                s_pair[rep] = add_up(squares[rep, p.core], s_pair[rep])
                onward(distance, rep, True)

            return carry

        lax.fori_loop(0, reps, visit, 0)
        g_job.hop(1)
        lax.fori_loop(reps, 2 * reps, visit, 0)
        first_keep = p.local(x_all, first_out, keep_sems.at[2])
        if depth > 2:
            g_job.hop(2)
        p.arrived(pair.at[p.rep], pair_sems.at[1, p.rep])
        p.arrived(s_pair.at[p.rep], s_pair_sems.at[1, p.rep])
        terms, square_terms = [own_part[...], pair[p.rep]], [squares[p.rep, p.core], s_pair[p.rep]]
        for distance in range(1, reps):
            p.arrived(s_into.at[distance], s_into_sems.at[1, distance])
            square_terms.append(s_into[distance])
            p.arrived(into.at[distance], into_sems.at[1, distance])
            terms.append(into[distance])
        scale_row = lax.rsqrt(add_up(*square_terms) / inner + EPS)
        scale_ref[...] = scale_row
        mixed = column_of(scale_row[0:1, :], rows) * add_up(*terms)
        mixed_ref[...] = mixed.astype(BF16)
        after = x_ref[...].astype(F32) + mixed
        after_ref[...] = after
        second[...] = (after * rms_rows(after) * post_gain_ref[...]).astype(BF16)
        job = ColumnGather(p, second, lambda z: second_out.at[z, p.core], second_sems, second_local,
                           shared=lambda z: second_out.at[z, 1 - p.core])
        for distance in range(3, depth):
            g_job.hop(distance)
        for distance in range(1, depth):
            job.hop(distance)
        job.finish()
        g_job.finish()
        for distance in range(reps):
            rep = p.rep_at(distance) if distance else p.rep
            swap(rep, False)
            if distance:
                onward(distance, rep, False)
        for slot in range(2):
            proj_copy(slot, p.rep, p.core).wait()
            mixed_copy(slot, p.rep, p.core).wait()
        for keep in (weight_keep, out_keep, first_keep):
            keep.wait()
        p.finish()

    return pl.pallas_call(
        kernel,
        in_specs=in_vmem(1) + anywhere(7),
        out_specs=in_vmem(10) + anywhere(8),
        out_shape=[
            jax.ShapeDtypeStruct((rows, model), F32),
            jax.ShapeDtypeStruct((rows, model), BF16),
            jax.ShapeDtypeStruct((8, rows), F32),
            jax.ShapeDtypeStruct((reps, 2, 8, LANES), F32),
            jax.ShapeDtypeStruct((1, model), F32),
            jax.ShapeDtypeStruct((1, model), F32),
            jax.ShapeDtypeStruct((8, channels + 2 * state), F32),
            jax.ShapeDtypeStruct((8, LANES), F32),
            jax.ShapeDtypeStruct((1, channels), F32),
            jax.ShapeDtypeStruct((1, channels), F32),
            jax.ShapeDtypeStruct((depth, 2) + table.shape, BF16),
            jax.ShapeDtypeStruct((depth, 2, rows, model), BF16),
            jax.ShapeDtypeStruct((depth, 2, rows, model), BF16),
            jax.ShapeDtypeStruct((reps, 2, rows, model), BF16),
            jax.ShapeDtypeStruct((depth, 2, part, wide), BF16),
            jax.ShapeDtypeStruct((reps, quarter, model), BF16),
            jax.ShapeDtypeStruct((reps, 2, rows, wide), F32),
            jax.ShapeDtypeStruct((reps, 2, rows, channels), F32),
        ],
        scratch_shapes=[item for group in groups for item in group]
        + [pltpu.VMEM((rows, model), BF16)]
        + ColumnGather.scratch(depth) * 2
        + [pltpu.VMEM((2, rows, wide), F32), pltpu.SemaphoreType.DMA((2,)), pltpu.SemaphoreType.DMA((3,)),
           pltpu.VMEM((rows, model), F32), pltpu.VMEM((2, rows, channels), F32), pltpu.SemaphoreType.DMA((2,))],
        compiler_params=remote_params(0),
        name="forward_mixer",
    )(tokens, cotangent, own_pair, other_pair, common, vectors, table, out_quarters)


def join_experts(
    own, gates, dots, hidden, shared_grad, router_t, shared_in, shared_out, cotangent, after, mixed, scale, post_gain,
    back, weighted, second, inner, reps, depth, capacity,
):
    rows, model = cotangent.shape
    local = own.shape[1]
    experts = gates.shape[1]
    half_rows = rows // 2
    stack = (rows, model)
    halves = (slice(0, half_rows), slice(half_rows, rows))
    groups = {
        "stream": [
            pltpu.VMEM((2, local, capacity, model), BF16), pltpu.SemaphoreType.DMA((2,)),
            pltpu.VMEM((2,) + stack, BF16), pltpu.SemaphoreType.DMA((2,)),
        ],
        "parts": [
            pltpu.VMEM((2,) + stack, BF16), pltpu.VMEM(stack, F32), pltpu.VMEM((depth, 2, half_rows, model), BF16),
            pltpu.SemaphoreType.DMA((2, depth)),
        ],
        "line": LineSum.scratch(depth, (half_rows, model), BF16) * 2,
        "low": [pltpu.VMEM((2, half_rows, model), BF16), pltpu.VMEM((2, 8, rows), F32)] + PlaneGather.scratch(reps) * 3,
        "logits": [pltpu.VMEM((2 * depth, 2 * experts, rows), BF16), pltpu.VMEM((2,) + stack, BF16),
                   pltpu.SemaphoreType.DMA((2,))],
    }

    def kernel(own_ref, gates_ref, dots_ref, hidden_ref, shared_ref, router_ref, in_ref, out_ref, g_ref, after_ref,
               mixed_ref, scale_ref, gain_ref, back_ref, weighted_ref, second_ref,
               grad_ref, gain_grad_ref, router_grad_ref, layer_out, low_out, scale_out, *scratch):
        work, cut = {}, 0
        for name, items in groups.items():
            work[name] = scratch[cut : cut + len(items)]
            cut += len(items)
        p = Place(reps, depth)
        slots, slot_sems, second_slots, second_sems = work["stream"]
        parts, own_part, pair, pair_sems = work["parts"]
        logits_all, layer_slots, layer_sems = work["logits"]
        lower = p.z < depth // 2

        def goal_at(index):
            distance = lax.rem(depth - 1 - index + depth, depth)
            return jnp.where(lower, lax.rem(p.z + distance, depth), lax.rem(p.z - distance + depth, depth))

        def block_at(at):
            return goal_at(at // 2), jnp.where(lax.rem(at, 2) == 0, 1 - p.core, p.core)

        def load(source, at):
            goal, core = block_at(at)
            start = pl.multiple_of((2 * goal + core) * capacity, capacity)
            return pltpu.make_async_copy(
                source.at[:, pl.ds(start, capacity)], slots.at[lax.rem(at, 2)], slot_sems.at[lax.rem(at, 2)]
            )

        def swap(goal, slot, start):
            for at, piece in enumerate(halves):
                copy = pltpu.make_async_remote_copy(
                    src_ref=parts.at[slot, pl.ds(half_rows * at, half_rows)], dst_ref=pair.at[goal, at],
                    send_sem=pair_sems.at[0, goal] if at == 0 else pair_sems_late.at[0, goal],
                    recv_sem=pair_sems.at[1, goal] if at == 0 else pair_sems_late.at[1, goal],
                    device_id=p.sibling(), device_id_type=MESH_ID,
                )
                copy.start() if start else copy.wait_send()

        pair_sems_late = work["late"][0]
        load(back_ref, 0).start()
        p.barrier(plane=True, column=True)
        expert = lax.broadcasted_iota(jnp.int32, (experts, rows), 0)
        shard = 2 * p.z + p.core

        def matches(q):
            table = own_ref[q].astype(F32)
            return [slot_match(table[i : i + 1, :], capacity, rows) for i in range(local)]

        def visit(at, carry):
            goal, core = block_at(at)
            q = 2 * goal + core
            turn = lax.rem(at, 2)
            load(back_ref, at).wait()

            @pl.when(at + 1 < 2 * depth)
            def _():
                load(back_ref, at + 1).start()

            start = pl.multiple_of(q * rows, rows)
            gates = gates_ref[q]
            gate_grad = jnp.zeros_like(gates)
            total = mm_nt(shared_ref[pl.ds(start, rows), :], in_ref[...])
            for i, match in enumerate(matches(q)):
                total = total + mm_tn(match.astype(BF16), slots[turn, i])
                dot = dots_ref[i, pl.ds(pl.multiple_of(q * capacity, capacity), capacity), 0:1]
                row = jnp.sum(jnp.where(match, dot, 0.0), axis=0, keepdims=True)
                gate_grad = jnp.where(expert == local * shard + i, row, gate_grad)
            logit_grad = gates * (gate_grad - jnp.sum(gates * gate_grad, axis=0, keepdims=True))
            logit_pair = jnp.concatenate(split_two(logit_grad), axis=0)
            logits_all[q] = logit_pair
            total = total + mm_tn(logit_pair, jnp.concatenate([router_ref[...], router_ref[...]], axis=0))

            @pl.when(turn == 0)
            def _():
                slot = lax.rem(at // 2, 2)

                @pl.when(at >= 4)
                def _():
                    swap(goal_at(at // 2 - 2), slot, False)

                parts[slot] = total.astype(BF16)
                swap(goal, slot, True)

            @pl.when(turn == 1)
            def _():
                p.arrived(pair.at[goal, 0], pair_sems.at[1, goal])
                p.arrived(pair.at[goal, 1], pair_sems_late.at[1, goal])

                @pl.when(goal == p.z)
                def _():
                    for index, piece in enumerate(halves):
                        own_part[piece, :] = add_up(total[piece, :], pair[goal, index])

                @pl.when(goal != p.z)
                def _():
                    for index, piece in enumerate(halves):
                        pair[goal, index] = add_up(total[piece, :], pair[goal, index]).astype(BF16)

            return carry

        lines = []
        for index in range(2):
            view = pair.at[:, index]
            into, sems = work["line"][2 * index : 2 * index + 2]

            def terms(goal, view=view, index=index):
                return [view[goal]]

            lines.append(LineSum(p, terms, view, into, sems))

        for step in range(depth - 1):
            lax.fori_loop(2 * step, 2 * step + 2, visit, 0)
            lines[0].step(step)
        for step in range(depth - 1):
            lines[1].step(step)
        lax.fori_loop(2 * depth - 2, 2 * depth, visit, 0)

        low, scales = work["low"][:2]
        gather_sems = work["low"][2:]
        gain_grad_ref[...] = jnp.zeros_like(gain_grad_ref)
        row_dots = []

        def norm_back(index):
            piece = halves[index]
            into = lines[index].into
            grad_ref[piece, :] = own_part[piece, :]
            lines[index].gather(grad_ref.at[pl.ds(half_rows * index, half_rows)])
            second_grad = grad_ref[piece, :]
            after_rows = after_ref[piece, :]
            after_scale = rms_rows(after_rows)
            gain_grad_ref[...] += jnp.sum(after_rows * second_grad * after_scale, axis=0, keepdims=True)
            weighted = second_grad * gain_ref[...]
            after_grad = (
                g_ref[piece, :].astype(F32)
                + after_scale * weighted
                - after_rows * after_scale**3 * jnp.mean(after_rows * weighted, axis=1, keepdims=True)
            )
            grad_ref[piece, :] = after_grad
            after_low = after_grad.astype(BF16)
            low[index] = after_low
            row_dots.append(
                jnp.sum(after_low.astype(F32) * mixed_ref[piece, :].astype(F32), axis=1, keepdims=True)
            )
            return PlaneGather(p, low.at[index], low_out.at[:, :, pl.ds(half_rows * index, half_rows)],
                               *gather_sems[2 * index : 2 * index + 2])

        first_job = norm_back(0)

        def layer_load(at):
            q = block_at(at)
            start = pl.multiple_of((2 * q[0] + q[1]) * rows, rows)
            return pltpu.make_async_copy(
                second_ref.at[pl.ds(start, rows)], second_slots.at[lax.rem(at, 2)], second_sems.at[lax.rem(at, 2)]
            )

        def layer_store(at):
            goal, core = block_at(at)
            return pltpu.make_async_copy(
                layer_slots.at[lax.rem(at, 2)], layer_out.at[goal, core], layer_sems.at[lax.rem(at, 2)]
            )

        def layer_visit(at, carry):
            goal, core = block_at(at)
            q = 2 * goal + core
            turn = lax.rem(at, 2)
            load(weighted_ref, at).wait()
            layer_load(at).wait()

            @pl.when(at + 1 < 2 * depth)
            def _():
                load(weighted_ref, at + 1).start()
                layer_load(at + 1).start()

            total = mm(hidden_ref[pl.ds(pl.multiple_of(q * rows, rows), rows), :], out_ref[...])
            for i, match in enumerate(matches(q)):
                total = total + mm_tn(match.astype(BF16), slots[turn, i])

            @pl.when(at >= 2)
            def _():
                layer_store(at).wait()

            layer_slots[turn] = total.astype(BF16)
            layer_store(at).start()
            both = mm(logits_all[q], second_slots[turn])
            router_grad_ref[...] += both[:experts, :] + both[experts:, :]
            return carry

        router_grad_ref[...] = jnp.zeros_like(router_grad_ref)
        load(weighted_ref, 0).start()
        layer_load(0).start()
        lax.fori_loop(0, depth, layer_visit, 0)
        first_job.relay()
        second_job = norm_back(1)
        dot_row = row_of(jnp.concatenate(row_dots, axis=0), rows)
        scale_row = scale_ref[...]
        scales[0] = scale_row
        scales[1] = scale_row**2 * dot_row / inner
        scale_job = PlaneGather(p, scales, scale_out, *gather_sems[4:6])
        lax.fori_loop(depth, 2 * depth, layer_visit, 0)
        scale_job.relay()
        second_job.relay()
        for job in (first_job, scale_job, second_job):
            job.finish()
        for slot in range(2):
            layer_store(slot).wait()
        for at in range(max(depth - 2, 0), depth):
            swap(goal_at(at), at % 2, False)
        for line in lines:
            line.finish()
        p.finish()

    groups["late"] = [pltpu.SemaphoreType.DMA((2, depth))]
    group = 2 * depth
    return pl.pallas_call(
        kernel,
        in_specs=in_vmem(13) + anywhere(3),
        out_specs=in_vmem(3) + anywhere(3),
        out_shape=[
            jax.ShapeDtypeStruct((rows, model), F32),
            jax.ShapeDtypeStruct((1, model), F32),
            jax.ShapeDtypeStruct((experts, model), F32),
            jax.ShapeDtypeStruct((depth, 2, rows, model), BF16),
            jax.ShapeDtypeStruct((reps, 2, rows, model), BF16),
            jax.ShapeDtypeStruct((reps, 2, 2, 8, rows), F32),
        ],
        scratch_shapes=[item for items in groups.values() for item in items],
        compiler_params=remote_params(2),
        name="join_experts",
    )(
        own, gates, dots, hidden, shared_grad, router_t, shared_in, shared_out, cotangent, after, mixed, scale,
        post_gain, back, weighted, second,
    )


def backward_mixer(
    scales, after, after_grad, tokens, in_gain, post_grad, router_parts, lengths, taps, head_rows, skip, norm, weight,
    out_weight, low, layer_parts, first, proj, gained, sizes,
):
    reps, depth, channels, width, state, sequences, inner, convolved = sizes
    rows, model = tokens.shape
    part = model // (2 * depth)
    wide = weight.shape[1]
    side = 2 * channels
    heads = channels // width
    per_shard = convolved // (2 * depth)
    quarter = channels // reps
    experts, router_width = router_parts.shape[2:]
    small_width = -(-max(per_shard, channels, router_width) // LANES) * LANES
    small_shape = (16 + experts, small_width)
    stack = (rows, model)
    groups = {
        "early": [pltpu.VMEM((2, rows, channels), F32), pltpu.SemaphoreType.DMA((2,))],
        "layer": [pltpu.SemaphoreType.DMA((1,))]
        + ColumnSum.scratch(depth, stack, BF16),
        "stream": [
            pltpu.VMEM(stack, BF16), pltpu.VMEM((2, rows, wide), F32), pltpu.VMEM((2,) + stack, BF16),
            pltpu.SemaphoreType.DMA((3, 2)),
        ],
        "sum": [
            pltpu.VMEM((2,) + stack, BF16), pltpu.VMEM(stack, F32),
            pltpu.VMEM((reps,) + stack, BF16), pltpu.SemaphoreType.DMA((2, reps)),
            pltpu.VMEM((reps - 1,) + stack, BF16), pltpu.SemaphoreType.DMA((2, reps)),
        ],
        "grads": [
            pltpu.VMEM((depth, 2, part, wide), F32), pltpu.VMEM((channels, model), F32),
            pltpu.VMEM((8, channels + 2 * state), F32), pltpu.VMEM((8, LANES), F32), pltpu.VMEM((8, channels), F32),
        ],
        "side": LineSum.scratch(depth, (2, part, channels), BF16) * 2
        + [pltpu.VMEM((2, 2, part, channels), BF16), pltpu.VMEM((2, part, channels), BF16),
           pltpu.SemaphoreType.DMA((2, 2))],
        "common": [pltpu.VMEM((depth, 2, part, wide - side), BF16)]
        + ColumnSum.scratch(depth, (part, wide - side), BF16)
        + [pltpu.VMEM((part, wide - side), F32), pltpu.VMEM((part, wide - side), BF16)],
        "out": [
            pltpu.VMEM((reps, quarter, model), BF16), pltpu.VMEM((reps, quarter, model), BF16),
            pltpu.SemaphoreType.DMA((2, reps)),
        ] + LineSum.scratch(depth, (quarter, model), BF16)
        + [pltpu.VMEM((quarter, model), BF16)],
        "small": [pltpu.VMEM((depth, 2) + small_shape, F32)] + ColumnSum.scratch(depth, small_shape, F32)
        + [pltpu.VMEM(small_shape, F32), pltpu.VMEM((reps,) + small_shape, F32)],
        "end": [pltpu.SemaphoreType.DMA((2, 5, reps)), pltpu.SemaphoreType.DMA((6,)), pltpu.VMEM((2, 32, model), F32)],
    }

    def kernel(scales_ref, after_ref, grad_ref, x_ref, gain_ref, post_grad_ref, router_ref, lengths_ref, taps_ref,
               heads_ref, skip_ref, norm_ref, weight_ref, out_ref, low_ref, layer_ref, first_ref, proj_ref, gained_ref,
               layer_out_ref, tokens_grad_ref, side_out, common_out, out_out, small_out, *scratch):
        work, cut = {}, 0
        for name, items in groups.items():
            work[name] = scratch[cut : cut + len(items)]
            cut += len(items)
        p = Place(reps, depth)
        first_slot, proj_slots, low_slots, stream_sems = work["stream"]
        gained_slots, gained_sems = work["early"]

        def first_load(rep, core):
            return pltpu.make_async_copy(first_ref.at[rep, core], first_slot, stream_sems.at[0, 0])

        def proj_load(slot, rep, core):
            return pltpu.make_async_copy(proj_ref.at[rep, core], proj_slots.at[slot], stream_sems.at[1, slot])

        def low_load(slot, rep, core):
            return pltpu.make_async_copy(low_ref.at[rep, core], low_slots.at[slot], stream_sems.at[2, slot])

        def gained_load(slot, rep, core):
            return pltpu.make_async_copy(gained_ref.at[rep, core], gained_slots.at[slot], gained_sems.at[slot])

        def early_place(at):
            return at // 2, lax.rem(at, 2)

        for at in range(2):
            gained_load(at, *early_place(at)).start()
            low_load(at, *early_place(at)).start()
        proj_load(0, p.rep_at(1), 1 - p.core).start()
        proj_load(1, p.rep_at(1), p.core).start()
        p.barrier(plane=True, column=True)
        layer_job = ColumnSum(p, layer_ref, *work["layer"][1:], own=(first_slot, work["layer"][0]))
        in_total, out_total, taps_total, heads_total, wide_total = work["grads"]
        for total in work["grads"]:
            total[...] = jnp.zeros_like(total)

        def early(at, carry):
            rep, core = early_place(at)
            turn = lax.rem(at, 2)
            gained_load(turn, rep, core).wait()
            low_load(turn, rep, core).wait()
            scale = column_of(scales_ref[rep, core, 0][0:1, :], rows)
            out_total[...] += mm_tn((gained_slots[turn] * scale).astype(BF16), low_slots[turn])

            @pl.when(at + 2 < 2 * reps)
            def _():
                gained_load(turn, *early_place(at + 2)).start()
                low_load(turn, *early_place(at + 2)).start()

            return carry

        lax.fori_loop(0, 2 * reps, early, 0)
        low_load(0, p.rep_at(1), 1 - p.core).start()
        low_load(1, p.rep_at(1), p.core).start()
        out_parts, out_mid, out_sems, out_into, out_line_sems, out_low = work["out"]
        out_line_total = out_total.at[pl.ds(0, quarter)]
        out_parts[...] = out_total[...].astype(BF16).reshape(reps, quarter, model)
        for distance in range(1, reps):
            rep = p.rep_at(distance)
            p.send(out_parts.at[rep], out_mid.at[p.rep], out_sems.at[0, distance], out_sems.at[1, distance],
                   p.device(rep=rep))
        out_mid[p.rep] = out_parts[p.rep]
        out_job = LineSum(p, lambda at: [out_mid[at]], out_into, out_into, out_line_sems)
        layer_job.ready()
        layer_job.step(0)

        parts, own_part, pair, pair_sems, into, into_sems = work["sum"]

        def swap(distance, rep, start):
            copy = pltpu.make_async_remote_copy(
                src_ref=parts.at[lax.rem(distance, 2)], dst_ref=pair.at[rep], send_sem=pair_sems.at[0, rep],
                recv_sem=pair_sems.at[1, rep], device_id=p.sibling(), device_id_type=MESH_ID,
            )
            copy.start() if start else copy.wait_send()

        def onward(distance, rep, start):
            copy = pltpu.make_async_remote_copy(
                src_ref=pair.at[rep], dst_ref=into.at[distance - 1], send_sem=into_sems.at[0, distance],
                recv_sem=into_sems.at[1, distance], device_id=p.device(rep=rep), device_id_type=MESH_ID,
            )
            copy.start() if start else copy.wait_send()

        def visit(at, carry):
            distance, turn = lax.rem(at // 2 + 1, reps), lax.rem(at, 2)
            rep = p.rep_at(distance)
            core = jnp.where(turn == 0, 1 - p.core, p.core)
            first_load(rep, core).start()
            low_load(turn, rep, core).wait()
            proj_load(turn, rep, core).wait()
            scale = column_of(scales_ref[rep, core, 0][0:1, :], rows)
            pull = column_of(scales_ref[rep, core, 1][0:1, :], rows)
            seg_column, seg_line = segments(lengths_ref[rep, core][0:1, :], sequences, rows)
            block = Block(
                proj_slots[turn], seg_column, seg_line, taps_ref[...], heads_ref[...], channels, width, state
            )
            low_rows = low_slots[turn]
            proj_grad, tap_grads, head_grads, wide_grads = block_back(
                block, low_rows, scale, pull, taps_ref, skip_ref, norm_ref, weight_ref, out_ref[...]
            )
            taps_total[0:5, :] += tap_grads
            heads_total[0:1, :] += head_grads[0]
            heads_total[1:2, :] += head_grads[1]
            wide_total[0:2, :] += wide_grads
            part_rows = mm_nt(proj_grad, weight_ref[...])

            @pl.when(turn == 0)
            def _():
                @pl.when(at >= 4)
                def _():
                    swap(at // 2 - 1, p.rep_at(at // 2 - 1), False)

                parts[lax.rem(distance, 2)] = part_rows.astype(BF16)
                swap(distance, rep, True)

            @pl.when((turn == 1) & (distance == 0))
            def _():
                own_part[...] = part_rows

            @pl.when((turn == 1) & (distance > 0))
            def _():
                p.arrived(pair.at[rep], pair_sems.at[1, rep])
                pair[rep] = add_up(part_rows, pair[rep]).astype(BF16)
                onward(distance, rep, True)

            first_load(rep, core).wait()
            for z in range(depth):
                columns = first_slot[:, 2 * part * z : 2 * part * (z + 1)]
                for start in range(0, wide, 384):
                    piece = slice(start, min(start + 384, wide))
                    in_total[z, :, :, piece] += mm_tn(columns, proj_grad[:, piece]).reshape(2, part, -1)

            @pl.when(at < 2 * reps - 2)
            def _():
                later = p.rep_at(lax.rem(at // 2 + 2, reps))
                proj_load(turn, later, core).start()
                low_load(turn, later, core).start()

            def out_start():
                for distance in range(1, reps):
                    p.arrived(out_mid.at[p.rep_at(distance)], out_sems.at[1, distance])
                out_job.step(0)

            pl.when(at == 1)(out_start)
            for step in range(1, depth - 1):
                pl.when(at == 2 * step)(functools.partial(layer_job.step, step))
                pl.when(at == 2 * step + 1)(functools.partial(out_job.step, step))
            return carry

        lax.fori_loop(0, 2 * reps, visit, 0)

        common_parts = work["common"][0]
        common_parts[...] = in_total[:, :, :, side:].astype(BF16)
        common_job = ColumnSum(p, common_parts, *work["common"][1:5])
        side_jobs = []
        for kind in range(2):
            columns = slice(kind * channels, (kind + 1) * channels)
            side_into, side_sems = work["side"][2 * kind : 2 * kind + 2]

            def terms(at, columns=columns):
                return [in_total[at, :, :, columns]]

            side_jobs.append(LineSum(p, terms, side_into, side_into, side_sems))
        side_pair, side_away, side_swap = work["side"][4:]
        side_total = gained_slots.at[:, pl.ds(0, part)]
        side_jobs[0].step(0)

        end_sems, keep_sems, late = work["end"]

        def late_load(source, chunk):
            return pltpu.make_async_copy(
                source.at[pl.ds(32 * chunk, 32)], late.at[chunk % 2], keep_sems.at[3 + chunk % 2]
            )

        late_load(grad_ref, 0).start()
        p.arrived(pair.at[p.rep], pair_sems.at[1, p.rep])
        common_job.ready()
        common_job.step(0)
        side_jobs[1].step(0)
        for distance in range(1, reps):
            p.arrived(into.at[distance - 1], into_sems.at[1, distance])
        gain_grad = jnp.zeros((1, model), F32)
        for start in range(0, rows, 32):
            piece = slice(start, start + 32)
            if start + 32 < rows:
                late_load(grad_ref, start // 32 + 1).start()
            late_load(grad_ref, start // 32).wait()
            first_grad = add_up(
                own_part[piece, :], pair[p.rep, piece, :], *[into[at, piece, :] for at in range(reps - 1)]
            )
            x = x_ref[piece, :].astype(F32)
            x_scale = rms_rows(x)
            gain_grad = gain_grad + jnp.sum(x * first_grad * x_scale, axis=0, keepdims=True)
            weighted = first_grad * gain_ref[...]
            tokens_grad_ref[piece, :] = (
                late[start // 32 % 2]
                + x_scale * weighted
                - x * x_scale**3 * jnp.mean(x * weighted, axis=1, keepdims=True)
            ).astype(BF16)

        small = work["small"][0]
        small[...] = jnp.zeros_like(small)
        team = 2 * p.rep + p.core
        own_taps = taps_total[:, :channels]
        blank = jnp.zeros_like(own_taps)
        taps_full = jnp.concatenate(
            [jnp.where(team == member, own_taps, blank) for member in range(2 * reps)] + [taps_total[:, channels:]],
            axis=1,
        )
        for z in range(depth):
            for core in range(2):
                shard = 2 * z + core
                small[z, core, 0:8, 0:per_shard] = taps_full[:, per_shard * shard : per_shard * (shard + 1)]
                small[z, core, 12:13, 0:part] = post_grad_ref[:, part * shard : part * (shard + 1)]
                small[z, core, 13:14, 0:part] = gain_grad[:, part * shard : part * (shard + 1)]
                small[z, core, 16 : 16 + experts, 0:router_width] = router_ref[z, core]
        lane = lax.broadcasted_iota(jnp.int32, (1, LANES), 1)
        skip_row = jnp.zeros((1, LANES), F32)
        for head in range(heads):
            value = jnp.sum(wide_total[1:2, head * width : (head + 1) * width], axis=1, keepdims=True)
            skip_row = jnp.where(lane == head, value, skip_row)
        small[p.rep, p.core, 8:10, 0:LANES] = heads_total[0:2, :]
        small[p.rep, p.core, 10:11, 0:LANES] = skip_row
        small[p.rep, p.core, 11:12, 0:channels] = wide_total[0:1, :]
        small_job = ColumnSum(p, small, *work["small"][1:5])
        small_job.ready()
        small_job.step(0)
        for at in range(1, depth - 1):
            for job in (common_job, side_jobs[0], small_job):
                job.step(at)

        def to_reps(source, target, at):
            for distance in range(1, reps):
                p.send(source, target.at[p.rep], end_sems.at[0, at, distance], end_sems.at[1, at, distance],
                       p.device(rep=p.rep_at(distance)))

        def from_reps(target, at):
            for distance in range(1, reps):
                p.arrived(target.at[p.rep_at(distance)], end_sems.at[1, at, distance])

        def side_finish(kind):
            side_jobs[kind].total(side_total)
            side_pair[kind, p.core] = side_total[p.core].astype(BF16)
            side_away[kind] = side_total[1 - p.core].astype(BF16)
            p.send(side_away.at[kind], side_pair.at[kind, p.core], side_swap.at[0, kind], side_swap.at[1, kind],
                   p.sibling())
            p.arrived(side_pair.at[kind, 1 - p.core], side_swap.at[1, kind])
            to_reps(side_pair.at[kind], side_out.at[kind], kind)
            return p.local(side_pair.at[kind], side_out.at[kind, p.rep], keep_sems.at[kind])

        keeps = [side_finish(0)]
        common_total, common_low = work["common"][5:]
        common_job.total(common_total)
        common_low[...] = common_total[...].astype(BF16)
        to_reps(common_low, common_out, 2)
        keeps.append(p.local(common_low, common_out.at[p.rep], keep_sems.at[2]))
        out_job.total(out_line_total)
        out_low[...] = out_line_total[...].astype(BF16)
        to_reps(out_low, out_out, 3)
        keeps.append(p.local(out_low, out_out.at[p.rep], keep_sems.at[5]))
        small_total, small_all = work["small"][5:]
        small_job.total(small_total)
        small_all[p.rep] = small_total[...]
        to_reps(small_total, small_all, 4)
        for at in range(1, depth - 1):
            side_jobs[1].step(at)
        keeps.append(side_finish(1))

        late_load(after_ref, 0).start()
        layer_job.total(own_part)
        for chunk in range(rows // 32):
            piece = slice(32 * chunk, 32 * chunk + 32)
            if chunk + 1 < rows // 32:
                late_load(after_ref, chunk + 1).start()
            late_load(after_ref, chunk).wait()
            layer_out_ref[piece, :] = (own_part[piece, :] + late[chunk % 2]).astype(BF16)
        from_reps(small_all, 4)
        small_out[...] = add_up(*[small_all[at] for at in range(reps)])
        for at, target in ((0, side_out.at[0]), (1, side_out.at[1]), (2, common_out), (3, out_out)):
            from_reps(target, at)
        for keep in keeps:
            keep.wait()
        for distance in range(reps):
            rep = p.rep_at(distance)
            if distance in (0, reps - 1):
                swap(distance, rep, False)
            if distance:
                onward(distance, rep, False)
        p.finish()

    return pl.pallas_call(
        kernel,
        in_specs=in_vmem(1) + anywhere(2) + in_vmem(11) + anywhere(5),
        out_specs=in_vmem(2) + anywhere(3) + in_vmem(1),
        out_shape=[
            jax.ShapeDtypeStruct((rows, model), BF16),
            jax.ShapeDtypeStruct((rows, model), BF16),
            jax.ShapeDtypeStruct((2, reps, 2, part, channels), BF16),
            jax.ShapeDtypeStruct((reps, part, wide - side), BF16),
            jax.ShapeDtypeStruct((reps, quarter, model), BF16),
            jax.ShapeDtypeStruct(small_shape, F32),
        ],
        scratch_shapes=[item for items in groups.values() for item in items],
        compiler_params=remote_params(3, 63),
        name="backward_mixer",
    )(
        scales, after, after_grad, tokens, in_gain, post_grad, router_parts, lengths, taps, head_rows, skip, norm,
        weight, out_weight, low, layer_parts, first, proj, gained,
    )


def assemble_kernel(channels, state, heads, side_ref, common_ref, out_ref, in_grad_ref, out_grad_ref):
    reps = side_ref.shape[1]
    inner = 2 * reps * channels
    for kind in range(2):
        for rep in range(reps):
            for core in range(2):
                at = kind * inner + (2 * rep + core) * channels
                in_grad_ref[:, at : at + channels] = side_ref[kind, rep, core].astype(F32)
    in_grad_ref[:, 2 * inner : 2 * inner + 2 * state] = add_up(
        *[common_ref[rep, :, : 2 * state] for rep in range(reps)]
    )
    start = 2 * inner + 2 * state
    tail = []
    for rep in range(reps):
        pair = common_ref[rep, :, 2 * state :].astype(F32)
        tail += [pair[:, :heads], pair[:, LANES // 2 : LANES // 2 + heads]]
    in_grad_ref[:, start:] = jnp.concatenate(tail, axis=1)
    out_grad_ref[...] = out_ref[...].astype(F32).reshape(out_grad_ref.shape)


def assemble(side, common, out_rows, channels, state, heads):
    reps, part = side.shape[1], side.shape[3]
    columns = 4 * reps * channels + 2 * state + 2 * reps * heads
    model = out_rows.shape[2]
    return pl.pallas_call(
        functools.partial(assemble_kernel, channels, state, heads),
        in_specs=in_vmem(3),
        out_specs=in_vmem(2),
        out_shape=[
            jax.ShapeDtypeStruct((part, columns), F32),
            jax.ShapeDtypeStruct((channels, model), F32),
        ],
        compiler_params=pltpu.CompilerParams(vmem_limit_bytes=48 * 2**20),
        name="assemble",
    )(side, common, out_rows)


def slot_match(table_row, capacity, rows):
    slot = lax.broadcasted_iota(jnp.int32, (capacity, rows), 0).astype(F32) + 1.0
    return table_row == slot


def dispatch_kernel(
    local, capacity, half,
    table_ref, own_ref, second_ref, g_ref, router_ref, in_ref, out_ref,
    buffer_ref, slot_g_ref, gate_slot_ref, gates_ref, hidden_ref, grad_ref, in_grad_ref, out_grad_ref,
    in_total, out_total,
):
    at = pl.program_id(0)
    second, g = second_ref[...], g_ref[...]
    rows = second.shape[0]
    table = table_ref[...].astype(F32)
    used = table > 0.0
    logits = mm_nt(router_ref[...], second)
    top = jnp.max(jnp.where(used, logits, -jnp.inf), axis=0, keepdims=True)
    raw = jnp.where(used, jnp.exp(jnp.where(used, logits - top, 0.0)), 0.0)
    gates = raw / jnp.sum(raw, axis=0, keepdims=True)
    gates_ref[...] = gates
    expert = lax.broadcasted_iota(jnp.int32, gates.shape, 0)
    shard = 2 * lax.axis_index("z") + lax.axis_index("core")
    for i in range(local):
        match = slot_match(own_ref[i : i + 1, :].astype(F32), capacity, rows)
        onehot = match.astype(BF16)
        buffer_ref[i] = mm(onehot, second).astype(BF16)
        slot_g_ref[i] = mm(onehot, g).astype(BF16)
        gate_row = jnp.sum(jnp.where(expert == local * shard + i, gates, 0.0), axis=0, keepdims=True)
        gate_slot = jnp.sum(jnp.where(match, gate_row, 0.0), axis=1, keepdims=True)
        gate_slot_ref[i] = jnp.broadcast_to(gate_slot, (capacity, LANES))
    pre = mm(second, in_ref[...])
    a, b = pre[:, :half], pre[:, half:]
    sig = jax.nn.sigmoid(a)
    hidden = (a * sig * b).astype(BF16)
    hidden_ref[...] = hidden
    back = mm_nt(g, out_ref[...])
    grad = jnp.concatenate([back * b * silu_slope(a, sig), back * a * sig], axis=1).astype(BF16)
    grad_ref[...] = grad

    @pl.when(at == 0)
    def _():
        in_total[...] = jnp.zeros_like(in_total)
        out_total[...] = jnp.zeros_like(out_total)

    in_total[...] += mm_tn(second, grad)
    out_total[...] += mm_tn(hidden, g)

    @pl.when(at == pl.num_programs(0) - 1)
    def _():
        in_grad_ref[...] = in_total[...].astype(BF16)
        out_grad_ref[...] = out_total[...].astype(BF16)


def dispatch(table, own, second, g, router_t, shared_in, shared_out, capacity):
    group, experts, rows = table.shape
    local = own.shape[1]
    model = second.shape[1]
    half = shared_out.shape[0]
    slots = group * capacity

    def by_block(*shape):
        return pl.BlockSpec((None,) + shape, lambda q: (q,) + (0,) * len(shape))

    def by_slots(width):
        return pl.BlockSpec((local, capacity, width), lambda q: (0, q, 0))

    return pl.pallas_call(
        functools.partial(dispatch_kernel, local, capacity, half),
        grid=(group,),
        in_specs=[
            by_block(experts, rows), by_block(local, rows), by_rows((rows, model)), by_rows((rows, model)),
            whole((experts, model)), whole((model, 2 * half)), whole((half, model)),
        ],
        out_specs=[
            by_slots(model), by_slots(model), by_slots(LANES), by_block(experts, rows), by_rows((rows, half)),
            by_rows((rows, 2 * half)), whole((model, 2 * half)), whole((half, model)),
        ],
        out_shape=[
            jax.ShapeDtypeStruct((local, slots, model), BF16),
            jax.ShapeDtypeStruct((local, slots, model), BF16),
            jax.ShapeDtypeStruct((local, slots, LANES), F32),
            jax.ShapeDtypeStruct((group, experts, rows), F32),
            jax.ShapeDtypeStruct((group * rows, half), BF16),
            jax.ShapeDtypeStruct((group * rows, 2 * half), BF16),
            jax.ShapeDtypeStruct((model, 2 * half), BF16),
            jax.ShapeDtypeStruct((half, model), BF16),
        ],
        scratch_shapes=[pltpu.VMEM((model, 2 * half), F32), pltpu.VMEM((half, model), F32)],
        compiler_params=pltpu.CompilerParams(vmem_limit_bytes=56 * 2**20),
        name="dispatch",
    )(table, own, second, g, router_t, shared_in, shared_out)


def experts_kernel(
    buffer_ref, slot_g_ref, gate_ref, in_ref, out_ref,
    weighted_ref, back_ref, dot_ref, in_grad_ref, out_grad_ref, in_total, out_total,
):
    at = pl.program_id(1)
    buffer, weight_in, weight_out = buffer_ref[...], in_ref[...], out_ref[...]
    half = weight_out.shape[0]
    pre = mm(buffer, weight_in)
    a, b = pre[:, :half], pre[:, half:]
    sig = jax.nn.sigmoid(a)
    act = a * sig
    hidden = (act * b).astype(BF16)
    gate = gate_ref[:, 0:1]
    slot_g = slot_g_ref[...].astype(F32)
    result = mm(hidden, weight_out).astype(BF16).astype(F32)
    weighted_ref[...] = (gate * result).astype(BF16)
    dot_ref[...] = jnp.broadcast_to(jnp.sum(slot_g * result, axis=1, keepdims=True), dot_ref.shape)
    result_grad = (gate * slot_g).astype(BF16)
    hidden_grad = mm_nt(result_grad, weight_out)
    pre_grad = jnp.concatenate([hidden_grad * b * silu_slope(a, sig), hidden_grad * act], axis=1).astype(BF16)
    back_ref[...] = mm_nt(pre_grad, weight_in).astype(BF16)

    @pl.when(at == 0)
    def _():
        in_total[...] = jnp.zeros_like(in_total)
        out_total[...] = jnp.zeros_like(out_total)

    in_total[...] += mm_tn(buffer, pre_grad)
    out_total[...] += mm_tn(hidden, result_grad)

    @pl.when(at == pl.num_programs(1) - 1)
    def _():
        in_grad_ref[...] = in_total[...].astype(BF16)
        out_grad_ref[...] = out_total[...].astype(BF16)


def run_experts(buffer, slot_g, gate_slot, expert_in, expert_out, step):
    local, slots, model = buffer.shape
    half = expert_out.shape[1]

    def by_step(width):
        return pl.BlockSpec((None, step, width), lambda i, m: (i, m, 0))

    def by_expert(*shape):
        return pl.BlockSpec((None,) + shape, lambda i, m: (i, 0, 0))

    return pl.pallas_call(
        experts_kernel,
        grid=(local, slots // step),
        in_specs=[
            by_step(model), by_step(model), by_step(LANES), by_expert(model, 2 * half), by_expert(half, model),
        ],
        out_specs=[
            by_step(model), by_step(model), by_step(LANES), by_expert(model, 2 * half), by_expert(half, model),
        ],
        out_shape=[
            jax.ShapeDtypeStruct((local, slots, model), BF16),
            jax.ShapeDtypeStruct((local, slots, model), BF16),
            jax.ShapeDtypeStruct((local, slots, LANES), F32),
            jax.ShapeDtypeStruct((local, model, 2 * half), BF16),
            jax.ShapeDtypeStruct((local, half, model), BF16),
        ],
        scratch_shapes=[pltpu.VMEM((model, 2 * half), F32), pltpu.VMEM((half, model), F32)],
        compiler_params=pltpu.CompilerParams(vmem_limit_bytes=62 * 2**20),
        name="run_experts",
    )(buffer, slot_g, gate_slot, expert_in, expert_out)


def gather(values, axes, axis=0):
    return lax.all_gather(values, axes, axis=axis, tiled=True)


def scatter_sum(values, axes, axis=0):
    return lax.psum_scatter(values, axes, scatter_dimension=axis, tiled=True)


def columns_of(values, start, size, axis=1):
    return lax.dynamic_slice_in_dim(values, start, size, axis=axis)


def shards(
    tokens,
    cotangent,
    dealt_to,
    lengths,
    routes,
    slot_index,
    in_norm,
    in_proj,
    conv_weight,
    conv_bias,
    dt_bias,
    decay_log,
    skip_gain,
    mixer_norm,
    out_proj,
    post_norm,
    router,
    shared_in,
    shared_out,
    expert_in,
    expert_out,
):
    reps, depth = lax.axis_size("rep"), lax.axis_size("z")
    group = 2 * depth
    rep, z, core = lax.axis_index("rep"), lax.axis_index("z"), lax.axis_index("core")
    shard = 2 * z + core
    team = 2 * rep + core
    members = 2 * reps
    rows, model = tokens.shape
    top = routes.shape[1]
    local = expert_in.shape[0]
    experts = local * group
    capacity = rows * top * 4 // (3 * experts)
    inner = mixer_norm.shape[0] * group
    convolved = conv_bias.shape[0] * group
    head_count = dt_bias.shape[0] * group
    width = inner // head_count
    state = (convolved - inner) // 2
    channels = inner // members
    heads = head_count // members
    shared = shared_out.shape[0]
    part = in_norm.shape[0]

    expert_ids = jnp.arange(experts, dtype=jnp.int32)
    table = jnp.sum(
        jnp.where(routes[:, None, :] == expert_ids[None, :, None], slot_index[:, None, :] + 1, 0), axis=2
    ).astype(BF16)
    numbers = jnp.concatenate([lengths[0], dealt_to]).astype(BF16)
    vector_rows = [in_norm[None], conv_weight, conv_bias[None], dt_bias[None], decay_log[None], skip_gain[None],
                   mixer_norm[None], post_norm[None], numbers[None]]
    vector_width = -(-max(row.shape[1] for row in vector_rows) // LANES) * LANES
    vectors = jnp.concatenate(
        [jnp.pad(row, ((0, 0), (0, vector_width - row.shape[1]))) for row in vector_rows]
        + [jnp.zeros((4, vector_width), BF16)], axis=0
    )
    part_wide = -(-part // LANES) * LANES
    table_block = jnp.concatenate([table.T, jnp.pad(router.T, ((0, 0), (0, part_wide - part)))], axis=1)
    pair_heads = 2 * heads
    dt_pair = columns_of(in_proj, inner + convolved + pair_heads * rep, pair_heads)
    blank = jnp.zeros((part, LANES // 2 - heads), BF16)
    common = jnp.concatenate(
        [in_proj[:, 2 * inner : 2 * inner + 2 * state], dt_pair[:, :heads], blank, dt_pair[:, heads:], blank], axis=1
    )

    def pair_of(member):
        return jnp.concatenate(
            [columns_of(in_proj, channels * member, channels), columns_of(in_proj, inner + channels * member, channels)],
            axis=1,
        )

    sequences = lengths.shape[1]
    (after, mixer_result, scale, lengths_plane, in_gain, post_gain, taps_own, head_rows, skip_own, norm_own, table_all,
     second_column, g_column, first, weight, out_own, projected, gained) = forward_mixer(
        tokens, cotangent, pair_of(team), pair_of(2 * rep + 1 - core), common, vectors, table_block,
        out_proj.reshape(reps, channels // reps, model),
        (reps, depth, channels, width, state, sequences, inner, convolved),
    )
    second_column = second_column.reshape(group * rows, model)
    g_column = g_column.reshape(group * rows, model)
    shared_in_own = lax.all_to_all(
        shared_in.reshape(part, 2, group, shared).transpose(2, 0, 1, 3).reshape(group * part, 2 * shared),
        COLUMN, split_axis=0, concat_axis=0, tiled=True,
    )

    table_all = table_all.reshape(group, experts, -1)
    router_t = table_all[:, :, rows : rows + part].transpose(1, 0, 2).reshape(experts, model)
    dealt_column = shard ^ dealt_to[0] ^ jnp.arange(group, dtype=jnp.int32)
    table_dealt = jnp.take(table_all[:, :, :rows], dealt_column, axis=0)
    table_own = columns_of(table_dealt, local * shard, local)

    buffer, slot_g, gate_slot, gates, shared_hidden, shared_grad, shared_in_grad, shared_out_grad = dispatch(
        table_dealt, table_own, second_column, g_column, router_t, shared_in_own, shared_out, capacity
    )
    weighted, buffer_grad, dots, grad_expert_in, grad_expert_out = run_experts(
        buffer, slot_g, gate_slot, expert_in, expert_out, group * capacity // 2
    )
    shared_in_rows = lax.all_to_all(shared_in_grad, COLUMN, split_axis=0, concat_axis=0, tiled=True)
    shared_in_rows = shared_in_rows.reshape(group, part, 2, shared).transpose(1, 2, 0, 3).reshape(part, -1)
    grad_expert_in, grad_expert_out, grad_shared_out, grad_shared_in = [
        values.astype(F32)
        for values in lax.psum((grad_expert_in, grad_expert_out, shared_out_grad, shared_in_rows), "rep")
    ]

    after_grad, post_grad, router_grad, layer_parts, low_plane, scales = join_experts(
        table_own, gates, dots, shared_hidden, shared_grad, router_t, shared_in_own, shared_out, cotangent, after,
        mixer_result, scale, post_gain, buffer_grad, weighted, second_column, inner, reps, depth, capacity,
    )
    router_parts = jnp.pad(
        router_grad.reshape(experts, depth, 2, part).transpose(1, 2, 0, 3), ((0, 0), (0, 0), (0, 0), (0, part_wide - part))
    )
    layer_out, grad_tokens, side_rows, common_rows, out_rows, small_sum = backward_mixer(
        scales, after, after_grad, tokens, in_gain, post_grad, router_parts, lengths_plane, taps_own, head_rows, skip_own, norm_own, weight.reshape(model, -1),
        out_own.reshape(channels, model), low_plane, layer_parts, first, projected, gained,
        (reps, depth, channels, width, state, sequences, inner, convolved),
    )
    grad_in_proj, grad_out_proj = assemble(side_rows, common_rows, out_rows, channels, state, heads)
    per_shard = conv_bias.shape[0]

    return (
        layer_out,
        grad_tokens,
        small_sum[13, :part],
        grad_in_proj,
        small_sum[:4, :per_shard],
        small_sum[4, :per_shard],
        small_sum[8, :heads],
        small_sum[9, :heads],
        small_sum[10, :heads],
        small_sum[11, :channels],
        grad_out_proj,
        small_sum[12, :part],
        small_sum[16:, :part].T,
        grad_shared_in,
        grad_shared_out,
        grad_expert_in,
        grad_expert_out,
    )


def solution(mesh):
    reps, group = mesh.shape["rep"], mesh.shape["shard"]
    split = Mesh(mesh.devices.reshape(reps, group // 2, 2), ALL)
    one, row = P(COLUMN), P(COLUMN, None)
    token = P(ALL, None)
    return jax.shard_map(
        shards,
        mesh=split,
        in_specs=(
            token, token, P(ALL), token, token, token, one, row, P(None, COLUMN), one, one, one, one, one, row,
            one, row, row, row, P(COLUMN, None, None), P(COLUMN, None, None),
        ),
        out_specs=(
            token, token, one, row, P(None, COLUMN), one, one, one, one, one, row, one, row, row, row,
            P(COLUMN, None, None), P(COLUMN, None, None),
        ),
        check_vma=False,
    )
```

```python
import functools

import jax
import jax.numpy as jnp
from jax import lax
from jax.experimental import pallas as pl
from jax.experimental.pallas import tpu as pltpu
from jax.sharding import Mesh
from jax.sharding import PartitionSpec as P

EPS = 1e-05
HIGH = lax.Precision.HIGHEST
F32 = jnp.float32
BF16 = jnp.bfloat16
ALL = ("rep", "z", "core")
COLUMN = ("z", "core")
PLANE = ("rep", "core")
LANES = 128


def rms_rows(values):
    return lax.rsqrt(jnp.mean(values * values, axis=-1, keepdims=True) + EPS)


def mm(left, right):
    return jnp.dot(left, right, preferred_element_type=F32)


def mm_nt(left, right):
    return lax.dot_general(left, right, (((1,), (1,)), ((), ())), preferred_element_type=F32)


def mm_tn(left, right):
    return lax.dot_general(left, right, (((0,), (0,)), ((), ())), preferred_element_type=F32)


def silu_slope(values, sig):
    return sig * (1.0 + values * (1.0 - sig))


def split_two(values):
    high = values.astype(BF16)
    return high, (values - high.astype(F32)).astype(BF16)


def segments(lengths_row, sequences, rows):
    column = lax.broadcasted_iota(jnp.int32, (rows, 1), 0).astype(F32)
    line = lax.broadcasted_iota(jnp.int32, (1, rows), 1).astype(F32)
    end = jnp.zeros((1, 1), F32)
    seg_column, seg_line = jnp.zeros_like(column), jnp.zeros_like(line)
    for at in range(sequences):
        end = end + lengths_row[:, at : at + 1]
        seg_column = seg_column + jnp.where(column >= end, 1.0, 0.0)
        seg_line = seg_line + jnp.where(line >= end, 1.0, 0.0)
    return seg_column, seg_line


class Block:
    def __init__(self, proj, seg_col, seg_row, taps, heads, channels, width, state):
        rows = proj.shape[0]
        self.rows, self.channels, self.width, self.state = rows, channels, width, state
        self.gate = proj[:, :channels]
        self.xbc = proj[:, channels : 2 * channels + 2 * state]
        self.turn = lax.axis_index("core") * (LANES // 2)
        dt_raw = pltpu.roll(proj[:, 2 * channels + 2 * state :], self.turn, 1)
        position = lax.broadcasted_iota(jnp.int32, (rows, 1), 0)
        seg_wide = jnp.broadcast_to(seg_col, (rows, LANES))
        self.masks = []
        conv = taps[4:5, :] + taps[3:4, :] * self.xbc
        for offset in (1, 2, 3):
            before = pltpu.roll(seg_wide, offset, 0)[:, :1]
            mask = jnp.where((before == seg_col) & (position >= offset), 1.0, 0.0)
            self.masks.append(mask)
            conv = conv + taps[3 - offset : 4 - offset, :] * (mask * pltpu.roll(self.xbc, offset, 0))
        self.conv = conv
        self.conv_sig = jax.nn.sigmoid(conv)
        act = conv * self.conv_sig
        self.xin = act[:, :channels]
        self.write = act[:, channels : channels + state]
        self.read = act[:, channels + state :]
        shifted = dt_raw + heads[0:1, :]
        self.step = jnp.maximum(shifted, 0.0) + jnp.log1p(jnp.exp(-jnp.abs(shifted)))
        self.step_sig = jax.nn.sigmoid(shifted)
        self.speed = heads[1:2, :]
        self.rate = -self.step * self.speed
        row_at = lax.broadcasted_iota(jnp.int32, (rows, rows), 0)
        col_at = lax.broadcasted_iota(jnp.int32, (rows, rows), 1)
        self.causal = row_at >= col_at
        self.keep = self.causal & (seg_col == seg_row)
        self.cum = jnp.dot(self.causal.astype(F32), self.rate, precision=HIGH, preferred_element_type=F32)
        self.cum_t = self.cum.T
        scores = lax.dot_general(
            self.read, self.write, (((1,), (1,)), ((), ())), precision=HIGH, preferred_element_type=F32
        )
        self.scores = jnp.where(self.keep, scores, 0.0)

    def groups(self):
        for start in range(0, self.channels, LANES):
            stop = min(start + LANES, self.channels)
            yield start, stop, list(range(start // self.width, (stop - 1) // self.width + 1))

    def spread(self, columns, start, stop, heads):
        lane = lax.broadcasted_iota(jnp.int32, (self.rows, stop - start), 1) + start
        result = jnp.broadcast_to(columns[:, heads[0] : heads[0] + 1], (self.rows, stop - start))
        for head in heads[1:]:
            result = jnp.where(lane >= head * self.width, columns[:, head : head + 1], result)
        return result

    def inside(self, start, stop, head):
        lane = lax.broadcasted_iota(jnp.int32, (self.rows, stop - start), 1) + start
        return (lane >= head * self.width) & (lane < (head + 1) * self.width)

    def decay(self, head):
        gaps = self.cum[:, head : head + 1] - self.cum_t[head : head + 1, :]
        return jnp.exp(jnp.where(self.keep, gaps, 0.0))


def block_back(block, low, scale, pull, taps_ref, skip_ref, norm_ref, weight, out_weight):
    rows, channels = block.rows, block.channels
    normed_grad = mm_nt(low, out_weight)
    taps = taps_ref[...]
    gate_grads, x_grads, norm_grads, skip_grads = [], [], [], []
    step_grad = jnp.zeros((rows, LANES), F32)
    cum_grad = jnp.zeros((rows, LANES), F32)
    cum_grad_t = jnp.zeros((LANES, rows), F32)
    score_grad = jnp.zeros((rows, rows), F32)
    lane_all = lax.broadcasted_iota(jnp.int32, (rows, LANES), 1)
    sub_all = lax.broadcasted_iota(jnp.int32, (LANES, rows), 0)
    for start, stop, heads in block.groups():
        xin = block.xin[:, start:stop]
        spread = block.spread(block.step, start, stop, heads)
        scaled, scaled_rest = split_two(xin * spread)
        scaled_wide = jnp.concatenate([scaled, scaled, scaled_rest], axis=1)
        weights, decays = [], []
        y = None
        for head in heads:
            decays.append(block.decay(head))
            weights.append(block.scores * decays[-1])
            term = mm(weights[-1].astype(BF16), scaled)
            y = term if y is None else jnp.where(block.inside(start, stop, head), term, y)
        skip = skip_ref[:, start:stop]
        y = y + skip * xin
        gate = block.gate[:, start:stop]
        gate_sig = jax.nn.sigmoid(gate)
        gate_act = gate * gate_sig
        mixed = y * gate_act
        q = normed_grad[:, start:stop]
        norm_grads.append(jnp.sum(mixed * scale * q, axis=0, keepdims=True))
        mixed_grad = scale * norm_ref[:, start:stop] * q - mixed * pull
        gate_grads.append(mixed_grad * y * silu_slope(gate, gate_sig))
        y_grad = mixed_grad * gate_act
        skip_grads.append(jnp.sum(y_grad * xin, axis=0, keepdims=True))
        y_low, y_rest = split_two(y_grad)
        scaled_grad = None
        for at, head in enumerate(heads):
            inside = block.inside(start, stop, head)
            term = mm_tn(weights[at].astype(BF16), y_low)
            scaled_grad = term if scaled_grad is None else jnp.where(inside, term, scaled_grad)
            blank = jnp.zeros_like(y_low)
            y_own = jnp.where(inside, y_low, blank)
            pair_grad = mm_nt(
                jnp.concatenate([y_own, jnp.where(inside, y_rest, blank), y_own], axis=1), scaled_wide
            )
            score_grad = score_grad + pair_grad * decays[at]
            exponent_grad = pair_grad * weights[at]
            cum_grad = jnp.where(lane_all == head, jnp.sum(exponent_grad, axis=1, keepdims=True), cum_grad)
            cum_grad_t = jnp.where(sub_all == head, jnp.sum(exponent_grad, axis=0, keepdims=True), cum_grad_t)
        for head in heads:
            inside = block.inside(start, stop, head)
            per_row = jnp.sum(jnp.where(inside, scaled_grad * xin, 0.0), axis=1, keepdims=True)
            step_grad = jnp.where(lane_all == head, per_row, step_grad)
        x_grads.append(scaled_grad * spread + skip * y_grad)
    score_grad = jnp.where(block.keep, score_grad, 0.0).astype(BF16)
    read_grad = mm(score_grad, block.write.astype(BF16))
    write_grad = mm_tn(score_grad, block.read.astype(BF16))
    cum_grad = cum_grad - cum_grad_t.T
    rate_grad = lax.dot_general(
        block.causal.astype(F32), cum_grad, (((0,), (0,)), ((), ())), precision=HIGH, preferred_element_type=F32
    )
    dt_grad = (step_grad - block.speed * rate_grad) * block.step_sig
    head_rows = [jnp.sum(dt_grad, axis=0, keepdims=True), jnp.sum(rate_grad * block.rate, axis=0, keepdims=True)]
    act_grad = jnp.concatenate(x_grads + [write_grad, read_grad], axis=1)
    conv_grad = act_grad * silu_slope(block.conv, block.conv_sig)
    tap_rows = {4: jnp.sum(conv_grad, axis=0, keepdims=True), 3: jnp.sum(conv_grad * block.xbc, axis=0, keepdims=True)}
    xbc_grad = taps[3:4, :] * conv_grad
    for offset in (1, 2, 3):
        masked = conv_grad * block.masks[offset - 1]
        tap_rows[3 - offset] = jnp.sum(masked * pltpu.roll(block.xbc, offset, 0), axis=0, keepdims=True)
        xbc_grad = xbc_grad + taps[3 - offset : 4 - offset, :] * pltpu.roll(masked, rows - offset, 0)
    proj_grad = jnp.concatenate(gate_grads + [xbc_grad, pltpu.roll(dt_grad, block.turn, 1)], axis=1).astype(BF16)
    tap_grads = jnp.concatenate([tap_rows[at] for at in range(5)], axis=0)
    wide_grads = jnp.concatenate(
        [jnp.concatenate(norm_grads, axis=1), jnp.concatenate(skip_grads, axis=1)], axis=0
    )
    return proj_grad, tap_grads, head_rows, wide_grads


def whole(shape):
    return pl.BlockSpec(shape, lambda i: (0,) * len(shape))


def by_rows(shape):
    return pl.BlockSpec(shape, lambda i: (i,) + (0,) * (len(shape) - 1))


MESH_ID = pl.DeviceIdType.MESH


def when(condition, action):
    if condition is True:
        action()
    elif condition is not False:
        pl.when(condition)(action)


class Place:
    def __init__(self, reps, depth):
        self.reps, self.depth = reps, depth
        self.rep, self.z, self.core = lax.axis_index("rep"), lax.axis_index("z"), lax.axis_index("core")
        self.here = {"rep": self.rep, "z": self.z, "core": self.core}
        self.pending = []

    def device(self, **changes):
        return {**self.here, **changes}

    def sibling(self):
        return self.device(core=1 - self.core)

    def rep_at(self, distance):
        result, place = 0, 1
        while place < self.reps:
            mine, other = lax.rem(self.rep // place, 2), lax.rem(distance // place, 2)
            result = result + place * (mine + other - 2 * mine * other)
            place *= 2
        return result

    def barrier(self, plane=False, column=False, everyone=False):
        semaphore = pltpu.get_barrier_semaphore()

        def greet(device):
            pl.semaphore_signal(semaphore, inc=1, device_id=device, device_id_type=MESH_ID)

        if everyone:
            count = self.reps * self.depth * 2
            mine = (self.rep * self.depth + self.z) * 2 + self.core

            def step(distance, carry):
                other = lax.rem(mine + distance, count)
                greet({"rep": other // (2 * self.depth), "z": lax.rem(other // 2, self.depth), "core": lax.rem(other, 2)})
                return carry

            lax.fori_loop(1, count, step, 0)
            pl.semaphore_wait(semaphore, count - 1)
            return
        amount = 1
        greet(self.sibling())
        if plane:
            for distance in range(1, self.reps):
                greet(self.device(rep=self.rep_at(distance)))
            amount = amount + self.reps - 1
        if column:
            above, below = self.z < self.depth - 1, self.z > 0
            when(above, lambda: greet(self.device(z=self.z + 1)))
            when(below, lambda: greet(self.device(z=self.z - 1)))
            amount = amount + jnp.where(above, 1, 0) + jnp.where(below, 1, 0)
        pl.semaphore_wait(semaphore, amount)

    def send(self, source, target, send_sem, recv_sem, device, condition=True):
        copy = pltpu.make_async_remote_copy(
            src_ref=source, dst_ref=target, send_sem=send_sem, recv_sem=recv_sem, device_id=device,
            device_id_type=MESH_ID,
        )
        when(condition, copy.start)
        self.pending.append((condition, copy))

    def local(self, source, target, sem):
        copy = pltpu.make_async_copy(source, target, sem)
        copy.start()
        return copy

    def arrived(self, target, recv_sem, condition=True):
        copy = pltpu.make_async_remote_copy(
            src_ref=target, dst_ref=target, send_sem=recv_sem, recv_sem=recv_sem, device_id=self.sibling(),
            device_id_type=MESH_ID,
        )
        when(condition, copy.wait_recv)

    def finish(self):
        for condition, copy in self.pending:
            when(condition, copy.wait_send)
        self.pending = []


class PlaneGather:
    @staticmethod
    def scratch(reps):
        return [pltpu.SemaphoreType.DMA((4, reps)), pltpu.SemaphoreType.DMA((1,))]

    def __init__(self, place, own, out, sems, local_sem):
        self.place, self.out, self.sems = place, out, sems
        p = place
        self.keep = p.local(own, out.at[p.rep, p.core], local_sem.at[0])
        for distance in range(1, p.reps):
            p.send(own, out.at[p.rep, p.core], sems.at[0, distance], sems.at[1, distance],
                   p.device(rep=p.rep_at(distance)))
        p.send(own, out.at[p.rep, p.core], sems.at[2, 0], sems.at[3, 0], p.sibling())

    def relay(self):
        p = self.place
        for distance in range(1, p.reps):
            source = self.out.at[p.rep_at(distance), p.core]
            p.arrived(source, self.sems.at[1, distance])
            p.send(source, source, self.sems.at[2, distance], self.sems.at[3, distance], p.sibling())

    def finish(self):
        p = self.place
        self.keep.wait()
        for distance in range(p.reps):
            source = p.rep_at(distance) if distance else p.rep
            p.arrived(self.out.at[source, 1 - p.core], self.sems.at[3, distance])


class ColumnGather:
    @staticmethod
    def scratch(depth):
        return [pltpu.SemaphoreType.DMA((8, depth)), pltpu.SemaphoreType.DMA((1,))]

    def __init__(self, place, own, slot, sems, local_sem, shared=None, keep=True, start=True):
        self.place, self.own, self.slot, self.sems, self.shared = place, own, slot, sems, shared
        self.keep = None
        if keep:
            self.keep = pltpu.make_async_copy(own, slot(place.z), local_sem.at[0])
        if start:
            self.start()

    def start(self):
        if self.keep is not None:
            self.keep.start()
        self.send(0)

    def ends(self, distance):
        p = self.place
        below, above = p.z >= distance, p.z + distance < p.depth
        return below, above, jnp.maximum(p.z - distance, 0), jnp.minimum(p.z + distance, p.depth - 1)

    def copies(self, distance):
        p = self.place

        def copy(source, target, at, device):
            return pltpu.make_async_remote_copy(
                src_ref=source, dst_ref=target, send_sem=self.sems.at[at, distance],
                recv_sem=self.sems.at[at + 1, distance], device_id=device, device_id_type=MESH_ID,
            )

        up, down = p.device(z=p.z + 1), p.device(z=p.z - 1)
        if distance == 0:
            target = self.slot(p.z)
            yield p.z < p.depth - 1, copy(self.own, target, 0, up)
            yield p.z > 0, copy(self.own, target, 2, down)
            if self.shared is not None:
                yield True, copy(self.own, target, 4, p.sibling())
            return
        below, above, low, high = self.ends(distance)
        low, high = self.slot(low), self.slot(high)
        yield below & (p.z < p.depth - 1), copy(low, low, 0, up)
        yield above & (p.z > 0), copy(high, high, 2, down)
        if self.shared is not None:
            yield below, copy(low, low, 4, p.sibling())
            yield above, copy(high, high, 6, p.sibling())

    def send(self, distance):
        for condition, copy in self.copies(distance):
            when(condition, copy.start)

    def hop(self, distance):
        below, above, low, high = self.ends(distance)
        self.place.arrived(self.slot(low), self.sems.at[1, distance - 1], below)
        self.place.arrived(self.slot(high), self.sems.at[3, distance - 1], above)
        self.send(distance)

    def finish(self):
        p = self.place
        if self.keep is not None:
            self.keep.wait()
        if self.shared is not None:
            p.arrived(self.shared(p.z), self.sems.at[5, 0])
            for distance in range(1, p.depth):
                below, above, low, high = self.ends(distance)
                p.arrived(self.shared(low), self.sems.at[5, distance], below)
                p.arrived(self.shared(high), self.sems.at[7, distance], above)
        for distance in range(p.depth):
            for condition, copy in self.copies(distance):
                when(condition, copy.wait_send)


def add_up(*terms):
    total = terms[0].astype(F32)
    for term in terms[1:]:
        total = total + term.astype(F32)
    return total


class PairSwap:
    @staticmethod
    def scratch(count, shape, dtype):
        return [pltpu.VMEM((count,) + shape, dtype), pltpu.SemaphoreType.DMA((2, count))]

    def __init__(self, place, parts, pair, sems, order, own=None):
        self.place, self.parts, self.pair, self.sems, self.own = place, parts, pair, sems, own
        for at in order:
            place.send(parts.at[at, 1 - place.core], pair.at[at], sems.at[0, at], sems.at[1, at], place.sibling())

    def wait(self, at):
        self.place.arrived(self.pair.at[at], self.sems.at[1, at])

    def terms(self, at):
        if self.own is None:
            return [self.parts[at, self.place.core], self.pair[at]]
        slot, sem = self.own
        self.place.local(self.parts.at[at, self.place.core], slot, sem.at[0]).wait()
        return [slot[...], self.pair[at]]


class PlaneSum:
    @staticmethod
    def scratch(reps, shape, dtype):
        return PairSwap.scratch(reps, shape, dtype) + [
            pltpu.VMEM((reps,) + shape, dtype), pltpu.SemaphoreType.DMA((2, reps)),
        ]

    def __init__(self, place, parts, pair, pair_sems, into, sems):
        self.place, self.pair, self.into, self.sems = place, pair, into, sems
        order = [place.rep_at(distance) for distance in range(1, place.reps)] + [place.rep]
        self.swap = PairSwap(place, parts, pair, pair_sems, order)

    def relay(self):
        p = self.place
        for distance in range(1, p.reps):
            rep = p.rep_at(distance)
            self.swap.wait(rep)
            self.pair[rep] = add_up(*self.swap.terms(rep)).astype(self.pair.dtype)
            p.send(self.pair.at[rep], self.into.at[distance], self.sems.at[0, distance], self.sems.at[1, distance],
                   p.device(rep=rep))

    def total(self):
        p = self.place
        self.swap.wait(p.rep)
        terms = self.swap.terms(p.rep)
        for distance in range(1, p.reps):
            p.arrived(self.into.at[distance], self.sems.at[1, distance])
            terms.append(self.into[distance])
        return add_up(*terms)


class LineSum:
    @staticmethod
    def scratch(depth, shape, dtype):
        return [pltpu.VMEM((depth + 1,) + shape, dtype), pltpu.SemaphoreType.DMA((4, depth))]

    def __init__(self, place, terms, out, into, sems):
        self.place, self.terms, self.out, self.into, self.sems = place, terms, out, into, sems

    def moves(self, at):
        p = self.place
        last = p.depth - 1
        for way, towards, goal, first, valid in (
            (0, p.z + 1, last - (at - p.z), p.z == 0, (at >= p.z) & (last - (at - p.z) > p.z)),
            (1, p.z - 1, at - (last - p.z), p.z == last, (at >= last - p.z) & (at - (last - p.z) < p.z)),
        ):
            goal = jnp.clip(goal, 0, last)
            slot = jnp.where(goal == towards, p.depth, goal) if way else goal
            copy = pltpu.make_async_remote_copy(
                src_ref=self.out.at[goal], dst_ref=self.into.at[slot], send_sem=self.sems.at[2 * way, goal],
                recv_sem=self.sems.at[2 * way + 1, goal], device_id=p.device(z=towards), device_id_type=MESH_ID,
            )
            yield way, goal, first, valid, copy

    def step(self, at):
        p = self.place
        for way, goal, first, valid, copy in self.moves(at):
            inner = valid & jnp.logical_not(first)
            p.arrived(self.into.at[goal], self.sems.at[2 * way + 1, goal], inner)

            def start(goal=goal):
                self.out[goal] = add_up(*self.terms(goal)).astype(self.out.dtype)

            def follow(goal=goal):
                self.out[goal] = add_up(*self.terms(goal), self.into[goal]).astype(self.out.dtype)

            when(valid & first, start)
            when(inner, follow)
            when(valid, copy.start)

    def finish(self):
        for at in range(self.place.depth - 1):
            for _, _, _, valid, copy in self.moves(at):
                when(valid, copy.wait_send)

    def total(self, result):
        result[...] = add_up(*self.terms(self.place.z))
        self.gather(result)
        self.finish()

    def gather(self, result):
        p = self.place
        for way, slot, condition in ((0, p.z, p.z > 0), (1, p.depth, p.z < p.depth - 1)):
            p.arrived(self.into.at[slot], self.sems.at[2 * way + 1, p.z], condition)

            def add(slot=slot):
                result[...] += self.into[slot].astype(F32)

            when(condition, add)


class ColumnSum:
    @staticmethod
    def scratch(depth, shape, dtype):
        return PairSwap.scratch(depth, shape, dtype) + LineSum.scratch(depth, shape, dtype)

    def __init__(self, place, parts, pair, pair_sems, into, sems, own=None):
        self.place = place
        order = [lax.rem(place.z + distance, place.depth) for distance in list(range(place.depth - 1, 0, -1)) + [0]]
        self.order = order
        self.swap = PairSwap(place, parts, pair, pair_sems, order, own)
        self.line = LineSum(place, self.swap.terms, pair, into, sems)

    def ready(self):
        for at in self.order:
            self.swap.wait(at)

    def step(self, at):
        self.line.step(at)

    def total(self, result):
        self.line.total(result)


def anywhere(count):
    return [pl.BlockSpec(memory_space=pl.ANY)] * count


def in_vmem(count):
    return [pl.BlockSpec(memory_space=pltpu.VMEM)] * count


def remote_params(identity, mebibytes=60):
    return pltpu.CompilerParams(
        collective_id=identity, has_side_effects=True, vmem_limit_bytes=mebibytes * 2**20
    )


def column_of(row_values, rows):
    return jnp.broadcast_to(row_values, (LANES, rows)).T[:, 0:1]


def row_of(column_values, rows):
    return jnp.broadcast_to(column_values, (rows, LANES)).T[0:8, :]


def forward_mixer(tokens, cotangent, own_pair, other_pair, common, small, table, out_quarters, sizes):
    reps, depth, channels, width, state, sequences, inner, convolved = sizes
    rows, model = tokens.shape
    part, side = own_pair.shape
    wide = side + common.shape[1]
    quarter = out_quarters.shape[1]
    vector_width = -(-max(piece.shape[1] for piece in small) // LANES) * LANES
    vector_rows = 16
    heads = channels // width
    per_shard = convolved // (2 * depth)

    x_scratch = [pltpu.VMEM((reps, 2, rows, model), BF16)] + PlaneGather.scratch(reps)
    w_scratch = [pltpu.VMEM((depth, 2, part, wide), BF16)] + ColumnGather.scratch(depth) * 3
    v_scratch = [pltpu.VMEM((depth, 2, vector_rows, vector_width), F32)] + ColumnGather.scratch(depth) * 2
    o_scratch = [
        pltpu.VMEM((depth, quarter, model), BF16), pltpu.VMEM((reps, quarter, model), BF16),
    ] + ColumnGather.scratch(depth) + [pltpu.SemaphoreType.DMA((2, max(reps, depth))), pltpu.SemaphoreType.DMA((2,))]
    n_scratch = [pltpu.VMEM((8, LANES), F32)] + PlaneGather.scratch(reps)
    sum_scratch = [
        pltpu.VMEM((reps, rows, model), BF16), pltpu.VMEM((reps, 2, 8, rows), F32),
    ] + PlaneSum.scratch(reps, (rows, model), BF16) + PlaneSum.scratch(reps, (8, rows), F32)
    groups = [x_scratch, w_scratch, v_scratch, o_scratch, n_scratch, sum_scratch]

    def kernel(x_ref, g_ref, own_ref, other_ref, common_ref, table_ref, quarters_ref, *refs):
        small_refs, refs = refs[: len(small)], refs[len(small) :]
        (after_ref, mixed_ref, scale_ref, lengths_ref, in_gain_ref, post_gain_ref, taps_ref, heads_ref, skip_ref,
               norm_ref, table_out, second_out, g_out, first_out, weight_out, out_out, proj_out, mixed_out), scratch = refs[:18], refs[18:]
        cut = [0]
        for group in groups:
            cut.append(cut[-1] + len(group))
        x_work, w_work, v_work, o_work, n_work, sum_work = [scratch[i:j] for i, j in zip(cut, cut[1:])]
        (second, second_sems, second_local, g_sems, g_local, proj_buffer, proj_sems, keep_sems,
         own_part, mixed_all, mixed_sems, vectors_ref) = scratch[cut[-1]:]
        p = Place(reps, depth)
        vectors_ref[...] = jnp.zeros_like(vectors_ref)
        row = 0
        for piece in small_refs:
            count, size = piece.shape
            vectors_ref[row : row + count, :size] = piece[...].astype(F32)
            row += count
        p.barrier(plane=True, column=True)

        x_all, weight_all, vectors_all = x_work[0], w_work[0], v_work[0]

        def left(core):
            return lambda z: weight_all.at[z, core, :, pl.ds(0, side)]

        def right(core):
            return lambda z: weight_all.at[z, core, :, pl.ds(side, wide - side)]

        vector_job = ColumnGather(p, vectors_ref, lambda z: vectors_all.at[z, p.core], v_work[1], v_work[2],
                                  shared=lambda z: vectors_all.at[z, 1 - p.core])
        own_slot, other_slot = left(p.core), left(1 - p.core)
        p.send(other_ref, own_slot(p.z), keep_sems.at[0], keep_sems.at[1], p.sibling())
        job_a = ColumnGather(p, own_ref, own_slot, w_work[1], w_work[2])
        job_c = ColumnGather(p, common_ref, right(p.core), w_work[3], w_work[4], shared=right(1 - p.core))
        x_job = PlaneGather(p, x_ref, x_all, x_work[1], x_work[2])
        p.arrived(other_slot(p.z), keep_sems.at[1])
        job_b = ColumnGather(p, other_slot(p.z), other_slot, w_work[5], w_work[6], keep=False)
        for distance in range(1, depth):
            vector_job.hop(distance)
        vector_job.finish()

        own_row = vectors_all[p.z, p.core].astype(F32)[11:12, :LANES]
        dealt = own_row[:, sequences : sequences + 1]
        lengths_row = jnp.zeros((1, LANES), F32)
        for z in range(depth):
            for core in range(2):
                row = vectors_all[z, core].astype(F32)[11:12, :LANES]
                lengths_row = jnp.where(dealt == float(2 * z + core), row, lengths_row)
        n_work[0][...] = jnp.broadcast_to(lengths_row, (8, LANES))
        n_job = PlaneGather(p, n_work[0], lengths_ref, n_work[1], n_work[2])

        pieces = [vectors_all[z, core].astype(F32) for z in range(depth) for core in range(2)]
        in_gain_ref[...] = jnp.concatenate([piece[0:1, :part] for piece in pieces], axis=1)
        post_gain_ref[...] = jnp.concatenate([piece[10:11, :part] for piece in pieces], axis=1)
        taps_full = jnp.concatenate([piece[0:8, :per_shard] for piece in pieces], axis=1)
        taps_full = jnp.concatenate([taps_full[1:6, :], jnp.zeros((3, convolved), F32)], axis=0)
        team = 2 * p.rep + p.core
        taps_own = taps_full[:, :channels]
        for member in range(1, 2 * reps):
            taps_own = jnp.where(team == member, taps_full[:, channels * member : channels * (member + 1)], taps_own)
        taps_ref[...] = jnp.concatenate([taps_own, taps_full[:, inner:]], axis=1)
        own = vectors_all[p.rep, p.core].astype(F32)
        lane = lax.broadcasted_iota(jnp.int32, (1, LANES), 1)
        speed = jnp.where(lane < heads, jnp.exp(jnp.where(lane < heads, own[7:8, :LANES], 0.0)), 0.0)
        heads_ref[...] = jnp.concatenate([own[6:7, :LANES], speed, jnp.zeros((6, LANES), F32)], axis=0)
        norm_ref[...] = own[9:10, :channels]
        wide_lane = lax.broadcasted_iota(jnp.int32, (1, channels), 1)
        skip = jnp.broadcast_to(own[8:9, 0:1], (1, channels))
        for head in range(1, heads):
            skip = jnp.where(wide_lane >= head * width, own[8:9, head : head + 1], skip)
        skip_ref[...] = skip

        n_job.relay()
        mid, out_all, o_sems, o_local, e_sems, e_local = o_work
        late_jobs = []
        for distance in range(1, depth):
            for job in (job_a, job_c, job_b):
                job.hop(distance)
            if distance == min(2, depth - 1):
                x_job.relay()
                late_jobs.append(ColumnGather(p, quarters_ref.at[p.rep], lambda z: mid.at[z], o_sems, o_local))
                late_jobs.append(
                    ColumnGather(p, table_ref, lambda z: table_out.at[z, p.core], v_work[3], v_work[4],
                                 shared=lambda z: table_out.at[z, 1 - p.core])
                )
        job_o, table_job = late_jobs
        job_o.keep.wait()
        job_o.keep = None
        for job in (n_job, x_job, job_a, job_b, job_c):
            job.finish()
        weight_keep = p.local(weight_all, weight_out, e_local.at[0])

        def exchange_copy(goal):
            return pltpu.make_async_remote_copy(
                src_ref=mid.at[goal], dst_ref=out_all.at[p.rep], send_sem=e_sems.at[0, goal],
                recv_sem=e_sems.at[1, p.rep], device_id=p.device(rep=goal), device_id_type=MESH_ID,
            )

        def exchange(goal, condition):
            def own():
                out_all[goal] = mid[goal]

            when(condition & (goal == p.rep), own)
            when(condition & (goal != p.rep), exchange_copy(goal).start)

        def out_tick(distance):
            if distance == 1:
                exchange(p.z, p.z >= 0)
            job_o.hop(distance)
            table_job.hop(distance)
            below, above, low, high = job_o.ends(distance)
            exchange(low, below)
            exchange(high, above)

        def out_wait():
            for rep in range(reps):
                p.arrived(out_all.at[rep], e_sems.at[1, rep], rep != p.rep)

        g_job = ColumnGather(p, g_ref, lambda z: g_out.at[z, p.core], g_sems, g_local,
                             shared=lambda z: g_out.at[z, 1 - p.core], start=False)
        p.finish()
        parts, squares = sum_work[0], sum_work[1]
        pair, pair_sems, into, into_sems = sum_work[2:6]
        s_pair, s_pair_sems, s_into, s_into_sems = sum_work[6:10]

        def swap(rep, start):
            for source, target, sems in (
                (parts.at[rep], pair, pair_sems), (squares.at[rep, 1 - p.core], s_pair, s_pair_sems)
            ):
                copy = pltpu.make_async_remote_copy(
                    src_ref=source, dst_ref=target.at[rep], send_sem=sems.at[0, rep],
                    recv_sem=sems.at[1, rep], device_id=p.sibling(), device_id_type=MESH_ID,
                )
                if start:
                    copy.start()
                else:
                    copy.wait_send()

        def onward(distance, rep, start):
            for values, target, sems in ((pair, into, into_sems), (s_pair, s_into, s_into_sems)):
                copy = pltpu.make_async_remote_copy(
                    src_ref=values.at[rep], dst_ref=target.at[distance], send_sem=sems.at[0, distance],
                    recv_sem=sems.at[1, distance], device_id=p.device(rep=rep), device_id_type=MESH_ID,
                )
                if start:
                    copy.start()
                else:
                    copy.wait_send()

        def proj_copy(slot, rep, core):
            return pltpu.make_async_copy(proj_buffer.at[slot], proj_out.at[rep, core], proj_sems.at[slot])

        def mixed_copy(at, rep, core):
            return pltpu.make_async_copy(mixed_all.at[at], mixed_out.at[rep, core], mixed_sems.at[at])

        def place_of(at):
            distance = lax.rem(at // 2 + 1, reps)
            turn = lax.rem(at, 2)
            return distance, p.rep_at(distance), turn, jnp.where(turn == 0, 1 - p.core, p.core)

        def mix(at):
            distance, rep, turn, core = place_of(at)
            x = x_all[rep, core].astype(F32)
            first = (x * rms_rows(x) * in_gain_ref[...]).astype(BF16)
            x_all[rep, core] = first
            proj = mm(first, weight_all[...].reshape(model, wide))

            @pl.when(at >= 2)
            def _():
                proj_copy(turn, rep, core).wait()

            proj_buffer[turn] = proj
            proj_copy(turn, rep, core).start()
            seg_column, seg_line = segments(lengths_ref[rep, core][0:1, :], sequences, rows)
            block = Block(proj, seg_column, seg_line, taps_ref[...], heads_ref[...], channels, width, state)
            mixed = []
            for start, stop, inside in block.groups():
                xin = block.xin[:, start:stop]
                scaled, rest = split_two(xin * block.spread(block.step, start, stop, inside))
                scaled = jnp.concatenate([scaled, scaled, rest], axis=0)
                y = None
                for head in inside:
                    weights, weights_rest = split_two(block.scores * block.decay(head))
                    term = mm(jnp.concatenate([weights, weights_rest, weights], axis=1), scaled)
                    y = term if y is None else jnp.where(block.inside(start, stop, head), term, y)
                gate = block.gate[:, start:stop]
                mixed.append((y + skip_ref[:, start:stop] * xin) * gate * jax.nn.sigmoid(gate))
            mixed = jnp.concatenate(mixed, axis=1)
            squares[rep, core] = row_of(jnp.sum(mixed * mixed, axis=1, keepdims=True), rows)
            mixed_all[at] = mixed * norm_ref[...]
            mixed_copy(at, rep, core).start()

        def put(at):
            distance, rep, turn, core = place_of(at)
            mixed, mixed_rest = split_two(mixed_all[at])
            out_weight = out_all[...].reshape(channels, model)
            part_rows = mm(mixed, out_weight) + mm(mixed_rest, out_weight)

            @pl.when(turn == 0)
            def _():
                parts[rep] = part_rows.astype(BF16)
                swap(rep, True)

            @pl.when((turn == 1) & (distance == 0))
            def _():
                own_part[...] = part_rows

            @pl.when((turn == 1) & (distance > 0))
            def _():
                p.arrived(pair.at[rep], pair_sems.at[1, rep])
                pair[rep] = add_up(part_rows, pair[rep]).astype(BF16)
                p.arrived(s_pair.at[rep], s_pair_sems.at[1, rep])
                s_pair[rep] = add_up(squares[rep, p.core], s_pair[rep])
                onward(distance, rep, True)

        delay = 4

        def visit(at, carry):
            pl.when(at < 2 * reps)(functools.partial(mix, at))
            for distance in range(1, depth):
                pl.when(at == min(distance - 1, delay - 1))(functools.partial(out_tick, distance))
            pl.when(at == delay - 1)(g_job.start)
            pl.when(at == delay)(out_wait)
            pl.when(at >= delay)(functools.partial(put, at - delay))
            pl.when(at == 2 * delay - 1)(functools.partial(g_job.hop, 1))
            return carry

        lax.fori_loop(0, 2 * reps + delay, visit, 0)
        out_keep = p.local(out_all, out_out, e_local.at[1])
        first_keep = p.local(x_all, first_out, keep_sems.at[2])
        if depth > 2:
            g_job.hop(2)
        p.arrived(pair.at[p.rep], pair_sems.at[1, p.rep])
        p.arrived(s_pair.at[p.rep], s_pair_sems.at[1, p.rep])
        terms, square_terms = [own_part[...], pair[p.rep]], [squares[p.rep, p.core], s_pair[p.rep]]
        for distance in range(1, reps):
            p.arrived(s_into.at[distance], s_into_sems.at[1, distance])
            square_terms.append(s_into[distance])
            p.arrived(into.at[distance], into_sems.at[1, distance])
            terms.append(into[distance])
        scale_row = lax.rsqrt(add_up(*square_terms) / inner + EPS)
        scale_ref[...] = scale_row
        mixed = column_of(scale_row[0:1, :], rows) * add_up(*terms)
        mixed_ref[...] = mixed.astype(BF16)
        after = x_ref[...].astype(F32) + mixed
        after_ref[...] = after
        second[...] = (after * rms_rows(after) * post_gain_ref[...]).astype(BF16)
        job = ColumnGather(p, second, lambda z: second_out.at[z, p.core], second_sems, second_local,
                           shared=lambda z: second_out.at[z, 1 - p.core])
        for distance in range(3, depth):
            g_job.hop(distance)
        for distance in range(1, depth):
            job.hop(distance)
        job.finish()
        g_job.finish()
        for distance in range(reps):
            rep = p.rep_at(distance) if distance else p.rep
            swap(rep, False)
            if distance:
                onward(distance, rep, False)
        for slot in range(2):
            proj_copy(slot, p.rep, p.core).wait()
        for at in range(2 * reps):
            mixed_copy(at, p.rep, p.core).wait()
        job_o.finish()
        table_job.finish()
        for goal in range(depth):
            when(goal != p.rep, exchange_copy(goal).wait_send)
        for keep in (weight_keep, out_keep, first_keep):
            keep.wait()
        p.finish()

    return pl.pallas_call(
        kernel,
        in_specs=in_vmem(1) + anywhere(6) + in_vmem(len(small)),
        out_specs=in_vmem(10) + anywhere(8),
        out_shape=[
            jax.ShapeDtypeStruct((rows, model), F32),
            jax.ShapeDtypeStruct((rows, model), BF16),
            jax.ShapeDtypeStruct((8, rows), F32),
            jax.ShapeDtypeStruct((reps, 2, 8, LANES), F32),
            jax.ShapeDtypeStruct((1, model), F32),
            jax.ShapeDtypeStruct((1, model), F32),
            jax.ShapeDtypeStruct((8, channels + 2 * state), F32),
            jax.ShapeDtypeStruct((8, LANES), F32),
            jax.ShapeDtypeStruct((1, channels), F32),
            jax.ShapeDtypeStruct((1, channels), F32),
            jax.ShapeDtypeStruct((depth, 2) + table.shape, BF16),
            jax.ShapeDtypeStruct((depth, 2, rows, model), BF16),
            jax.ShapeDtypeStruct((depth, 2, rows, model), BF16),
            jax.ShapeDtypeStruct((reps, 2, rows, model), BF16),
            jax.ShapeDtypeStruct((depth, 2, part, wide), BF16),
            jax.ShapeDtypeStruct((reps, quarter, model), BF16),
            jax.ShapeDtypeStruct((reps, 2, rows, wide), F32),
            jax.ShapeDtypeStruct((reps, 2, rows, channels), F32),
        ],
        scratch_shapes=[item for group in groups for item in group]
        + [pltpu.VMEM((rows, model), BF16)]
        + ColumnGather.scratch(depth) * 2
        + [pltpu.VMEM((2, rows, wide), F32), pltpu.SemaphoreType.DMA((2,)), pltpu.SemaphoreType.DMA((3,)),
           pltpu.VMEM((rows, model), F32), pltpu.VMEM((2 * reps, rows, channels), F32),
           pltpu.SemaphoreType.DMA((2 * reps,)), pltpu.VMEM((vector_rows, vector_width), F32)],
        compiler_params=remote_params(0),
        name="forward_mixer",
    )(tokens, cotangent, own_pair, other_pair, common, table, out_quarters, *small)


def join_experts(
    own, gates, dots, hidden, shared_grad, router_t, shared_in, shared_out, cotangent, after, mixed, scale, post_gain,
    back, weighted, second, inner, reps, depth, capacity,
):
    rows, model = cotangent.shape
    local = own.shape[1]
    experts = gates.shape[1]
    half_rows = rows // 2
    stack = (rows, model)
    halves = (slice(0, half_rows), slice(half_rows, rows))
    groups = {
        "stream": [
            pltpu.VMEM((2, local, capacity, model), BF16), pltpu.SemaphoreType.DMA((2,)),
            pltpu.VMEM((2,) + stack, BF16), pltpu.SemaphoreType.DMA((2,)),
        ],
        "parts": [
            pltpu.VMEM((2,) + stack, BF16), pltpu.VMEM(stack, F32), pltpu.VMEM((depth, 2, half_rows, model), BF16),
            pltpu.SemaphoreType.DMA((2, depth)),
        ],
        "line": LineSum.scratch(depth, (half_rows, model), BF16) * 2,
        "low": [pltpu.VMEM((2, half_rows, model), BF16), pltpu.VMEM((2, 8, rows), F32)] + PlaneGather.scratch(reps) * 3,
        "logits": [pltpu.VMEM((2 * depth, 2 * experts, rows), BF16), pltpu.VMEM((2,) + stack, BF16),
                   pltpu.SemaphoreType.DMA((2,))],
    }

    def kernel(own_ref, gates_ref, dots_ref, hidden_ref, shared_ref, router_ref, in_ref, out_ref, g_ref, after_ref,
               mixed_ref, scale_ref, gain_ref, back_ref, weighted_ref, second_ref,
               grad_ref, gain_grad_ref, router_grad_ref, layer_out, low_out, scale_out, *scratch):
        work, cut = {}, 0
        for name, items in groups.items():
            work[name] = scratch[cut : cut + len(items)]
            cut += len(items)
        p = Place(reps, depth)
        slots, slot_sems, second_slots, second_sems = work["stream"]
        parts, own_part, pair, pair_sems = work["parts"]
        logits_all, layer_slots, layer_sems = work["logits"]
        lower = p.z < depth // 2

        def goal_at(index):
            distance = lax.rem(depth - 1 - index + depth, depth)
            return jnp.where(lower, lax.rem(p.z + distance, depth), lax.rem(p.z - distance + depth, depth))

        def block_at(at):
            return goal_at(at // 2), jnp.where(lax.rem(at, 2) == 0, 1 - p.core, p.core)

        def load(source, at):
            goal, core = block_at(at)
            start = pl.multiple_of((2 * goal + core) * capacity, capacity)
            return pltpu.make_async_copy(
                source.at[:, pl.ds(start, capacity)], slots.at[lax.rem(at, 2)], slot_sems.at[lax.rem(at, 2)]
            )

        def swap(goal, slot, start):
            for at, piece in enumerate(halves):
                copy = pltpu.make_async_remote_copy(
                    src_ref=parts.at[slot, pl.ds(half_rows * at, half_rows)], dst_ref=pair.at[goal, at],
                    send_sem=pair_sems.at[0, goal] if at == 0 else pair_sems_late.at[0, goal],
                    recv_sem=pair_sems.at[1, goal] if at == 0 else pair_sems_late.at[1, goal],
                    device_id=p.sibling(), device_id_type=MESH_ID,
                )
                copy.start() if start else copy.wait_send()

        pair_sems_late = work["late"][0]
        load(back_ref, 0).start()
        p.barrier(plane=True, column=True)
        expert = lax.broadcasted_iota(jnp.int32, (experts, rows), 0)
        shard = 2 * p.z + p.core

        def matches(q):
            table = own_ref[q].astype(F32)
            return [slot_match(table[i : i + 1, :], capacity, rows) for i in range(local)]

        def visit(at, carry):
            goal, core = block_at(at)
            q = 2 * goal + core
            turn = lax.rem(at, 2)
            load(back_ref, at).wait()

            @pl.when(at + 1 < 2 * depth)
            def _():
                load(back_ref, at + 1).start()

            start = pl.multiple_of(q * rows, rows)
            gates = gates_ref[q]
            gate_grad = jnp.zeros_like(gates)
            total = mm_nt(shared_ref[pl.ds(start, rows), :], in_ref[...])
            for i, match in enumerate(matches(q)):
                total = total + mm_tn(match.astype(BF16), slots[turn, i])
                dot = dots_ref[i, pl.ds(pl.multiple_of(q * capacity, capacity), capacity), 0:1]
                row = jnp.sum(jnp.where(match, dot, 0.0), axis=0, keepdims=True)
                gate_grad = jnp.where(expert == local * shard + i, row, gate_grad)
            logit_grad = gates * (gate_grad - jnp.sum(gates * gate_grad, axis=0, keepdims=True))
            logit_pair = jnp.concatenate(split_two(logit_grad), axis=0)
            logits_all[q] = logit_pair
            total = total + mm_tn(logit_pair, jnp.concatenate([router_ref[...], router_ref[...]], axis=0))

            @pl.when(turn == 0)
            def _():
                slot = lax.rem(at // 2, 2)

                @pl.when(at >= 4)
                def _():
                    swap(goal_at(at // 2 - 2), slot, False)

                parts[slot] = total.astype(BF16)
                swap(goal, slot, True)

            @pl.when(turn == 1)
            def _():
                p.arrived(pair.at[goal, 0], pair_sems.at[1, goal])
                p.arrived(pair.at[goal, 1], pair_sems_late.at[1, goal])

                @pl.when(goal == p.z)
                def _():
                    for index, piece in enumerate(halves):
                        own_part[piece, :] = add_up(total[piece, :], pair[goal, index])

                @pl.when(goal != p.z)
                def _():
                    for index, piece in enumerate(halves):
                        pair[goal, index] = add_up(total[piece, :], pair[goal, index]).astype(BF16)

            return carry

        lines = []
        for index in range(2):
            view = pair.at[:, index]
            into, sems = work["line"][2 * index : 2 * index + 2]

            def terms(goal, view=view, index=index):
                return [view[goal]]

            lines.append(LineSum(p, terms, view, into, sems))

        for step in range(depth - 1):
            lax.fori_loop(2 * step, 2 * step + 2, visit, 0)
            lines[0].step(step)
        for step in range(depth - 1):
            lines[1].step(step)
        lax.fori_loop(2 * depth - 2, 2 * depth, visit, 0)

        low, scales = work["low"][:2]
        gather_sems = work["low"][2:]
        gain_grad_ref[...] = jnp.zeros_like(gain_grad_ref)
        row_dots = []

        def norm_back(index):
            piece = halves[index]
            into = lines[index].into
            grad_ref[piece, :] = own_part[piece, :]
            lines[index].gather(grad_ref.at[pl.ds(half_rows * index, half_rows)])
            second_grad = grad_ref[piece, :]
            after_rows = after_ref[piece, :]
            after_scale = rms_rows(after_rows)
            gain_grad_ref[...] += jnp.sum(after_rows * second_grad * after_scale, axis=0, keepdims=True)
            weighted = second_grad * gain_ref[...]
            after_grad = (
                g_ref[piece, :].astype(F32)
                + after_scale * weighted
                - after_rows * after_scale**3 * jnp.mean(after_rows * weighted, axis=1, keepdims=True)
            )
            grad_ref[piece, :] = after_grad
            after_low = after_grad.astype(BF16)
            low[index] = after_low
            row_dots.append(
                jnp.sum(after_low.astype(F32) * mixed_ref[piece, :].astype(F32), axis=1, keepdims=True)
            )
            return PlaneGather(p, low.at[index], low_out.at[:, :, pl.ds(half_rows * index, half_rows)],
                               *gather_sems[2 * index : 2 * index + 2])

        first_job = norm_back(0)

        def layer_load(at):
            q = block_at(at)
            start = pl.multiple_of((2 * q[0] + q[1]) * rows, rows)
            return pltpu.make_async_copy(
                second_ref.at[pl.ds(start, rows)], second_slots.at[lax.rem(at, 2)], second_sems.at[lax.rem(at, 2)]
            )

        def layer_store(at):
            goal, core = block_at(at)
            return pltpu.make_async_copy(
                layer_slots.at[lax.rem(at, 2)], layer_out.at[goal, core], layer_sems.at[lax.rem(at, 2)]
            )

        def layer_visit(at, carry):
            goal, core = block_at(at)
            q = 2 * goal + core
            turn = lax.rem(at, 2)
            load(weighted_ref, at).wait()
            layer_load(at).wait()

            @pl.when(at + 1 < 2 * depth)
            def _():
                load(weighted_ref, at + 1).start()
                layer_load(at + 1).start()

            total = mm(hidden_ref[pl.ds(pl.multiple_of(q * rows, rows), rows), :], out_ref[...])
            for i, match in enumerate(matches(q)):
                total = total + mm_tn(match.astype(BF16), slots[turn, i])

            @pl.when(at >= 2)
            def _():
                layer_store(at).wait()

            layer_slots[turn] = total.astype(BF16)
            layer_store(at).start()
            both = mm(logits_all[q], second_slots[turn])
            router_grad_ref[...] += both[:experts, :] + both[experts:, :]
            return carry

        router_grad_ref[...] = jnp.zeros_like(router_grad_ref)
        load(weighted_ref, 0).start()
        layer_load(0).start()
        lax.fori_loop(0, depth, layer_visit, 0)
        first_job.relay()
        second_job = norm_back(1)
        dot_row = row_of(jnp.concatenate(row_dots, axis=0), rows)
        scale_row = scale_ref[...]
        scales[0] = scale_row
        scales[1] = scale_row**2 * dot_row / inner
        scale_job = PlaneGather(p, scales, scale_out, *gather_sems[4:6])
        lax.fori_loop(depth, 2 * depth, layer_visit, 0)
        scale_job.relay()
        second_job.relay()
        for job in (first_job, scale_job, second_job):
            job.finish()
        for slot in range(2):
            layer_store(slot).wait()
        for at in range(max(depth - 2, 0), depth):
            swap(goal_at(at), at % 2, False)
        for line in lines:
            line.finish()
        p.finish()

    groups["late"] = [pltpu.SemaphoreType.DMA((2, depth))]
    group = 2 * depth
    return pl.pallas_call(
        kernel,
        in_specs=in_vmem(13) + anywhere(3),
        out_specs=in_vmem(3) + anywhere(3),
        out_shape=[
            jax.ShapeDtypeStruct((rows, model), F32),
            jax.ShapeDtypeStruct((1, model), F32),
            jax.ShapeDtypeStruct((experts, model), F32),
            jax.ShapeDtypeStruct((depth, 2, rows, model), BF16),
            jax.ShapeDtypeStruct((reps, 2, rows, model), BF16),
            jax.ShapeDtypeStruct((reps, 2, 2, 8, rows), F32),
        ],
        scratch_shapes=[item for items in groups.values() for item in items],
        compiler_params=remote_params(2),
        name="join_experts",
    )(
        own, gates, dots, hidden, shared_grad, router_t, shared_in, shared_out, cotangent, after, mixed, scale,
        post_gain, back, weighted, second,
    )


def backward_mixer(
    scales, after, after_grad, tokens, in_gain, post_grad, router_parts, lengths, taps, head_rows, skip, norm, weight,
    out_weight, low, layer_parts, first, proj, gained, sizes,
):
    reps, depth, channels, width, state, sequences, inner, convolved = sizes
    rows, model = tokens.shape
    part = model // (2 * depth)
    wide = weight.shape[1]
    side = 2 * channels
    heads = channels // width
    per_shard = convolved // (2 * depth)
    quarter = channels // reps
    experts, router_width = router_parts.shape[2:]
    small_width = -(-max(per_shard, channels, router_width) // LANES) * LANES
    small_shape = (16 + experts, small_width)
    stack = (rows, model)
    groups = {
        "early": [pltpu.VMEM((2, rows, channels), F32), pltpu.SemaphoreType.DMA((2,))],
        "layer": [pltpu.SemaphoreType.DMA((1,))]
        + ColumnSum.scratch(depth, stack, BF16),
        "stream": [
            pltpu.VMEM(stack, BF16), pltpu.VMEM((2, rows, wide), F32), pltpu.VMEM((2,) + stack, BF16),
            pltpu.SemaphoreType.DMA((3, 2)),
        ],
        "sum": [
            pltpu.VMEM((2,) + stack, BF16), pltpu.VMEM(stack, F32),
            pltpu.VMEM((reps,) + stack, BF16), pltpu.SemaphoreType.DMA((2, reps)),
            pltpu.VMEM((reps - 1,) + stack, BF16), pltpu.SemaphoreType.DMA((2, reps)),
        ],
        "grads": [
            pltpu.VMEM((depth, 2, part, wide), F32), pltpu.VMEM((channels, model), F32),
            pltpu.VMEM((8, channels + 2 * state), F32), pltpu.VMEM((8, LANES), F32), pltpu.VMEM((8, channels), F32),
        ],
        "side": LineSum.scratch(depth, (2, part, channels), BF16) * 2
        + [pltpu.VMEM((2, 2, part, channels), BF16), pltpu.VMEM((2, part, channels), BF16),
           pltpu.SemaphoreType.DMA((2, 2))],
        "common": [pltpu.VMEM((depth, 2, part, wide - side), BF16)]
        + ColumnSum.scratch(depth, (part, wide - side), BF16)
        + [pltpu.VMEM((part, wide - side), F32), pltpu.VMEM((part, wide - side), BF16)],
        "out": [
            pltpu.VMEM((reps, quarter, model), BF16), pltpu.VMEM((reps, quarter, model), BF16),
            pltpu.SemaphoreType.DMA((2, reps)),
        ] + LineSum.scratch(depth, (quarter, model), BF16)
        + [pltpu.VMEM((quarter, model), BF16)],
        "small": [pltpu.VMEM((depth, 2) + small_shape, F32)] + ColumnSum.scratch(depth, small_shape, F32)
        + [pltpu.VMEM(small_shape, F32), pltpu.VMEM((reps,) + small_shape, F32)],
        "end": [pltpu.SemaphoreType.DMA((2, 5, reps)), pltpu.SemaphoreType.DMA((6,)), pltpu.VMEM((2, 32, model), F32)],
    }

    def kernel(scales_ref, after_ref, grad_ref, x_ref, gain_ref, post_grad_ref, router_ref, lengths_ref, taps_ref,
               heads_ref, skip_ref, norm_ref, weight_ref, out_ref, low_ref, layer_ref, first_ref, proj_ref, gained_ref,
               layer_out_ref, tokens_grad_ref, side_out, common_out, out_out, small_out, *scratch):
        work, cut = {}, 0
        for name, items in groups.items():
            work[name] = scratch[cut : cut + len(items)]
            cut += len(items)
        p = Place(reps, depth)
        first_slot, proj_slots, low_slots, stream_sems = work["stream"]
        gained_slots, gained_sems = work["early"]

        def first_load(rep, core):
            return pltpu.make_async_copy(first_ref.at[rep, core], first_slot, stream_sems.at[0, 0])

        def proj_load(slot, rep, core):
            return pltpu.make_async_copy(proj_ref.at[rep, core], proj_slots.at[slot], stream_sems.at[1, slot])

        def low_load(slot, rep, core):
            return pltpu.make_async_copy(low_ref.at[rep, core], low_slots.at[slot], stream_sems.at[2, slot])

        def gained_load(slot, rep, core):
            return pltpu.make_async_copy(gained_ref.at[rep, core], gained_slots.at[slot], gained_sems.at[slot])

        def early_place(at):
            return at // 2, lax.rem(at, 2)

        for at in range(2):
            gained_load(at, *early_place(at)).start()
            low_load(at, *early_place(at)).start()
        proj_load(0, p.rep_at(1), 1 - p.core).start()
        proj_load(1, p.rep_at(1), p.core).start()
        p.barrier(plane=True, column=True)
        layer_job = ColumnSum(p, layer_ref, *work["layer"][1:], own=(first_slot, work["layer"][0]))
        in_total, out_total, taps_total, heads_total, wide_total = work["grads"]
        for total in work["grads"]:
            total[...] = jnp.zeros_like(total)

        def early(at, carry):
            rep, core = early_place(at)
            turn = lax.rem(at, 2)
            gained_load(turn, rep, core).wait()
            low_load(turn, rep, core).wait()
            scale = column_of(scales_ref[rep, core, 0][0:1, :], rows)
            out_total[...] += mm_tn((gained_slots[turn] * scale).astype(BF16), low_slots[turn])

            @pl.when(at + 2 < 2 * reps)
            def _():
                gained_load(turn, *early_place(at + 2)).start()
                low_load(turn, *early_place(at + 2)).start()

            return carry

        lax.fori_loop(0, 2 * reps, early, 0)
        low_load(0, p.rep_at(1), 1 - p.core).start()
        low_load(1, p.rep_at(1), p.core).start()
        out_parts, out_mid, out_sems, out_into, out_line_sems, out_low = work["out"]
        out_line_total = out_total.at[pl.ds(0, quarter)]
        out_parts[...] = out_total[...].astype(BF16).reshape(reps, quarter, model)
        for distance in range(1, reps):
            rep = p.rep_at(distance)
            p.send(out_parts.at[rep], out_mid.at[p.rep], out_sems.at[0, distance], out_sems.at[1, distance],
                   p.device(rep=rep))
        out_mid[p.rep] = out_parts[p.rep]
        out_job = LineSum(p, lambda at: [out_mid[at]], out_into, out_into, out_line_sems)
        layer_job.ready()
        layer_job.step(0)

        parts, own_part, pair, pair_sems, into, into_sems = work["sum"]

        def swap(distance, rep, start):
            copy = pltpu.make_async_remote_copy(
                src_ref=parts.at[lax.rem(distance, 2)], dst_ref=pair.at[rep], send_sem=pair_sems.at[0, rep],
                recv_sem=pair_sems.at[1, rep], device_id=p.sibling(), device_id_type=MESH_ID,
            )
            copy.start() if start else copy.wait_send()

        def onward(distance, rep, start):
            copy = pltpu.make_async_remote_copy(
                src_ref=pair.at[rep], dst_ref=into.at[distance - 1], send_sem=into_sems.at[0, distance],
                recv_sem=into_sems.at[1, distance], device_id=p.device(rep=rep), device_id_type=MESH_ID,
            )
            copy.start() if start else copy.wait_send()

        def visit(at, carry):
            distance, turn = lax.rem(at // 2 + 1, reps), lax.rem(at, 2)
            rep = p.rep_at(distance)
            core = jnp.where(turn == 0, 1 - p.core, p.core)
            first_load(rep, core).start()
            low_load(turn, rep, core).wait()
            proj_load(turn, rep, core).wait()
            scale = column_of(scales_ref[rep, core, 0][0:1, :], rows)
            pull = column_of(scales_ref[rep, core, 1][0:1, :], rows)
            seg_column, seg_line = segments(lengths_ref[rep, core][0:1, :], sequences, rows)
            block = Block(
                proj_slots[turn], seg_column, seg_line, taps_ref[...], heads_ref[...], channels, width, state
            )
            low_rows = low_slots[turn]
            proj_grad, tap_grads, head_grads, wide_grads = block_back(
                block, low_rows, scale, pull, taps_ref, skip_ref, norm_ref, weight_ref, out_ref[...]
            )
            taps_total[0:5, :] += tap_grads
            heads_total[0:1, :] += head_grads[0]
            heads_total[1:2, :] += head_grads[1]
            wide_total[0:2, :] += wide_grads
            part_rows = mm_nt(proj_grad, weight_ref[...])

            @pl.when(turn == 0)
            def _():
                @pl.when(at >= 4)
                def _():
                    swap(at // 2 - 1, p.rep_at(at // 2 - 1), False)

                parts[lax.rem(distance, 2)] = part_rows.astype(BF16)
                swap(distance, rep, True)

            @pl.when((turn == 1) & (distance == 0))
            def _():
                own_part[...] = part_rows

            @pl.when((turn == 1) & (distance > 0))
            def _():
                p.arrived(pair.at[rep], pair_sems.at[1, rep])
                pair[rep] = add_up(part_rows, pair[rep]).astype(BF16)
                onward(distance, rep, True)

            first_load(rep, core).wait()
            for z in range(depth):
                columns = first_slot[:, 2 * part * z : 2 * part * (z + 1)]
                for start in range(0, wide, 384):
                    piece = slice(start, min(start + 384, wide))
                    in_total[z, :, :, piece] += mm_tn(columns, proj_grad[:, piece]).reshape(2, part, -1)

            @pl.when(at < 2 * reps - 2)
            def _():
                later = p.rep_at(lax.rem(at // 2 + 2, reps))
                proj_load(turn, later, core).start()
                low_load(turn, later, core).start()

            def out_start():
                for distance in range(1, reps):
                    p.arrived(out_mid.at[p.rep_at(distance)], out_sems.at[1, distance])
                out_job.step(0)

            pl.when(at == 1)(out_start)
            for step in range(1, depth - 1):
                pl.when(at == 2 * step)(functools.partial(layer_job.step, step))
                pl.when(at == 2 * step + 1)(functools.partial(out_job.step, step))
            return carry

        lax.fori_loop(0, 2 * reps, visit, 0)

        common_parts = work["common"][0]
        common_parts[...] = in_total[:, :, :, side:].astype(BF16)
        common_job = ColumnSum(p, common_parts, *work["common"][1:5])
        side_jobs = []
        for kind in range(2):
            columns = slice(kind * channels, (kind + 1) * channels)
            side_into, side_sems = work["side"][2 * kind : 2 * kind + 2]

            def terms(at, columns=columns):
                return [in_total[at, :, :, columns]]

            side_jobs.append(LineSum(p, terms, side_into, side_into, side_sems))
        side_pair, side_away, side_swap = work["side"][4:]
        side_total = gained_slots.at[:, pl.ds(0, part)]
        side_jobs[0].step(0)

        end_sems, keep_sems, late = work["end"]

        def late_load(source, chunk):
            return pltpu.make_async_copy(
                source.at[pl.ds(32 * chunk, 32)], late.at[chunk % 2], keep_sems.at[3 + chunk % 2]
            )

        late_load(grad_ref, 0).start()
        p.arrived(pair.at[p.rep], pair_sems.at[1, p.rep])
        common_job.ready()
        common_job.step(0)
        side_jobs[1].step(0)
        for distance in range(1, reps):
            p.arrived(into.at[distance - 1], into_sems.at[1, distance])
        gain_grad = jnp.zeros((1, model), F32)
        for start in range(0, rows, 32):
            piece = slice(start, start + 32)
            if start + 32 < rows:
                late_load(grad_ref, start // 32 + 1).start()
            late_load(grad_ref, start // 32).wait()
            first_grad = add_up(
                own_part[piece, :], pair[p.rep, piece, :], *[into[at, piece, :] for at in range(reps - 1)]
            )
            x = x_ref[piece, :].astype(F32)
            x_scale = rms_rows(x)
            gain_grad = gain_grad + jnp.sum(x * first_grad * x_scale, axis=0, keepdims=True)
            weighted = first_grad * gain_ref[...]
            tokens_grad_ref[piece, :] = (
                late[start // 32 % 2]
                + x_scale * weighted
                - x * x_scale**3 * jnp.mean(x * weighted, axis=1, keepdims=True)
            ).astype(BF16)

        small = work["small"][0]
        small[...] = jnp.zeros_like(small)
        team = 2 * p.rep + p.core
        own_taps = taps_total[:, :channels]
        blank = jnp.zeros_like(own_taps)
        taps_full = jnp.concatenate(
            [jnp.where(team == member, own_taps, blank) for member in range(2 * reps)] + [taps_total[:, channels:]],
            axis=1,
        )
        for z in range(depth):
            for core in range(2):
                shard = 2 * z + core
                small[z, core, 0:8, 0:per_shard] = taps_full[:, per_shard * shard : per_shard * (shard + 1)]
                small[z, core, 12:13, 0:part] = post_grad_ref[:, part * shard : part * (shard + 1)]
                small[z, core, 13:14, 0:part] = gain_grad[:, part * shard : part * (shard + 1)]
                small[z, core, 16 : 16 + experts, 0:router_width] = router_ref[z, core]
        lane = lax.broadcasted_iota(jnp.int32, (1, LANES), 1)
        skip_row = jnp.zeros((1, LANES), F32)
        for head in range(heads):
            value = jnp.sum(wide_total[1:2, head * width : (head + 1) * width], axis=1, keepdims=True)
            skip_row = jnp.where(lane == head, value, skip_row)
        small[p.rep, p.core, 8:10, 0:LANES] = heads_total[0:2, :]
        small[p.rep, p.core, 10:11, 0:LANES] = skip_row
        small[p.rep, p.core, 11:12, 0:channels] = wide_total[0:1, :]
        small_job = ColumnSum(p, small, *work["small"][1:5])
        small_job.ready()
        small_job.step(0)
        for at in range(1, depth - 1):
            for job in (common_job, side_jobs[0], small_job):
                job.step(at)

        def to_reps(source, target, at):
            for distance in range(1, reps):
                p.send(source, target.at[p.rep], end_sems.at[0, at, distance], end_sems.at[1, at, distance],
                       p.device(rep=p.rep_at(distance)))

        def from_reps(target, at):
            for distance in range(1, reps):
                p.arrived(target.at[p.rep_at(distance)], end_sems.at[1, at, distance])

        def side_finish(kind):
            side_jobs[kind].total(side_total)
            side_pair[kind, p.core] = side_total[p.core].astype(BF16)
            side_away[kind] = side_total[1 - p.core].astype(BF16)
            p.send(side_away.at[kind], side_pair.at[kind, p.core], side_swap.at[0, kind], side_swap.at[1, kind],
                   p.sibling())
            p.arrived(side_pair.at[kind, 1 - p.core], side_swap.at[1, kind])
            to_reps(side_pair.at[kind], side_out.at[kind], kind)
            return p.local(side_pair.at[kind], side_out.at[kind, p.rep], keep_sems.at[kind])

        keeps = [side_finish(0)]
        common_total, common_low = work["common"][5:]
        common_job.total(common_total)
        common_low[...] = common_total[...].astype(BF16)
        to_reps(common_low, common_out, 2)
        keeps.append(p.local(common_low, common_out.at[p.rep], keep_sems.at[2]))
        out_job.total(out_line_total)
        out_low[...] = out_line_total[...].astype(BF16)
        to_reps(out_low, out_out, 3)
        keeps.append(p.local(out_low, out_out.at[p.rep], keep_sems.at[5]))
        small_total, small_all = work["small"][5:]
        small_job.total(small_total)
        small_all[p.rep] = small_total[...]
        to_reps(small_total, small_all, 4)
        for at in range(1, depth - 1):
            side_jobs[1].step(at)
        keeps.append(side_finish(1))

        late_load(after_ref, 0).start()
        layer_job.total(own_part)
        for chunk in range(rows // 32):
            piece = slice(32 * chunk, 32 * chunk + 32)
            if chunk + 1 < rows // 32:
                late_load(after_ref, chunk + 1).start()
            late_load(after_ref, chunk).wait()
            layer_out_ref[piece, :] = (own_part[piece, :] + late[chunk % 2]).astype(BF16)
        from_reps(small_all, 4)
        small_out[...] = add_up(*[small_all[at] for at in range(reps)])
        for at, target in ((0, side_out.at[0]), (1, side_out.at[1]), (2, common_out), (3, out_out)):
            from_reps(target, at)
        for keep in keeps:
            keep.wait()
        for distance in range(reps):
            rep = p.rep_at(distance)
            if distance in (0, reps - 1):
                swap(distance, rep, False)
            if distance:
                onward(distance, rep, False)
        p.finish()

    return pl.pallas_call(
        kernel,
        in_specs=in_vmem(1) + anywhere(2) + in_vmem(11) + anywhere(5),
        out_specs=in_vmem(2) + anywhere(3) + in_vmem(1),
        out_shape=[
            jax.ShapeDtypeStruct((rows, model), BF16),
            jax.ShapeDtypeStruct((rows, model), BF16),
            jax.ShapeDtypeStruct((2, reps, 2, part, channels), BF16),
            jax.ShapeDtypeStruct((reps, part, wide - side), BF16),
            jax.ShapeDtypeStruct((reps, quarter, model), BF16),
            jax.ShapeDtypeStruct(small_shape, F32),
        ],
        scratch_shapes=[item for items in groups.values() for item in items],
        compiler_params=remote_params(3, 63),
        name="backward_mixer",
    )(
        scales, after, after_grad, tokens, in_gain, post_grad, router_parts, lengths, taps, head_rows, skip, norm,
        weight, out_weight, low, layer_parts, first, proj, gained,
    )


def assemble_kernel(
    channels, state, heads, side_ref, common_ref, out_ref, small_ref, in_grad_ref, out_grad_ref, *small_refs
):
    reps = side_ref.shape[1]
    inner = 2 * reps * channels
    for kind in range(2):
        for rep in range(reps):
            for core in range(2):
                at = kind * inner + (2 * rep + core) * channels
                in_grad_ref[:, at : at + channels] = side_ref[kind, rep, core].astype(F32)
    in_grad_ref[:, 2 * inner : 2 * inner + 2 * state] = add_up(
        *[common_ref[rep, :, : 2 * state] for rep in range(reps)]
    )
    start = 2 * inner + 2 * state
    tail = []
    for rep in range(reps):
        pair = common_ref[rep, :, 2 * state :].astype(F32)
        tail += [pair[:, :heads], pair[:, LANES // 2 : LANES // 2 + heads]]
    in_grad_ref[:, start:] = jnp.concatenate(tail, axis=1)
    out_grad_ref[...] = out_ref[...].astype(F32).reshape(out_grad_ref.shape)
    router_grad_ref = small_refs[-1]
    for ref, row in zip(small_refs[:-1], (0, 4, 8, 9, 10, 11, 12, 13)):
        ref[...] = small_ref[row : row + ref.shape[0], : ref.shape[1]]
    part, experts = router_grad_ref.shape
    wide = -(-part // LANES) * LANES
    router = jnp.concatenate([small_ref[16:, :wide], jnp.zeros((LANES - experts, wide), F32)], axis=0)
    router_grad_ref[...] = router.T[:part, :experts]


def assemble(side, common, out_rows, small, small_shapes, channels, state, heads):
    reps, part = side.shape[1], side.shape[3]
    columns = 4 * reps * channels + 2 * state + 2 * reps * heads
    model = out_rows.shape[2]
    return pl.pallas_call(
        functools.partial(assemble_kernel, channels, state, heads),
        in_specs=in_vmem(4),
        out_specs=in_vmem(2 + len(small_shapes)),
        out_shape=[
            jax.ShapeDtypeStruct((part, columns), F32),
            jax.ShapeDtypeStruct((channels, model), F32),
        ] + [jax.ShapeDtypeStruct(shape, F32) for shape in small_shapes],
        compiler_params=pltpu.CompilerParams(vmem_limit_bytes=48 * 2**20),
        name="assemble",
    )(side, common, out_rows, small)


def slot_match(table_row, capacity, rows):
    slot = lax.broadcasted_iota(jnp.int32, (capacity, rows), 0).astype(F32) + 1.0
    return table_row == slot


def dispatch_kernel(
    local, capacity, half,
    table_ref, own_ref, second_ref, g_ref, router_ref, in_ref, out_ref,
    buffer_ref, slot_g_ref, gate_slot_ref, gates_ref, hidden_ref, grad_ref, in_grad_ref, out_grad_ref,
    in_total, out_total,
):
    at = pl.program_id(0)
    second, g = second_ref[...], g_ref[...]
    rows = second.shape[0]
    table = table_ref[...].astype(F32)
    used = table > 0.0
    logits = mm_nt(router_ref[...], second)
    top = jnp.max(jnp.where(used, logits, -jnp.inf), axis=0, keepdims=True)
    raw = jnp.where(used, jnp.exp(jnp.where(used, logits - top, 0.0)), 0.0)
    gates = raw / jnp.sum(raw, axis=0, keepdims=True)
    gates_ref[...] = gates
    expert = lax.broadcasted_iota(jnp.int32, gates.shape, 0)
    shard = 2 * lax.axis_index("z") + lax.axis_index("core")
    for i in range(local):
        match = slot_match(own_ref[i : i + 1, :].astype(F32), capacity, rows)
        onehot = match.astype(BF16)
        buffer_ref[i] = mm(onehot, second).astype(BF16)
        slot_g_ref[i] = mm(onehot, g).astype(BF16)
        gate_row = jnp.sum(jnp.where(expert == local * shard + i, gates, 0.0), axis=0, keepdims=True)
        gate_slot = jnp.sum(jnp.where(match, gate_row, 0.0), axis=1, keepdims=True)
        gate_slot_ref[i] = jnp.broadcast_to(gate_slot, (capacity, LANES))
    pre = mm(second, in_ref[...])
    a, b = pre[:, :half], pre[:, half:]
    sig = jax.nn.sigmoid(a)
    hidden = (a * sig * b).astype(BF16)
    hidden_ref[...] = hidden
    back = mm_nt(g, out_ref[...])
    grad = jnp.concatenate([back * b * silu_slope(a, sig), back * a * sig], axis=1).astype(BF16)
    grad_ref[...] = grad

    @pl.when(at == 0)
    def _():
        in_total[...] = jnp.zeros_like(in_total)
        out_total[...] = jnp.zeros_like(out_total)

    in_total[...] += mm_tn(second, grad)
    out_total[...] += mm_tn(hidden, g)

    @pl.when(at == pl.num_programs(0) - 1)
    def _():
        in_grad_ref[...] = in_total[...].astype(BF16)
        out_grad_ref[...] = out_total[...].astype(BF16)


def dispatch(table, own, second, g, router_t, shared_in, shared_out, capacity):
    group, experts, rows = table.shape
    local = own.shape[1]
    model = second.shape[1]
    half = shared_out.shape[0]
    slots = group * capacity

    def by_block(*shape):
        return pl.BlockSpec((None,) + shape, lambda q: (q,) + (0,) * len(shape))

    def by_slots(width):
        return pl.BlockSpec((local, capacity, width), lambda q: (0, q, 0))

    return pl.pallas_call(
        functools.partial(dispatch_kernel, local, capacity, half),
        grid=(group,),
        in_specs=[
            by_block(experts, rows), by_block(local, rows), by_rows((rows, model)), by_rows((rows, model)),
            whole((experts, model)), whole((model, 2 * half)), whole((half, model)),
        ],
        out_specs=[
            by_slots(model), by_slots(model), by_slots(LANES), by_block(experts, rows), by_rows((rows, half)),
            by_rows((rows, 2 * half)), whole((model, 2 * half)), whole((half, model)),
        ],
        out_shape=[
            jax.ShapeDtypeStruct((local, slots, model), BF16),
            jax.ShapeDtypeStruct((local, slots, model), BF16),
            jax.ShapeDtypeStruct((local, slots, LANES), F32),
            jax.ShapeDtypeStruct((group, experts, rows), F32),
            jax.ShapeDtypeStruct((group * rows, half), BF16),
            jax.ShapeDtypeStruct((group * rows, 2 * half), BF16),
            jax.ShapeDtypeStruct((model, 2 * half), BF16),
            jax.ShapeDtypeStruct((half, model), BF16),
        ],
        scratch_shapes=[pltpu.VMEM((model, 2 * half), F32), pltpu.VMEM((half, model), F32)],
        compiler_params=pltpu.CompilerParams(vmem_limit_bytes=56 * 2**20),
        name="dispatch",
    )(table, own, second, g, router_t, shared_in, shared_out)


def experts_kernel(
    buffer_ref, slot_g_ref, gate_ref, in_ref, out_ref,
    weighted_ref, back_ref, dot_ref, in_grad_ref, out_grad_ref, in_total, out_total,
):
    at = pl.program_id(1)
    buffer, weight_in, weight_out = buffer_ref[...], in_ref[...], out_ref[...]
    half = weight_out.shape[0]
    pre = mm(buffer, weight_in)
    a, b = pre[:, :half], pre[:, half:]
    sig = jax.nn.sigmoid(a)
    act = a * sig
    hidden = (act * b).astype(BF16)
    gate = gate_ref[:, 0:1]
    slot_g = slot_g_ref[...].astype(F32)
    result = mm(hidden, weight_out).astype(BF16).astype(F32)
    weighted_ref[...] = (gate * result).astype(BF16)
    dot_ref[...] = jnp.broadcast_to(jnp.sum(slot_g * result, axis=1, keepdims=True), dot_ref.shape)
    result_grad = (gate * slot_g).astype(BF16)
    hidden_grad = mm_nt(result_grad, weight_out)
    pre_grad = jnp.concatenate([hidden_grad * b * silu_slope(a, sig), hidden_grad * act], axis=1).astype(BF16)
    back_ref[...] = mm_nt(pre_grad, weight_in).astype(BF16)

    @pl.when(at == 0)
    def _():
        in_total[...] = jnp.zeros_like(in_total)
        out_total[...] = jnp.zeros_like(out_total)

    in_total[...] += mm_tn(buffer, pre_grad)
    out_total[...] += mm_tn(hidden, result_grad)

    @pl.when(at == pl.num_programs(1) - 1)
    def _():
        in_grad_ref[...] = in_total[...].astype(BF16)
        out_grad_ref[...] = out_total[...].astype(BF16)


def run_experts(buffer, slot_g, gate_slot, expert_in, expert_out, step):
    local, slots, model = buffer.shape
    half = expert_out.shape[1]

    def by_step(width):
        return pl.BlockSpec((None, step, width), lambda i, m: (i, m, 0))

    def by_expert(*shape):
        return pl.BlockSpec((None,) + shape, lambda i, m: (i, 0, 0))

    return pl.pallas_call(
        experts_kernel,
        grid=(local, slots // step),
        in_specs=[
            by_step(model), by_step(model), by_step(LANES), by_expert(model, 2 * half), by_expert(half, model),
        ],
        out_specs=[
            by_step(model), by_step(model), by_step(LANES), by_expert(model, 2 * half), by_expert(half, model),
        ],
        out_shape=[
            jax.ShapeDtypeStruct((local, slots, model), BF16),
            jax.ShapeDtypeStruct((local, slots, model), BF16),
            jax.ShapeDtypeStruct((local, slots, LANES), F32),
            jax.ShapeDtypeStruct((local, model, 2 * half), BF16),
            jax.ShapeDtypeStruct((local, half, model), BF16),
        ],
        scratch_shapes=[pltpu.VMEM((model, 2 * half), F32), pltpu.VMEM((half, model), F32)],
        compiler_params=pltpu.CompilerParams(vmem_limit_bytes=62 * 2**20),
        name="run_experts",
    )(buffer, slot_g, gate_slot, expert_in, expert_out)


def gather(values, axes, axis=0):
    return lax.all_gather(values, axes, axis=axis, tiled=True)


def scatter_sum(values, axes, axis=0):
    return lax.psum_scatter(values, axes, scatter_dimension=axis, tiled=True)


def columns_of(values, start, size, axis=1):
    return lax.dynamic_slice_in_dim(values, start, size, axis=axis)


def shards(
    tokens,
    cotangent,
    dealt_to,
    lengths,
    routes,
    slot_index,
    in_norm,
    in_proj,
    conv_weight,
    conv_bias,
    dt_bias,
    decay_log,
    skip_gain,
    mixer_norm,
    out_proj,
    post_norm,
    router,
    shared_in,
    shared_out,
    expert_in,
    expert_out,
):
    reps, depth = lax.axis_size("rep"), lax.axis_size("z")
    group = 2 * depth
    rep, z, core = lax.axis_index("rep"), lax.axis_index("z"), lax.axis_index("core")
    shard = 2 * z + core
    team = 2 * rep + core
    members = 2 * reps
    rows, model = tokens.shape
    top = routes.shape[1]
    local = expert_in.shape[0]
    experts = local * group
    capacity = rows * top * 4 // (3 * experts)
    inner = mixer_norm.shape[0] * group
    convolved = conv_bias.shape[0] * group
    head_count = dt_bias.shape[0] * group
    width = inner // head_count
    state = (convolved - inner) // 2
    channels = inner // members
    heads = head_count // members
    shared = shared_out.shape[0]
    part = in_norm.shape[0]

    expert_ids = jnp.arange(experts, dtype=jnp.int32)
    table = jnp.sum(
        jnp.where(routes[:, None, :] == expert_ids[None, :, None], slot_index[:, None, :] + 1, 0), axis=2
    ).astype(BF16)
    small = [in_norm[None], conv_weight, conv_bias[None], dt_bias[None], decay_log[None], skip_gain[None],
             mixer_norm[None], post_norm[None], jnp.concatenate([lengths, dealt_to[None]], axis=1)]
    part_wide = -(-part // LANES) * LANES
    table_block = jnp.concatenate([table.T, jnp.pad(router.T, ((0, 0), (0, part_wide - part)))], axis=1)
    pair_heads = 2 * heads
    dt_pair = columns_of(in_proj, inner + convolved + pair_heads * rep, pair_heads)
    blank = jnp.zeros((part, LANES // 2 - heads), BF16)
    common = jnp.concatenate(
        [in_proj[:, 2 * inner : 2 * inner + 2 * state], dt_pair[:, :heads], blank, dt_pair[:, heads:], blank], axis=1
    )

    def pair_of(member):
        return jnp.concatenate(
            [columns_of(in_proj, channels * member, channels), columns_of(in_proj, inner + channels * member, channels)],
            axis=1,
        )

    sequences = lengths.shape[1]
    (after, mixer_result, scale, lengths_plane, in_gain, post_gain, taps_own, head_rows, skip_own, norm_own, table_all,
     second_column, g_column, first, weight, out_own, projected, gained) = forward_mixer(
        tokens, cotangent, pair_of(team), pair_of(2 * rep + 1 - core), common, small, table_block,
        out_proj.reshape(reps, channels // reps, model),
        (reps, depth, channels, width, state, sequences, inner, convolved),
    )
    second_column = second_column.reshape(group * rows, model)
    g_column = g_column.reshape(group * rows, model)
    shared_in_own = lax.all_to_all(
        shared_in.reshape(part, 2, group, shared).transpose(2, 0, 1, 3).reshape(group * part, 2 * shared),
        COLUMN, split_axis=0, concat_axis=0, tiled=True,
    )

    table_all = table_all.reshape(group, experts, -1)
    router_t = table_all[:, :, rows : rows + part].transpose(1, 0, 2).reshape(experts, model)
    dealt_column = shard ^ dealt_to[0] ^ jnp.arange(group, dtype=jnp.int32)
    table_dealt = jnp.take(table_all[:, :, :rows], dealt_column, axis=0)
    table_own = columns_of(table_dealt, local * shard, local)

    buffer, slot_g, gate_slot, gates, shared_hidden, shared_grad, shared_in_grad, shared_out_grad = dispatch(
        table_dealt, table_own, second_column, g_column, router_t, shared_in_own, shared_out, capacity
    )
    weighted, buffer_grad, dots, grad_expert_in, grad_expert_out = run_experts(
        buffer, slot_g, gate_slot, expert_in, expert_out, group * capacity // 2
    )
    shared_in_rows = lax.all_to_all(shared_in_grad, COLUMN, split_axis=0, concat_axis=0, tiled=True)
    shared_in_rows = shared_in_rows.reshape(group, part, 2, shared).transpose(1, 2, 0, 3).reshape(part, -1)
    grad_expert_in, grad_expert_out, grad_shared_out, grad_shared_in = [
        values.astype(F32)
        for values in lax.psum((grad_expert_in, grad_expert_out, shared_out_grad, shared_in_rows), "rep")
    ]

    after_grad, post_grad, router_grad, layer_parts, low_plane, scales = join_experts(
        table_own, gates, dots, shared_hidden, shared_grad, router_t, shared_in_own, shared_out, cotangent, after,
        mixer_result, scale, post_gain, buffer_grad, weighted, second_column, inner, reps, depth, capacity,
    )
    router_parts = jnp.pad(
        router_grad.reshape(experts, depth, 2, part).transpose(1, 2, 0, 3), ((0, 0), (0, 0), (0, 0), (0, part_wide - part))
    )
    layer_out, grad_tokens, side_rows, common_rows, out_rows, small_sum = backward_mixer(
        scales, after, after_grad, tokens, in_gain, post_grad, router_parts, lengths_plane, taps_own, head_rows, skip_own, norm_own, weight.reshape(model, -1),
        out_own.reshape(channels, model), low_plane, layer_parts, first, projected, gained,
        (reps, depth, channels, width, state, sequences, inner, convolved),
    )
    per_shard = conv_bias.shape[0]
    small_shapes = [
        (4, per_shard), (1, per_shard), (1, heads), (1, heads), (1, heads), (1, channels), (1, part), (1, part),
        (part, experts),
    ]
    (grad_in_proj, grad_out_proj, grad_taps, grad_bias, grad_dt, grad_decay, grad_skip, grad_mixer_norm, grad_post,
     grad_in_norm, grad_router) = assemble(
        side_rows, common_rows, out_rows, small_sum, small_shapes, channels, state, heads
    )
    return (
        layer_out,
        grad_tokens,
        grad_in_norm[0],
        grad_in_proj,
        grad_taps,
        grad_bias[0],
        grad_dt[0],
        grad_decay[0],
        grad_skip[0],
        grad_mixer_norm[0],
        grad_out_proj,
        grad_post[0],
        grad_router,
        grad_shared_in,
        grad_shared_out,
        grad_expert_in,
        grad_expert_out,
    )


def solution(mesh):
    reps, group = mesh.shape["rep"], mesh.shape["shard"]
    split = Mesh(mesh.devices.reshape(reps, group // 2, 2), ALL)
    one, row = P(COLUMN), P(COLUMN, None)
    token = P(ALL, None)
    return jax.shard_map(
        shards,
        mesh=split,
        in_specs=(
            token, token, P(ALL), token, token, token, one, row, P(None, COLUMN), one, one, one, one, one, row,
            one, row, row, row, P(COLUMN, None, None), P(COLUMN, None, None),
        ),
        out_specs=(
            token, token, one, row, P(None, COLUMN), one, one, one, one, one, row, one, row, row, row,
            P(COLUMN, None, None), P(COLUMN, None, None),
        ),
        check_vma=False,
    )
```

```python
import functools

import jax
import jax.numpy as jnp
from jax import lax
from jax.experimental import pallas as pl
from jax.experimental.pallas import tpu as pltpu
from jax.sharding import Mesh
from jax.sharding import PartitionSpec as P

EPS = 1e-05
HIGH = lax.Precision.HIGHEST
F32 = jnp.float32
BF16 = jnp.bfloat16
ALL = ("rep", "z", "core")
COLUMN = ("z", "core")
PLANE = ("rep", "core")
LANES = 128


def rms_rows(values):
    return lax.rsqrt(jnp.mean(values * values, axis=-1, keepdims=True) + EPS)


def mm(left, right):
    return jnp.dot(left, right, preferred_element_type=F32)


def mm_nt(left, right):
    return lax.dot_general(left, right, (((1,), (1,)), ((), ())), preferred_element_type=F32)


def mm_tn(left, right):
    return lax.dot_general(left, right, (((0,), (0,)), ((), ())), preferred_element_type=F32)


def silu_slope(values, sig):
    return sig * (1.0 + values * (1.0 - sig))


def split_two(values):
    high = values.astype(BF16)
    return high, (values - high.astype(F32)).astype(BF16)


def segments(lengths_row, sequences, rows):
    column = lax.broadcasted_iota(jnp.int32, (rows, 1), 0).astype(F32)
    line = lax.broadcasted_iota(jnp.int32, (1, rows), 1).astype(F32)
    end = jnp.zeros((1, 1), F32)
    seg_column, seg_line = jnp.zeros_like(column), jnp.zeros_like(line)
    for at in range(sequences):
        end = end + lengths_row[:, at : at + 1]
        seg_column = seg_column + jnp.where(column >= end, 1.0, 0.0)
        seg_line = seg_line + jnp.where(line >= end, 1.0, 0.0)
    return seg_column, seg_line


class Block:
    def __init__(self, proj, seg_col, seg_row, taps, heads, channels, width, state):
        rows = proj.shape[0]
        self.rows, self.channels, self.width, self.state = rows, channels, width, state
        self.gate = proj[:, :channels]
        self.xbc = proj[:, channels : 2 * channels + 2 * state]
        self.turn = lax.axis_index("core") * (LANES // 2)
        dt_raw = pltpu.roll(proj[:, 2 * channels + 2 * state :], self.turn, 1)
        position = lax.broadcasted_iota(jnp.int32, (rows, 1), 0)
        seg_wide = jnp.broadcast_to(seg_col, (rows, LANES))
        self.masks = []
        conv = taps[4:5, :] + taps[3:4, :] * self.xbc
        for offset in (1, 2, 3):
            before = pltpu.roll(seg_wide, offset, 0)[:, :1]
            mask = jnp.where((before == seg_col) & (position >= offset), 1.0, 0.0)
            self.masks.append(mask)
            conv = conv + taps[3 - offset : 4 - offset, :] * (mask * pltpu.roll(self.xbc, offset, 0))
        self.conv = conv
        self.conv_sig = jax.nn.sigmoid(conv)
        act = conv * self.conv_sig
        self.xin = act[:, :channels]
        self.write = act[:, channels : channels + state]
        self.read = act[:, channels + state :]
        shifted = dt_raw + heads[0:1, :]
        self.step = jnp.maximum(shifted, 0.0) + jnp.log1p(jnp.exp(-jnp.abs(shifted)))
        self.step_sig = jax.nn.sigmoid(shifted)
        self.speed = heads[1:2, :]
        self.rate = -self.step * self.speed
        row_at = lax.broadcasted_iota(jnp.int32, (rows, rows), 0)
        col_at = lax.broadcasted_iota(jnp.int32, (rows, rows), 1)
        self.causal = row_at >= col_at
        self.keep = self.causal & (seg_col == seg_row)
        self.cum = jnp.dot(self.causal.astype(F32), self.rate, precision=HIGH, preferred_element_type=F32)
        self.cum_t = self.cum.T
        scores = lax.dot_general(
            self.read, self.write, (((1,), (1,)), ((), ())), precision=HIGH, preferred_element_type=F32
        )
        self.scores = jnp.where(self.keep, scores, 0.0)

    def groups(self):
        for start in range(0, self.channels, LANES):
            stop = min(start + LANES, self.channels)
            yield start, stop, list(range(start // self.width, (stop - 1) // self.width + 1))

    def spread(self, columns, start, stop, heads):
        lane = lax.broadcasted_iota(jnp.int32, (self.rows, stop - start), 1) + start
        result = jnp.broadcast_to(columns[:, heads[0] : heads[0] + 1], (self.rows, stop - start))
        for head in heads[1:]:
            result = jnp.where(lane >= head * self.width, columns[:, head : head + 1], result)
        return result

    def inside(self, start, stop, head):
        lane = lax.broadcasted_iota(jnp.int32, (self.rows, stop - start), 1) + start
        return (lane >= head * self.width) & (lane < (head + 1) * self.width)

    def decay(self, head):
        gaps = self.cum[:, head : head + 1] - self.cum_t[head : head + 1, :]
        return jnp.exp(jnp.where(self.keep, gaps, 0.0))


def block_back(block, low, scale, pull, taps_ref, skip_ref, norm_ref, weight, out_weight):
    rows, channels = block.rows, block.channels
    normed_grad = mm_nt(low, out_weight)
    taps = taps_ref[...]
    gate_grads, x_grads, norm_grads, skip_grads = [], [], [], []
    step_grad = jnp.zeros((rows, LANES), F32)
    cum_grad = jnp.zeros((rows, LANES), F32)
    cum_grad_t = jnp.zeros((LANES, rows), F32)
    score_grad = jnp.zeros((rows, rows), F32)
    lane_all = lax.broadcasted_iota(jnp.int32, (rows, LANES), 1)
    sub_all = lax.broadcasted_iota(jnp.int32, (LANES, rows), 0)
    for start, stop, heads in block.groups():
        xin = block.xin[:, start:stop]
        spread = block.spread(block.step, start, stop, heads)
        scaled, scaled_rest = split_two(xin * spread)
        scaled_wide = jnp.concatenate([scaled, scaled, scaled_rest], axis=1)
        weights, decays = [], []
        y = None
        for head in heads:
            decays.append(block.decay(head))
            weights.append(block.scores * decays[-1])
            term = mm(weights[-1].astype(BF16), scaled)
            y = term if y is None else jnp.where(block.inside(start, stop, head), term, y)
        skip = skip_ref[:, start:stop]
        y = y + skip * xin
        gate = block.gate[:, start:stop]
        gate_sig = jax.nn.sigmoid(gate)
        gate_act = gate * gate_sig
        mixed = y * gate_act
        q = normed_grad[:, start:stop]
        norm_grads.append(jnp.sum(mixed * scale * q, axis=0, keepdims=True))
        mixed_grad = scale * norm_ref[:, start:stop] * q - mixed * pull
        gate_grads.append(mixed_grad * y * silu_slope(gate, gate_sig))
        y_grad = mixed_grad * gate_act
        skip_grads.append(jnp.sum(y_grad * xin, axis=0, keepdims=True))
        y_low, y_rest = split_two(y_grad)
        scaled_grad = None
        for at, head in enumerate(heads):
            inside = block.inside(start, stop, head)
            term = mm_tn(weights[at].astype(BF16), y_low)
            scaled_grad = term if scaled_grad is None else jnp.where(inside, term, scaled_grad)
            blank = jnp.zeros_like(y_low)
            y_own = jnp.where(inside, y_low, blank)
            pair_grad = mm_nt(
                jnp.concatenate([y_own, jnp.where(inside, y_rest, blank), y_own], axis=1), scaled_wide
            )
            score_grad = score_grad + pair_grad * decays[at]
            exponent_grad = pair_grad * weights[at]
            cum_grad = jnp.where(lane_all == head, jnp.sum(exponent_grad, axis=1, keepdims=True), cum_grad)
            cum_grad_t = jnp.where(sub_all == head, jnp.sum(exponent_grad, axis=0, keepdims=True), cum_grad_t)
        for head in heads:
            inside = block.inside(start, stop, head)
            per_row = jnp.sum(jnp.where(inside, scaled_grad * xin, 0.0), axis=1, keepdims=True)
            step_grad = jnp.where(lane_all == head, per_row, step_grad)
        x_grads.append(scaled_grad * spread + skip * y_grad)
    score_grad = jnp.where(block.keep, score_grad, 0.0).astype(BF16)
    read_grad = mm(score_grad, block.write.astype(BF16))
    write_grad = mm_tn(score_grad, block.read.astype(BF16))
    cum_grad = cum_grad - cum_grad_t.T
    rate_grad = lax.dot_general(
        block.causal.astype(F32), cum_grad, (((0,), (0,)), ((), ())), precision=HIGH, preferred_element_type=F32
    )
    dt_grad = (step_grad - block.speed * rate_grad) * block.step_sig
    head_rows = [jnp.sum(dt_grad, axis=0, keepdims=True), jnp.sum(rate_grad * block.rate, axis=0, keepdims=True)]
    act_grad = jnp.concatenate(x_grads + [write_grad, read_grad], axis=1)
    conv_grad = act_grad * silu_slope(block.conv, block.conv_sig)
    tap_rows = {4: jnp.sum(conv_grad, axis=0, keepdims=True), 3: jnp.sum(conv_grad * block.xbc, axis=0, keepdims=True)}
    xbc_grad = taps[3:4, :] * conv_grad
    for offset in (1, 2, 3):
        masked = conv_grad * block.masks[offset - 1]
        tap_rows[3 - offset] = jnp.sum(masked * pltpu.roll(block.xbc, offset, 0), axis=0, keepdims=True)
        xbc_grad = xbc_grad + taps[3 - offset : 4 - offset, :] * pltpu.roll(masked, rows - offset, 0)
    proj_grad = jnp.concatenate(gate_grads + [xbc_grad, pltpu.roll(dt_grad, block.turn, 1)], axis=1).astype(BF16)
    tap_grads = jnp.concatenate([tap_rows[at] for at in range(5)], axis=0)
    wide_grads = jnp.concatenate(
        [jnp.concatenate(norm_grads, axis=1), jnp.concatenate(skip_grads, axis=1)], axis=0
    )
    return proj_grad, tap_grads, head_rows, wide_grads


def whole(shape):
    return pl.BlockSpec(shape, lambda i: (0,) * len(shape))


def by_rows(shape):
    return pl.BlockSpec(shape, lambda i: (i,) + (0,) * (len(shape) - 1))


MESH_ID = pl.DeviceIdType.MESH


def when(condition, action):
    if condition is True:
        action()
    elif condition is not False:
        pl.when(condition)(action)


class Place:
    def __init__(self, reps, depth):
        self.reps, self.depth = reps, depth
        self.rep, self.z, self.core = lax.axis_index("rep"), lax.axis_index("z"), lax.axis_index("core")
        self.here = {"rep": self.rep, "z": self.z, "core": self.core}
        self.pending = []

    def device(self, **changes):
        return {**self.here, **changes}

    def sibling(self):
        return self.device(core=1 - self.core)

    def rep_at(self, distance):
        result, place = 0, 1
        while place < self.reps:
            mine, other = lax.rem(self.rep // place, 2), lax.rem(distance // place, 2)
            result = result + place * (mine + other - 2 * mine * other)
            place *= 2
        return result

    def in_column(self, distance):
        other = lax.rem(2 * self.z + self.core + distance, 2 * self.depth)
        return self.device(z=other // 2, core=lax.rem(other, 2))

    def barrier(self, plane=False, column=False, whole=False):
        semaphore = pltpu.get_barrier_semaphore()

        def greet(device):
            pl.semaphore_signal(semaphore, inc=1, device_id=device, device_id_type=MESH_ID)

        amount = 1
        if whole:
            for distance in range(1, 2 * self.depth):
                greet(self.in_column(distance))
            amount = 2 * self.depth - 1
        else:
            greet(self.sibling())
        if plane:
            for distance in range(1, self.reps):
                greet(self.device(rep=self.rep_at(distance)))
            amount = amount + self.reps - 1
        if column and not whole:
            above, below = self.z < self.depth - 1, self.z > 0
            when(above, lambda: greet(self.device(z=self.z + 1)))
            when(below, lambda: greet(self.device(z=self.z - 1)))
            amount = amount + jnp.where(above, 1, 0) + jnp.where(below, 1, 0)
        pl.semaphore_wait(semaphore, amount)

    def send(self, source, target, send_sem, recv_sem, device, condition=True):
        copy = pltpu.make_async_remote_copy(
            src_ref=source, dst_ref=target, send_sem=send_sem, recv_sem=recv_sem, device_id=device,
            device_id_type=MESH_ID,
        )
        when(condition, copy.start)
        self.pending.append((condition, copy))

    def local(self, source, target, sem):
        copy = pltpu.make_async_copy(source, target, sem)
        copy.start()
        return copy

    def arrived(self, target, recv_sem, condition=True):
        copy = pltpu.make_async_remote_copy(
            src_ref=target, dst_ref=target, send_sem=recv_sem, recv_sem=recv_sem, device_id=self.sibling(),
            device_id_type=MESH_ID,
        )
        when(condition, copy.wait_recv)

    def finish(self):
        for condition, copy in self.pending:
            when(condition, copy.wait_send)
        self.pending = []


class PlaneGather:
    @staticmethod
    def scratch(reps):
        return [pltpu.SemaphoreType.DMA((4, reps + 1)), pltpu.SemaphoreType.DMA((1,))]

    def __init__(self, place, own, out, sems, local_sem, corner=True):
        self.place, self.out, self.sems = place, out, sems
        p = place
        self.half = own.shape[0] // 2
        self.corner = corner and p.reps == 4 and self.half % 16 == 0
        self.keep = p.local(own, out.at[p.rep, p.core], local_sem.at[0])
        for distance in range(1, 3 if self.corner else p.reps):
            p.send(own, out.at[p.rep, p.core], sems.at[0, distance], sems.at[1, distance],
                   p.device(rep=p.rep_at(distance)))
        p.send(own, out.at[p.rep, p.core], sems.at[2, 0], sems.at[3, 0], p.sibling())

    def part(self, distance, at):
        p = self.place
        return self.out.at[p.rep_at(distance), p.core, pl.ds(self.half * at, self.half)]

    def relay(self):
        p = self.place
        for distance in range(1, p.reps):
            source = self.out.at[p.rep_at(distance), p.core]
            if self.corner and distance == 3:
                for at in range(2):
                    p.arrived(self.part(3, at), self.sems.at[1, 3 + at])
            else:
                p.arrived(source, self.sems.at[1, distance])
            if self.corner and distance < 3:
                piece, at = self.part(distance, distance - 1), distance + 2
                p.send(piece, piece, self.sems.at[0, at], self.sems.at[1, at], p.device(rep=p.rep_at(3 - distance)))
            p.send(source, source, self.sems.at[2, distance], self.sems.at[3, distance], p.sibling())

    def finish(self):
        p = self.place
        self.keep.wait()
        for distance in range(p.reps):
            source = p.rep_at(distance) if distance else p.rep
            p.arrived(self.out.at[source, 1 - p.core], self.sems.at[3, distance])


class ColumnGather:
    @staticmethod
    def scratch(depth):
        return [pltpu.SemaphoreType.DMA((8, depth)), pltpu.SemaphoreType.DMA((1,))]

    def __init__(self, place, own, slot, sems, local_sem, shared=None, keep=True, start=True):
        self.place, self.own, self.slot, self.sems, self.shared = place, own, slot, sems, shared
        self.keep = None
        if keep:
            self.keep = pltpu.make_async_copy(own, slot(place.z), local_sem.at[0])
        if start:
            self.start()

    def start(self):
        if self.keep is not None:
            self.keep.start()
        self.send(0)

    def ends(self, distance):
        p = self.place
        below, above = p.z >= distance, p.z + distance < p.depth
        return below, above, jnp.maximum(p.z - distance, 0), jnp.minimum(p.z + distance, p.depth - 1)

    def copies(self, distance):
        p = self.place

        def copy(source, target, at, device):
            return pltpu.make_async_remote_copy(
                src_ref=source, dst_ref=target, send_sem=self.sems.at[at, distance],
                recv_sem=self.sems.at[at + 1, distance], device_id=device, device_id_type=MESH_ID,
            )

        up, down = p.device(z=p.z + 1), p.device(z=p.z - 1)
        if distance == 0:
            target = self.slot(p.z)
            yield p.z < p.depth - 1, copy(self.own, target, 0, up)
            yield p.z > 0, copy(self.own, target, 2, down)
            if self.shared is not None:
                yield True, copy(self.own, target, 4, p.sibling())
            return
        below, above, low, high = self.ends(distance)
        low, high = self.slot(low), self.slot(high)
        yield below & (p.z < p.depth - 1), copy(low, low, 0, up)
        yield above & (p.z > 0), copy(high, high, 2, down)
        if self.shared is not None:
            yield below, copy(low, low, 4, p.sibling())
            yield above, copy(high, high, 6, p.sibling())

    def send(self, distance):
        for condition, copy in self.copies(distance):
            when(condition, copy.start)

    def hop(self, distance):
        below, above, low, high = self.ends(distance)
        self.place.arrived(self.slot(low), self.sems.at[1, distance - 1], below)
        self.place.arrived(self.slot(high), self.sems.at[3, distance - 1], above)
        self.send(distance)

    def finish(self):
        p = self.place
        if self.keep is not None:
            self.keep.wait()
        if self.shared is not None:
            p.arrived(self.shared(p.z), self.sems.at[5, 0])
            for distance in range(1, p.depth):
                below, above, low, high = self.ends(distance)
                p.arrived(self.shared(low), self.sems.at[5, distance], below)
                p.arrived(self.shared(high), self.sems.at[7, distance], above)
        for distance in range(p.depth):
            for condition, copy in self.copies(distance):
                when(condition, copy.wait_send)


def add_up(*terms):
    total = terms[0].astype(F32)
    for term in terms[1:]:
        total = total + term.astype(F32)
    return total


class PairSwap:
    @staticmethod
    def scratch(count, shape, dtype):
        return [pltpu.VMEM((count,) + shape, dtype), pltpu.SemaphoreType.DMA((2, count))]

    def __init__(self, place, parts, pair, sems, order, own=None):
        self.place, self.parts, self.pair, self.sems, self.own = place, parts, pair, sems, own
        for at in order:
            place.send(parts.at[at, 1 - place.core], pair.at[at], sems.at[0, at], sems.at[1, at], place.sibling())

    def wait(self, at):
        self.place.arrived(self.pair.at[at], self.sems.at[1, at])

    def terms(self, at):
        if self.own is None:
            return [self.parts[at, self.place.core], self.pair[at]]
        slot, sem = self.own
        self.place.local(self.parts.at[at, self.place.core], slot, sem.at[0]).wait()
        return [slot[...], self.pair[at]]


class PlaneSum:
    @staticmethod
    def scratch(reps, shape, dtype):
        return PairSwap.scratch(reps, shape, dtype) + [
            pltpu.VMEM((reps,) + shape, dtype), pltpu.SemaphoreType.DMA((2, reps)),
        ]

    def __init__(self, place, parts, pair, pair_sems, into, sems):
        self.place, self.pair, self.into, self.sems = place, pair, into, sems
        order = [place.rep_at(distance) for distance in range(1, place.reps)] + [place.rep]
        self.swap = PairSwap(place, parts, pair, pair_sems, order)

    def relay(self):
        p = self.place
        for distance in range(1, p.reps):
            rep = p.rep_at(distance)
            self.swap.wait(rep)
            self.pair[rep] = add_up(*self.swap.terms(rep)).astype(self.pair.dtype)
            p.send(self.pair.at[rep], self.into.at[distance], self.sems.at[0, distance], self.sems.at[1, distance],
                   p.device(rep=rep))

    def total(self):
        p = self.place
        self.swap.wait(p.rep)
        terms = self.swap.terms(p.rep)
        for distance in range(1, p.reps):
            p.arrived(self.into.at[distance], self.sems.at[1, distance])
            terms.append(self.into[distance])
        return add_up(*terms)


class LineSum:
    @staticmethod
    def scratch(depth, shape, dtype):
        return [pltpu.VMEM((depth + 1,) + shape, dtype), pltpu.SemaphoreType.DMA((4, depth))]

    def __init__(self, place, terms, out, into, sems):
        self.place, self.terms, self.out, self.into, self.sems = place, terms, out, into, sems

    def moves(self, at):
        p = self.place
        last = p.depth - 1
        for way, towards, goal, first, valid in (
            (0, p.z + 1, last - (at - p.z), p.z == 0, (at >= p.z) & (last - (at - p.z) > p.z)),
            (1, p.z - 1, at - (last - p.z), p.z == last, (at >= last - p.z) & (at - (last - p.z) < p.z)),
        ):
            goal = jnp.clip(goal, 0, last)
            slot = jnp.where(goal == towards, p.depth, goal) if way else goal
            copy = pltpu.make_async_remote_copy(
                src_ref=self.out.at[goal], dst_ref=self.into.at[slot], send_sem=self.sems.at[2 * way, goal],
                recv_sem=self.sems.at[2 * way + 1, goal], device_id=p.device(z=towards), device_id_type=MESH_ID,
            )
            yield way, goal, first, valid, copy

    def step(self, at):
        p = self.place
        for way, goal, first, valid, copy in self.moves(at):
            inner = valid & jnp.logical_not(first)
            p.arrived(self.into.at[goal], self.sems.at[2 * way + 1, goal], inner)

            def start(goal=goal):
                self.out[goal] = add_up(*self.terms(goal)).astype(self.out.dtype)

            def follow(goal=goal):
                self.out[goal] = add_up(*self.terms(goal), self.into[goal]).astype(self.out.dtype)

            when(valid & first, start)
            when(inner, follow)
            when(valid, copy.start)

    def finish(self):
        for at in range(self.place.depth - 1):
            for _, _, _, valid, copy in self.moves(at):
                when(valid, copy.wait_send)

    def total(self, result):
        result[...] = add_up(*self.terms(self.place.z))
        self.gather(result)
        self.finish()

    def gather(self, result):
        p = self.place
        for way, slot, condition in ((0, p.z, p.z > 0), (1, p.depth, p.z < p.depth - 1)):
            p.arrived(self.into.at[slot], self.sems.at[2 * way + 1, p.z], condition)

            def add(slot=slot):
                result[...] += self.into[slot].astype(F32)

            when(condition, add)


class ColumnSum:
    @staticmethod
    def scratch(depth, shape, dtype):
        return PairSwap.scratch(depth, shape, dtype) + LineSum.scratch(depth, shape, dtype)

    def __init__(self, place, parts, pair, pair_sems, into, sems, own=None):
        self.place = place
        order = [lax.rem(place.z + distance, place.depth) for distance in list(range(place.depth - 1, 0, -1)) + [0]]
        self.order = order
        self.swap = PairSwap(place, parts, pair, pair_sems, order, own)
        self.line = LineSum(place, self.swap.terms, pair, into, sems)

    def ready(self):
        for at in self.order:
            self.swap.wait(at)

    def step(self, at):
        self.line.step(at)

    def total(self, result):
        self.line.total(result)


def anywhere(count):
    return [pl.BlockSpec(memory_space=pl.ANY)] * count


def in_vmem(count):
    return [pl.BlockSpec(memory_space=pltpu.VMEM)] * count


def remote_params(identity, mebibytes=60):
    return pltpu.CompilerParams(
        collective_id=identity, has_side_effects=True, vmem_limit_bytes=mebibytes * 2**20
    )


def column_of(row_values, rows):
    return jnp.broadcast_to(row_values, (LANES, rows)).T[:, 0:1]


def row_of(column_values, rows):
    return jnp.broadcast_to(column_values, (rows, LANES)).T[0:8, :]


def forward_mixer(tokens, cotangent, own_pair, other_pair, common, small, table, out_quarters, shared_in, sizes):
    reps, depth, channels, width, state, sequences, inner, convolved = sizes
    rows, model = tokens.shape
    part, side = own_pair.shape
    wide = side + common.shape[1]
    quarter = out_quarters.shape[1]
    vector_width = -(-max(piece.shape[1] for piece in small) // LANES) * LANES
    vector_rows = 16
    group = 2 * depth
    shared = shared_in.shape[1] // (2 * group)
    heads = channels // width
    per_shard = convolved // (2 * depth)

    x_scratch = [pltpu.VMEM((reps, 2, rows, model), BF16)] + PlaneGather.scratch(reps)
    w_scratch = [pltpu.VMEM((depth, 2, part, wide), BF16)] + ColumnGather.scratch(depth) * 3
    v_scratch = [pltpu.VMEM((depth, 2, vector_rows, vector_width), F32)] + ColumnGather.scratch(depth) * 2
    o_scratch = [
        pltpu.VMEM((depth, quarter, model), BF16), pltpu.VMEM((reps, quarter, model), BF16),
    ] + ColumnGather.scratch(depth) + [pltpu.SemaphoreType.DMA((2, max(reps, depth))), pltpu.SemaphoreType.DMA((2,))]
    n_scratch = [pltpu.VMEM((8, LANES), F32)] + PlaneGather.scratch(reps)
    sum_scratch = [
        pltpu.VMEM((reps, rows, model), BF16), pltpu.VMEM((reps, 2, 8, rows), F32),
    ] + PlaneSum.scratch(reps, (rows, model), BF16) + PlaneSum.scratch(reps, (8, rows), F32)
    groups = [x_scratch, w_scratch, v_scratch, o_scratch, n_scratch, sum_scratch]

    def kernel(x_ref, g_ref, own_ref, other_ref, common_ref, table_ref, quarters_ref, shared_ref, *refs):
        small_refs, refs = refs[: len(small)], refs[len(small) :]
        (after_ref, mixed_ref, scale_ref, lengths_ref, in_gain_ref, post_gain_ref, taps_ref, heads_ref, skip_ref,
               norm_ref, table_out, second_out, g_out, first_out, weight_out, out_out, proj_out, mixed_out, shared_out), scratch = refs[:19], refs[19:]
        cut = [0]
        for items in groups:
            cut.append(cut[-1] + len(items))
        x_work, w_work, v_work, o_work, n_work, sum_work = [scratch[i:j] for i, j in zip(cut, cut[1:])]
        (second, second_sems, second_local, g_sems, g_local, proj_buffer, proj_sems, keep_sems,
         own_part, mixed_all, mixed_sems, vectors_ref, shared_sems, shared_local) = scratch[cut[-1]:]
        p = Place(reps, depth)
        vectors_ref[...] = jnp.zeros_like(vectors_ref)
        row = 0
        for piece in small_refs:
            count, size = piece.shape
            vectors_ref[row : row + count, :size] = piece[...].astype(F32)
            row += count
        p.barrier(plane=True, column=True, whole=True)

        x_all, weight_all, vectors_all = x_work[0], w_work[0], v_work[0]

        def left(core):
            return lambda z: weight_all.at[z, core, :, pl.ds(0, side)]

        def right(core):
            return lambda z: weight_all.at[z, core, :, pl.ds(side, wide - side)]

        vector_job = ColumnGather(p, vectors_ref, lambda z: vectors_all.at[z, p.core], v_work[1], v_work[2],
                                  shared=lambda z: vectors_all.at[z, 1 - p.core])
        own_slot, other_slot = left(p.core), left(1 - p.core)
        p.send(other_ref, own_slot(p.z), keep_sems.at[0], keep_sems.at[1], p.sibling())
        job_a = ColumnGather(p, own_ref, own_slot, w_work[1], w_work[2])
        job_c = ColumnGather(p, common_ref, right(p.core), w_work[3], w_work[4], shared=right(1 - p.core))
        x_job = PlaneGather(p, x_ref, x_all, x_work[1], x_work[2])
        p.arrived(other_slot(p.z), keep_sems.at[1])
        job_b = ColumnGather(p, other_slot(p.z), other_slot, w_work[5], w_work[6], keep=False)
        for distance in range(1, depth):
            vector_job.hop(distance)
        vector_job.finish()

        own_row = vectors_all[p.z, p.core].astype(F32)[11:12, :LANES]
        dealt = own_row[:, sequences : sequences + 1]
        lengths_row = jnp.zeros((1, LANES), F32)
        for z in range(depth):
            for core in range(2):
                row = vectors_all[z, core].astype(F32)[11:12, :LANES]
                lengths_row = jnp.where(dealt == float(2 * z + core), row, lengths_row)
        n_work[0][...] = jnp.broadcast_to(lengths_row, (8, LANES))
        n_job = PlaneGather(p, n_work[0], lengths_ref, n_work[1], n_work[2], corner=False)

        pieces = [vectors_all[z, core].astype(F32) for z in range(depth) for core in range(2)]
        in_gain_ref[...] = jnp.concatenate([piece[0:1, :part] for piece in pieces], axis=1)
        post_gain_ref[...] = jnp.concatenate([piece[10:11, :part] for piece in pieces], axis=1)
        taps_full = jnp.concatenate([piece[0:8, :per_shard] for piece in pieces], axis=1)
        taps_full = jnp.concatenate([taps_full[1:6, :], jnp.zeros((3, convolved), F32)], axis=0)
        team = 2 * p.rep + p.core
        taps_own = taps_full[:, :channels]
        for member in range(1, 2 * reps):
            taps_own = jnp.where(team == member, taps_full[:, channels * member : channels * (member + 1)], taps_own)
        taps_ref[...] = jnp.concatenate([taps_own, taps_full[:, inner:]], axis=1)
        own = vectors_all[p.rep, p.core].astype(F32)
        lane = lax.broadcasted_iota(jnp.int32, (1, LANES), 1)
        speed = jnp.where(lane < heads, jnp.exp(jnp.where(lane < heads, own[7:8, :LANES], 0.0)), 0.0)
        heads_ref[...] = jnp.concatenate([own[6:7, :LANES], speed, jnp.zeros((6, LANES), F32)], axis=0)
        norm_ref[...] = own[9:10, :channels]
        wide_lane = lax.broadcasted_iota(jnp.int32, (1, channels), 1)
        skip = jnp.broadcast_to(own[8:9, 0:1], (1, channels))
        for head in range(1, heads):
            skip = jnp.where(wide_lane >= head * width, own[8:9, head : head + 1], skip)
        skip_ref[...] = skip

        n_job.relay()
        mid, out_all, o_sems, o_local, e_sems, e_local = o_work
        late_jobs = []
        for distance in range(1, depth):
            for job in (job_a, job_c, job_b):
                job.hop(distance)
            if distance == min(2, depth - 1):
                x_job.relay()
                late_jobs.append(ColumnGather(p, quarters_ref.at[p.rep], lambda z: mid.at[z], o_sems, o_local))
                late_jobs.append(
                    ColumnGather(p, table_ref, lambda z: table_out.at[z, p.core], v_work[3], v_work[4],
                                 shared=lambda z: table_out.at[z, 1 - p.core])
                )
        job_o, table_job = late_jobs
        shard = 2 * p.z + p.core

        def shared_piece(kind, other):
            start = pl.multiple_of((kind * group + other) * shared, LANES)
            return shared_ref.at[:, pl.ds(start, shared)]

        def shared_slot(kind, other):
            return shared_out.at[other, :, pl.ds(kind * shared, shared)]

        shared_keep = [
            p.local(shared_piece(kind, shard), shared_slot(kind, shard), shared_local.at[kind]) for kind in range(2)
        ]
        for distance in range(1, group):
            goal = p.in_column(distance)
            for kind in range(2):
                p.send(shared_piece(kind, 2 * goal["z"] + goal["core"]), shared_slot(kind, shard),
                       shared_sems.at[2 * kind, distance], shared_sems.at[2 * kind + 1, distance], goal)
        shared_pending, p.pending = p.pending[-2 * (group - 1) :], p.pending[: -2 * (group - 1)]
        job_o.keep.wait()
        job_o.keep = None
        for job in (n_job, x_job, job_a, job_b, job_c):
            job.finish()
        weight_keep = p.local(weight_all, weight_out, e_local.at[0])

        def exchange_copy(goal):
            return pltpu.make_async_remote_copy(
                src_ref=mid.at[goal], dst_ref=out_all.at[p.rep], send_sem=e_sems.at[0, goal],
                recv_sem=e_sems.at[1, p.rep], device_id=p.device(rep=goal), device_id_type=MESH_ID,
            )

        def exchange(goal, condition):
            def own():
                out_all[goal] = mid[goal]

            when(condition & (goal == p.rep), own)
            when(condition & (goal != p.rep), exchange_copy(goal).start)

        def out_tick(distance):
            if distance == 1:
                exchange(p.z, p.z >= 0)
            job_o.hop(distance)
            table_job.hop(distance)
            below, above, low, high = job_o.ends(distance)
            exchange(low, below)
            exchange(high, above)

        def out_wait():
            for rep in range(reps):
                p.arrived(out_all.at[rep], e_sems.at[1, rep], rep != p.rep)

        g_job = ColumnGather(p, g_ref, lambda z: g_out.at[z, p.core], g_sems, g_local,
                             shared=lambda z: g_out.at[z, 1 - p.core], start=False)
        p.finish()
        parts, squares = sum_work[0], sum_work[1]
        pair, pair_sems, into, into_sems = sum_work[2:6]
        s_pair, s_pair_sems, s_into, s_into_sems = sum_work[6:10]

        def swap(rep, start):
            for source, target, sems in (
                (parts.at[rep], pair, pair_sems), (squares.at[rep, 1 - p.core], s_pair, s_pair_sems)
            ):
                copy = pltpu.make_async_remote_copy(
                    src_ref=source, dst_ref=target.at[rep], send_sem=sems.at[0, rep],
                    recv_sem=sems.at[1, rep], device_id=p.sibling(), device_id_type=MESH_ID,
                )
                if start:
                    copy.start()
                else:
                    copy.wait_send()

        def onward(distance, rep, start):
            for values, target, sems in ((pair, into, into_sems), (s_pair, s_into, s_into_sems)):
                copy = pltpu.make_async_remote_copy(
                    src_ref=values.at[rep], dst_ref=target.at[distance], send_sem=sems.at[0, distance],
                    recv_sem=sems.at[1, distance], device_id=p.device(rep=rep), device_id_type=MESH_ID,
                )
                if start:
                    copy.start()
                else:
                    copy.wait_send()

        def proj_copy(slot, rep, core):
            return pltpu.make_async_copy(proj_buffer.at[slot], proj_out.at[rep, core], proj_sems.at[slot])

        def mixed_copy(at, rep, core):
            return pltpu.make_async_copy(mixed_all.at[at], mixed_out.at[rep, core], mixed_sems.at[at])

        def place_of(at):
            distance = lax.rem(at // 2 + 1, reps)
            turn = lax.rem(at, 2)
            return distance, p.rep_at(distance), turn, jnp.where(turn == 0, 1 - p.core, p.core)

        def mix(at):
            distance, rep, turn, core = place_of(at)
            x = x_all[rep, core].astype(F32)
            first = (x * rms_rows(x) * in_gain_ref[...]).astype(BF16)
            x_all[rep, core] = first
            proj = mm(first, weight_all[...].reshape(model, wide))

            @pl.when(at >= 2)
            def _():
                proj_copy(turn, rep, core).wait()

            proj_buffer[turn] = proj
            proj_copy(turn, rep, core).start()
            seg_column, seg_line = segments(lengths_ref[rep, core][0:1, :], sequences, rows)
            block = Block(proj, seg_column, seg_line, taps_ref[...], heads_ref[...], channels, width, state)
            mixed = []
            for start, stop, inside in block.groups():
                xin = block.xin[:, start:stop]
                scaled, rest = split_two(xin * block.spread(block.step, start, stop, inside))
                scaled = jnp.concatenate([scaled, scaled, rest], axis=0)
                y = None
                for head in inside:
                    weights, weights_rest = split_two(block.scores * block.decay(head))
                    term = mm(jnp.concatenate([weights, weights_rest, weights], axis=1), scaled)
                    y = term if y is None else jnp.where(block.inside(start, stop, head), term, y)
                gate = block.gate[:, start:stop]
                mixed.append((y + skip_ref[:, start:stop] * xin) * gate * jax.nn.sigmoid(gate))
            mixed = jnp.concatenate(mixed, axis=1)
            squares[rep, core] = row_of(jnp.sum(mixed * mixed, axis=1, keepdims=True), rows)
            mixed_all[at] = mixed * norm_ref[...]
            mixed_copy(at, rep, core).start()

        def put(at):
            distance, rep, turn, core = place_of(at)
            mixed, mixed_rest = split_two(mixed_all[at])
            out_weight = out_all[...].reshape(channels, model)
            part_rows = mm(mixed, out_weight) + mm(mixed_rest, out_weight)

            @pl.when(turn == 0)
            def _():
                parts[rep] = part_rows.astype(BF16)
                swap(rep, True)

            @pl.when((turn == 1) & (distance == 0))
            def _():
                own_part[...] = part_rows

            @pl.when((turn == 1) & (distance > 0))
            def _():
                p.arrived(pair.at[rep], pair_sems.at[1, rep])
                pair[rep] = add_up(part_rows, pair[rep]).astype(BF16)
                p.arrived(s_pair.at[rep], s_pair_sems.at[1, rep])
                s_pair[rep] = add_up(squares[rep, p.core], s_pair[rep])
                onward(distance, rep, True)

        delay = 4

        def visit(at, carry):
            pl.when(at < 2 * reps)(functools.partial(mix, at))
            for distance in range(1, depth):
                pl.when(at == min(distance - 1, delay - 1))(functools.partial(out_tick, distance))
            pl.when(at == delay - 1)(g_job.start)
            pl.when(at == delay)(out_wait)
            pl.when(at >= delay)(functools.partial(put, at - delay))
            pl.when(at == 2 * delay - 1)(functools.partial(g_job.hop, 1))
            return carry

        lax.fori_loop(0, 2 * reps + delay, visit, 0)
        out_keep = p.local(out_all, out_out, e_local.at[1])
        first_keep = p.local(x_all, first_out, keep_sems.at[2])
        if depth > 2:
            g_job.hop(2)
        p.arrived(pair.at[p.rep], pair_sems.at[1, p.rep])
        p.arrived(s_pair.at[p.rep], s_pair_sems.at[1, p.rep])
        terms, square_terms = [own_part[...], pair[p.rep]], [squares[p.rep, p.core], s_pair[p.rep]]
        for distance in range(1, reps):
            p.arrived(s_into.at[distance], s_into_sems.at[1, distance])
            square_terms.append(s_into[distance])
            p.arrived(into.at[distance], into_sems.at[1, distance])
            terms.append(into[distance])
        scale_row = lax.rsqrt(add_up(*square_terms) / inner + EPS)
        scale_ref[...] = scale_row
        mixed = column_of(scale_row[0:1, :], rows) * add_up(*terms)
        mixed_ref[...] = mixed.astype(BF16)
        after = x_ref[...].astype(F32) + mixed
        after_ref[...] = after
        second[...] = (after * rms_rows(after) * post_gain_ref[...]).astype(BF16)
        job = ColumnGather(p, second, lambda z: second_out.at[z, p.core], second_sems, second_local,
                           shared=lambda z: second_out.at[z, 1 - p.core])
        for distance in range(3, depth):
            g_job.hop(distance)
        for distance in range(1, depth):
            job.hop(distance)
        job.finish()
        g_job.finish()
        for distance in range(reps):
            rep = p.rep_at(distance) if distance else p.rep
            swap(rep, False)
            if distance:
                onward(distance, rep, False)
        for slot in range(2):
            proj_copy(slot, p.rep, p.core).wait()
        for at in range(2 * reps):
            mixed_copy(at, p.rep, p.core).wait()
        job_o.finish()
        table_job.finish()
        for distance in range(1, group):
            other = lax.rem(shard - distance + group, group)
            for kind in range(2):
                p.arrived(shared_slot(kind, other), shared_sems.at[2 * kind + 1, distance])
        for keep in shared_keep:
            keep.wait()
        p.pending = p.pending + shared_pending
        for goal in range(depth):
            when(goal != p.rep, exchange_copy(goal).wait_send)
        for keep in (weight_keep, out_keep, first_keep):
            keep.wait()
        p.finish()

    return pl.pallas_call(
        kernel,
        in_specs=in_vmem(1) + anywhere(7) + in_vmem(len(small)),
        out_specs=in_vmem(10) + anywhere(9),
        out_shape=[
            jax.ShapeDtypeStruct((rows, model), F32),
            jax.ShapeDtypeStruct((rows, model), BF16),
            jax.ShapeDtypeStruct((8, rows), F32),
            jax.ShapeDtypeStruct((reps, 2, 8, LANES), F32),
            jax.ShapeDtypeStruct((1, model), F32),
            jax.ShapeDtypeStruct((1, model), F32),
            jax.ShapeDtypeStruct((8, channels + 2 * state), F32),
            jax.ShapeDtypeStruct((8, LANES), F32),
            jax.ShapeDtypeStruct((1, channels), F32),
            jax.ShapeDtypeStruct((1, channels), F32),
            jax.ShapeDtypeStruct((depth, 2) + table.shape, BF16),
            jax.ShapeDtypeStruct((depth, 2, rows, model), BF16),
            jax.ShapeDtypeStruct((depth, 2, rows, model), BF16),
            jax.ShapeDtypeStruct((reps, 2, rows, model), BF16),
            jax.ShapeDtypeStruct((depth, 2, part, wide), BF16),
            jax.ShapeDtypeStruct((reps, quarter, model), BF16),
            jax.ShapeDtypeStruct((reps, 2, rows, wide), F32),
            jax.ShapeDtypeStruct((reps, 2, rows, channels), F32),
            jax.ShapeDtypeStruct((group, part, 2 * shared), BF16),
        ],
        scratch_shapes=[item for items in groups for item in items]
        + [pltpu.VMEM((rows, model), BF16)]
        + ColumnGather.scratch(depth) * 2
        + [pltpu.VMEM((2, rows, wide), F32), pltpu.SemaphoreType.DMA((2,)), pltpu.SemaphoreType.DMA((3,)),
           pltpu.VMEM((rows, model), F32), pltpu.VMEM((2 * reps, rows, channels), F32),
           pltpu.SemaphoreType.DMA((2 * reps,)), pltpu.VMEM((vector_rows, vector_width), F32),
           pltpu.SemaphoreType.DMA((4, group)), pltpu.SemaphoreType.DMA((2,))],
        compiler_params=remote_params(0),
        name="forward_mixer",
    )(tokens, cotangent, own_pair, other_pair, common, table, out_quarters, shared_in, *small)


def join_experts(
    own, gates, dots, hidden, shared_grad, router_t, shared_in, shared_out, cotangent, after, mixed, scale, post_gain,
    back, weighted, second, inner, reps, depth, capacity,
):
    rows, model = cotangent.shape
    local = own.shape[1]
    experts = gates.shape[1]
    half_rows = rows // 2
    stack = (rows, model)
    halves = (slice(0, half_rows), slice(half_rows, rows))
    groups = {
        "stream": [
            pltpu.VMEM((2, local, capacity, model), BF16), pltpu.SemaphoreType.DMA((2,)),
            pltpu.VMEM((2,) + stack, BF16), pltpu.SemaphoreType.DMA((2,)),
        ],
        "parts": [
            pltpu.VMEM((2,) + stack, BF16), pltpu.VMEM(stack, F32), pltpu.VMEM((depth, 2, half_rows, model), BF16),
            pltpu.SemaphoreType.DMA((2, depth)),
        ],
        "line": LineSum.scratch(depth, (half_rows, model), BF16) * 2,
        "low": [pltpu.VMEM((2, half_rows, model), BF16), pltpu.VMEM((2, 8, rows), F32)] + PlaneGather.scratch(reps) * 3,
        "logits": [pltpu.VMEM((2 * depth, 2 * experts, rows), BF16)],
        "layer": [
            pltpu.VMEM((2,) + stack, BF16), pltpu.VMEM(stack, F32), pltpu.VMEM((depth,) + stack, BF16),
            pltpu.SemaphoreType.DMA((2, depth)),
        ] + LineSum.scratch(depth, stack, BF16),
    }

    def kernel(own_ref, gates_ref, dots_ref, hidden_ref, shared_ref, router_ref, in_ref, out_ref, g_ref, after_ref,
               mixed_ref, scale_ref, gain_ref, back_ref, weighted_ref, second_ref,
               grad_ref, gain_grad_ref, router_grad_ref, layer_out_ref, low_out, scale_out, *scratch):
        work, cut = {}, 0
        for name, items in groups.items():
            work[name] = scratch[cut : cut + len(items)]
            cut += len(items)
        p = Place(reps, depth)
        slots, slot_sems, second_slots, second_sems = work["stream"]
        parts, own_part, pair, pair_sems = work["parts"]
        logits_all = work["logits"][0]
        layer_parts, layer_own, layer_pair, layer_pair_sems, layer_into, layer_sems = work["layer"]
        lower = p.z < depth // 2

        def goal_at(index):
            distance = lax.rem(depth - 1 - index + depth, depth)
            return jnp.where(lower, lax.rem(p.z + distance, depth), lax.rem(p.z - distance + depth, depth))

        def block_at(at):
            return goal_at(at // 2), jnp.where(lax.rem(at, 2) == 0, 1 - p.core, p.core)

        def load(source, at):
            goal, core = block_at(at)
            start = pl.multiple_of((2 * goal + core) * capacity, capacity)
            return pltpu.make_async_copy(
                source.at[:, pl.ds(start, capacity)], slots.at[lax.rem(at, 2)], slot_sems.at[lax.rem(at, 2)]
            )

        def swap(goal, slot, start):
            for at, piece in enumerate(halves):
                copy = pltpu.make_async_remote_copy(
                    src_ref=parts.at[slot, pl.ds(half_rows * at, half_rows)], dst_ref=pair.at[goal, at],
                    send_sem=pair_sems.at[0, goal] if at == 0 else pair_sems_late.at[0, goal],
                    recv_sem=pair_sems.at[1, goal] if at == 0 else pair_sems_late.at[1, goal],
                    device_id=p.sibling(), device_id_type=MESH_ID,
                )
                copy.start() if start else copy.wait_send()

        pair_sems_late = work["late"][0]
        load(back_ref, 0).start()
        p.barrier(plane=True, column=True)
        expert = lax.broadcasted_iota(jnp.int32, (experts, rows), 0)
        shard = 2 * p.z + p.core

        def matches(q):
            table = own_ref[q].astype(F32)
            return [slot_match(table[i : i + 1, :], capacity, rows) for i in range(local)]

        def visit(at, carry):
            goal, core = block_at(at)
            q = 2 * goal + core
            turn = lax.rem(at, 2)
            load(back_ref, at).wait()

            @pl.when(at + 1 < 2 * depth)
            def _():
                load(back_ref, at + 1).start()

            start = pl.multiple_of(q * rows, rows)
            gates = gates_ref[q]
            gate_grad = jnp.zeros_like(gates)
            total = mm_nt(shared_ref[pl.ds(start, rows), :], in_ref[...])
            for i, match in enumerate(matches(q)):
                total = total + mm_tn(match.astype(BF16), slots[turn, i])
                dot = dots_ref[i, pl.ds(pl.multiple_of(q * capacity, capacity), capacity), 0:1]
                row = jnp.sum(jnp.where(match, dot, 0.0), axis=0, keepdims=True)
                gate_grad = jnp.where(expert == local * shard + i, row, gate_grad)
            logit_grad = gates * (gate_grad - jnp.sum(gates * gate_grad, axis=0, keepdims=True))
            logit_pair = jnp.concatenate(split_two(logit_grad), axis=0)
            logits_all[q] = logit_pair
            total = total + mm_tn(logit_pair, jnp.concatenate([router_ref[...], router_ref[...]], axis=0))

            @pl.when(turn == 0)
            def _():
                slot = lax.rem(at // 2, 2)

                @pl.when(at >= 4)
                def _():
                    swap(goal_at(at // 2 - 2), slot, False)

                parts[slot] = total.astype(BF16)
                swap(goal, slot, True)

            @pl.when(turn == 1)
            def _():
                p.arrived(pair.at[goal, 0], pair_sems.at[1, goal])
                p.arrived(pair.at[goal, 1], pair_sems_late.at[1, goal])

                @pl.when(goal == p.z)
                def _():
                    for index, piece in enumerate(halves):
                        own_part[piece, :] = add_up(total[piece, :], pair[goal, index])

                @pl.when(goal != p.z)
                def _():
                    for index, piece in enumerate(halves):
                        pair[goal, index] = add_up(total[piece, :], pair[goal, index]).astype(BF16)

            return carry

        lines = []
        for index in range(2):
            view = pair.at[:, index]
            into, sems = work["line"][2 * index : 2 * index + 2]

            def terms(goal, view=view, index=index):
                return [view[goal]]

            lines.append(LineSum(p, terms, view, into, sems))

        for step in range(depth - 1):
            lax.fori_loop(2 * step, 2 * step + 2, visit, 0)
            lines[0].step(step)
        for step in range(depth - 1):
            lines[1].step(step)
        lax.fori_loop(2 * depth - 2, 2 * depth, visit, 0)

        low, scales = work["low"][:2]
        gather_sems = work["low"][2:]
        gain_grad_ref[...] = jnp.zeros_like(gain_grad_ref)
        row_dots = []

        def norm_back(index):
            piece = halves[index]
            into = lines[index].into
            grad_ref[piece, :] = own_part[piece, :]
            lines[index].gather(grad_ref.at[pl.ds(half_rows * index, half_rows)])
            second_grad = grad_ref[piece, :]
            after_rows = after_ref[piece, :]
            after_scale = rms_rows(after_rows)
            gain_grad_ref[...] += jnp.sum(after_rows * second_grad * after_scale, axis=0, keepdims=True)
            weighted = second_grad * gain_ref[...]
            after_grad = (
                g_ref[piece, :].astype(F32)
                + after_scale * weighted
                - after_rows * after_scale**3 * jnp.mean(after_rows * weighted, axis=1, keepdims=True)
            )
            grad_ref[piece, :] = after_grad
            after_low = after_grad.astype(BF16)
            low[index] = after_low
            row_dots.append(
                jnp.sum(after_low.astype(F32) * mixed_ref[piece, :].astype(F32), axis=1, keepdims=True)
            )
            return PlaneGather(p, low.at[index], low_out.at[:, :, pl.ds(half_rows * index, half_rows)],
                               *gather_sems[2 * index : 2 * index + 2])

        first_job = norm_back(0)

        def layer_load(at):
            q = block_at(at)
            start = pl.multiple_of((2 * q[0] + q[1]) * rows, rows)
            return pltpu.make_async_copy(
                second_ref.at[pl.ds(start, rows)], second_slots.at[lax.rem(at, 2)], second_sems.at[lax.rem(at, 2)]
            )

        def layer_swap(goal, slot):
            return pltpu.make_async_remote_copy(
                src_ref=layer_parts.at[slot], dst_ref=layer_pair.at[goal], send_sem=layer_pair_sems.at[0, goal],
                recv_sem=layer_pair_sems.at[1, goal], device_id=p.sibling(), device_id_type=MESH_ID,
            )

        def layer_visit(at, carry):
            goal, core = block_at(at)
            q = 2 * goal + core
            turn = lax.rem(at, 2)
            load(weighted_ref, at).wait()
            layer_load(at).wait()

            @pl.when(at + 1 < 2 * depth)
            def _():
                load(weighted_ref, at + 1).start()
                layer_load(at + 1).start()

            total = mm(hidden_ref[pl.ds(pl.multiple_of(q * rows, rows), rows), :], out_ref[...])
            for i, match in enumerate(matches(q)):
                total = total + mm_tn(match.astype(BF16), slots[turn, i])

            @pl.when(turn == 0)
            def _():
                slot = lax.rem(at // 2, 2)

                @pl.when(at >= 4)
                def _():
                    layer_swap(goal_at(at // 2 - 2), slot).wait_send()

                layer_parts[slot] = total.astype(BF16)
                layer_swap(goal, slot).start()

            @pl.when(turn == 1)
            def _():
                p.arrived(layer_pair.at[goal], layer_pair_sems.at[1, goal])

                @pl.when(goal == p.z)
                def _():
                    layer_own[...] = add_up(total, layer_pair[goal])

                @pl.when(goal != p.z)
                def _():
                    layer_pair[goal] = add_up(total, layer_pair[goal]).astype(BF16)

            both = mm(logits_all[q], second_slots[turn])
            router_grad_ref[...] += both[:experts, :] + both[experts:, :]
            return carry

        router_grad_ref[...] = jnp.zeros_like(router_grad_ref)
        load(weighted_ref, 0).start()
        layer_load(0).start()
        lax.fori_loop(0, 2 * depth, layer_visit, 0)
        first_job.relay()
        second_job = norm_back(1)
        layer_line = LineSum(p, lambda goal: [layer_pair[goal]], layer_pair, layer_into, layer_sems)
        layer_line.step(0)
        dot_row = row_of(jnp.concatenate(row_dots, axis=0), rows)
        scale_row = scale_ref[...]
        scales[0] = scale_row
        scales[1] = scale_row**2 * dot_row / inner
        scale_job = PlaneGather(p, scales, scale_out, *gather_sems[4:6], corner=False)
        for step in range(1, depth - 1):
            layer_line.step(step)
        scale_job.relay()
        second_job.relay()
        layer_line.gather(layer_own)
        layer_out_ref[...] = (layer_own[...] + after_ref[...]).astype(BF16)
        for job in (first_job, scale_job, second_job):
            job.finish()
        for at in range(max(depth - 2, 0), depth):
            swap(goal_at(at), at % 2, False)
            layer_swap(goal_at(at), at % 2).wait_send()
        layer_line.finish()
        for line in lines:
            line.finish()
        p.finish()

    groups["late"] = [pltpu.SemaphoreType.DMA((2, depth))]
    group = 2 * depth
    return pl.pallas_call(
        kernel,
        in_specs=in_vmem(13) + anywhere(3),
        out_specs=in_vmem(4) + anywhere(2),
        out_shape=[
            jax.ShapeDtypeStruct((rows, model), F32),
            jax.ShapeDtypeStruct((1, model), F32),
            jax.ShapeDtypeStruct((experts, model), F32),
            jax.ShapeDtypeStruct((rows, model), BF16),
            jax.ShapeDtypeStruct((reps, 2, rows, model), BF16),
            jax.ShapeDtypeStruct((reps, 2, 2, 8, rows), F32),
        ],
        scratch_shapes=[item for items in groups.values() for item in items],
        compiler_params=remote_params(2),
        name="join_experts",
    )(
        own, gates, dots, hidden, shared_grad, router_t, shared_in, shared_out, cotangent, after, mixed, scale,
        post_gain, back, weighted, second,
    )


def backward_mixer(
    scales, after_grad, tokens, in_gain, post_grad, router_parts, lengths, taps, head_rows, skip, norm, weight,
    out_weight, low, first, proj, gained, sizes,
):
    reps, depth, channels, width, state, sequences, inner, convolved = sizes
    rows, model = tokens.shape
    part = model // (2 * depth)
    wide = weight.shape[1]
    side = 2 * channels
    heads = channels // width
    per_shard = convolved // (2 * depth)
    quarter = channels // reps
    experts, router_width = router_parts.shape[2:]
    small_width = -(-max(per_shard, channels, router_width) // LANES) * LANES
    small_shape = (16 + experts, small_width)
    stack = (rows, model)
    groups = {
        "early": [pltpu.VMEM((2, rows, channels), F32), pltpu.SemaphoreType.DMA((2,))],
        "stream": [
            pltpu.VMEM(stack, BF16), pltpu.VMEM((2, rows, wide), F32), pltpu.VMEM((2,) + stack, BF16),
            pltpu.SemaphoreType.DMA((3, 2)),
        ],
        "sum": [
            pltpu.VMEM((2,) + stack, BF16), pltpu.VMEM(stack, F32),
            pltpu.VMEM((reps,) + stack, BF16), pltpu.SemaphoreType.DMA((2, reps)),
            pltpu.VMEM((reps - 1,) + stack, BF16), pltpu.SemaphoreType.DMA((2, reps)),
        ],
        "grads": [
            pltpu.VMEM((depth, 2, part, wide), F32), pltpu.VMEM((channels, model), F32),
            pltpu.VMEM((8, channels + 2 * state), F32), pltpu.VMEM((8, LANES), F32), pltpu.VMEM((8, channels), F32),
        ],
        "side": LineSum.scratch(depth, (2, part, channels), BF16) * 2
        + [pltpu.VMEM((2, 2, part, channels), BF16), pltpu.VMEM((2, part, channels), BF16),
           pltpu.SemaphoreType.DMA((2, 2))],
        "common": [pltpu.VMEM((depth, 2, part, wide - side), BF16)]
        + ColumnSum.scratch(depth, (part, wide - side), BF16)
        + [pltpu.VMEM((part, wide - side), F32), pltpu.VMEM((part, wide - side), BF16)],
        "out": [
            pltpu.VMEM((reps, quarter, model), BF16), pltpu.VMEM((reps, quarter, model), BF16),
            pltpu.SemaphoreType.DMA((2, reps)),
        ] + LineSum.scratch(depth, (quarter, model), BF16)
        + [pltpu.VMEM((quarter, model), BF16)],
        "small": [pltpu.VMEM((depth, 2) + small_shape, F32)] + ColumnSum.scratch(depth, small_shape, F32)
        + [pltpu.VMEM(small_shape, F32), pltpu.VMEM((reps,) + small_shape, F32)],
        "end": [pltpu.SemaphoreType.DMA((2, 5, reps)), pltpu.SemaphoreType.DMA((6,)), pltpu.VMEM((2, 32, model), F32)],
    }

    def kernel(scales_ref, grad_ref, x_ref, gain_ref, post_grad_ref, router_ref, lengths_ref, taps_ref,
               heads_ref, skip_ref, norm_ref, weight_ref, out_ref, low_ref, first_ref, proj_ref, gained_ref,
               tokens_grad_ref, side_out, common_out, out_out, small_out, *scratch):
        work, cut = {}, 0
        for name, items in groups.items():
            work[name] = scratch[cut : cut + len(items)]
            cut += len(items)
        p = Place(reps, depth)
        first_slot, proj_slots, low_slots, stream_sems = work["stream"]
        gained_slots, gained_sems = work["early"]

        def first_load(rep, core):
            return pltpu.make_async_copy(first_ref.at[rep, core], first_slot, stream_sems.at[0, 0])

        def proj_load(slot, rep, core):
            return pltpu.make_async_copy(proj_ref.at[rep, core], proj_slots.at[slot], stream_sems.at[1, slot])

        def low_load(slot, rep, core):
            return pltpu.make_async_copy(low_ref.at[rep, core], low_slots.at[slot], stream_sems.at[2, slot])

        def gained_load(slot, rep, core):
            return pltpu.make_async_copy(gained_ref.at[rep, core], gained_slots.at[slot], gained_sems.at[slot])

        def early_place(at):
            return at // 2, lax.rem(at, 2)

        for at in range(2):
            gained_load(at, *early_place(at)).start()
            low_load(at, *early_place(at)).start()
        proj_load(0, p.rep_at(1), 1 - p.core).start()
        proj_load(1, p.rep_at(1), p.core).start()
        p.barrier(plane=True, column=True)
        in_total, out_total, taps_total, heads_total, wide_total = work["grads"]
        for total in work["grads"]:
            total[...] = jnp.zeros_like(total)

        def early(at, carry):
            rep, core = early_place(at)
            turn = lax.rem(at, 2)
            gained_load(turn, rep, core).wait()
            low_load(turn, rep, core).wait()
            scale = column_of(scales_ref[rep, core, 0][0:1, :], rows)
            out_total[...] += mm_tn((gained_slots[turn] * scale).astype(BF16), low_slots[turn])

            @pl.when(at + 2 < 2 * reps)
            def _():
                gained_load(turn, *early_place(at + 2)).start()
                low_load(turn, *early_place(at + 2)).start()

            return carry

        lax.fori_loop(0, 2 * reps, early, 0)
        low_load(0, p.rep_at(1), 1 - p.core).start()
        low_load(1, p.rep_at(1), p.core).start()
        out_parts, out_mid, out_sems, out_into, out_line_sems, out_low = work["out"]
        out_line_total = out_total.at[pl.ds(0, quarter)]
        out_parts[...] = out_total[...].astype(BF16).reshape(reps, quarter, model)
        for distance in range(1, reps):
            rep = p.rep_at(distance)
            p.send(out_parts.at[rep], out_mid.at[p.rep], out_sems.at[0, distance], out_sems.at[1, distance],
                   p.device(rep=rep))
        out_mid[p.rep] = out_parts[p.rep]
        out_job = LineSum(p, lambda at: [out_mid[at]], out_into, out_into, out_line_sems)

        parts, own_part, pair, pair_sems, into, into_sems = work["sum"]

        def swap(distance, rep, start):
            copy = pltpu.make_async_remote_copy(
                src_ref=parts.at[lax.rem(distance, 2)], dst_ref=pair.at[rep], send_sem=pair_sems.at[0, rep],
                recv_sem=pair_sems.at[1, rep], device_id=p.sibling(), device_id_type=MESH_ID,
            )
            copy.start() if start else copy.wait_send()

        def onward(distance, rep, start):
            copy = pltpu.make_async_remote_copy(
                src_ref=pair.at[rep], dst_ref=into.at[distance - 1], send_sem=into_sems.at[0, distance],
                recv_sem=into_sems.at[1, distance], device_id=p.device(rep=rep), device_id_type=MESH_ID,
            )
            copy.start() if start else copy.wait_send()

        def visit(at, carry):
            distance, turn = lax.rem(at // 2 + 1, reps), lax.rem(at, 2)
            rep = p.rep_at(distance)
            core = jnp.where(turn == 0, 1 - p.core, p.core)
            first_load(rep, core).start()
            low_load(turn, rep, core).wait()
            proj_load(turn, rep, core).wait()
            scale = column_of(scales_ref[rep, core, 0][0:1, :], rows)
            pull = column_of(scales_ref[rep, core, 1][0:1, :], rows)
            seg_column, seg_line = segments(lengths_ref[rep, core][0:1, :], sequences, rows)
            block = Block(
                proj_slots[turn], seg_column, seg_line, taps_ref[...], heads_ref[...], channels, width, state
            )
            low_rows = low_slots[turn]
            proj_grad, tap_grads, head_grads, wide_grads = block_back(
                block, low_rows, scale, pull, taps_ref, skip_ref, norm_ref, weight_ref, out_ref[...]
            )
            taps_total[0:5, :] += tap_grads
            heads_total[0:1, :] += head_grads[0]
            heads_total[1:2, :] += head_grads[1]
            wide_total[0:2, :] += wide_grads
            part_rows = mm_nt(proj_grad, weight_ref[...])

            @pl.when(turn == 0)
            def _():
                @pl.when(at >= 4)
                def _():
                    swap(at // 2 - 1, p.rep_at(at // 2 - 1), False)

                parts[lax.rem(distance, 2)] = part_rows.astype(BF16)
                swap(distance, rep, True)

            @pl.when((turn == 1) & (distance == 0))
            def _():
                own_part[...] = part_rows

            @pl.when((turn == 1) & (distance > 0))
            def _():
                p.arrived(pair.at[rep], pair_sems.at[1, rep])
                pair[rep] = add_up(part_rows, pair[rep]).astype(BF16)
                onward(distance, rep, True)

            first_load(rep, core).wait()
            for z in range(depth):
                columns = first_slot[:, 2 * part * z : 2 * part * (z + 1)]
                for start in range(0, wide, 384):
                    piece = slice(start, min(start + 384, wide))
                    in_total[z, :, :, piece] += mm_tn(columns, proj_grad[:, piece]).reshape(2, part, -1)

            @pl.when(at < 2 * reps - 2)
            def _():
                later = p.rep_at(lax.rem(at // 2 + 2, reps))
                proj_load(turn, later, core).start()
                low_load(turn, later, core).start()

            def out_start():
                for distance in range(1, reps):
                    p.arrived(out_mid.at[p.rep_at(distance)], out_sems.at[1, distance])
                out_job.step(0)

            pl.when(at == 1)(out_start)
            for step in range(1, depth - 1):
                pl.when(at == 2 * step + 1)(functools.partial(out_job.step, step))
            return carry

        lax.fori_loop(0, 2 * reps, visit, 0)

        common_parts = work["common"][0]
        common_parts[...] = in_total[:, :, :, side:].astype(BF16)
        common_job = ColumnSum(p, common_parts, *work["common"][1:5])
        side_jobs = []
        for kind in range(2):
            columns = slice(kind * channels, (kind + 1) * channels)
            side_into, side_sems = work["side"][2 * kind : 2 * kind + 2]

            def terms(at, columns=columns):
                return [in_total[at, :, :, columns]]

            side_jobs.append(LineSum(p, terms, side_into, side_into, side_sems))
        side_pair, side_away, side_swap = work["side"][4:]
        side_total = gained_slots.at[:, pl.ds(0, part)]
        side_jobs[0].step(0)

        end_sems, keep_sems, late = work["end"]

        def late_load(source, chunk):
            return pltpu.make_async_copy(
                source.at[pl.ds(32 * chunk, 32)], late.at[chunk % 2], keep_sems.at[3 + chunk % 2]
            )

        late_load(grad_ref, 0).start()
        p.arrived(pair.at[p.rep], pair_sems.at[1, p.rep])
        common_job.ready()
        common_job.step(0)
        side_jobs[1].step(0)
        for distance in range(1, reps):
            p.arrived(into.at[distance - 1], into_sems.at[1, distance])
        gain_grad = jnp.zeros((1, model), F32)
        for start in range(0, rows, 32):
            piece = slice(start, start + 32)
            if start + 32 < rows:
                late_load(grad_ref, start // 32 + 1).start()
            late_load(grad_ref, start // 32).wait()
            first_grad = add_up(
                own_part[piece, :], pair[p.rep, piece, :], *[into[at, piece, :] for at in range(reps - 1)]
            )
            x = x_ref[piece, :].astype(F32)
            x_scale = rms_rows(x)
            gain_grad = gain_grad + jnp.sum(x * first_grad * x_scale, axis=0, keepdims=True)
            weighted = first_grad * gain_ref[...]
            tokens_grad_ref[piece, :] = (
                late[start // 32 % 2]
                + x_scale * weighted
                - x * x_scale**3 * jnp.mean(x * weighted, axis=1, keepdims=True)
            ).astype(BF16)

        small = work["small"][0]
        small[...] = jnp.zeros_like(small)
        team = 2 * p.rep + p.core
        own_taps = taps_total[:, :channels]
        blank = jnp.zeros_like(own_taps)
        taps_full = jnp.concatenate(
            [jnp.where(team == member, own_taps, blank) for member in range(2 * reps)] + [taps_total[:, channels:]],
            axis=1,
        )
        for z in range(depth):
            for core in range(2):
                shard = 2 * z + core
                small[z, core, 0:8, 0:per_shard] = taps_full[:, per_shard * shard : per_shard * (shard + 1)]
                small[z, core, 12:13, 0:part] = post_grad_ref[:, part * shard : part * (shard + 1)]
                small[z, core, 13:14, 0:part] = gain_grad[:, part * shard : part * (shard + 1)]
                small[z, core, 16 : 16 + experts, 0:router_width] = router_ref[z, core]
        lane = lax.broadcasted_iota(jnp.int32, (1, LANES), 1)
        skip_row = jnp.zeros((1, LANES), F32)
        for head in range(heads):
            value = jnp.sum(wide_total[1:2, head * width : (head + 1) * width], axis=1, keepdims=True)
            skip_row = jnp.where(lane == head, value, skip_row)
        small[p.rep, p.core, 8:10, 0:LANES] = heads_total[0:2, :]
        small[p.rep, p.core, 10:11, 0:LANES] = skip_row
        small[p.rep, p.core, 11:12, 0:channels] = wide_total[0:1, :]
        small_job = ColumnSum(p, small, *work["small"][1:5])
        small_job.ready()
        small_job.step(0)
        for at in range(1, depth - 1):
            for job in (common_job, side_jobs[0], small_job):
                job.step(at)

        def to_reps(source, target, at):
            for distance in range(1, reps):
                p.send(source, target.at[p.rep], end_sems.at[0, at, distance], end_sems.at[1, at, distance],
                       p.device(rep=p.rep_at(distance)))

        def from_reps(target, at):
            for distance in range(1, reps):
                p.arrived(target.at[p.rep_at(distance)], end_sems.at[1, at, distance])

        def side_finish(kind):
            side_jobs[kind].total(side_total)
            side_pair[kind, p.core] = side_total[p.core].astype(BF16)
            side_away[kind] = side_total[1 - p.core].astype(BF16)
            p.send(side_away.at[kind], side_pair.at[kind, p.core], side_swap.at[0, kind], side_swap.at[1, kind],
                   p.sibling())
            p.arrived(side_pair.at[kind, 1 - p.core], side_swap.at[1, kind])
            to_reps(side_pair.at[kind], side_out.at[kind], kind)
            return p.local(side_pair.at[kind], side_out.at[kind, p.rep], keep_sems.at[kind])

        keeps = [side_finish(0)]
        common_total, common_low = work["common"][5:]
        common_job.total(common_total)
        common_low[...] = common_total[...].astype(BF16)
        to_reps(common_low, common_out, 2)
        keeps.append(p.local(common_low, common_out.at[p.rep], keep_sems.at[2]))
        out_job.total(out_line_total)
        out_low[...] = out_line_total[...].astype(BF16)
        to_reps(out_low, out_out, 3)
        keeps.append(p.local(out_low, out_out.at[p.rep], keep_sems.at[5]))
        small_total, small_all = work["small"][5:]
        small_job.total(small_total)
        small_all[p.rep] = small_total[...]
        to_reps(small_total, small_all, 4)
        for at in range(1, depth - 1):
            side_jobs[1].step(at)
        keeps.append(side_finish(1))

        from_reps(small_all, 4)
        small_out[...] = add_up(*[small_all[at] for at in range(reps)])
        for at, target in ((0, side_out.at[0]), (1, side_out.at[1]), (2, common_out), (3, out_out)):
            from_reps(target, at)
        for keep in keeps:
            keep.wait()
        for distance in range(reps):
            rep = p.rep_at(distance)
            if distance in (0, reps - 1):
                swap(distance, rep, False)
            if distance:
                onward(distance, rep, False)
        p.finish()

    return pl.pallas_call(
        kernel,
        in_specs=in_vmem(1) + anywhere(1) + in_vmem(11) + anywhere(4),
        out_specs=in_vmem(1) + anywhere(3) + in_vmem(1),
        out_shape=[
            jax.ShapeDtypeStruct((rows, model), BF16),
            jax.ShapeDtypeStruct((2, reps, 2, part, channels), BF16),
            jax.ShapeDtypeStruct((reps, part, wide - side), BF16),
            jax.ShapeDtypeStruct((reps, quarter, model), BF16),
            jax.ShapeDtypeStruct(small_shape, F32),
        ],
        scratch_shapes=[item for items in groups.values() for item in items],
        compiler_params=remote_params(3, 63),
        name="backward_mixer",
    )(
        scales, after_grad, tokens, in_gain, post_grad, router_parts, lengths, taps, head_rows, skip, norm,
        weight, out_weight, low, first, proj, gained,
    )


def assemble_kernel(
    channels, state, heads, side_ref, common_ref, out_ref, small_ref, in_grad_ref, out_grad_ref, *small_refs
):
    reps = side_ref.shape[1]
    inner = 2 * reps * channels
    for kind in range(2):
        for rep in range(reps):
            for core in range(2):
                at = kind * inner + (2 * rep + core) * channels
                in_grad_ref[:, at : at + channels] = side_ref[kind, rep, core].astype(F32)
    in_grad_ref[:, 2 * inner : 2 * inner + 2 * state] = add_up(
        *[common_ref[rep, :, : 2 * state] for rep in range(reps)]
    )
    start = 2 * inner + 2 * state
    tail = []
    for rep in range(reps):
        pair = common_ref[rep, :, 2 * state :].astype(F32)
        tail += [pair[:, :heads], pair[:, LANES // 2 : LANES // 2 + heads]]
    in_grad_ref[:, start:] = jnp.concatenate(tail, axis=1)
    out_grad_ref[...] = out_ref[...].astype(F32).reshape(out_grad_ref.shape)
    router_grad_ref = small_refs[-1]
    for ref, row in zip(small_refs[:-1], (0, 4, 8, 9, 10, 11, 12, 13)):
        ref[...] = small_ref[row : row + ref.shape[0], : ref.shape[1]]
    part, experts = router_grad_ref.shape
    wide = -(-part // LANES) * LANES
    router = jnp.concatenate([small_ref[16:, :wide], jnp.zeros((LANES - experts, wide), F32)], axis=0)
    router_grad_ref[...] = router.T[:part, :experts]


def assemble(side, common, out_rows, small, small_shapes, channels, state, heads):
    reps, part = side.shape[1], side.shape[3]
    columns = 4 * reps * channels + 2 * state + 2 * reps * heads
    model = out_rows.shape[2]
    return pl.pallas_call(
        functools.partial(assemble_kernel, channels, state, heads),
        in_specs=in_vmem(4),
        out_specs=in_vmem(2 + len(small_shapes)),
        out_shape=[
            jax.ShapeDtypeStruct((part, columns), F32),
            jax.ShapeDtypeStruct((channels, model), F32),
        ] + [jax.ShapeDtypeStruct(shape, F32) for shape in small_shapes],
        compiler_params=pltpu.CompilerParams(vmem_limit_bytes=48 * 2**20),
        name="assemble",
    )(side, common, out_rows, small)


def slot_match(table_row, capacity, rows):
    slot = lax.broadcasted_iota(jnp.int32, (capacity, rows), 0).astype(F32) + 1.0
    return table_row == slot


def dispatch_kernel(
    local, capacity, half,
    table_ref, own_ref, second_ref, g_ref, router_ref, in_ref, out_ref,
    buffer_ref, slot_g_ref, gate_slot_ref, gates_ref, hidden_ref, grad_ref, in_grad_ref, out_grad_ref,
    in_total, out_total,
):
    at = pl.program_id(0)
    second, g = second_ref[...], g_ref[...]
    rows = second.shape[0]
    table = table_ref[...].astype(F32)
    used = table > 0.0
    logits = mm_nt(router_ref[...], second)
    top = jnp.max(jnp.where(used, logits, -jnp.inf), axis=0, keepdims=True)
    raw = jnp.where(used, jnp.exp(jnp.where(used, logits - top, 0.0)), 0.0)
    gates = raw / jnp.sum(raw, axis=0, keepdims=True)
    gates_ref[...] = gates
    expert = lax.broadcasted_iota(jnp.int32, gates.shape, 0)
    shard = 2 * lax.axis_index("z") + lax.axis_index("core")
    for i in range(local):
        match = slot_match(own_ref[i : i + 1, :].astype(F32), capacity, rows)
        onehot = match.astype(BF16)
        buffer_ref[i] = mm(onehot, second).astype(BF16)
        slot_g_ref[i] = mm(onehot, g).astype(BF16)
        gate_row = jnp.sum(jnp.where(expert == local * shard + i, gates, 0.0), axis=0, keepdims=True)
        gate_slot = jnp.sum(jnp.where(match, gate_row, 0.0), axis=1, keepdims=True)
        gate_slot_ref[i] = jnp.broadcast_to(gate_slot, (capacity, LANES))
    pre = mm(second, in_ref[...])
    a, b = pre[:, :half], pre[:, half:]
    sig = jax.nn.sigmoid(a)
    hidden = (a * sig * b).astype(BF16)
    hidden_ref[...] = hidden
    back = mm_nt(g, out_ref[...])
    grad = jnp.concatenate([back * b * silu_slope(a, sig), back * a * sig], axis=1).astype(BF16)
    grad_ref[...] = grad

    @pl.when(at == 0)
    def _():
        in_total[...] = jnp.zeros_like(in_total)
        out_total[...] = jnp.zeros_like(out_total)

    in_total[...] += mm_tn(second, grad)
    out_total[...] += mm_tn(hidden, g)

    @pl.when(at == pl.num_programs(0) - 1)
    def _():
        in_grad_ref[...] = in_total[...].astype(BF16)
        out_grad_ref[...] = out_total[...].astype(BF16)


def dispatch(table, own, second, g, router_t, shared_in, shared_out, capacity):
    group, experts, rows = table.shape
    local = own.shape[1]
    model = second.shape[1]
    half = shared_out.shape[0]
    slots = group * capacity

    def by_block(*shape):
        return pl.BlockSpec((None,) + shape, lambda q: (q,) + (0,) * len(shape))

    def by_slots(width):
        return pl.BlockSpec((local, capacity, width), lambda q: (0, q, 0))

    return pl.pallas_call(
        functools.partial(dispatch_kernel, local, capacity, half),
        grid=(group,),
        in_specs=[
            by_block(experts, rows), by_block(local, rows), by_rows((rows, model)), by_rows((rows, model)),
            whole((experts, model)), whole((model, 2 * half)), whole((half, model)),
        ],
        out_specs=[
            by_slots(model), by_slots(model), by_slots(LANES), by_block(experts, rows), by_rows((rows, half)),
            by_rows((rows, 2 * half)), whole((model, 2 * half)), whole((half, model)),
        ],
        out_shape=[
            jax.ShapeDtypeStruct((local, slots, model), BF16),
            jax.ShapeDtypeStruct((local, slots, model), BF16),
            jax.ShapeDtypeStruct((local, slots, LANES), F32),
            jax.ShapeDtypeStruct((group, experts, rows), F32),
            jax.ShapeDtypeStruct((group * rows, half), BF16),
            jax.ShapeDtypeStruct((group * rows, 2 * half), BF16),
            jax.ShapeDtypeStruct((model, 2 * half), BF16),
            jax.ShapeDtypeStruct((half, model), BF16),
        ],
        scratch_shapes=[pltpu.VMEM((model, 2 * half), F32), pltpu.VMEM((half, model), F32)],
        compiler_params=pltpu.CompilerParams(vmem_limit_bytes=56 * 2**20),
        name="dispatch",
    )(table, own, second, g, router_t, shared_in, shared_out)


def experts_kernel(
    buffer_ref, slot_g_ref, gate_ref, in_ref, out_ref,
    weighted_ref, back_ref, dot_ref, in_grad_ref, out_grad_ref, in_total, out_total,
):
    at = pl.program_id(1)
    buffer, weight_in, weight_out = buffer_ref[...], in_ref[...], out_ref[...]
    half = weight_out.shape[0]
    pre = mm(buffer, weight_in)
    a, b = pre[:, :half], pre[:, half:]
    sig = jax.nn.sigmoid(a)
    act = a * sig
    hidden = (act * b).astype(BF16)
    gate = gate_ref[:, 0:1]
    slot_g = slot_g_ref[...].astype(F32)
    result = mm(hidden, weight_out).astype(BF16).astype(F32)
    weighted_ref[...] = (gate * result).astype(BF16)
    dot_ref[...] = jnp.broadcast_to(jnp.sum(slot_g * result, axis=1, keepdims=True), dot_ref.shape)
    result_grad = (gate * slot_g).astype(BF16)
    hidden_grad = mm_nt(result_grad, weight_out)
    pre_grad = jnp.concatenate([hidden_grad * b * silu_slope(a, sig), hidden_grad * act], axis=1).astype(BF16)
    back_ref[...] = mm_nt(pre_grad, weight_in).astype(BF16)

    @pl.when(at == 0)
    def _():
        in_total[...] = jnp.zeros_like(in_total)
        out_total[...] = jnp.zeros_like(out_total)

    in_total[...] += mm_tn(buffer, pre_grad)
    out_total[...] += mm_tn(hidden, result_grad)

    @pl.when(at == pl.num_programs(1) - 1)
    def _():
        in_grad_ref[...] = in_total[...].astype(BF16)
        out_grad_ref[...] = out_total[...].astype(BF16)


def run_experts(buffer, slot_g, gate_slot, expert_in, expert_out, step):
    local, slots, model = buffer.shape
    half = expert_out.shape[1]

    def by_step(width):
        return pl.BlockSpec((None, step, width), lambda i, m: (i, m, 0))

    def by_expert(*shape):
        return pl.BlockSpec((None,) + shape, lambda i, m: (i, 0, 0))

    return pl.pallas_call(
        experts_kernel,
        grid=(local, slots // step),
        in_specs=[
            by_step(model), by_step(model), by_step(LANES), by_expert(model, 2 * half), by_expert(half, model),
        ],
        out_specs=[
            by_step(model), by_step(model), by_step(LANES), by_expert(model, 2 * half), by_expert(half, model),
        ],
        out_shape=[
            jax.ShapeDtypeStruct((local, slots, model), BF16),
            jax.ShapeDtypeStruct((local, slots, model), BF16),
            jax.ShapeDtypeStruct((local, slots, LANES), F32),
            jax.ShapeDtypeStruct((local, model, 2 * half), BF16),
            jax.ShapeDtypeStruct((local, half, model), BF16),
        ],
        scratch_shapes=[pltpu.VMEM((model, 2 * half), F32), pltpu.VMEM((half, model), F32)],
        compiler_params=pltpu.CompilerParams(vmem_limit_bytes=62 * 2**20),
        name="run_experts",
    )(buffer, slot_g, gate_slot, expert_in, expert_out)


def gather(values, axes, axis=0):
    return lax.all_gather(values, axes, axis=axis, tiled=True)


def scatter_sum(values, axes, axis=0):
    return lax.psum_scatter(values, axes, scatter_dimension=axis, tiled=True)


def columns_of(values, start, size, axis=1):
    return lax.dynamic_slice_in_dim(values, start, size, axis=axis)


def shards(
    tokens,
    cotangent,
    dealt_to,
    lengths,
    routes,
    slot_index,
    in_norm,
    in_proj,
    conv_weight,
    conv_bias,
    dt_bias,
    decay_log,
    skip_gain,
    mixer_norm,
    out_proj,
    post_norm,
    router,
    shared_in,
    shared_out,
    expert_in,
    expert_out,
):
    reps, depth = lax.axis_size("rep"), lax.axis_size("z")
    group = 2 * depth
    rep, z, core = lax.axis_index("rep"), lax.axis_index("z"), lax.axis_index("core")
    shard = 2 * z + core
    team = 2 * rep + core
    members = 2 * reps
    rows, model = tokens.shape
    top = routes.shape[1]
    local = expert_in.shape[0]
    experts = local * group
    capacity = rows * top * 4 // (3 * experts)
    inner = mixer_norm.shape[0] * group
    convolved = conv_bias.shape[0] * group
    head_count = dt_bias.shape[0] * group
    width = inner // head_count
    state = (convolved - inner) // 2
    channels = inner // members
    heads = head_count // members
    shared = shared_out.shape[0]
    part = in_norm.shape[0]

    expert_ids = jnp.arange(experts, dtype=jnp.int32)
    table = jnp.sum(
        jnp.where(routes[:, None, :] == expert_ids[None, :, None], slot_index[:, None, :] + 1, 0), axis=2
    ).astype(BF16)
    small = [in_norm[None], conv_weight, conv_bias[None], dt_bias[None], decay_log[None], skip_gain[None],
             mixer_norm[None], post_norm[None], jnp.concatenate([lengths, dealt_to[None]], axis=1)]
    part_wide = -(-part // LANES) * LANES
    table_block = jnp.concatenate([table.T, jnp.pad(router.T, ((0, 0), (0, part_wide - part)))], axis=1)
    pair_heads = 2 * heads
    dt_pair = columns_of(in_proj, inner + convolved + pair_heads * rep, pair_heads)
    blank = jnp.zeros((part, LANES // 2 - heads), BF16)
    common = jnp.concatenate(
        [in_proj[:, 2 * inner : 2 * inner + 2 * state], dt_pair[:, :heads], blank, dt_pair[:, heads:], blank], axis=1
    )

    def pair_of(member):
        return jnp.concatenate(
            [columns_of(in_proj, channels * member, channels), columns_of(in_proj, inner + channels * member, channels)],
            axis=1,
        )

    shared_lanes = -(-shared // LANES) * LANES
    shared_padded = shared_in
    if shared_lanes != shared:
        shared_padded = jnp.pad(
            shared_in.reshape(part, 2 * group, shared), ((0, 0), (0, 0), (0, shared_lanes - shared))
        ).reshape(part, -1)
    sequences = lengths.shape[1]
    (after, mixer_result, scale, lengths_plane, in_gain, post_gain, taps_own, head_rows, skip_own, norm_own, table_all,
     second_column, g_column, first, weight, out_own, projected, gained, shared_in_own) = forward_mixer(
        tokens, cotangent, pair_of(team), pair_of(2 * rep + 1 - core), common, small, table_block,
        out_proj.reshape(reps, channels // reps, model), shared_padded,
        (reps, depth, channels, width, state, sequences, inner, convolved),
    )
    second_column = second_column.reshape(group * rows, model)
    g_column = g_column.reshape(group * rows, model)
    shared_in_own = shared_in_own.reshape(model, 2, shared_lanes)[:, :, :shared].reshape(model, 2 * shared)

    table_all = table_all.reshape(group, experts, -1)
    router_t = table_all[:, :, rows : rows + part].transpose(1, 0, 2).reshape(experts, model)
    dealt_column = shard ^ dealt_to[0] ^ jnp.arange(group, dtype=jnp.int32)
    table_dealt = jnp.take(table_all[:, :, :rows], dealt_column, axis=0)
    table_own = columns_of(table_dealt, local * shard, local)

    buffer, slot_g, gate_slot, gates, shared_hidden, shared_grad, shared_in_grad, shared_out_grad = dispatch(
        table_dealt, table_own, second_column, g_column, router_t, shared_in_own, shared_out, capacity
    )
    weighted, buffer_grad, dots, grad_expert_in, grad_expert_out = run_experts(
        buffer, slot_g, gate_slot, expert_in, expert_out, group * capacity // 2
    )
    shared_in_rows = lax.all_to_all(shared_in_grad, COLUMN, split_axis=0, concat_axis=0, tiled=True)
    shared_in_rows = shared_in_rows.reshape(group, part, 2, shared).transpose(1, 2, 0, 3).reshape(part, -1)
    grad_expert_in, grad_expert_out, grad_shared_out, grad_shared_in = [
        values.astype(F32)
        for values in lax.psum((grad_expert_in, grad_expert_out, shared_out_grad, shared_in_rows), "rep")
    ]

    after_grad, post_grad, router_grad, layer_out, low_plane, scales = join_experts(
        table_own, gates, dots, shared_hidden, shared_grad, router_t, shared_in_own, shared_out, cotangent, after,
        mixer_result, scale, post_gain, buffer_grad, weighted, second_column, inner, reps, depth, capacity,
    )
    router_parts = jnp.pad(
        router_grad.reshape(experts, depth, 2, part).transpose(1, 2, 0, 3), ((0, 0), (0, 0), (0, 0), (0, part_wide - part))
    )
    grad_tokens, side_rows, common_rows, out_rows, small_sum = backward_mixer(
        scales, after_grad, tokens, in_gain, post_grad, router_parts, lengths_plane, taps_own, head_rows, skip_own, norm_own, weight.reshape(model, -1),
        out_own.reshape(channels, model), low_plane, first, projected, gained,
        (reps, depth, channels, width, state, sequences, inner, convolved),
    )
    per_shard = conv_bias.shape[0]
    small_shapes = [
        (4, per_shard), (1, per_shard), (1, heads), (1, heads), (1, heads), (1, channels), (1, part), (1, part),
        (part, experts),
    ]
    (grad_in_proj, grad_out_proj, grad_taps, grad_bias, grad_dt, grad_decay, grad_skip, grad_mixer_norm, grad_post,
     grad_in_norm, grad_router) = assemble(
        side_rows, common_rows, out_rows, small_sum, small_shapes, channels, state, heads
    )
    return (
        layer_out,
        grad_tokens,
        grad_in_norm[0],
        grad_in_proj,
        grad_taps,
        grad_bias[0],
        grad_dt[0],
        grad_decay[0],
        grad_skip[0],
        grad_mixer_norm[0],
        grad_out_proj,
        grad_post[0],
        grad_router,
        grad_shared_in,
        grad_shared_out,
        grad_expert_in,
        grad_expert_out,
    )


def solution(mesh):
    reps, group = mesh.shape["rep"], mesh.shape["shard"]
    split = Mesh(mesh.devices.reshape(reps, group // 2, 2), ALL)
    one, row = P(COLUMN), P(COLUMN, None)
    token = P(ALL, None)
    return jax.shard_map(
        shards,
        mesh=split,
        in_specs=(
            token, token, P(ALL), token, token, token, one, row, P(None, COLUMN), one, one, one, one, one, row,
            one, row, row, row, P(COLUMN, None, None), P(COLUMN, None, None),
        ),
        out_specs=(
            token, token, one, row, P(None, COLUMN), one, one, one, one, one, row, one, row, row, row,
            P(COLUMN, None, None), P(COLUMN, None, None),
        ),
        check_vma=False,
    )
```

```python
import functools

import jax
import jax.numpy as jnp
from jax import lax
from jax.experimental import pallas as pl
from jax.experimental.pallas import tpu as pltpu
from jax.sharding import Mesh
from jax.sharding import PartitionSpec as P

EPS = 1e-05
HIGH = lax.Precision.HIGHEST
F32 = jnp.float32
BF16 = jnp.bfloat16
ALL = ("rep", "z", "core")
COLUMN = ("z", "core")
PLANE = ("rep", "core")
LANES = 128


def rms_rows(values):
    return lax.rsqrt(jnp.mean(values * values, axis=-1, keepdims=True) + EPS)


def mm(left, right):
    return jnp.dot(left, right, preferred_element_type=F32)


def mm_nt(left, right):
    return lax.dot_general(left, right, (((1,), (1,)), ((), ())), preferred_element_type=F32)


def mm_tn(left, right):
    return lax.dot_general(left, right, (((0,), (0,)), ((), ())), preferred_element_type=F32)


def silu_slope(values, sig):
    return sig * (1.0 + values * (1.0 - sig))


def split_two(values):
    high = values.astype(BF16)
    return high, (values - high.astype(F32)).astype(BF16)


def segments(lengths_row, sequences, rows):
    column = lax.broadcasted_iota(jnp.int32, (rows, 1), 0).astype(F32)
    line = lax.broadcasted_iota(jnp.int32, (1, rows), 1).astype(F32)
    end = jnp.zeros((1, 1), F32)
    seg_column, seg_line = jnp.zeros_like(column), jnp.zeros_like(line)
    for at in range(sequences):
        end = end + lengths_row[:, at : at + 1]
        seg_column = seg_column + jnp.where(column >= end, 1.0, 0.0)
        seg_line = seg_line + jnp.where(line >= end, 1.0, 0.0)
    return seg_column, seg_line


class Block:
    def __init__(self, proj, seg_col, seg_row, taps, heads, channels, width, state):
        rows = proj.shape[0]
        self.rows, self.channels, self.width, self.state = rows, channels, width, state
        self.gate = proj[:, :channels]
        self.xbc = proj[:, channels : 2 * channels + 2 * state]
        self.turn = lax.axis_index("core") * (LANES // 2)
        dt_raw = pltpu.roll(proj[:, 2 * channels + 2 * state :], self.turn, 1)
        position = lax.broadcasted_iota(jnp.int32, (rows, 1), 0)
        seg_wide = jnp.broadcast_to(seg_col, (rows, LANES))
        self.masks = []
        conv = taps[4:5, :] + taps[3:4, :] * self.xbc
        for offset in (1, 2, 3):
            before = pltpu.roll(seg_wide, offset, 0)[:, :1]
            mask = jnp.where((before == seg_col) & (position >= offset), 1.0, 0.0)
            self.masks.append(mask)
            conv = conv + taps[3 - offset : 4 - offset, :] * (mask * pltpu.roll(self.xbc, offset, 0))
        self.conv = conv
        self.conv_sig = jax.nn.sigmoid(conv)
        act = conv * self.conv_sig
        self.xin = act[:, :channels]
        self.write = act[:, channels : channels + state]
        self.read = act[:, channels + state :]
        shifted = dt_raw + heads[0:1, :]
        self.step = jnp.maximum(shifted, 0.0) + jnp.log1p(jnp.exp(-jnp.abs(shifted)))
        self.step_sig = jax.nn.sigmoid(shifted)
        self.speed = heads[1:2, :]
        self.rate = -self.step * self.speed
        row_at = lax.broadcasted_iota(jnp.int32, (rows, rows), 0)
        col_at = lax.broadcasted_iota(jnp.int32, (rows, rows), 1)
        self.causal = row_at >= col_at
        self.keep = self.causal & (seg_col == seg_row)
        self.cum = jnp.dot(self.causal.astype(F32), self.rate, precision=HIGH, preferred_element_type=F32)
        self.cum_t = self.cum.T
        scores = lax.dot_general(
            self.read, self.write, (((1,), (1,)), ((), ())), precision=HIGH, preferred_element_type=F32
        )
        self.scores = jnp.where(self.keep, scores, 0.0)

    def groups(self):
        for start in range(0, self.channels, LANES):
            stop = min(start + LANES, self.channels)
            yield start, stop, list(range(start // self.width, (stop - 1) // self.width + 1))

    def spread(self, columns, start, stop, heads):
        lane = lax.broadcasted_iota(jnp.int32, (self.rows, stop - start), 1) + start
        result = jnp.broadcast_to(columns[:, heads[0] : heads[0] + 1], (self.rows, stop - start))
        for head in heads[1:]:
            result = jnp.where(lane >= head * self.width, columns[:, head : head + 1], result)
        return result

    def inside(self, start, stop, head):
        lane = lax.broadcasted_iota(jnp.int32, (self.rows, stop - start), 1) + start
        return (lane >= head * self.width) & (lane < (head + 1) * self.width)

    def decay(self, head):
        gaps = self.cum[:, head : head + 1] - self.cum_t[head : head + 1, :]
        return jnp.exp(jnp.where(self.keep, gaps, 0.0))


def block_back(block, low, scale, pull, taps_ref, skip_ref, norm_ref, weight, out_weight):
    rows, channels = block.rows, block.channels
    normed_grad = mm_nt(low, out_weight)
    taps = taps_ref[...]
    gate_grads, x_grads, norm_grads, skip_grads = [], [], [], []
    step_grad = jnp.zeros((rows, LANES), F32)
    cum_grad = jnp.zeros((rows, LANES), F32)
    cum_grad_t = jnp.zeros((LANES, rows), F32)
    score_grad = jnp.zeros((rows, rows), F32)
    lane_all = lax.broadcasted_iota(jnp.int32, (rows, LANES), 1)
    sub_all = lax.broadcasted_iota(jnp.int32, (LANES, rows), 0)
    for start, stop, heads in block.groups():
        xin = block.xin[:, start:stop]
        spread = block.spread(block.step, start, stop, heads)
        scaled, scaled_rest = split_two(xin * spread)
        scaled_wide = jnp.concatenate([scaled, scaled, scaled_rest], axis=1)
        weights, decays = [], []
        y = None
        for head in heads:
            decays.append(block.decay(head))
            weights.append(block.scores * decays[-1])
            term = mm(weights[-1].astype(BF16), scaled)
            y = term if y is None else jnp.where(block.inside(start, stop, head), term, y)
        skip = skip_ref[:, start:stop]
        y = y + skip * xin
        gate = block.gate[:, start:stop]
        gate_sig = jax.nn.sigmoid(gate)
        gate_act = gate * gate_sig
        mixed = y * gate_act
        q = normed_grad[:, start:stop]
        norm_grads.append(jnp.sum(mixed * scale * q, axis=0, keepdims=True))
        mixed_grad = scale * norm_ref[:, start:stop] * q - mixed * pull
        gate_grads.append(mixed_grad * y * silu_slope(gate, gate_sig))
        y_grad = mixed_grad * gate_act
        skip_grads.append(jnp.sum(y_grad * xin, axis=0, keepdims=True))
        y_low, y_rest = split_two(y_grad)
        scaled_grad = None
        for at, head in enumerate(heads):
            inside = block.inside(start, stop, head)
            term = mm_tn(weights[at].astype(BF16), y_low)
            scaled_grad = term if scaled_grad is None else jnp.where(inside, term, scaled_grad)
            blank = jnp.zeros_like(y_low)
            y_own = jnp.where(inside, y_low, blank)
            pair_grad = mm_nt(
                jnp.concatenate([y_own, jnp.where(inside, y_rest, blank), y_own], axis=1), scaled_wide
            )
            score_grad = score_grad + pair_grad * decays[at]
            exponent_grad = pair_grad * weights[at]
            cum_grad = jnp.where(lane_all == head, jnp.sum(exponent_grad, axis=1, keepdims=True), cum_grad)
            cum_grad_t = jnp.where(sub_all == head, jnp.sum(exponent_grad, axis=0, keepdims=True), cum_grad_t)
        for head in heads:
            inside = block.inside(start, stop, head)
            per_row = jnp.sum(jnp.where(inside, scaled_grad * xin, 0.0), axis=1, keepdims=True)
            step_grad = jnp.where(lane_all == head, per_row, step_grad)
        x_grads.append(scaled_grad * spread + skip * y_grad)
    score_grad = jnp.where(block.keep, score_grad, 0.0).astype(BF16)
    read_grad = mm(score_grad, block.write.astype(BF16))
    write_grad = mm_tn(score_grad, block.read.astype(BF16))
    cum_grad = cum_grad - cum_grad_t.T
    rate_grad = lax.dot_general(
        block.causal.astype(F32), cum_grad, (((0,), (0,)), ((), ())), precision=HIGH, preferred_element_type=F32
    )
    dt_grad = (step_grad - block.speed * rate_grad) * block.step_sig
    head_rows = [jnp.sum(dt_grad, axis=0, keepdims=True), jnp.sum(rate_grad * block.rate, axis=0, keepdims=True)]
    act_grad = jnp.concatenate(x_grads + [write_grad, read_grad], axis=1)
    conv_grad = act_grad * silu_slope(block.conv, block.conv_sig)
    tap_rows = {4: jnp.sum(conv_grad, axis=0, keepdims=True), 3: jnp.sum(conv_grad * block.xbc, axis=0, keepdims=True)}
    xbc_grad = taps[3:4, :] * conv_grad
    for offset in (1, 2, 3):
        masked = conv_grad * block.masks[offset - 1]
        tap_rows[3 - offset] = jnp.sum(masked * pltpu.roll(block.xbc, offset, 0), axis=0, keepdims=True)
        xbc_grad = xbc_grad + taps[3 - offset : 4 - offset, :] * pltpu.roll(masked, rows - offset, 0)
    proj_grad = jnp.concatenate(gate_grads + [xbc_grad, pltpu.roll(dt_grad, block.turn, 1)], axis=1).astype(BF16)
    tap_grads = jnp.concatenate([tap_rows[at] for at in range(5)], axis=0)
    wide_grads = jnp.concatenate(
        [jnp.concatenate(norm_grads, axis=1), jnp.concatenate(skip_grads, axis=1)], axis=0
    )
    return proj_grad, tap_grads, head_rows, wide_grads


def whole(shape):
    return pl.BlockSpec(shape, lambda i: (0,) * len(shape))


def by_rows(shape):
    return pl.BlockSpec(shape, lambda i: (i,) + (0,) * (len(shape) - 1))


MESH_ID = pl.DeviceIdType.MESH


def when(condition, action):
    if condition is True:
        action()
    elif condition is not False:
        pl.when(condition)(action)


class Place:
    def __init__(self, reps, depth):
        self.reps, self.depth = reps, depth
        self.rep, self.z, self.core = lax.axis_index("rep"), lax.axis_index("z"), lax.axis_index("core")
        self.here = {"rep": self.rep, "z": self.z, "core": self.core}
        self.pending = []

    def device(self, **changes):
        return {**self.here, **changes}

    def sibling(self):
        return self.device(core=1 - self.core)

    def rep_at(self, distance):
        result, place = 0, 1
        while place < self.reps:
            mine, other = lax.rem(self.rep // place, 2), lax.rem(distance // place, 2)
            result = result + place * (mine + other - 2 * mine * other)
            place *= 2
        return result

    def in_column(self, distance):
        other = lax.rem(2 * self.z + self.core + distance, 2 * self.depth)
        return self.device(z=other // 2, core=lax.rem(other, 2))

    def barrier(self, plane=False, column=False, whole=False):
        semaphore = pltpu.get_barrier_semaphore()

        def greet(device):
            pl.semaphore_signal(semaphore, inc=1, device_id=device, device_id_type=MESH_ID)

        amount = 1
        if whole:
            for distance in range(1, 2 * self.depth):
                greet(self.in_column(distance))
            amount = 2 * self.depth - 1
        else:
            greet(self.sibling())
        if plane:
            for distance in range(1, self.reps):
                greet(self.device(rep=self.rep_at(distance)))
            amount = amount + self.reps - 1
        if column and not whole:
            above, below = self.z < self.depth - 1, self.z > 0
            when(above, lambda: greet(self.device(z=self.z + 1)))
            when(below, lambda: greet(self.device(z=self.z - 1)))
            amount = amount + jnp.where(above, 1, 0) + jnp.where(below, 1, 0)
        pl.semaphore_wait(semaphore, amount)

    def send(self, source, target, send_sem, recv_sem, device, condition=True):
        copy = pltpu.make_async_remote_copy(
            src_ref=source, dst_ref=target, send_sem=send_sem, recv_sem=recv_sem, device_id=device,
            device_id_type=MESH_ID,
        )
        when(condition, copy.start)
        self.pending.append((condition, copy))

    def local(self, source, target, sem):
        copy = pltpu.make_async_copy(source, target, sem)
        copy.start()
        return copy

    def arrived(self, target, recv_sem, condition=True):
        copy = pltpu.make_async_remote_copy(
            src_ref=target, dst_ref=target, send_sem=recv_sem, recv_sem=recv_sem, device_id=self.sibling(),
            device_id_type=MESH_ID,
        )
        when(condition, copy.wait_recv)

    def finish(self):
        for condition, copy in self.pending:
            when(condition, copy.wait_send)
        self.pending = []


class PlaneGather:
    @staticmethod
    def scratch(reps):
        return [pltpu.SemaphoreType.DMA((4, reps + 1)), pltpu.SemaphoreType.DMA((1,))]

    def __init__(self, place, own, out, sems, local_sem, corner=True):
        self.place, self.out, self.sems = place, out, sems
        p = place
        self.half = own.shape[0] // 2
        self.corner = corner and p.reps == 4 and self.half % 16 == 0
        self.keep = p.local(own, out.at[p.rep, p.core], local_sem.at[0])
        for distance in range(1, 3 if self.corner else p.reps):
            p.send(own, out.at[p.rep, p.core], sems.at[0, distance], sems.at[1, distance],
                   p.device(rep=p.rep_at(distance)))
        p.send(own, out.at[p.rep, p.core], sems.at[2, 0], sems.at[3, 0], p.sibling())

    def part(self, distance, at):
        p = self.place
        return self.out.at[p.rep_at(distance), p.core, pl.ds(self.half * at, self.half)]

    def relay(self):
        p = self.place
        for distance in range(1, p.reps):
            source = self.out.at[p.rep_at(distance), p.core]
            if self.corner and distance == 3:
                for at in range(2):
                    p.arrived(self.part(3, at), self.sems.at[1, 3 + at])
            else:
                p.arrived(source, self.sems.at[1, distance])
            if self.corner and distance < 3:
                piece, at = self.part(distance, distance - 1), distance + 2
                p.send(piece, piece, self.sems.at[0, at], self.sems.at[1, at], p.device(rep=p.rep_at(3 - distance)))
            p.send(source, source, self.sems.at[2, distance], self.sems.at[3, distance], p.sibling())

    def finish(self):
        p = self.place
        self.keep.wait()
        for distance in range(p.reps):
            source = p.rep_at(distance) if distance else p.rep
            p.arrived(self.out.at[source, 1 - p.core], self.sems.at[3, distance])


class ColumnGather:
    @staticmethod
    def scratch(depth):
        return [pltpu.SemaphoreType.DMA((8, depth)), pltpu.SemaphoreType.DMA((1,))]

    def __init__(self, place, own, slot, sems, local_sem, shared=None, keep=True, start=True):
        self.place, self.own, self.slot, self.sems, self.shared = place, own, slot, sems, shared
        self.keep = None
        if keep:
            self.keep = pltpu.make_async_copy(own, slot(place.z), local_sem.at[0])
        if start:
            self.start()

    def start(self):
        if self.keep is not None:
            self.keep.start()
        self.send(0)

    def ends(self, distance):
        p = self.place
        below, above = p.z >= distance, p.z + distance < p.depth
        return below, above, jnp.maximum(p.z - distance, 0), jnp.minimum(p.z + distance, p.depth - 1)

    def copies(self, distance):
        p = self.place

        def copy(source, target, at, device):
            return pltpu.make_async_remote_copy(
                src_ref=source, dst_ref=target, send_sem=self.sems.at[at, distance],
                recv_sem=self.sems.at[at + 1, distance], device_id=device, device_id_type=MESH_ID,
            )

        up, down = p.device(z=p.z + 1), p.device(z=p.z - 1)
        if distance == 0:
            target = self.slot(p.z)
            yield p.z < p.depth - 1, copy(self.own, target, 0, up)
            yield p.z > 0, copy(self.own, target, 2, down)
            if self.shared is not None:
                yield True, copy(self.own, target, 4, p.sibling())
            return
        below, above, low, high = self.ends(distance)
        low, high = self.slot(low), self.slot(high)
        yield below & (p.z < p.depth - 1), copy(low, low, 0, up)
        yield above & (p.z > 0), copy(high, high, 2, down)
        if self.shared is not None:
            yield below, copy(low, low, 4, p.sibling())
            yield above, copy(high, high, 6, p.sibling())

    def send(self, distance):
        for condition, copy in self.copies(distance):
            when(condition, copy.start)

    def hop(self, distance):
        below, above, low, high = self.ends(distance)
        self.place.arrived(self.slot(low), self.sems.at[1, distance - 1], below)
        self.place.arrived(self.slot(high), self.sems.at[3, distance - 1], above)
        self.send(distance)

    def finish(self):
        p = self.place
        if self.keep is not None:
            self.keep.wait()
        if self.shared is not None:
            p.arrived(self.shared(p.z), self.sems.at[5, 0])
            for distance in range(1, p.depth):
                below, above, low, high = self.ends(distance)
                p.arrived(self.shared(low), self.sems.at[5, distance], below)
                p.arrived(self.shared(high), self.sems.at[7, distance], above)
        for distance in range(p.depth):
            for condition, copy in self.copies(distance):
                when(condition, copy.wait_send)


def add_up(*terms):
    total = terms[0].astype(F32)
    for term in terms[1:]:
        total = total + term.astype(F32)
    return total


class PairSwap:
    @staticmethod
    def scratch(count, shape, dtype):
        return [pltpu.VMEM((count,) + shape, dtype), pltpu.SemaphoreType.DMA((2, count))]

    def __init__(self, place, parts, pair, sems, order, own=None):
        self.place, self.parts, self.pair, self.sems, self.own = place, parts, pair, sems, own
        for at in order:
            place.send(parts.at[at, 1 - place.core], pair.at[at], sems.at[0, at], sems.at[1, at], place.sibling())

    def wait(self, at):
        self.place.arrived(self.pair.at[at], self.sems.at[1, at])

    def terms(self, at):
        if self.own is None:
            return [self.parts[at, self.place.core], self.pair[at]]
        slot, sem = self.own
        self.place.local(self.parts.at[at, self.place.core], slot, sem.at[0]).wait()
        return [slot[...], self.pair[at]]


class PlaneSum:
    @staticmethod
    def scratch(reps, shape, dtype):
        return PairSwap.scratch(reps, shape, dtype) + [
            pltpu.VMEM((reps,) + shape, dtype), pltpu.SemaphoreType.DMA((2, reps)),
        ]

    def __init__(self, place, parts, pair, pair_sems, into, sems):
        self.place, self.pair, self.into, self.sems = place, pair, into, sems
        order = [place.rep_at(distance) for distance in range(1, place.reps)] + [place.rep]
        self.swap = PairSwap(place, parts, pair, pair_sems, order)

    def relay(self):
        p = self.place
        for distance in range(1, p.reps):
            rep = p.rep_at(distance)
            self.swap.wait(rep)
            self.pair[rep] = add_up(*self.swap.terms(rep)).astype(self.pair.dtype)
            p.send(self.pair.at[rep], self.into.at[distance], self.sems.at[0, distance], self.sems.at[1, distance],
                   p.device(rep=rep))

    def total(self):
        p = self.place
        self.swap.wait(p.rep)
        terms = self.swap.terms(p.rep)
        for distance in range(1, p.reps):
            p.arrived(self.into.at[distance], self.sems.at[1, distance])
            terms.append(self.into[distance])
        return add_up(*terms)


class LineSum:
    @staticmethod
    def scratch(depth, shape, dtype):
        return [pltpu.VMEM((depth + 1,) + shape, dtype), pltpu.SemaphoreType.DMA((4, depth))]

    def __init__(self, place, terms, out, into, sems):
        self.place, self.terms, self.out, self.into, self.sems = place, terms, out, into, sems

    def moves(self, at):
        p = self.place
        last = p.depth - 1
        for way, towards, goal, first, valid in (
            (0, p.z + 1, last - (at - p.z), p.z == 0, (at >= p.z) & (last - (at - p.z) > p.z)),
            (1, p.z - 1, at - (last - p.z), p.z == last, (at >= last - p.z) & (at - (last - p.z) < p.z)),
        ):
            goal = jnp.clip(goal, 0, last)
            slot = jnp.where(goal == towards, p.depth, goal) if way else goal
            copy = pltpu.make_async_remote_copy(
                src_ref=self.out.at[goal], dst_ref=self.into.at[slot], send_sem=self.sems.at[2 * way, goal],
                recv_sem=self.sems.at[2 * way + 1, goal], device_id=p.device(z=towards), device_id_type=MESH_ID,
            )
            yield way, goal, first, valid, copy

    def step(self, at):
        p = self.place
        for way, goal, first, valid, copy in self.moves(at):
            inner = valid & jnp.logical_not(first)
            p.arrived(self.into.at[goal], self.sems.at[2 * way + 1, goal], inner)

            def start(goal=goal):
                self.out[goal] = add_up(*self.terms(goal)).astype(self.out.dtype)

            def follow(goal=goal):
                self.out[goal] = add_up(*self.terms(goal), self.into[goal]).astype(self.out.dtype)

            when(valid & first, start)
            when(inner, follow)
            when(valid, copy.start)

    def finish(self):
        for at in range(self.place.depth - 1):
            for _, _, _, valid, copy in self.moves(at):
                when(valid, copy.wait_send)

    def total(self, result):
        result[...] = add_up(*self.terms(self.place.z))
        self.gather(result)
        self.finish()

    def gather(self, result):
        p = self.place
        for way, slot, condition in ((0, p.z, p.z > 0), (1, p.depth, p.z < p.depth - 1)):
            p.arrived(self.into.at[slot], self.sems.at[2 * way + 1, p.z], condition)

            def add(slot=slot):
                result[...] += self.into[slot].astype(F32)

            when(condition, add)


class ColumnSum:
    @staticmethod
    def scratch(depth, shape, dtype):
        return PairSwap.scratch(depth, shape, dtype) + LineSum.scratch(depth, shape, dtype)

    def __init__(self, place, parts, pair, pair_sems, into, sems, own=None):
        self.place = place
        order = [lax.rem(place.z + distance, place.depth) for distance in list(range(place.depth - 1, 0, -1)) + [0]]
        self.order = order
        self.swap = PairSwap(place, parts, pair, pair_sems, order, own)
        self.line = LineSum(place, self.swap.terms, pair, into, sems)

    def ready(self):
        for at in self.order:
            self.swap.wait(at)

    def step(self, at):
        self.line.step(at)

    def total(self, result):
        self.line.total(result)


def anywhere(count):
    return [pl.BlockSpec(memory_space=pl.ANY)] * count


def in_vmem(count):
    return [pl.BlockSpec(memory_space=pltpu.VMEM)] * count


def remote_params(identity, mebibytes=60):
    return pltpu.CompilerParams(
        collective_id=identity, has_side_effects=True, vmem_limit_bytes=mebibytes * 2**20
    )


def column_of(row_values, rows):
    return jnp.broadcast_to(row_values, (LANES, rows)).T[:, 0:1]


def row_of(column_values, rows):
    return jnp.broadcast_to(column_values, (rows, LANES)).T[0:8, :]


def forward_mixer(tokens, cotangent, own_pair, other_pair, common, small, table, out_quarters, shared_in, sizes):
    reps, depth, channels, width, state, sequences, inner, convolved = sizes
    rows, model = tokens.shape
    part, side = own_pair.shape
    wide = side + common.shape[1]
    quarter = out_quarters.shape[1]
    vector_width = -(-max(piece.shape[1] for piece in small) // LANES) * LANES
    vector_rows = 16
    group = 2 * depth
    shared = shared_in.shape[1] // (2 * group)
    heads = channels // width
    per_shard = convolved // (2 * depth)

    x_scratch = [pltpu.VMEM((reps, 2, rows, model), BF16)] + PlaneGather.scratch(reps)
    w_scratch = [pltpu.VMEM((depth, 2, part, wide), BF16)] + ColumnGather.scratch(depth) * 3
    v_scratch = [pltpu.VMEM((depth, 2, vector_rows, vector_width), F32)] + ColumnGather.scratch(depth) * 2
    o_scratch = [
        pltpu.VMEM((depth, quarter, model), BF16), pltpu.VMEM((reps, quarter, model), BF16),
    ] + ColumnGather.scratch(depth) + [pltpu.SemaphoreType.DMA((2, max(reps, depth))), pltpu.SemaphoreType.DMA((2,))]
    n_scratch = [pltpu.VMEM((8, LANES), F32)] + PlaneGather.scratch(reps)
    sum_scratch = [
        pltpu.VMEM((reps, rows, model), BF16), pltpu.VMEM((reps, 2, 8, rows), F32),
    ] + PlaneSum.scratch(reps, (rows, model), BF16) + PlaneSum.scratch(reps, (8, rows), F32)
    groups = [x_scratch, w_scratch, v_scratch, o_scratch, n_scratch, sum_scratch]

    def kernel(x_ref, g_ref, own_ref, other_ref, common_ref, table_ref, quarters_ref, shared_ref, *refs):
        small_refs, refs = refs[: len(small)], refs[len(small) :]
        (after_ref, mixed_ref, scale_ref, lengths_ref, in_gain_ref, post_gain_ref, taps_ref, heads_ref, skip_ref,
               norm_ref, table_out, second_out, g_out, first_out, weight_out, out_out, proj_out, mixed_out, shared_out), scratch = refs[:19], refs[19:]
        cut = [0]
        for items in groups:
            cut.append(cut[-1] + len(items))
        x_work, w_work, v_work, o_work, n_work, sum_work = [scratch[i:j] for i, j in zip(cut, cut[1:])]
        (second, second_sems, second_local, g_sems, g_local, proj_buffer, proj_sems, keep_sems,
         own_part, mixed_all, mixed_sems, vectors_ref, shared_sems, shared_local) = scratch[cut[-1]:]
        p = Place(reps, depth)
        vectors_ref[...] = jnp.zeros_like(vectors_ref)
        row = 0
        for piece in small_refs:
            count, size = piece.shape
            vectors_ref[row : row + count, :size] = piece[...].astype(F32)
            row += count
        p.barrier(plane=True, column=True, whole=True)

        x_all, weight_all, vectors_all = x_work[0], w_work[0], v_work[0]

        def left(core):
            return lambda z: weight_all.at[z, core, :, pl.ds(0, side)]

        def right(core):
            return lambda z: weight_all.at[z, core, :, pl.ds(side, wide - side)]

        vector_job = ColumnGather(p, vectors_ref, lambda z: vectors_all.at[z, p.core], v_work[1], v_work[2],
                                  shared=lambda z: vectors_all.at[z, 1 - p.core])
        own_slot, other_slot = left(p.core), left(1 - p.core)
        p.send(other_ref, own_slot(p.z), keep_sems.at[0], keep_sems.at[1], p.sibling())
        job_a = ColumnGather(p, own_ref, own_slot, w_work[1], w_work[2])
        job_c = ColumnGather(p, common_ref, right(p.core), w_work[3], w_work[4], shared=right(1 - p.core))
        x_job = PlaneGather(p, x_ref, x_all, x_work[1], x_work[2])
        p.arrived(other_slot(p.z), keep_sems.at[1])
        job_b = ColumnGather(p, other_slot(p.z), other_slot, w_work[5], w_work[6], keep=False)
        for distance in range(1, depth):
            vector_job.hop(distance)
        vector_job.finish()

        own_row = vectors_all[p.z, p.core].astype(F32)[11:12, :LANES]
        dealt = own_row[:, sequences : sequences + 1]
        lengths_row = jnp.zeros((1, LANES), F32)
        for z in range(depth):
            for core in range(2):
                row = vectors_all[z, core].astype(F32)[11:12, :LANES]
                lengths_row = jnp.where(dealt == float(2 * z + core), row, lengths_row)
        n_work[0][...] = jnp.broadcast_to(lengths_row, (8, LANES))
        n_job = PlaneGather(p, n_work[0], lengths_ref, n_work[1], n_work[2], corner=False)

        pieces = [vectors_all[z, core].astype(F32) for z in range(depth) for core in range(2)]
        in_gain_ref[...] = jnp.concatenate([piece[0:1, :part] for piece in pieces], axis=1)
        post_gain_ref[...] = jnp.concatenate([piece[10:11, :part] for piece in pieces], axis=1)
        taps_full = jnp.concatenate([piece[0:8, :per_shard] for piece in pieces], axis=1)
        taps_full = jnp.concatenate([taps_full[1:6, :], jnp.zeros((3, convolved), F32)], axis=0)
        team = 2 * p.rep + p.core
        taps_own = taps_full[:, :channels]
        for member in range(1, 2 * reps):
            taps_own = jnp.where(team == member, taps_full[:, channels * member : channels * (member + 1)], taps_own)
        taps_ref[...] = jnp.concatenate([taps_own, taps_full[:, inner:]], axis=1)
        own = vectors_all[p.rep, p.core].astype(F32)
        lane = lax.broadcasted_iota(jnp.int32, (1, LANES), 1)
        speed = jnp.where(lane < heads, jnp.exp(jnp.where(lane < heads, own[7:8, :LANES], 0.0)), 0.0)
        heads_ref[...] = jnp.concatenate([own[6:7, :LANES], speed, jnp.zeros((6, LANES), F32)], axis=0)
        norm_ref[...] = own[9:10, :channels]
        wide_lane = lax.broadcasted_iota(jnp.int32, (1, channels), 1)
        skip = jnp.broadcast_to(own[8:9, 0:1], (1, channels))
        for head in range(1, heads):
            skip = jnp.where(wide_lane >= head * width, own[8:9, head : head + 1], skip)
        skip_ref[...] = skip

        n_job.relay()
        mid, out_all, o_sems, o_local, e_sems, e_local = o_work
        late_jobs = []
        for distance in range(1, depth):
            for job in (job_a, job_c, job_b):
                job.hop(distance)
            if distance == min(2, depth - 1):
                x_job.relay()
                late_jobs.append(ColumnGather(p, quarters_ref.at[p.rep], lambda z: mid.at[z], o_sems, o_local))
                late_jobs.append(
                    ColumnGather(p, table_ref, lambda z: table_out.at[z, p.core], v_work[3], v_work[4],
                                 shared=lambda z: table_out.at[z, 1 - p.core])
                )
        job_o, table_job = late_jobs
        shard = 2 * p.z + p.core

        def shared_piece(kind, other):
            start = pl.multiple_of((kind * group + other) * shared, LANES)
            return shared_ref.at[:, pl.ds(start, shared)]

        def shared_slot(kind, other):
            return shared_out.at[other, :, pl.ds(kind * shared, shared)]

        shared_keep = [
            p.local(shared_piece(kind, shard), shared_slot(kind, shard), shared_local.at[kind]) for kind in range(2)
        ]
        for distance in range(1, group):
            goal = p.in_column(distance)
            for kind in range(2):
                p.send(shared_piece(kind, 2 * goal["z"] + goal["core"]), shared_slot(kind, shard),
                       shared_sems.at[2 * kind, distance], shared_sems.at[2 * kind + 1, distance], goal)
        shared_pending, p.pending = p.pending[-2 * (group - 1) :], p.pending[: -2 * (group - 1)]
        job_o.keep.wait()
        job_o.keep = None
        for job in (n_job, x_job, job_a, job_b, job_c):
            job.finish()
        weight_keep = p.local(weight_all, weight_out, e_local.at[0])

        def exchange_copy(goal):
            return pltpu.make_async_remote_copy(
                src_ref=mid.at[goal], dst_ref=out_all.at[p.rep], send_sem=e_sems.at[0, goal],
                recv_sem=e_sems.at[1, p.rep], device_id=p.device(rep=goal), device_id_type=MESH_ID,
            )

        def exchange(goal, condition):
            def own():
                out_all[goal] = mid[goal]

            when(condition & (goal == p.rep), own)
            when(condition & (goal != p.rep), exchange_copy(goal).start)

        def out_tick(distance):
            if distance == 1:
                exchange(p.z, p.z >= 0)
            job_o.hop(distance)
            table_job.hop(distance)
            below, above, low, high = job_o.ends(distance)
            exchange(low, below)
            exchange(high, above)

        def out_wait():
            for rep in range(reps):
                p.arrived(out_all.at[rep], e_sems.at[1, rep], rep != p.rep)

        g_job = ColumnGather(p, g_ref, lambda z: g_out.at[z, p.core], g_sems, g_local,
                             shared=lambda z: g_out.at[z, 1 - p.core], start=False)
        p.finish()
        parts, squares = sum_work[0], sum_work[1]
        pair, pair_sems, into, into_sems = sum_work[2:6]
        s_pair, s_pair_sems, s_into, s_into_sems = sum_work[6:10]

        def swap(rep, start):
            for source, target, sems in (
                (parts.at[rep], pair, pair_sems), (squares.at[rep, 1 - p.core], s_pair, s_pair_sems)
            ):
                copy = pltpu.make_async_remote_copy(
                    src_ref=source, dst_ref=target.at[rep], send_sem=sems.at[0, rep],
                    recv_sem=sems.at[1, rep], device_id=p.sibling(), device_id_type=MESH_ID,
                )
                if start:
                    copy.start()
                else:
                    copy.wait_send()

        corner = reps == 4 and rows % 32 == 0
        half_rows = rows // 2

        def distance_at(index):
            if corner:
                return jnp.where(index == 0, 3, jnp.where(index == 3, 0, index))
            return lax.rem(index + 1, reps)

        def to_corner(start):
            for half, index in ((0, 3), (1, 0)):
                piece = pl.ds(half_rows * half, half_rows)
                copy = pltpu.make_async_remote_copy(
                    src_ref=pair.at[p.rep_at(3), piece], dst_ref=into.at[0, piece],
                    send_sem=into_sems.at[0, index], recv_sem=into_sems.at[1, index],
                    device_id=p.device(rep=p.rep_at(half + 1)), device_id_type=MESH_ID,
                )
                copy.start() if start else copy.wait_send()

        def add_corner(rep, half, index):
            piece = pl.ds(half_rows * half, half_rows)
            p.arrived(into.at[0, piece], into_sems.at[1, index])
            pair[rep, piece, :] = add_up(pair[rep, piece, :], into[0, piece, :]).astype(BF16)

        def onward(distance, rep, start, rows_too=True):
            kinds = [(s_pair, s_into, s_into_sems)] + ([(pair, into, into_sems)] if rows_too else [])
            for values, target, sems in kinds:
                copy = pltpu.make_async_remote_copy(
                    src_ref=values.at[rep], dst_ref=target.at[distance], send_sem=sems.at[0, distance],
                    recv_sem=sems.at[1, distance], device_id=p.device(rep=rep), device_id_type=MESH_ID,
                )
                if start:
                    copy.start()
                else:
                    copy.wait_send()

        def proj_copy(slot, rep, core):
            return pltpu.make_async_copy(proj_buffer.at[slot], proj_out.at[rep, core], proj_sems.at[slot])

        def mixed_copy(at, rep, core):
            return pltpu.make_async_copy(mixed_all.at[at], mixed_out.at[rep, core], mixed_sems.at[at])

        def place_of(at):
            distance = distance_at(at // 2)
            turn = lax.rem(at, 2)
            return distance, p.rep_at(distance), turn, jnp.where(turn == 0, 1 - p.core, p.core)

        def mix(at):
            distance, rep, turn, core = place_of(at)
            x = x_all[rep, core].astype(F32)
            first = (x * rms_rows(x) * in_gain_ref[...]).astype(BF16)
            x_all[rep, core] = first
            proj = mm(first, weight_all[...].reshape(model, wide))

            @pl.when(at >= 2)
            def _():
                proj_copy(turn, rep, core).wait()

            proj_buffer[turn] = proj
            proj_copy(turn, rep, core).start()
            seg_column, seg_line = segments(lengths_ref[rep, core][0:1, :], sequences, rows)
            block = Block(proj, seg_column, seg_line, taps_ref[...], heads_ref[...], channels, width, state)
            mixed = []
            for start, stop, inside in block.groups():
                xin = block.xin[:, start:stop]
                scaled, rest = split_two(xin * block.spread(block.step, start, stop, inside))
                scaled = jnp.concatenate([scaled, scaled, rest], axis=0)
                y = None
                for head in inside:
                    weights, weights_rest = split_two(block.scores * block.decay(head))
                    term = mm(jnp.concatenate([weights, weights_rest, weights], axis=1), scaled)
                    y = term if y is None else jnp.where(block.inside(start, stop, head), term, y)
                gate = block.gate[:, start:stop]
                mixed.append((y + skip_ref[:, start:stop] * xin) * gate * jax.nn.sigmoid(gate))
            mixed = jnp.concatenate(mixed, axis=1)
            squares[rep, core] = row_of(jnp.sum(mixed * mixed, axis=1, keepdims=True), rows)
            mixed_all[at] = mixed * norm_ref[...]
            mixed_copy(at, rep, core).start()

        def put(at):
            distance, rep, turn, core = place_of(at)
            mixed, mixed_rest = split_two(mixed_all[at])
            out_weight = out_all[...].reshape(channels, model)
            part_rows = mm(mixed, out_weight) + mm(mixed_rest, out_weight)

            @pl.when(turn == 0)
            def _():
                parts[rep] = part_rows.astype(BF16)
                swap(rep, True)

            @pl.when((turn == 1) & (distance == 0))
            def _():
                own_part[...] = part_rows

            @pl.when((turn == 1) & (distance > 0))
            def _():
                p.arrived(pair.at[rep], pair_sems.at[1, rep])
                pair[rep] = add_up(part_rows, pair[rep]).astype(BF16)
                p.arrived(s_pair.at[rep], s_pair_sems.at[1, rep])
                s_pair[rep] = add_up(squares[rep, p.core], s_pair[rep])
                if corner:
                    pl.when(distance == 1)(functools.partial(add_corner, rep, 1, 0))
                    pl.when(distance == 2)(functools.partial(add_corner, rep, 0, 3))
                    pl.when(distance < 3)(functools.partial(onward, distance, rep, True))
                    pl.when(distance == 3)(functools.partial(onward, distance, rep, True, False))
                    pl.when(distance == 3)(functools.partial(to_corner, True))
                else:
                    onward(distance, rep, True)

        delay = 4

        def visit(at, carry):
            pl.when(at < 2 * reps)(functools.partial(mix, at))
            for distance in range(1, depth):
                pl.when(at == min(distance - 1, delay - 1))(functools.partial(out_tick, distance))
            pl.when(at == delay - 1)(g_job.start)
            pl.when(at == delay)(out_wait)
            pl.when(at >= delay)(functools.partial(put, at - delay))
            pl.when(at == 2 * delay - 1)(functools.partial(g_job.hop, 1))
            return carry

        lax.fori_loop(0, 2 * reps + delay, visit, 0)
        out_keep = p.local(out_all, out_out, e_local.at[1])
        first_keep = p.local(x_all, first_out, keep_sems.at[2])
        if depth > 2:
            g_job.hop(2)
        p.arrived(pair.at[p.rep], pair_sems.at[1, p.rep])
        p.arrived(s_pair.at[p.rep], s_pair_sems.at[1, p.rep])
        terms, square_terms = [own_part[...], pair[p.rep]], [squares[p.rep, p.core], s_pair[p.rep]]
        for distance in range(1, reps):
            p.arrived(s_into.at[distance], s_into_sems.at[1, distance])
            square_terms.append(s_into[distance])
            if not (corner and distance == 3):
                p.arrived(into.at[distance], into_sems.at[1, distance])
                terms.append(into[distance])
        scale_row = lax.rsqrt(add_up(*square_terms) / inner + EPS)
        scale_ref[...] = scale_row
        mixed = column_of(scale_row[0:1, :], rows) * add_up(*terms)
        mixed_ref[...] = mixed.astype(BF16)
        after = x_ref[...].astype(F32) + mixed
        after_ref[...] = after
        second[...] = (after * rms_rows(after) * post_gain_ref[...]).astype(BF16)
        job = ColumnGather(p, second, lambda z: second_out.at[z, p.core], second_sems, second_local,
                           shared=lambda z: second_out.at[z, 1 - p.core])
        for distance in range(3, depth):
            g_job.hop(distance)
        for distance in range(1, depth):
            job.hop(distance)
        job.finish()
        g_job.finish()
        for distance in range(reps):
            rep = p.rep_at(distance) if distance else p.rep
            swap(rep, False)
            if distance:
                onward(distance, rep, False, not (corner and distance == 3))
        if corner:
            to_corner(False)
        for slot in range(2):
            proj_copy(slot, p.rep, p.core).wait()
        for at in range(2 * reps):
            mixed_copy(at, p.rep, p.core).wait()
        job_o.finish()
        table_job.finish()
        for distance in range(1, group):
            other = lax.rem(shard - distance + group, group)
            for kind in range(2):
                p.arrived(shared_slot(kind, other), shared_sems.at[2 * kind + 1, distance])
        for keep in shared_keep:
            keep.wait()
        p.pending = p.pending + shared_pending
        for goal in range(depth):
            when(goal != p.rep, exchange_copy(goal).wait_send)
        for keep in (weight_keep, out_keep, first_keep):
            keep.wait()
        p.finish()

    return pl.pallas_call(
        kernel,
        in_specs=in_vmem(1) + anywhere(7) + in_vmem(len(small)),
        out_specs=in_vmem(10) + anywhere(9),
        out_shape=[
            jax.ShapeDtypeStruct((rows, model), F32),
            jax.ShapeDtypeStruct((rows, model), BF16),
            jax.ShapeDtypeStruct((8, rows), F32),
            jax.ShapeDtypeStruct((reps, 2, 8, LANES), F32),
            jax.ShapeDtypeStruct((1, model), F32),
            jax.ShapeDtypeStruct((1, model), F32),
            jax.ShapeDtypeStruct((8, channels + 2 * state), F32),
            jax.ShapeDtypeStruct((8, LANES), F32),
            jax.ShapeDtypeStruct((1, channels), F32),
            jax.ShapeDtypeStruct((1, channels), F32),
            jax.ShapeDtypeStruct((depth, 2) + table.shape, BF16),
            jax.ShapeDtypeStruct((depth, 2, rows, model), BF16),
            jax.ShapeDtypeStruct((depth, 2, rows, model), BF16),
            jax.ShapeDtypeStruct((reps, 2, rows, model), BF16),
            jax.ShapeDtypeStruct((depth, 2, part, wide), BF16),
            jax.ShapeDtypeStruct((reps, quarter, model), BF16),
            jax.ShapeDtypeStruct((reps, 2, rows, wide), F32),
            jax.ShapeDtypeStruct((reps, 2, rows, channels), F32),
            jax.ShapeDtypeStruct((group, part, 2 * shared), BF16),
        ],
        scratch_shapes=[item for items in groups for item in items]
        + [pltpu.VMEM((rows, model), BF16)]
        + ColumnGather.scratch(depth) * 2
        + [pltpu.VMEM((2, rows, wide), F32), pltpu.SemaphoreType.DMA((2,)), pltpu.SemaphoreType.DMA((3,)),
           pltpu.VMEM((rows, model), F32), pltpu.VMEM((2 * reps, rows, channels), F32),
           pltpu.SemaphoreType.DMA((2 * reps,)), pltpu.VMEM((vector_rows, vector_width), F32),
           pltpu.SemaphoreType.DMA((4, group)), pltpu.SemaphoreType.DMA((2,))],
        compiler_params=remote_params(0),
        name="forward_mixer",
    )(tokens, cotangent, own_pair, other_pair, common, table, out_quarters, shared_in, *small)


def join_experts(
    own, gates, dots, hidden, shared_grad, router_t, shared_in, shared_out, cotangent, after, mixed, scale, post_gain,
    back, weighted, second, inner, reps, depth, capacity,
):
    rows, model = cotangent.shape
    local = own.shape[1]
    experts = gates.shape[1]
    half_rows = rows // 2
    stack = (rows, model)
    halves = (slice(0, half_rows), slice(half_rows, rows))
    groups = {
        "stream": [
            pltpu.VMEM((2, local, capacity, model), BF16), pltpu.SemaphoreType.DMA((2,)),
            pltpu.VMEM((2,) + stack, BF16), pltpu.SemaphoreType.DMA((2,)),
        ],
        "parts": [
            pltpu.VMEM((2,) + stack, BF16), pltpu.VMEM(stack, F32), pltpu.VMEM((depth, 2, half_rows, model), BF16),
            pltpu.SemaphoreType.DMA((2, depth)),
        ],
        "line": LineSum.scratch(depth, (half_rows, model), BF16) * 2,
        "low": [pltpu.VMEM((2, half_rows, model), BF16), pltpu.VMEM((2, 8, rows), F32)] + PlaneGather.scratch(reps) * 3,
        "logits": [pltpu.VMEM((2 * depth, 2 * experts, rows), BF16)],
        "layer": [
            pltpu.VMEM((2,) + stack, BF16), pltpu.VMEM(stack, F32), pltpu.VMEM((depth,) + stack, BF16),
            pltpu.SemaphoreType.DMA((2, depth)),
        ] + LineSum.scratch(depth, stack, BF16),
    }

    def kernel(own_ref, gates_ref, dots_ref, hidden_ref, shared_ref, router_ref, in_ref, out_ref, g_ref, after_ref,
               mixed_ref, scale_ref, gain_ref, back_ref, weighted_ref, second_ref,
               grad_ref, gain_grad_ref, router_grad_ref, layer_out_ref, low_out, scale_out, *scratch):
        work, cut = {}, 0
        for name, items in groups.items():
            work[name] = scratch[cut : cut + len(items)]
            cut += len(items)
        p = Place(reps, depth)
        slots, slot_sems, second_slots, second_sems = work["stream"]
        parts, own_part, pair, pair_sems = work["parts"]
        logits_all = work["logits"][0]
        layer_parts, layer_own, layer_pair, layer_pair_sems, layer_into, layer_sems = work["layer"]
        lower = p.z < depth // 2

        def goal_at(index):
            distance = lax.rem(depth - 1 - index + depth, depth)
            return jnp.where(lower, lax.rem(p.z + distance, depth), lax.rem(p.z - distance + depth, depth))

        def block_at(at):
            return goal_at(at // 2), jnp.where(lax.rem(at, 2) == 0, 1 - p.core, p.core)

        def load(source, at):
            goal, core = block_at(at)
            start = pl.multiple_of((2 * goal + core) * capacity, capacity)
            return pltpu.make_async_copy(
                source.at[:, pl.ds(start, capacity)], slots.at[lax.rem(at, 2)], slot_sems.at[lax.rem(at, 2)]
            )

        def swap(goal, slot, start):
            for at, piece in enumerate(halves):
                copy = pltpu.make_async_remote_copy(
                    src_ref=parts.at[slot, pl.ds(half_rows * at, half_rows)], dst_ref=pair.at[goal, at],
                    send_sem=pair_sems.at[0, goal] if at == 0 else pair_sems_late.at[0, goal],
                    recv_sem=pair_sems.at[1, goal] if at == 0 else pair_sems_late.at[1, goal],
                    device_id=p.sibling(), device_id_type=MESH_ID,
                )
                copy.start() if start else copy.wait_send()

        pair_sems_late = work["late"][0]
        load(back_ref, 0).start()
        p.barrier(plane=True, column=True)
        expert = lax.broadcasted_iota(jnp.int32, (experts, rows), 0)
        shard = 2 * p.z + p.core

        def matches(q):
            table = own_ref[q].astype(F32)
            return [slot_match(table[i : i + 1, :], capacity, rows) for i in range(local)]

        def visit(at, carry):
            goal, core = block_at(at)
            q = 2 * goal + core
            turn = lax.rem(at, 2)
            load(back_ref, at).wait()

            @pl.when(at + 1 < 2 * depth)
            def _():
                load(back_ref, at + 1).start()

            start = pl.multiple_of(q * rows, rows)
            gates = gates_ref[q]
            gate_grad = jnp.zeros_like(gates)
            total = mm_nt(shared_ref[pl.ds(start, rows), :], in_ref[...])
            for i, match in enumerate(matches(q)):
                total = total + mm_tn(match.astype(BF16), slots[turn, i])
                dot = dots_ref[i, pl.ds(pl.multiple_of(q * capacity, capacity), capacity), 0:1]
                row = jnp.sum(jnp.where(match, dot, 0.0), axis=0, keepdims=True)
                gate_grad = jnp.where(expert == local * shard + i, row, gate_grad)
            logit_grad = gates * (gate_grad - jnp.sum(gates * gate_grad, axis=0, keepdims=True))
            logit_pair = jnp.concatenate(split_two(logit_grad), axis=0)
            logits_all[q] = logit_pair
            total = total + mm_tn(logit_pair, jnp.concatenate([router_ref[...], router_ref[...]], axis=0))

            @pl.when(turn == 0)
            def _():
                slot = lax.rem(at // 2, 2)

                @pl.when(at >= 4)
                def _():
                    swap(goal_at(at // 2 - 2), slot, False)

                parts[slot] = total.astype(BF16)
                swap(goal, slot, True)

            @pl.when(turn == 1)
            def _():
                p.arrived(pair.at[goal, 0], pair_sems.at[1, goal])
                p.arrived(pair.at[goal, 1], pair_sems_late.at[1, goal])

                @pl.when(goal == p.z)
                def _():
                    for index, piece in enumerate(halves):
                        own_part[piece, :] = add_up(total[piece, :], pair[goal, index])

                @pl.when(goal != p.z)
                def _():
                    for index, piece in enumerate(halves):
                        pair[goal, index] = add_up(total[piece, :], pair[goal, index]).astype(BF16)

            return carry

        lines = []
        for index in range(2):
            view = pair.at[:, index]
            into, sems = work["line"][2 * index : 2 * index + 2]

            def terms(goal, view=view, index=index):
                return [view[goal]]

            lines.append(LineSum(p, terms, view, into, sems))

        for step in range(depth - 1):
            lax.fori_loop(2 * step, 2 * step + 2, visit, 0)
            lines[0].step(step)
        for step in range(depth - 1):
            lines[1].step(step)
        lax.fori_loop(2 * depth - 2, 2 * depth, visit, 0)

        low, scales = work["low"][:2]
        gather_sems = work["low"][2:]
        gain_grad_ref[...] = jnp.zeros_like(gain_grad_ref)
        row_dots = []

        def norm_back(index):
            piece = halves[index]
            into = lines[index].into
            grad_ref[piece, :] = own_part[piece, :]
            lines[index].gather(grad_ref.at[pl.ds(half_rows * index, half_rows)])
            second_grad = grad_ref[piece, :]
            after_rows = after_ref[piece, :]
            after_scale = rms_rows(after_rows)
            gain_grad_ref[...] += jnp.sum(after_rows * second_grad * after_scale, axis=0, keepdims=True)
            weighted = second_grad * gain_ref[...]
            after_grad = (
                g_ref[piece, :].astype(F32)
                + after_scale * weighted
                - after_rows * after_scale**3 * jnp.mean(after_rows * weighted, axis=1, keepdims=True)
            )
            grad_ref[piece, :] = after_grad
            after_low = after_grad.astype(BF16)
            low[index] = after_low
            row_dots.append(
                jnp.sum(after_low.astype(F32) * mixed_ref[piece, :].astype(F32), axis=1, keepdims=True)
            )
            return PlaneGather(p, low.at[index], low_out.at[:, :, pl.ds(half_rows * index, half_rows)],
                               *gather_sems[2 * index : 2 * index + 2])

        first_job = norm_back(0)

        def layer_load(at):
            q = block_at(at)
            start = pl.multiple_of((2 * q[0] + q[1]) * rows, rows)
            return pltpu.make_async_copy(
                second_ref.at[pl.ds(start, rows)], second_slots.at[lax.rem(at, 2)], second_sems.at[lax.rem(at, 2)]
            )

        def layer_swap(goal, slot):
            return pltpu.make_async_remote_copy(
                src_ref=layer_parts.at[slot], dst_ref=layer_pair.at[goal], send_sem=layer_pair_sems.at[0, goal],
                recv_sem=layer_pair_sems.at[1, goal], device_id=p.sibling(), device_id_type=MESH_ID,
            )

        def layer_visit(at, carry):
            goal, core = block_at(at)
            q = 2 * goal + core
            turn = lax.rem(at, 2)
            load(weighted_ref, at).wait()
            layer_load(at).wait()

            @pl.when(at + 1 < 2 * depth)
            def _():
                load(weighted_ref, at + 1).start()
                layer_load(at + 1).start()

            total = mm(hidden_ref[pl.ds(pl.multiple_of(q * rows, rows), rows), :], out_ref[...])
            for i, match in enumerate(matches(q)):
                total = total + mm_tn(match.astype(BF16), slots[turn, i])

            @pl.when(turn == 0)
            def _():
                slot = lax.rem(at // 2, 2)

                @pl.when(at >= 4)
                def _():
                    layer_swap(goal_at(at // 2 - 2), slot).wait_send()

                layer_parts[slot] = total.astype(BF16)
                layer_swap(goal, slot).start()

            @pl.when(turn == 1)
            def _():
                p.arrived(layer_pair.at[goal], layer_pair_sems.at[1, goal])

                @pl.when(goal == p.z)
                def _():
                    layer_own[...] = add_up(total, layer_pair[goal])

                @pl.when(goal != p.z)
                def _():
                    layer_pair[goal] = add_up(total, layer_pair[goal]).astype(BF16)

            both = mm(logits_all[q], second_slots[turn])
            router_grad_ref[...] += both[:experts, :] + both[experts:, :]
            return carry

        router_grad_ref[...] = jnp.zeros_like(router_grad_ref)
        load(weighted_ref, 0).start()
        layer_load(0).start()
        lax.fori_loop(0, 2 * depth, layer_visit, 0)
        first_job.relay()
        second_job = norm_back(1)
        layer_line = LineSum(p, lambda goal: [layer_pair[goal]], layer_pair, layer_into, layer_sems)
        layer_line.step(0)
        dot_row = row_of(jnp.concatenate(row_dots, axis=0), rows)
        scale_row = scale_ref[...]
        scales[0] = scale_row
        scales[1] = scale_row**2 * dot_row / inner
        scale_job = PlaneGather(p, scales, scale_out, *gather_sems[4:6], corner=False)
        for step in range(1, depth - 1):
            layer_line.step(step)
        scale_job.relay()
        second_job.relay()
        layer_line.gather(layer_own)
        layer_out_ref[...] = (layer_own[...] + after_ref[...]).astype(BF16)
        for job in (first_job, scale_job, second_job):
            job.finish()
        for at in range(max(depth - 2, 0), depth):
            swap(goal_at(at), at % 2, False)
            layer_swap(goal_at(at), at % 2).wait_send()
        layer_line.finish()
        for line in lines:
            line.finish()
        p.finish()

    groups["late"] = [pltpu.SemaphoreType.DMA((2, depth))]
    group = 2 * depth
    return pl.pallas_call(
        kernel,
        in_specs=in_vmem(13) + anywhere(3),
        out_specs=in_vmem(4) + anywhere(2),
        out_shape=[
            jax.ShapeDtypeStruct((rows, model), F32),
            jax.ShapeDtypeStruct((1, model), F32),
            jax.ShapeDtypeStruct((experts, model), F32),
            jax.ShapeDtypeStruct((rows, model), BF16),
            jax.ShapeDtypeStruct((reps, 2, rows, model), BF16),
            jax.ShapeDtypeStruct((reps, 2, 2, 8, rows), F32),
        ],
        scratch_shapes=[item for items in groups.values() for item in items],
        compiler_params=remote_params(2),
        name="join_experts",
    )(
        own, gates, dots, hidden, shared_grad, router_t, shared_in, shared_out, cotangent, after, mixed, scale,
        post_gain, back, weighted, second,
    )


def backward_mixer(
    scales, after_grad, tokens, in_gain, post_grad, router_parts, lengths, taps, head_rows, skip, norm, weight,
    out_weight, low, first, proj, gained, sizes,
):
    reps, depth, channels, width, state, sequences, inner, convolved = sizes
    rows, model = tokens.shape
    part = model // (2 * depth)
    wide = weight.shape[1]
    side = 2 * channels
    heads = channels // width
    per_shard = convolved // (2 * depth)
    quarter = channels // reps
    experts, router_width = router_parts.shape[2:]
    small_width = -(-max(per_shard, channels, router_width) // LANES) * LANES
    small_shape = (16 + experts, small_width)
    stack = (rows, model)
    corner = reps == 4 and rows % 32 == 0
    half_rows = rows // 2
    groups = {
        "early": [pltpu.VMEM((2, rows, channels), F32), pltpu.SemaphoreType.DMA((2,))],
        "stream": [
            pltpu.VMEM(stack, BF16), pltpu.VMEM((2, rows, wide), F32), pltpu.VMEM((2,) + stack, BF16),
            pltpu.SemaphoreType.DMA((3, 2)),
        ],
        "sum": [
            pltpu.VMEM((2,) + stack, BF16), pltpu.VMEM(stack, F32),
            pltpu.VMEM((reps,) + stack, BF16), pltpu.SemaphoreType.DMA((2, reps)),
            pltpu.VMEM((2 if corner else reps - 1,) + stack, BF16), pltpu.SemaphoreType.DMA((2, reps)),
            pltpu.VMEM((2, half_rows, model), BF16),
        ],
        "grads": [
            pltpu.VMEM((depth, 2, part, wide), F32), pltpu.VMEM((channels, model), F32),
            pltpu.VMEM((8, channels + 2 * state), F32), pltpu.VMEM((8, LANES), F32), pltpu.VMEM((8, channels), F32),
        ],
        "side": LineSum.scratch(depth, (2, part, channels), BF16) * 2
        + [pltpu.VMEM((2, 2, part, channels), BF16), pltpu.VMEM((2, part, channels), BF16),
           pltpu.SemaphoreType.DMA((2, 2))],
        "common": [pltpu.VMEM((depth, 2, part, wide - side), BF16)]
        + ColumnSum.scratch(depth, (part, wide - side), BF16)
        + [pltpu.VMEM((part, wide - side), F32), pltpu.VMEM((part, wide - side), BF16)],
        "out": [
            pltpu.VMEM((reps, quarter, model), BF16), pltpu.VMEM((reps, quarter, model), BF16),
            pltpu.SemaphoreType.DMA((2, reps)),
        ] + LineSum.scratch(depth, (quarter, model), BF16)
        + [pltpu.VMEM((quarter, model), BF16)],
        "small": [pltpu.VMEM((depth, 2) + small_shape, F32)] + ColumnSum.scratch(depth, small_shape, F32)
        + [pltpu.VMEM(small_shape, F32), pltpu.VMEM((reps,) + small_shape, F32)],
        "end": [pltpu.SemaphoreType.DMA((2, 5, reps)), pltpu.SemaphoreType.DMA((6,)), pltpu.VMEM((2, 32, model), F32)],
    }

    def kernel(scales_ref, grad_ref, x_ref, gain_ref, post_grad_ref, router_ref, lengths_ref, taps_ref,
               heads_ref, skip_ref, norm_ref, weight_ref, out_ref, low_ref, first_ref, proj_ref, gained_ref,
               tokens_grad_ref, side_out, common_out, out_out, small_out, *scratch):
        work, cut = {}, 0
        for name, items in groups.items():
            work[name] = scratch[cut : cut + len(items)]
            cut += len(items)
        p = Place(reps, depth)
        first_slot, proj_slots, low_slots, stream_sems = work["stream"]
        gained_slots, gained_sems = work["early"]

        def first_load(rep, core):
            return pltpu.make_async_copy(first_ref.at[rep, core], first_slot, stream_sems.at[0, 0])

        def proj_load(slot, rep, core):
            return pltpu.make_async_copy(proj_ref.at[rep, core], proj_slots.at[slot], stream_sems.at[1, slot])

        def low_load(slot, rep, core):
            return pltpu.make_async_copy(low_ref.at[rep, core], low_slots.at[slot], stream_sems.at[2, slot])

        def gained_load(slot, rep, core):
            return pltpu.make_async_copy(gained_ref.at[rep, core], gained_slots.at[slot], gained_sems.at[slot])

        def early_place(at):
            return at // 2, lax.rem(at, 2)

        for at in range(2):
            gained_load(at, *early_place(at)).start()
            low_load(at, *early_place(at)).start()
        def distance_at(index):
            if corner:
                return jnp.where(index == 0, 3, jnp.where(index == 3, 0, index))
            return lax.rem(index + 1, reps)

        opening = p.rep_at(distance_at(0))
        proj_load(0, opening, 1 - p.core).start()
        proj_load(1, opening, p.core).start()
        p.barrier(plane=True, column=True)
        in_total, out_total, taps_total, heads_total, wide_total = work["grads"]
        for total in work["grads"]:
            total[...] = jnp.zeros_like(total)

        def early(at, carry):
            rep, core = early_place(at)
            turn = lax.rem(at, 2)
            gained_load(turn, rep, core).wait()
            low_load(turn, rep, core).wait()
            scale = column_of(scales_ref[rep, core, 0][0:1, :], rows)
            out_total[...] += mm_tn((gained_slots[turn] * scale).astype(BF16), low_slots[turn])

            @pl.when(at + 2 < 2 * reps)
            def _():
                gained_load(turn, *early_place(at + 2)).start()
                low_load(turn, *early_place(at + 2)).start()

            return carry

        lax.fori_loop(0, 2 * reps, early, 0)
        low_load(0, opening, 1 - p.core).start()
        low_load(1, opening, p.core).start()
        out_parts, out_mid, out_sems, out_into, out_line_sems, out_low = work["out"]
        out_line_total = out_total.at[pl.ds(0, quarter)]
        out_parts[...] = out_total[...].astype(BF16).reshape(reps, quarter, model)
        for distance in range(1, reps):
            rep = p.rep_at(distance)
            p.send(out_parts.at[rep], out_mid.at[p.rep], out_sems.at[0, distance], out_sems.at[1, distance],
                   p.device(rep=rep))
        out_mid[p.rep] = out_parts[p.rep]
        out_job = LineSum(p, lambda at: [out_mid[at]], out_into, out_into, out_line_sems)

        parts, own_part, pair, pair_sems, into, into_sems, extra = work["sum"]

        def swap(index, start):
            rep = p.rep_at(distance_at(index))
            copy = pltpu.make_async_remote_copy(
                src_ref=parts.at[lax.rem(index, 2)], dst_ref=pair.at[rep], send_sem=pair_sems.at[0, rep],
                recv_sem=pair_sems.at[1, rep], device_id=p.sibling(), device_id_type=MESH_ID,
            )
            copy.start() if start else copy.wait_send()

        def onward(distance, rep, start):
            copy = pltpu.make_async_remote_copy(
                src_ref=pair.at[rep], dst_ref=into.at[distance - 1], send_sem=into_sems.at[0, distance],
                recv_sem=into_sems.at[1, distance], device_id=p.device(rep=rep), device_id_type=MESH_ID,
            )
            copy.start() if start else copy.wait_send()

        def to_corner(start):
            for half, index in ((0, 3), (1, 0)):
                copy = pltpu.make_async_remote_copy(
                    src_ref=pair.at[p.rep_at(3), pl.ds(half_rows * half, half_rows)], dst_ref=extra.at[half],
                    send_sem=into_sems.at[0, index], recv_sem=into_sems.at[1, index],
                    device_id=p.device(rep=p.rep_at(half + 1)), device_id_type=MESH_ID,
                )
                copy.start() if start else copy.wait_send()

        def add_corner(rep, half, index):
            piece = pl.ds(half_rows * half, half_rows)
            p.arrived(extra.at[half], into_sems.at[1, index])
            pair[rep, piece, :] = add_up(pair[rep, piece, :], extra[half]).astype(BF16)

        def visit(at, carry):
            distance, turn = distance_at(at // 2), lax.rem(at, 2)
            rep = p.rep_at(distance)
            core = jnp.where(turn == 0, 1 - p.core, p.core)
            first_load(rep, core).start()
            low_load(turn, rep, core).wait()
            proj_load(turn, rep, core).wait()
            scale = column_of(scales_ref[rep, core, 0][0:1, :], rows)
            pull = column_of(scales_ref[rep, core, 1][0:1, :], rows)
            seg_column, seg_line = segments(lengths_ref[rep, core][0:1, :], sequences, rows)
            block = Block(
                proj_slots[turn], seg_column, seg_line, taps_ref[...], heads_ref[...], channels, width, state
            )
            low_rows = low_slots[turn]
            proj_grad, tap_grads, head_grads, wide_grads = block_back(
                block, low_rows, scale, pull, taps_ref, skip_ref, norm_ref, weight_ref, out_ref[...]
            )
            taps_total[0:5, :] += tap_grads
            heads_total[0:1, :] += head_grads[0]
            heads_total[1:2, :] += head_grads[1]
            wide_total[0:2, :] += wide_grads
            part_rows = mm_nt(proj_grad, weight_ref[...])

            @pl.when(turn == 0)
            def _():
                @pl.when(at >= 4)
                def _():
                    swap(at // 2 - 2, False)

                parts[lax.rem(at // 2, 2)] = part_rows.astype(BF16)
                swap(at // 2, True)

            @pl.when((turn == 1) & (distance == 0))
            def _():
                own_part[...] = part_rows

            @pl.when((turn == 1) & (distance > 0))
            def _():
                p.arrived(pair.at[rep], pair_sems.at[1, rep])
                pair[rep] = add_up(part_rows, pair[rep]).astype(BF16)
                if corner:
                    pl.when(distance == 3)(functools.partial(to_corner, True))
                    pl.when(distance == 1)(functools.partial(add_corner, rep, 1, 0))
                    pl.when(distance == 2)(functools.partial(add_corner, rep, 0, 3))
                    pl.when(distance < 3)(functools.partial(onward, distance, rep, True))
                else:
                    onward(distance, rep, True)

            first_load(rep, core).wait()
            for z in range(depth):
                columns = first_slot[:, 2 * part * z : 2 * part * (z + 1)]
                for start in range(0, wide, 384):
                    piece = slice(start, min(start + 384, wide))
                    in_total[z, :, :, piece] += mm_tn(columns, proj_grad[:, piece]).reshape(2, part, -1)

            @pl.when(at < 2 * reps - 2)
            def _():
                later = p.rep_at(distance_at(at // 2 + 1))
                proj_load(turn, later, core).start()
                low_load(turn, later, core).start()

            def out_start():
                for distance in range(1, reps):
                    p.arrived(out_mid.at[p.rep_at(distance)], out_sems.at[1, distance])
                out_job.step(0)

            pl.when(at == 1)(out_start)
            for step in range(1, depth - 1):
                pl.when(at == 2 * step + 1)(functools.partial(out_job.step, step))
            return carry

        lax.fori_loop(0, 2 * reps, visit, 0)

        common_parts = work["common"][0]
        common_parts[...] = in_total[:, :, :, side:].astype(BF16)
        common_job = ColumnSum(p, common_parts, *work["common"][1:5])
        side_jobs = []
        for kind in range(2):
            columns = slice(kind * channels, (kind + 1) * channels)
            side_into, side_sems = work["side"][2 * kind : 2 * kind + 2]

            def terms(at, columns=columns):
                return [in_total[at, :, :, columns]]

            side_jobs.append(LineSum(p, terms, side_into, side_into, side_sems))
        side_pair, side_away, side_swap = work["side"][4:]
        side_total = gained_slots.at[:, pl.ds(0, part)]
        side_jobs[0].step(0)

        end_sems, keep_sems, late = work["end"]

        def late_load(source, chunk):
            return pltpu.make_async_copy(
                source.at[pl.ds(32 * chunk, 32)], late.at[chunk % 2], keep_sems.at[3 + chunk % 2]
            )

        late_load(grad_ref, 0).start()
        p.arrived(pair.at[p.rep], pair_sems.at[1, p.rep])
        common_job.ready()
        common_job.step(0)
        side_jobs[1].step(0)
        sources = 2 if corner else reps - 1
        for distance in range(1, sources + 1):
            p.arrived(into.at[distance - 1], into_sems.at[1, distance])
        gain_grad = jnp.zeros((1, model), F32)
        for start in range(0, rows, 32):
            piece = slice(start, start + 32)
            if start + 32 < rows:
                late_load(grad_ref, start // 32 + 1).start()
            late_load(grad_ref, start // 32).wait()
            first_grad = add_up(
                own_part[piece, :], pair[p.rep, piece, :], *[into[at, piece, :] for at in range(sources)]
            )
            x = x_ref[piece, :].astype(F32)
            x_scale = rms_rows(x)
            gain_grad = gain_grad + jnp.sum(x * first_grad * x_scale, axis=0, keepdims=True)
            weighted = first_grad * gain_ref[...]
            tokens_grad_ref[piece, :] = (
                late[start // 32 % 2]
                + x_scale * weighted
                - x * x_scale**3 * jnp.mean(x * weighted, axis=1, keepdims=True)
            ).astype(BF16)

        small = work["small"][0]
        small[...] = jnp.zeros_like(small)
        team = 2 * p.rep + p.core
        own_taps = taps_total[:, :channels]
        blank = jnp.zeros_like(own_taps)
        taps_full = jnp.concatenate(
            [jnp.where(team == member, own_taps, blank) for member in range(2 * reps)] + [taps_total[:, channels:]],
            axis=1,
        )
        for z in range(depth):
            for core in range(2):
                shard = 2 * z + core
                small[z, core, 0:8, 0:per_shard] = taps_full[:, per_shard * shard : per_shard * (shard + 1)]
                small[z, core, 12:13, 0:part] = post_grad_ref[:, part * shard : part * (shard + 1)]
                small[z, core, 13:14, 0:part] = gain_grad[:, part * shard : part * (shard + 1)]
                small[z, core, 16 : 16 + experts, 0:router_width] = router_ref[z, core]
        lane = lax.broadcasted_iota(jnp.int32, (1, LANES), 1)
        skip_row = jnp.zeros((1, LANES), F32)
        for head in range(heads):
            value = jnp.sum(wide_total[1:2, head * width : (head + 1) * width], axis=1, keepdims=True)
            skip_row = jnp.where(lane == head, value, skip_row)
        small[p.rep, p.core, 8:10, 0:LANES] = heads_total[0:2, :]
        small[p.rep, p.core, 10:11, 0:LANES] = skip_row
        small[p.rep, p.core, 11:12, 0:channels] = wide_total[0:1, :]
        small_job = ColumnSum(p, small, *work["small"][1:5])
        small_job.ready()
        small_job.step(0)
        for at in range(1, depth - 1):
            for job in (common_job, side_jobs[0], small_job):
                job.step(at)

        def to_reps(source, target, at):
            for distance in range(1, reps):
                p.send(source, target.at[p.rep], end_sems.at[0, at, distance], end_sems.at[1, at, distance],
                       p.device(rep=p.rep_at(distance)))

        def from_reps(target, at):
            for distance in range(1, reps):
                p.arrived(target.at[p.rep_at(distance)], end_sems.at[1, at, distance])

        def side_finish(kind):
            side_jobs[kind].total(side_total)
            side_pair[kind, p.core] = side_total[p.core].astype(BF16)
            side_away[kind] = side_total[1 - p.core].astype(BF16)
            p.send(side_away.at[kind], side_pair.at[kind, p.core], side_swap.at[0, kind], side_swap.at[1, kind],
                   p.sibling())
            p.arrived(side_pair.at[kind, 1 - p.core], side_swap.at[1, kind])
            to_reps(side_pair.at[kind], side_out.at[kind], kind)
            return p.local(side_pair.at[kind], side_out.at[kind, p.rep], keep_sems.at[kind])

        keeps = [side_finish(0)]
        common_total, common_low = work["common"][5:]
        common_job.total(common_total)
        common_low[...] = common_total[...].astype(BF16)
        to_reps(common_low, common_out, 2)
        keeps.append(p.local(common_low, common_out.at[p.rep], keep_sems.at[2]))
        out_job.total(out_line_total)
        out_low[...] = out_line_total[...].astype(BF16)
        to_reps(out_low, out_out, 3)
        keeps.append(p.local(out_low, out_out.at[p.rep], keep_sems.at[5]))
        small_total, small_all = work["small"][5:]
        small_job.total(small_total)
        small_all[p.rep] = small_total[...]
        to_reps(small_total, small_all, 4)
        for at in range(1, depth - 1):
            side_jobs[1].step(at)
        keeps.append(side_finish(1))

        from_reps(small_all, 4)
        small_out[...] = add_up(*[small_all[at] for at in range(reps)])
        for at, target in ((0, side_out.at[0]), (1, side_out.at[1]), (2, common_out), (3, out_out)):
            from_reps(target, at)
        for keep in keeps:
            keep.wait()
        for index in (reps - 2, reps - 1):
            swap(index, False)
        for distance in range(1, sources + 1):
            onward(distance, p.rep_at(distance), False)
        if corner:
            to_corner(False)
        p.finish()

    return pl.pallas_call(
        kernel,
        in_specs=in_vmem(1) + anywhere(1) + in_vmem(11) + anywhere(4),
        out_specs=in_vmem(1) + anywhere(3) + in_vmem(1),
        out_shape=[
            jax.ShapeDtypeStruct((rows, model), BF16),
            jax.ShapeDtypeStruct((2, reps, 2, part, channels), BF16),
            jax.ShapeDtypeStruct((reps, part, wide - side), BF16),
            jax.ShapeDtypeStruct((reps, quarter, model), BF16),
            jax.ShapeDtypeStruct(small_shape, F32),
        ],
        scratch_shapes=[item for items in groups.values() for item in items],
        compiler_params=remote_params(3, 63),
        name="backward_mixer",
    )(
        scales, after_grad, tokens, in_gain, post_grad, router_parts, lengths, taps, head_rows, skip, norm,
        weight, out_weight, low, first, proj, gained,
    )


def assemble_kernel(
    channels, state, heads, side_ref, common_ref, out_ref, small_ref, in_grad_ref, out_grad_ref, *small_refs
):
    reps = side_ref.shape[1]
    inner = 2 * reps * channels
    for kind in range(2):
        for rep in range(reps):
            for core in range(2):
                at = kind * inner + (2 * rep + core) * channels
                in_grad_ref[:, at : at + channels] = side_ref[kind, rep, core].astype(F32)
    in_grad_ref[:, 2 * inner : 2 * inner + 2 * state] = add_up(
        *[common_ref[rep, :, : 2 * state] for rep in range(reps)]
    )
    start = 2 * inner + 2 * state
    tail = []
    for rep in range(reps):
        pair = common_ref[rep, :, 2 * state :].astype(F32)
        tail += [pair[:, :heads], pair[:, LANES // 2 : LANES // 2 + heads]]
    in_grad_ref[:, start:] = jnp.concatenate(tail, axis=1)
    out_grad_ref[...] = out_ref[...].astype(F32).reshape(out_grad_ref.shape)
    router_grad_ref = small_refs[-1]
    for ref, row in zip(small_refs[:-1], (0, 4, 8, 9, 10, 11, 12, 13)):
        ref[...] = small_ref[row : row + ref.shape[0], : ref.shape[1]]
    part, experts = router_grad_ref.shape
    wide = -(-part // LANES) * LANES
    router = jnp.concatenate([small_ref[16:, :wide], jnp.zeros((LANES - experts, wide), F32)], axis=0)
    router_grad_ref[...] = router.T[:part, :experts]


def assemble(side, common, out_rows, small, small_shapes, channels, state, heads):
    reps, part = side.shape[1], side.shape[3]
    columns = 4 * reps * channels + 2 * state + 2 * reps * heads
    model = out_rows.shape[2]
    return pl.pallas_call(
        functools.partial(assemble_kernel, channels, state, heads),
        in_specs=in_vmem(4),
        out_specs=in_vmem(2 + len(small_shapes)),
        out_shape=[
            jax.ShapeDtypeStruct((part, columns), F32),
            jax.ShapeDtypeStruct((channels, model), F32),
        ] + [jax.ShapeDtypeStruct(shape, F32) for shape in small_shapes],
        compiler_params=pltpu.CompilerParams(vmem_limit_bytes=48 * 2**20),
        name="assemble",
    )(side, common, out_rows, small)


def slot_match(table_row, capacity, rows):
    slot = lax.broadcasted_iota(jnp.int32, (capacity, rows), 0).astype(F32) + 1.0
    return table_row == slot


def dispatch_kernel(
    local, capacity, half,
    table_ref, own_ref, second_ref, g_ref, router_ref, in_ref, out_ref,
    buffer_ref, slot_g_ref, gate_slot_ref, gates_ref, hidden_ref, grad_ref, in_grad_ref, out_grad_ref,
    in_total, out_total,
):
    at = pl.program_id(0)
    second, g = second_ref[...], g_ref[...]
    rows = second.shape[0]
    table = table_ref[...].astype(F32)
    used = table > 0.0
    logits = mm_nt(router_ref[...], second)
    top = jnp.max(jnp.where(used, logits, -jnp.inf), axis=0, keepdims=True)
    raw = jnp.where(used, jnp.exp(jnp.where(used, logits - top, 0.0)), 0.0)
    gates = raw / jnp.sum(raw, axis=0, keepdims=True)
    gates_ref[...] = gates
    expert = lax.broadcasted_iota(jnp.int32, gates.shape, 0)
    shard = 2 * lax.axis_index("z") + lax.axis_index("core")
    for i in range(local):
        match = slot_match(own_ref[i : i + 1, :].astype(F32), capacity, rows)
        onehot = match.astype(BF16)
        buffer_ref[i] = mm(onehot, second).astype(BF16)
        slot_g_ref[i] = mm(onehot, g).astype(BF16)
        gate_row = jnp.sum(jnp.where(expert == local * shard + i, gates, 0.0), axis=0, keepdims=True)
        gate_slot = jnp.sum(jnp.where(match, gate_row, 0.0), axis=1, keepdims=True)
        gate_slot_ref[i] = jnp.broadcast_to(gate_slot, (capacity, LANES))
    pre = mm(second, in_ref[...])
    a, b = pre[:, :half], pre[:, half:]
    sig = jax.nn.sigmoid(a)
    hidden = (a * sig * b).astype(BF16)
    hidden_ref[...] = hidden
    back = mm_nt(g, out_ref[...])
    grad = jnp.concatenate([back * b * silu_slope(a, sig), back * a * sig], axis=1).astype(BF16)
    grad_ref[...] = grad

    @pl.when(at == 0)
    def _():
        in_total[...] = jnp.zeros_like(in_total)
        out_total[...] = jnp.zeros_like(out_total)

    in_total[...] += mm_tn(second, grad)
    out_total[...] += mm_tn(hidden, g)

    @pl.when(at == pl.num_programs(0) - 1)
    def _():
        in_grad_ref[...] = in_total[...].astype(BF16)
        out_grad_ref[...] = out_total[...].astype(BF16)


def dispatch(table, own, second, g, router_t, shared_in, shared_out, capacity):
    group, experts, rows = table.shape
    local = own.shape[1]
    model = second.shape[1]
    half = shared_out.shape[0]
    slots = group * capacity

    def by_block(*shape):
        return pl.BlockSpec((None,) + shape, lambda q: (q,) + (0,) * len(shape))

    def by_slots(width):
        return pl.BlockSpec((local, capacity, width), lambda q: (0, q, 0))

    return pl.pallas_call(
        functools.partial(dispatch_kernel, local, capacity, half),
        grid=(group,),
        in_specs=[
            by_block(experts, rows), by_block(local, rows), by_rows((rows, model)), by_rows((rows, model)),
            whole((experts, model)), whole((model, 2 * half)), whole((half, model)),
        ],
        out_specs=[
            by_slots(model), by_slots(model), by_slots(LANES), by_block(experts, rows), by_rows((rows, half)),
            by_rows((rows, 2 * half)), whole((model, 2 * half)), whole((half, model)),
        ],
        out_shape=[
            jax.ShapeDtypeStruct((local, slots, model), BF16),
            jax.ShapeDtypeStruct((local, slots, model), BF16),
            jax.ShapeDtypeStruct((local, slots, LANES), F32),
            jax.ShapeDtypeStruct((group, experts, rows), F32),
            jax.ShapeDtypeStruct((group * rows, half), BF16),
            jax.ShapeDtypeStruct((group * rows, 2 * half), BF16),
            jax.ShapeDtypeStruct((model, 2 * half), BF16),
            jax.ShapeDtypeStruct((half, model), BF16),
        ],
        scratch_shapes=[pltpu.VMEM((model, 2 * half), F32), pltpu.VMEM((half, model), F32)],
        compiler_params=pltpu.CompilerParams(vmem_limit_bytes=56 * 2**20),
        name="dispatch",
    )(table, own, second, g, router_t, shared_in, shared_out)


def experts_kernel(
    buffer_ref, slot_g_ref, gate_ref, in_ref, out_ref,
    weighted_ref, back_ref, dot_ref, in_grad_ref, out_grad_ref, in_total, out_total,
):
    at = pl.program_id(1)
    buffer, weight_in, weight_out = buffer_ref[...], in_ref[...], out_ref[...]
    half = weight_out.shape[0]
    pre = mm(buffer, weight_in)
    a, b = pre[:, :half], pre[:, half:]
    sig = jax.nn.sigmoid(a)
    act = a * sig
    hidden = (act * b).astype(BF16)
    gate = gate_ref[:, 0:1]
    slot_g = slot_g_ref[...].astype(F32)
    result = mm(hidden, weight_out).astype(BF16).astype(F32)
    weighted_ref[...] = (gate * result).astype(BF16)
    dot_ref[...] = jnp.broadcast_to(jnp.sum(slot_g * result, axis=1, keepdims=True), dot_ref.shape)
    result_grad = (gate * slot_g).astype(BF16)
    hidden_grad = mm_nt(result_grad, weight_out)
    pre_grad = jnp.concatenate([hidden_grad * b * silu_slope(a, sig), hidden_grad * act], axis=1).astype(BF16)
    back_ref[...] = mm_nt(pre_grad, weight_in).astype(BF16)

    @pl.when(at == 0)
    def _():
        in_total[...] = mm_tn(buffer, pre_grad)
        out_total[...] = mm_tn(hidden, result_grad)

    @pl.when(at == 1)
    def _():
        in_grad_ref[...] = (in_total[...] + mm_tn(buffer, pre_grad)).astype(BF16)
        out_grad_ref[...] = (out_total[...] + mm_tn(hidden, result_grad)).astype(BF16)


def run_experts(buffer, slot_g, gate_slot, expert_in, expert_out):
    local, slots, model = buffer.shape
    step = slots // 2
    half = expert_out.shape[1]

    def by_step(width):
        return pl.BlockSpec((None, step, width), lambda i, m: (i, m, 0))

    def by_expert(*shape):
        return pl.BlockSpec((None,) + shape, lambda i, m: (i, 0, 0))

    return pl.pallas_call(
        experts_kernel,
        grid=(local, 2),
        in_specs=[
            by_step(model), by_step(model), by_step(LANES), by_expert(model, 2 * half), by_expert(half, model),
        ],
        out_specs=[
            by_step(model), by_step(model), by_step(LANES), by_expert(model, 2 * half), by_expert(half, model),
        ],
        out_shape=[
            jax.ShapeDtypeStruct((local, slots, model), BF16),
            jax.ShapeDtypeStruct((local, slots, model), BF16),
            jax.ShapeDtypeStruct((local, slots, LANES), F32),
            jax.ShapeDtypeStruct((local, model, 2 * half), BF16),
            jax.ShapeDtypeStruct((local, half, model), BF16),
        ],
        scratch_shapes=[pltpu.VMEM((model, 2 * half), F32), pltpu.VMEM((half, model), F32)],
        compiler_params=pltpu.CompilerParams(vmem_limit_bytes=62 * 2**20),
        name="run_experts",
    )(buffer, slot_g, gate_slot, expert_in, expert_out)


def gather(values, axes, axis=0):
    return lax.all_gather(values, axes, axis=axis, tiled=True)


def scatter_sum(values, axes, axis=0):
    return lax.psum_scatter(values, axes, scatter_dimension=axis, tiled=True)


def columns_of(values, start, size, axis=1):
    return lax.dynamic_slice_in_dim(values, start, size, axis=axis)


def shards(
    tokens,
    cotangent,
    dealt_to,
    lengths,
    routes,
    slot_index,
    in_norm,
    in_proj,
    conv_weight,
    conv_bias,
    dt_bias,
    decay_log,
    skip_gain,
    mixer_norm,
    out_proj,
    post_norm,
    router,
    shared_in,
    shared_out,
    expert_in,
    expert_out,
):
    reps, depth = lax.axis_size("rep"), lax.axis_size("z")
    group = 2 * depth
    rep, z, core = lax.axis_index("rep"), lax.axis_index("z"), lax.axis_index("core")
    shard = 2 * z + core
    team = 2 * rep + core
    members = 2 * reps
    rows, model = tokens.shape
    top = routes.shape[1]
    local = expert_in.shape[0]
    experts = local * group
    capacity = rows * top * 4 // (3 * experts)
    inner = mixer_norm.shape[0] * group
    convolved = conv_bias.shape[0] * group
    head_count = dt_bias.shape[0] * group
    width = inner // head_count
    state = (convolved - inner) // 2
    channels = inner // members
    heads = head_count // members
    shared = shared_out.shape[0]
    part = in_norm.shape[0]

    expert_ids = jnp.arange(experts, dtype=jnp.int32)
    table = jnp.sum(
        jnp.where(routes[:, None, :] == expert_ids[None, :, None], slot_index[:, None, :] + 1, 0), axis=2
    ).astype(BF16)
    small = [in_norm[None], conv_weight, conv_bias[None], dt_bias[None], decay_log[None], skip_gain[None],
             mixer_norm[None], post_norm[None], jnp.concatenate([lengths, dealt_to[None]], axis=1)]
    part_wide = -(-part // LANES) * LANES
    table_block = jnp.concatenate([table.T, jnp.pad(router.T, ((0, 0), (0, part_wide - part)))], axis=1)
    pair_heads = 2 * heads
    dt_pair = columns_of(in_proj, inner + convolved + pair_heads * rep, pair_heads)
    blank = jnp.zeros((part, LANES // 2 - heads), BF16)
    common = jnp.concatenate(
        [in_proj[:, 2 * inner : 2 * inner + 2 * state], dt_pair[:, :heads], blank, dt_pair[:, heads:], blank], axis=1
    )

    def pair_of(member):
        return jnp.concatenate(
            [columns_of(in_proj, channels * member, channels), columns_of(in_proj, inner + channels * member, channels)],
            axis=1,
        )

    shared_lanes = -(-shared // LANES) * LANES
    shared_padded = shared_in
    if shared_lanes != shared:
        shared_padded = jnp.pad(
            shared_in.reshape(part, 2 * group, shared), ((0, 0), (0, 0), (0, shared_lanes - shared))
        ).reshape(part, -1)
    sequences = lengths.shape[1]
    (after, mixer_result, scale, lengths_plane, in_gain, post_gain, taps_own, head_rows, skip_own, norm_own, table_all,
     second_column, g_column, first, weight, out_own, projected, gained, shared_in_own) = forward_mixer(
        tokens, cotangent, pair_of(team), pair_of(2 * rep + 1 - core), common, small, table_block,
        out_proj.reshape(reps, channels // reps, model), shared_padded,
        (reps, depth, channels, width, state, sequences, inner, convolved),
    )
    second_column = second_column.reshape(group * rows, model)
    g_column = g_column.reshape(group * rows, model)
    shared_in_own = shared_in_own.reshape(model, 2, shared_lanes)[:, :, :shared].reshape(model, 2 * shared)

    table_all = table_all.reshape(group, experts, -1)
    router_t = table_all[:, :, rows : rows + part].transpose(1, 0, 2).reshape(experts, model)
    dealt_column = shard ^ dealt_to[0] ^ jnp.arange(group, dtype=jnp.int32)
    table_dealt = jnp.take(table_all[:, :, :rows], dealt_column, axis=0)
    table_own = columns_of(table_dealt, local * shard, local)

    buffer, slot_g, gate_slot, gates, shared_hidden, shared_grad, shared_in_grad, shared_out_grad = dispatch(
        table_dealt, table_own, second_column, g_column, router_t, shared_in_own, shared_out, capacity
    )
    weighted, buffer_grad, dots, grad_expert_in, grad_expert_out = run_experts(
        buffer, slot_g, gate_slot, expert_in, expert_out
    )
    shared_in_rows = lax.all_to_all(shared_in_grad, COLUMN, split_axis=0, concat_axis=0, tiled=True)
    shared_in_rows = shared_in_rows.reshape(group, part, 2, shared).transpose(1, 2, 0, 3).reshape(part, -1)
    grad_expert_in, grad_expert_out, grad_shared_out, grad_shared_in = [
        values.astype(F32)
        for values in lax.psum((grad_expert_in, grad_expert_out, shared_out_grad, shared_in_rows), "rep")
    ]

    after_grad, post_grad, router_grad, layer_out, low_plane, scales = join_experts(
        table_own, gates, dots, shared_hidden, shared_grad, router_t, shared_in_own, shared_out, cotangent, after,
        mixer_result, scale, post_gain, buffer_grad, weighted, second_column, inner, reps, depth, capacity,
    )
    router_parts = jnp.pad(
        router_grad.reshape(experts, depth, 2, part).transpose(1, 2, 0, 3), ((0, 0), (0, 0), (0, 0), (0, part_wide - part))
    )
    grad_tokens, side_rows, common_rows, out_rows, small_sum = backward_mixer(
        scales, after_grad, tokens, in_gain, post_grad, router_parts, lengths_plane, taps_own, head_rows, skip_own, norm_own, weight.reshape(model, -1),
        out_own.reshape(channels, model), low_plane, first, projected, gained,
        (reps, depth, channels, width, state, sequences, inner, convolved),
    )
    per_shard = conv_bias.shape[0]
    small_shapes = [
        (4, per_shard), (1, per_shard), (1, heads), (1, heads), (1, heads), (1, channels), (1, part), (1, part),
        (part, experts),
    ]
    (grad_in_proj, grad_out_proj, grad_taps, grad_bias, grad_dt, grad_decay, grad_skip, grad_mixer_norm, grad_post,
     grad_in_norm, grad_router) = assemble(
        side_rows, common_rows, out_rows, small_sum, small_shapes, channels, state, heads
    )
    return (
        layer_out,
        grad_tokens,
        grad_in_norm[0],
        grad_in_proj,
        grad_taps,
        grad_bias[0],
        grad_dt[0],
        grad_decay[0],
        grad_skip[0],
        grad_mixer_norm[0],
        grad_out_proj,
        grad_post[0],
        grad_router,
        grad_shared_in,
        grad_shared_out,
        grad_expert_in,
        grad_expert_out,
    )


def solution(mesh):
    reps, group = mesh.shape["rep"], mesh.shape["shard"]
    split = Mesh(mesh.devices.reshape(reps, group // 2, 2), ALL)
    one, row = P(COLUMN), P(COLUMN, None)
    token = P(ALL, None)
    return jax.shard_map(
        shards,
        mesh=split,
        in_specs=(
            token, token, P(ALL), token, token, token, one, row, P(None, COLUMN), one, one, one, one, one, row,
            one, row, row, row, P(COLUMN, None, None), P(COLUMN, None, None),
        ),
        out_specs=(
            token, token, one, row, P(None, COLUMN), one, one, one, one, one, row, one, row, row, row,
            P(COLUMN, None, None), P(COLUMN, None, None),
        ),
        check_vma=False,
    )
```

```python
import functools

import jax
import jax.numpy as jnp
from jax import lax
from jax.experimental import pallas as pl
from jax.experimental.pallas import tpu as pltpu
from jax.sharding import Mesh
from jax.sharding import PartitionSpec as P

EPS = 1e-05
HIGH = lax.Precision.HIGHEST
F32 = jnp.float32
BF16 = jnp.bfloat16
ALL = ("rep", "z", "core")
COLUMN = ("z", "core")
PLANE = ("rep", "core")
LANES = 128


def rms_rows(values):
    return lax.rsqrt(jnp.mean(values * values, axis=-1, keepdims=True) + EPS)


def mm(left, right):
    return jnp.dot(left, right, preferred_element_type=F32)


def mm_nt(left, right):
    return lax.dot_general(left, right, (((1,), (1,)), ((), ())), preferred_element_type=F32)


def mm_tn(left, right):
    return lax.dot_general(left, right, (((0,), (0,)), ((), ())), preferred_element_type=F32)


def silu_slope(values, sig):
    return sig * (1.0 + values * (1.0 - sig))


def split_two(values):
    high = values.astype(BF16)
    return high, (values - high.astype(F32)).astype(BF16)


def segments(lengths_row, sequences, rows):
    column = lax.broadcasted_iota(jnp.int32, (rows, 1), 0).astype(F32)
    line = lax.broadcasted_iota(jnp.int32, (1, rows), 1).astype(F32)
    end = jnp.zeros((1, 1), F32)
    seg_column, seg_line = jnp.zeros_like(column), jnp.zeros_like(line)
    for at in range(sequences):
        end = end + lengths_row[:, at : at + 1]
        seg_column = seg_column + jnp.where(column >= end, 1.0, 0.0)
        seg_line = seg_line + jnp.where(line >= end, 1.0, 0.0)
    return seg_column, seg_line


class Block:
    def __init__(self, proj, seg_col, seg_row, taps, heads, channels, width, state):
        rows = proj.shape[0]
        self.rows, self.channels, self.width, self.state = rows, channels, width, state
        self.gate = proj[:, :channels]
        self.xbc = proj[:, channels : 2 * channels + 2 * state]
        self.turn = lax.axis_index("core") * (LANES // 2)
        dt_raw = pltpu.roll(proj[:, 2 * channels + 2 * state :], self.turn, 1)
        position = lax.broadcasted_iota(jnp.int32, (rows, 1), 0)
        seg_wide = jnp.broadcast_to(seg_col, (rows, LANES))
        self.masks = []
        conv = taps[4:5, :] + taps[3:4, :] * self.xbc
        for offset in (1, 2, 3):
            before = pltpu.roll(seg_wide, offset, 0)[:, :1]
            mask = jnp.where((before == seg_col) & (position >= offset), 1.0, 0.0)
            self.masks.append(mask)
            conv = conv + taps[3 - offset : 4 - offset, :] * (mask * pltpu.roll(self.xbc, offset, 0))
        self.conv = conv
        self.conv_sig = jax.nn.sigmoid(conv)
        act = conv * self.conv_sig
        self.xin = act[:, :channels]
        self.write = act[:, channels : channels + state]
        self.read = act[:, channels + state :]
        shifted = dt_raw + heads[0:1, :]
        self.step = jnp.maximum(shifted, 0.0) + jnp.log1p(jnp.exp(-jnp.abs(shifted)))
        self.step_sig = jax.nn.sigmoid(shifted)
        self.speed = heads[1:2, :]
        self.rate = -self.step * self.speed
        row_at = lax.broadcasted_iota(jnp.int32, (rows, rows), 0)
        col_at = lax.broadcasted_iota(jnp.int32, (rows, rows), 1)
        self.causal = row_at >= col_at
        self.keep = self.causal & (seg_col == seg_row)
        self.cum = jnp.dot(self.causal.astype(F32), self.rate, precision=HIGH, preferred_element_type=F32)
        self.cum_t = self.cum.T
        scores = lax.dot_general(
            self.read, self.write, (((1,), (1,)), ((), ())), precision=HIGH, preferred_element_type=F32
        )
        self.scores = jnp.where(self.keep, scores, 0.0)

    def groups(self):
        for start in range(0, self.channels, LANES):
            stop = min(start + LANES, self.channels)
            yield start, stop, list(range(start // self.width, (stop - 1) // self.width + 1))

    def spread(self, columns, start, stop, heads):
        lane = lax.broadcasted_iota(jnp.int32, (self.rows, stop - start), 1) + start
        result = jnp.broadcast_to(columns[:, heads[0] : heads[0] + 1], (self.rows, stop - start))
        for head in heads[1:]:
            result = jnp.where(lane >= head * self.width, columns[:, head : head + 1], result)
        return result

    def inside(self, start, stop, head):
        lane = lax.broadcasted_iota(jnp.int32, (self.rows, stop - start), 1) + start
        return (lane >= head * self.width) & (lane < (head + 1) * self.width)

    def decay(self, head):
        gaps = self.cum[:, head : head + 1] - self.cum_t[head : head + 1, :]
        return jnp.exp(jnp.where(self.keep, gaps, 0.0))


def block_back(block, low, scale, pull, taps_ref, skip_ref, norm_ref, weight, out_weight):
    rows, channels = block.rows, block.channels
    normed_grad = mm_nt(low, out_weight)
    taps = taps_ref[...]
    gate_grads, x_grads, norm_grads, skip_grads = [], [], [], []
    step_grad = jnp.zeros((rows, LANES), F32)
    cum_grad = jnp.zeros((rows, LANES), F32)
    cum_grad_t = jnp.zeros((LANES, rows), F32)
    score_grad = jnp.zeros((rows, rows), F32)
    lane_all = lax.broadcasted_iota(jnp.int32, (rows, LANES), 1)
    sub_all = lax.broadcasted_iota(jnp.int32, (LANES, rows), 0)
    for start, stop, heads in block.groups():
        xin = block.xin[:, start:stop]
        spread = block.spread(block.step, start, stop, heads)
        scaled, scaled_rest = split_two(xin * spread)
        scaled_wide = jnp.concatenate([scaled, scaled, scaled_rest], axis=1)
        weights, decays = [], []
        y = None
        for head in heads:
            decays.append(block.decay(head))
            weights.append(block.scores * decays[-1])
            term = mm(weights[-1].astype(BF16), scaled)
            y = term if y is None else jnp.where(block.inside(start, stop, head), term, y)
        skip = skip_ref[:, start:stop]
        y = y + skip * xin
        gate = block.gate[:, start:stop]
        gate_sig = jax.nn.sigmoid(gate)
        gate_act = gate * gate_sig
        mixed = y * gate_act
        q = normed_grad[:, start:stop]
        norm_grads.append(jnp.sum(mixed * scale * q, axis=0, keepdims=True))
        mixed_grad = scale * norm_ref[:, start:stop] * q - mixed * pull
        gate_grads.append(mixed_grad * y * silu_slope(gate, gate_sig))
        y_grad = mixed_grad * gate_act
        skip_grads.append(jnp.sum(y_grad * xin, axis=0, keepdims=True))
        y_low, y_rest = split_two(y_grad)
        scaled_grad = None
        for at, head in enumerate(heads):
            inside = block.inside(start, stop, head)
            term = mm_tn(weights[at].astype(BF16), y_low)
            scaled_grad = term if scaled_grad is None else jnp.where(inside, term, scaled_grad)
            blank = jnp.zeros_like(y_low)
            y_own = jnp.where(inside, y_low, blank)
            pair_grad = mm_nt(
                jnp.concatenate([y_own, jnp.where(inside, y_rest, blank), y_own], axis=1), scaled_wide
            )
            score_grad = score_grad + pair_grad * decays[at]
            exponent_grad = pair_grad * weights[at]
            cum_grad = jnp.where(lane_all == head, jnp.sum(exponent_grad, axis=1, keepdims=True), cum_grad)
            cum_grad_t = jnp.where(sub_all == head, jnp.sum(exponent_grad, axis=0, keepdims=True), cum_grad_t)
        for head in heads:
            inside = block.inside(start, stop, head)
            per_row = jnp.sum(jnp.where(inside, scaled_grad * xin, 0.0), axis=1, keepdims=True)
            step_grad = jnp.where(lane_all == head, per_row, step_grad)
        x_grads.append(scaled_grad * spread + skip * y_grad)
    score_grad = jnp.where(block.keep, score_grad, 0.0).astype(BF16)
    read_grad = mm(score_grad, block.write.astype(BF16))
    write_grad = mm_tn(score_grad, block.read.astype(BF16))
    cum_grad = cum_grad - cum_grad_t.T
    rate_grad = lax.dot_general(
        block.causal.astype(F32), cum_grad, (((0,), (0,)), ((), ())), precision=HIGH, preferred_element_type=F32
    )
    dt_grad = (step_grad - block.speed * rate_grad) * block.step_sig
    head_rows = [jnp.sum(dt_grad, axis=0, keepdims=True), jnp.sum(rate_grad * block.rate, axis=0, keepdims=True)]
    act_grad = jnp.concatenate(x_grads + [write_grad, read_grad], axis=1)
    conv_grad = act_grad * silu_slope(block.conv, block.conv_sig)
    tap_rows = {4: jnp.sum(conv_grad, axis=0, keepdims=True), 3: jnp.sum(conv_grad * block.xbc, axis=0, keepdims=True)}
    xbc_grad = taps[3:4, :] * conv_grad
    for offset in (1, 2, 3):
        masked = conv_grad * block.masks[offset - 1]
        tap_rows[3 - offset] = jnp.sum(masked * pltpu.roll(block.xbc, offset, 0), axis=0, keepdims=True)
        xbc_grad = xbc_grad + taps[3 - offset : 4 - offset, :] * pltpu.roll(masked, rows - offset, 0)
    proj_grad = jnp.concatenate(gate_grads + [xbc_grad, pltpu.roll(dt_grad, block.turn, 1)], axis=1).astype(BF16)
    tap_grads = jnp.concatenate([tap_rows[at] for at in range(5)], axis=0)
    wide_grads = jnp.concatenate(
        [jnp.concatenate(norm_grads, axis=1), jnp.concatenate(skip_grads, axis=1)], axis=0
    )
    return proj_grad, tap_grads, head_rows, wide_grads


def whole(shape):
    return pl.BlockSpec(shape, lambda i: (0,) * len(shape))


def by_rows(shape):
    return pl.BlockSpec(shape, lambda i: (i,) + (0,) * (len(shape) - 1))


MESH_ID = pl.DeviceIdType.MESH


def when(condition, action):
    if condition is True:
        action()
    elif condition is not False:
        pl.when(condition)(action)


class Place:
    def __init__(self, reps, depth):
        self.reps, self.depth = reps, depth
        self.rep, self.z, self.core = lax.axis_index("rep"), lax.axis_index("z"), lax.axis_index("core")
        self.here = {"rep": self.rep, "z": self.z, "core": self.core}
        self.pending = []

    def device(self, **changes):
        return {**self.here, **changes}

    def sibling(self):
        return self.device(core=1 - self.core)

    def rep_at(self, distance):
        result, place = 0, 1
        while place < self.reps:
            mine, other = lax.rem(self.rep // place, 2), lax.rem(distance // place, 2)
            result = result + place * (mine + other - 2 * mine * other)
            place *= 2
        return result

    def in_column(self, distance):
        other = lax.rem(2 * self.z + self.core + distance, 2 * self.depth)
        return self.device(z=other // 2, core=lax.rem(other, 2))

    def barrier(self, plane=False, column=False, whole=False):
        semaphore = pltpu.get_barrier_semaphore()

        def greet(device):
            pl.semaphore_signal(semaphore, inc=1, device_id=device, device_id_type=MESH_ID)

        amount = 1
        if whole:
            for distance in range(1, 2 * self.depth):
                greet(self.in_column(distance))
            amount = 2 * self.depth - 1
        else:
            greet(self.sibling())
        if plane:
            for distance in range(1, self.reps):
                greet(self.device(rep=self.rep_at(distance)))
            amount = amount + self.reps - 1
        if column and not whole:
            above, below = self.z < self.depth - 1, self.z > 0
            when(above, lambda: greet(self.device(z=self.z + 1)))
            when(below, lambda: greet(self.device(z=self.z - 1)))
            amount = amount + jnp.where(above, 1, 0) + jnp.where(below, 1, 0)
        pl.semaphore_wait(semaphore, amount)

    def send(self, source, target, send_sem, recv_sem, device, condition=True):
        copy = pltpu.make_async_remote_copy(
            src_ref=source, dst_ref=target, send_sem=send_sem, recv_sem=recv_sem, device_id=device,
            device_id_type=MESH_ID,
        )
        when(condition, copy.start)
        self.pending.append((condition, copy))

    def local(self, source, target, sem):
        copy = pltpu.make_async_copy(source, target, sem)
        copy.start()
        return copy

    def arrived(self, target, recv_sem, condition=True):
        copy = pltpu.make_async_remote_copy(
            src_ref=target, dst_ref=target, send_sem=recv_sem, recv_sem=recv_sem, device_id=self.sibling(),
            device_id_type=MESH_ID,
        )
        when(condition, copy.wait_recv)

    def finish(self):
        for condition, copy in self.pending:
            when(condition, copy.wait_send)
        self.pending = []


class PlaneGather:
    @staticmethod
    def scratch(reps):
        return [pltpu.SemaphoreType.DMA((4, reps + 1)), pltpu.SemaphoreType.DMA((1,))]

    def __init__(self, place, own, out, sems, local_sem, corner=True):
        self.place, self.out, self.sems = place, out, sems
        p = place
        self.half = own.shape[0] // 2
        self.corner = corner and p.reps == 4 and self.half % 16 == 0
        self.keep = p.local(own, out.at[p.rep, p.core], local_sem.at[0])
        for distance in range(1, 3 if self.corner else p.reps):
            p.send(own, out.at[p.rep, p.core], sems.at[0, distance], sems.at[1, distance],
                   p.device(rep=p.rep_at(distance)))
        p.send(own, out.at[p.rep, p.core], sems.at[2, 0], sems.at[3, 0], p.sibling())

    def part(self, distance, at):
        p = self.place
        return self.out.at[p.rep_at(distance), p.core, pl.ds(self.half * at, self.half)]

    def relay(self):
        p = self.place
        for distance in range(1, p.reps):
            source = self.out.at[p.rep_at(distance), p.core]
            if self.corner and distance == 3:
                for at in range(2):
                    p.arrived(self.part(3, at), self.sems.at[1, 3 + at])
            else:
                p.arrived(source, self.sems.at[1, distance])
            if self.corner and distance < 3:
                piece, at = self.part(distance, distance - 1), distance + 2
                p.send(piece, piece, self.sems.at[0, at], self.sems.at[1, at], p.device(rep=p.rep_at(3 - distance)))
            p.send(source, source, self.sems.at[2, distance], self.sems.at[3, distance], p.sibling())

    def finish(self):
        p = self.place
        self.keep.wait()
        for distance in range(p.reps):
            source = p.rep_at(distance) if distance else p.rep
            p.arrived(self.out.at[source, 1 - p.core], self.sems.at[3, distance])


class ColumnGather:
    @staticmethod
    def scratch(depth):
        return [pltpu.SemaphoreType.DMA((8, depth)), pltpu.SemaphoreType.DMA((1,))]

    def __init__(self, place, own, slot, sems, local_sem, shared=None, keep=True, start=True):
        self.place, self.own, self.slot, self.sems, self.shared = place, own, slot, sems, shared
        self.keep = None
        if keep:
            self.keep = pltpu.make_async_copy(own, slot(place.z), local_sem.at[0])
        if start:
            self.start()

    def start(self):
        if self.keep is not None:
            self.keep.start()
        self.send(0)

    def ends(self, distance):
        p = self.place
        below, above = p.z >= distance, p.z + distance < p.depth
        return below, above, jnp.maximum(p.z - distance, 0), jnp.minimum(p.z + distance, p.depth - 1)

    def copies(self, distance):
        p = self.place

        def copy(source, target, at, device):
            return pltpu.make_async_remote_copy(
                src_ref=source, dst_ref=target, send_sem=self.sems.at[at, distance],
                recv_sem=self.sems.at[at + 1, distance], device_id=device, device_id_type=MESH_ID,
            )

        up, down = p.device(z=p.z + 1), p.device(z=p.z - 1)
        if distance == 0:
            target = self.slot(p.z)
            yield p.z < p.depth - 1, copy(self.own, target, 0, up)
            yield p.z > 0, copy(self.own, target, 2, down)
            if self.shared is not None:
                yield True, copy(self.own, target, 4, p.sibling())
            return
        below, above, low, high = self.ends(distance)
        low, high = self.slot(low), self.slot(high)
        yield below & (p.z < p.depth - 1), copy(low, low, 0, up)
        yield above & (p.z > 0), copy(high, high, 2, down)
        if self.shared is not None:
            yield below, copy(low, low, 4, p.sibling())
            yield above, copy(high, high, 6, p.sibling())

    def send(self, distance):
        for condition, copy in self.copies(distance):
            when(condition, copy.start)

    def hop(self, distance):
        below, above, low, high = self.ends(distance)
        self.place.arrived(self.slot(low), self.sems.at[1, distance - 1], below)
        self.place.arrived(self.slot(high), self.sems.at[3, distance - 1], above)
        self.send(distance)

    def finish(self):
        p = self.place
        if self.keep is not None:
            self.keep.wait()
        if self.shared is not None:
            p.arrived(self.shared(p.z), self.sems.at[5, 0])
            for distance in range(1, p.depth):
                below, above, low, high = self.ends(distance)
                p.arrived(self.shared(low), self.sems.at[5, distance], below)
                p.arrived(self.shared(high), self.sems.at[7, distance], above)
        for distance in range(p.depth):
            for condition, copy in self.copies(distance):
                when(condition, copy.wait_send)


def add_up(*terms):
    total = terms[0].astype(F32)
    for term in terms[1:]:
        total = total + term.astype(F32)
    return total


class PairSwap:
    @staticmethod
    def scratch(count, shape, dtype):
        return [pltpu.VMEM((count,) + shape, dtype), pltpu.SemaphoreType.DMA((2, count))]

    def __init__(self, place, parts, pair, sems, order, own=None):
        self.place, self.parts, self.pair, self.sems, self.own = place, parts, pair, sems, own
        for at in order:
            place.send(parts.at[at, 1 - place.core], pair.at[at], sems.at[0, at], sems.at[1, at], place.sibling())

    def wait(self, at):
        self.place.arrived(self.pair.at[at], self.sems.at[1, at])

    def terms(self, at):
        if self.own is None:
            return [self.parts[at, self.place.core], self.pair[at]]
        slot, sem = self.own
        self.place.local(self.parts.at[at, self.place.core], slot, sem.at[0]).wait()
        return [slot[...], self.pair[at]]


class PlaneSum:
    @staticmethod
    def scratch(reps, shape, dtype):
        return PairSwap.scratch(reps, shape, dtype) + [
            pltpu.VMEM((reps,) + shape, dtype), pltpu.SemaphoreType.DMA((2, reps)),
        ]

    def __init__(self, place, parts, pair, pair_sems, into, sems):
        self.place, self.pair, self.into, self.sems = place, pair, into, sems
        order = [place.rep_at(distance) for distance in range(1, place.reps)] + [place.rep]
        self.swap = PairSwap(place, parts, pair, pair_sems, order)

    def relay(self):
        p = self.place
        for distance in range(1, p.reps):
            rep = p.rep_at(distance)
            self.swap.wait(rep)
            self.pair[rep] = add_up(*self.swap.terms(rep)).astype(self.pair.dtype)
            p.send(self.pair.at[rep], self.into.at[distance], self.sems.at[0, distance], self.sems.at[1, distance],
                   p.device(rep=rep))

    def total(self):
        p = self.place
        self.swap.wait(p.rep)
        terms = self.swap.terms(p.rep)
        for distance in range(1, p.reps):
            p.arrived(self.into.at[distance], self.sems.at[1, distance])
            terms.append(self.into[distance])
        return add_up(*terms)


class LineSum:
    @staticmethod
    def scratch(depth, shape, dtype):
        return [pltpu.VMEM((depth + 1,) + shape, dtype), pltpu.SemaphoreType.DMA((4, depth))]

    def __init__(self, place, terms, out, into, sems):
        self.place, self.terms, self.out, self.into, self.sems = place, terms, out, into, sems

    def moves(self, at):
        p = self.place
        last = p.depth - 1
        for way, towards, goal, first, valid in (
            (0, p.z + 1, last - (at - p.z), p.z == 0, (at >= p.z) & (last - (at - p.z) > p.z)),
            (1, p.z - 1, at - (last - p.z), p.z == last, (at >= last - p.z) & (at - (last - p.z) < p.z)),
        ):
            goal = jnp.clip(goal, 0, last)
            slot = jnp.where(goal == towards, p.depth, goal) if way else goal
            copy = pltpu.make_async_remote_copy(
                src_ref=self.out.at[goal], dst_ref=self.into.at[slot], send_sem=self.sems.at[2 * way, goal],
                recv_sem=self.sems.at[2 * way + 1, goal], device_id=p.device(z=towards), device_id_type=MESH_ID,
            )
            yield way, goal, first, valid, copy

    def step(self, at):
        p = self.place
        for way, goal, first, valid, copy in self.moves(at):
            inner = valid & jnp.logical_not(first)
            p.arrived(self.into.at[goal], self.sems.at[2 * way + 1, goal], inner)

            def start(goal=goal):
                self.out[goal] = add_up(*self.terms(goal)).astype(self.out.dtype)

            def follow(goal=goal):
                self.out[goal] = add_up(*self.terms(goal), self.into[goal]).astype(self.out.dtype)

            when(valid & first, start)
            when(inner, follow)
            when(valid, copy.start)

    def finish(self):
        for at in range(self.place.depth - 1):
            for _, _, _, valid, copy in self.moves(at):
                when(valid, copy.wait_send)

    def total(self, result):
        result[...] = add_up(*self.terms(self.place.z))
        self.gather(result)
        self.finish()

    def gather(self, result):
        p = self.place
        for way, slot, condition in ((0, p.z, p.z > 0), (1, p.depth, p.z < p.depth - 1)):
            p.arrived(self.into.at[slot], self.sems.at[2 * way + 1, p.z], condition)

            def add(slot=slot):
                result[...] += self.into[slot].astype(F32)

            when(condition, add)


class ColumnSum:
    @staticmethod
    def scratch(depth, shape, dtype):
        return PairSwap.scratch(depth, shape, dtype) + LineSum.scratch(depth, shape, dtype)

    def __init__(self, place, parts, pair, pair_sems, into, sems, own=None):
        self.place = place
        order = [lax.rem(place.z + distance, place.depth) for distance in list(range(place.depth - 1, 0, -1)) + [0]]
        self.order = order
        self.swap = PairSwap(place, parts, pair, pair_sems, order, own)
        self.line = LineSum(place, self.swap.terms, pair, into, sems)

    def ready(self):
        for at in self.order:
            self.swap.wait(at)

    def step(self, at):
        self.line.step(at)

    def total(self, result):
        self.line.total(result)


def anywhere(count):
    return [pl.BlockSpec(memory_space=pl.ANY)] * count


def in_vmem(count):
    return [pl.BlockSpec(memory_space=pltpu.VMEM)] * count


def remote_params(identity, mebibytes=60):
    return pltpu.CompilerParams(
        collective_id=identity, has_side_effects=True, vmem_limit_bytes=mebibytes * 2**20
    )


def column_of(row_values, rows):
    return jnp.broadcast_to(row_values, (LANES, rows)).T[:, 0:1]


def row_of(column_values, rows):
    return jnp.broadcast_to(column_values, (rows, LANES)).T[0:8, :]


def forward_mixer(tokens, cotangent, own_pair, other_pair, common, small, table, out_quarters, shared_in, sizes):
    reps, depth, channels, width, state, sequences, inner, convolved = sizes
    rows, model = tokens.shape
    part, side = own_pair.shape
    wide = side + common.shape[1]
    quarter = out_quarters.shape[1]
    vector_width = -(-max(piece.shape[1] for piece in small) // LANES) * LANES
    vector_rows = 16
    group = 2 * depth
    shared = shared_in.shape[1] // (2 * group)
    heads = channels // width
    per_shard = convolved // (2 * depth)

    x_scratch = [pltpu.VMEM((reps, 2, rows, model), BF16)] + PlaneGather.scratch(reps)
    w_scratch = [pltpu.VMEM((depth, 2, part, wide), BF16)] + ColumnGather.scratch(depth) * 3
    v_scratch = [pltpu.VMEM((depth, 2, vector_rows, vector_width), F32)] + ColumnGather.scratch(depth) * 2
    o_scratch = [
        pltpu.VMEM((depth, quarter, model), BF16), pltpu.VMEM((reps, quarter, model), BF16),
    ] + ColumnGather.scratch(depth) + [pltpu.SemaphoreType.DMA((2, max(reps, depth))), pltpu.SemaphoreType.DMA((2,))]
    n_scratch = [pltpu.VMEM((8, LANES), F32)] + PlaneGather.scratch(reps)
    sum_scratch = [
        pltpu.VMEM((reps, rows, model), BF16), pltpu.VMEM((reps, 2, 8, rows), F32),
    ] + PlaneSum.scratch(reps, (rows, model), BF16) + PlaneSum.scratch(reps, (8, rows), F32)
    groups = [x_scratch, w_scratch, v_scratch, o_scratch, n_scratch, sum_scratch]

    def kernel(x_ref, g_ref, own_ref, other_ref, common_ref, table_ref, quarters_ref, shared_ref, *refs):
        small_refs, refs = refs[: len(small)], refs[len(small) :]
        (after_ref, mixed_ref, scale_ref, lengths_ref, in_gain_ref, post_gain_ref, taps_ref, heads_ref, skip_ref,
               norm_ref, table_out, second_out, g_out, first_out, weight_out, out_out, proj_out, mixed_out, shared_out), scratch = refs[:19], refs[19:]
        cut = [0]
        for items in groups:
            cut.append(cut[-1] + len(items))
        x_work, w_work, v_work, o_work, n_work, sum_work = [scratch[i:j] for i, j in zip(cut, cut[1:])]
        (second, second_sems, second_local, g_sems, g_local, proj_buffer, proj_sems, keep_sems,
         own_part, mixed_all, mixed_sems, vectors_ref, shared_sems, shared_local) = scratch[cut[-1]:]
        p = Place(reps, depth)
        vectors_ref[...] = jnp.zeros_like(vectors_ref)
        row = 0
        for piece in small_refs:
            count, size = piece.shape
            vectors_ref[row : row + count, :size] = piece[...].astype(F32)
            row += count
        p.barrier(plane=True, column=True, whole=True)

        x_all, weight_all, vectors_all = x_work[0], w_work[0], v_work[0]

        def left(core):
            return lambda z: weight_all.at[z, core, :, pl.ds(0, side)]

        def right(core):
            return lambda z: weight_all.at[z, core, :, pl.ds(side, wide - side)]

        vector_job = ColumnGather(p, vectors_ref, lambda z: vectors_all.at[z, p.core], v_work[1], v_work[2],
                                  shared=lambda z: vectors_all.at[z, 1 - p.core])
        own_slot, other_slot = left(p.core), left(1 - p.core)
        p.send(other_ref, own_slot(p.z), keep_sems.at[0], keep_sems.at[1], p.sibling())
        job_a = ColumnGather(p, own_ref, own_slot, w_work[1], w_work[2])
        job_c = ColumnGather(p, common_ref, right(p.core), w_work[3], w_work[4], shared=right(1 - p.core))
        x_job = PlaneGather(p, x_ref, x_all, x_work[1], x_work[2])
        p.arrived(other_slot(p.z), keep_sems.at[1])
        job_b = ColumnGather(p, other_slot(p.z), other_slot, w_work[5], w_work[6], keep=False)
        for distance in range(1, depth):
            vector_job.hop(distance)
        vector_job.finish()

        dealt = vectors_all[p.z, p.core].astype(F32)[12:13, 0:1]
        lengths_row = jnp.zeros((1, LANES), F32)
        for z in range(depth):
            for core in range(2):
                row = vectors_all[z, core].astype(F32)[11:12, :LANES]
                lengths_row = jnp.where(dealt == float(2 * z + core), row, lengths_row)
        n_work[0][...] = jnp.broadcast_to(lengths_row, (8, LANES))
        n_job = PlaneGather(p, n_work[0], lengths_ref, n_work[1], n_work[2], corner=False)

        pieces = [vectors_all[z, core].astype(F32) for z in range(depth) for core in range(2)]
        in_gain_ref[...] = jnp.concatenate([piece[0:1, :part] for piece in pieces], axis=1)
        post_gain_ref[...] = jnp.concatenate([piece[10:11, :part] for piece in pieces], axis=1)
        taps_full = jnp.concatenate([piece[0:8, :per_shard] for piece in pieces], axis=1)
        taps_full = jnp.concatenate([taps_full[1:6, :], jnp.zeros((3, convolved), F32)], axis=0)
        team = 2 * p.rep + p.core
        taps_own = taps_full[:, :channels]
        for member in range(1, 2 * reps):
            taps_own = jnp.where(team == member, taps_full[:, channels * member : channels * (member + 1)], taps_own)
        taps_ref[...] = jnp.concatenate([taps_own, taps_full[:, inner:]], axis=1)
        own = vectors_all[p.rep, p.core].astype(F32)
        lane = lax.broadcasted_iota(jnp.int32, (1, LANES), 1)
        speed = jnp.where(lane < heads, jnp.exp(jnp.where(lane < heads, own[7:8, :LANES], 0.0)), 0.0)
        heads_ref[...] = jnp.concatenate([own[6:7, :LANES], speed, jnp.zeros((6, LANES), F32)], axis=0)
        norm_ref[...] = own[9:10, :channels]
        wide_lane = lax.broadcasted_iota(jnp.int32, (1, channels), 1)
        skip = jnp.broadcast_to(own[8:9, 0:1], (1, channels))
        for head in range(1, heads):
            skip = jnp.where(wide_lane >= head * width, own[8:9, head : head + 1], skip)
        skip_ref[...] = skip

        n_job.relay()
        mid, out_all, o_sems, o_local, e_sems, e_local = o_work
        late_jobs = []
        for distance in range(1, depth):
            for job in (job_a, job_c, job_b):
                job.hop(distance)
            if distance == min(2, depth - 1):
                x_job.relay()
                late_jobs.append(ColumnGather(p, quarters_ref.at[p.rep], lambda z: mid.at[z], o_sems, o_local))
                late_jobs.append(
                    ColumnGather(p, table_ref, lambda z: table_out.at[z, p.core], v_work[3], v_work[4],
                                 shared=lambda z: table_out.at[z, 1 - p.core])
                )
        job_o, table_job = late_jobs
        shard = 2 * p.z + p.core

        def shared_piece(kind, other):
            start = pl.multiple_of((kind * group + other) * shared, LANES)
            return shared_ref.at[:, pl.ds(start, shared)]

        def shared_slot(kind, other):
            return shared_out.at[other, :, pl.ds(kind * shared, shared)]

        shared_keep = [
            p.local(shared_piece(kind, shard), shared_slot(kind, shard), shared_local.at[kind]) for kind in range(2)
        ]
        for distance in range(1, group):
            goal = p.in_column(distance)
            for kind in range(2):
                p.send(shared_piece(kind, 2 * goal["z"] + goal["core"]), shared_slot(kind, shard),
                       shared_sems.at[2 * kind, distance], shared_sems.at[2 * kind + 1, distance], goal)
        shared_pending, p.pending = p.pending[-2 * (group - 1) :], p.pending[: -2 * (group - 1)]
        job_o.keep.wait()
        job_o.keep = None
        for job in (n_job, x_job, job_a, job_b, job_c):
            job.finish()
        weight_keep = p.local(weight_all, weight_out, e_local.at[0])

        def exchange_copy(goal):
            return pltpu.make_async_remote_copy(
                src_ref=mid.at[goal], dst_ref=out_all.at[p.rep], send_sem=e_sems.at[0, goal],
                recv_sem=e_sems.at[1, p.rep], device_id=p.device(rep=goal), device_id_type=MESH_ID,
            )

        def exchange(goal, condition):
            def own():
                out_all[goal] = mid[goal]

            when(condition & (goal == p.rep), own)
            when(condition & (goal != p.rep), exchange_copy(goal).start)

        def out_tick(distance):
            if distance == 1:
                exchange(p.z, p.z >= 0)
            job_o.hop(distance)
            table_job.hop(distance)
            below, above, low, high = job_o.ends(distance)
            exchange(low, below)
            exchange(high, above)

        def out_wait():
            for rep in range(reps):
                p.arrived(out_all.at[rep], e_sems.at[1, rep], rep != p.rep)

        g_job = ColumnGather(p, g_ref, lambda z: g_out.at[z, p.core], g_sems, g_local,
                             shared=lambda z: g_out.at[z, 1 - p.core], start=False)
        p.finish()
        parts, squares = sum_work[0], sum_work[1]
        pair, pair_sems, into, into_sems = sum_work[2:6]
        s_pair, s_pair_sems, s_into, s_into_sems = sum_work[6:10]

        def swap(rep, start):
            for source, target, sems in (
                (parts.at[rep], pair, pair_sems), (squares.at[rep, 1 - p.core], s_pair, s_pair_sems)
            ):
                copy = pltpu.make_async_remote_copy(
                    src_ref=source, dst_ref=target.at[rep], send_sem=sems.at[0, rep],
                    recv_sem=sems.at[1, rep], device_id=p.sibling(), device_id_type=MESH_ID,
                )
                if start:
                    copy.start()
                else:
                    copy.wait_send()

        corner = reps == 4 and rows % 32 == 0
        half_rows = rows // 2

        def distance_at(index):
            if corner:
                return jnp.where(index == 0, 3, jnp.where(index == 3, 0, index))
            return lax.rem(index + 1, reps)

        def to_corner(start):
            for half, index in ((0, 3), (1, 0)):
                piece = pl.ds(half_rows * half, half_rows)
                copy = pltpu.make_async_remote_copy(
                    src_ref=pair.at[p.rep_at(3), piece], dst_ref=into.at[0, piece],
                    send_sem=into_sems.at[0, index], recv_sem=into_sems.at[1, index],
                    device_id=p.device(rep=p.rep_at(half + 1)), device_id_type=MESH_ID,
                )
                copy.start() if start else copy.wait_send()

        def add_corner(rep, half, index):
            piece = pl.ds(half_rows * half, half_rows)
            p.arrived(into.at[0, piece], into_sems.at[1, index])
            pair[rep, piece, :] = add_up(pair[rep, piece, :], into[0, piece, :]).astype(BF16)

        def onward(distance, rep, start, rows_too=True):
            kinds = [(s_pair, s_into, s_into_sems)] + ([(pair, into, into_sems)] if rows_too else [])
            for values, target, sems in kinds:
                copy = pltpu.make_async_remote_copy(
                    src_ref=values.at[rep], dst_ref=target.at[distance], send_sem=sems.at[0, distance],
                    recv_sem=sems.at[1, distance], device_id=p.device(rep=rep), device_id_type=MESH_ID,
                )
                if start:
                    copy.start()
                else:
                    copy.wait_send()

        def proj_copy(slot, rep, core):
            return pltpu.make_async_copy(proj_buffer.at[slot], proj_out.at[rep, core], proj_sems.at[slot])

        def mixed_copy(at, rep, core):
            return pltpu.make_async_copy(mixed_all.at[at], mixed_out.at[rep, core], mixed_sems.at[at])

        def place_of(at):
            distance = distance_at(at // 2)
            turn = lax.rem(at, 2)
            return distance, p.rep_at(distance), turn, jnp.where(turn == 0, 1 - p.core, p.core)

        def mix(at):
            distance, rep, turn, core = place_of(at)
            x = x_all[rep, core].astype(F32)
            first = (x * rms_rows(x) * in_gain_ref[...]).astype(BF16)
            x_all[rep, core] = first
            proj = mm(first, weight_all[...].reshape(model, wide))

            @pl.when(at >= 2)
            def _():
                proj_copy(turn, rep, core).wait()

            proj_buffer[turn] = proj
            proj_copy(turn, rep, core).start()
            seg_column, seg_line = segments(lengths_ref[rep, core][0:1, :], sequences, rows)
            block = Block(proj, seg_column, seg_line, taps_ref[...], heads_ref[...], channels, width, state)
            mixed = []
            for start, stop, inside in block.groups():
                xin = block.xin[:, start:stop]
                scaled, rest = split_two(xin * block.spread(block.step, start, stop, inside))
                scaled = jnp.concatenate([scaled, scaled, rest], axis=0)
                y = None
                for head in inside:
                    weights, weights_rest = split_two(block.scores * block.decay(head))
                    term = mm(jnp.concatenate([weights, weights_rest, weights], axis=1), scaled)
                    y = term if y is None else jnp.where(block.inside(start, stop, head), term, y)
                gate = block.gate[:, start:stop]
                mixed.append((y + skip_ref[:, start:stop] * xin) * gate * jax.nn.sigmoid(gate))
            mixed = jnp.concatenate(mixed, axis=1)
            squares[rep, core] = row_of(jnp.sum(mixed * mixed, axis=1, keepdims=True), rows)
            mixed_all[at] = mixed * norm_ref[...]
            mixed_copy(at, rep, core).start()

        def put(at):
            distance, rep, turn, core = place_of(at)
            mixed, mixed_rest = split_two(mixed_all[at])
            out_weight = out_all[...].reshape(channels, model)
            part_rows = mm(mixed, out_weight) + mm(mixed_rest, out_weight)

            @pl.when(turn == 0)
            def _():
                parts[rep] = part_rows.astype(BF16)
                swap(rep, True)

            @pl.when((turn == 1) & (distance == 0))
            def _():
                own_part[...] = part_rows

            @pl.when((turn == 1) & (distance > 0))
            def _():
                p.arrived(pair.at[rep], pair_sems.at[1, rep])
                pair[rep] = add_up(part_rows, pair[rep]).astype(BF16)
                p.arrived(s_pair.at[rep], s_pair_sems.at[1, rep])
                s_pair[rep] = add_up(squares[rep, p.core], s_pair[rep])
                if corner:
                    pl.when(distance == 1)(functools.partial(add_corner, rep, 1, 0))
                    pl.when(distance == 2)(functools.partial(add_corner, rep, 0, 3))
                    pl.when(distance < 3)(functools.partial(onward, distance, rep, True))
                    pl.when(distance == 3)(functools.partial(onward, distance, rep, True, False))
                    pl.when(distance == 3)(functools.partial(to_corner, True))
                else:
                    onward(distance, rep, True)

        delay = 4

        def visit(at, carry):
            pl.when(at < 2 * reps)(functools.partial(mix, at))
            for distance in range(1, depth):
                pl.when(at == min(distance - 1, delay - 1))(functools.partial(out_tick, distance))
            pl.when(at == delay - 1)(g_job.start)
            pl.when(at == delay)(out_wait)
            pl.when(at >= delay)(functools.partial(put, at - delay))
            pl.when(at == 2 * delay - 1)(functools.partial(g_job.hop, 1))
            return carry

        lax.fori_loop(0, 2 * reps + delay, visit, 0)
        out_keep = p.local(out_all, out_out, e_local.at[1])
        first_keep = p.local(x_all, first_out, keep_sems.at[2])
        if depth > 2:
            g_job.hop(2)
        p.arrived(pair.at[p.rep], pair_sems.at[1, p.rep])
        p.arrived(s_pair.at[p.rep], s_pair_sems.at[1, p.rep])
        terms, square_terms = [own_part[...], pair[p.rep]], [squares[p.rep, p.core], s_pair[p.rep]]
        for distance in range(1, reps):
            p.arrived(s_into.at[distance], s_into_sems.at[1, distance])
            square_terms.append(s_into[distance])
            if not (corner and distance == 3):
                p.arrived(into.at[distance], into_sems.at[1, distance])
                terms.append(into[distance])
        scale_row = lax.rsqrt(add_up(*square_terms) / inner + EPS)
        scale_ref[...] = scale_row
        mixed = column_of(scale_row[0:1, :], rows) * add_up(*terms)
        mixed_ref[...] = mixed.astype(BF16)
        after = x_ref[...].astype(F32) + mixed
        after_ref[...] = after
        second[...] = (after * rms_rows(after) * post_gain_ref[...]).astype(BF16)
        job = ColumnGather(p, second, lambda z: second_out.at[z, p.core], second_sems, second_local,
                           shared=lambda z: second_out.at[z, 1 - p.core])
        for distance in range(3, depth):
            g_job.hop(distance)
        for distance in range(1, depth):
            job.hop(distance)
        job.finish()
        g_job.finish()
        for distance in range(reps):
            rep = p.rep_at(distance) if distance else p.rep
            swap(rep, False)
            if distance:
                onward(distance, rep, False, not (corner and distance == 3))
        if corner:
            to_corner(False)
        for slot in range(2):
            proj_copy(slot, p.rep, p.core).wait()
        for at in range(2 * reps):
            mixed_copy(at, p.rep, p.core).wait()
        job_o.finish()
        table_job.finish()
        for distance in range(1, group):
            other = lax.rem(shard - distance + group, group)
            for kind in range(2):
                p.arrived(shared_slot(kind, other), shared_sems.at[2 * kind + 1, distance])
        for keep in shared_keep:
            keep.wait()
        p.pending = p.pending + shared_pending
        for goal in range(depth):
            when(goal != p.rep, exchange_copy(goal).wait_send)
        for keep in (weight_keep, out_keep, first_keep):
            keep.wait()
        p.finish()

    return pl.pallas_call(
        kernel,
        in_specs=in_vmem(1) + anywhere(7) + in_vmem(len(small)),
        out_specs=in_vmem(10) + anywhere(9),
        out_shape=[
            jax.ShapeDtypeStruct((rows, model), F32),
            jax.ShapeDtypeStruct((rows, model), BF16),
            jax.ShapeDtypeStruct((8, rows), F32),
            jax.ShapeDtypeStruct((reps, 2, 8, LANES), F32),
            jax.ShapeDtypeStruct((1, model), F32),
            jax.ShapeDtypeStruct((1, model), F32),
            jax.ShapeDtypeStruct((8, channels + 2 * state), F32),
            jax.ShapeDtypeStruct((8, LANES), F32),
            jax.ShapeDtypeStruct((1, channels), F32),
            jax.ShapeDtypeStruct((1, channels), F32),
            jax.ShapeDtypeStruct((depth, 2) + table.shape, BF16),
            jax.ShapeDtypeStruct((depth, 2, rows, model), BF16),
            jax.ShapeDtypeStruct((depth, 2, rows, model), BF16),
            jax.ShapeDtypeStruct((reps, 2, rows, model), BF16),
            jax.ShapeDtypeStruct((depth, 2, part, wide), BF16),
            jax.ShapeDtypeStruct((reps, quarter, model), BF16),
            jax.ShapeDtypeStruct((reps, 2, rows, wide), F32),
            jax.ShapeDtypeStruct((reps, 2, rows, channels), F32),
            jax.ShapeDtypeStruct((group, part, 2 * shared), BF16),
        ],
        scratch_shapes=[item for items in groups for item in items]
        + [pltpu.VMEM((rows, model), BF16)]
        + ColumnGather.scratch(depth) * 2
        + [pltpu.VMEM((2, rows, wide), F32), pltpu.SemaphoreType.DMA((2,)), pltpu.SemaphoreType.DMA((3,)),
           pltpu.VMEM((rows, model), F32), pltpu.VMEM((2 * reps, rows, channels), F32),
           pltpu.SemaphoreType.DMA((2 * reps,)), pltpu.VMEM((vector_rows, vector_width), F32),
           pltpu.SemaphoreType.DMA((4, group)), pltpu.SemaphoreType.DMA((2,))],
        compiler_params=remote_params(0),
        name="forward_mixer",
    )(tokens, cotangent, own_pair, other_pair, common, table, out_quarters, shared_in, *small)


def join_experts(
    own, gates, dots, hidden, shared_grad, router_t, shared_in, shared_out, cotangent, after, mixed, scale, post_gain,
    back, weighted, second, inner, reps, depth, capacity,
):
    rows, model = cotangent.shape
    local = own.shape[1]
    experts = gates.shape[1]
    half_rows = rows // 2
    stack = (rows, model)
    halves = (slice(0, half_rows), slice(half_rows, rows))
    groups = {
        "stream": [
            pltpu.VMEM((2, local, capacity, model), BF16), pltpu.SemaphoreType.DMA((2,)),
            pltpu.VMEM((2,) + stack, BF16), pltpu.SemaphoreType.DMA((2,)),
        ],
        "parts": [
            pltpu.VMEM((2,) + stack, BF16), pltpu.VMEM(stack, F32), pltpu.VMEM((depth, 2, half_rows, model), BF16),
            pltpu.SemaphoreType.DMA((2, depth)),
        ],
        "line": LineSum.scratch(depth, (half_rows, model), BF16) * 2,
        "low": [pltpu.VMEM((2, half_rows, model), BF16), pltpu.VMEM((2, 8, rows), F32)] + PlaneGather.scratch(reps) * 3,
        "logits": [pltpu.VMEM((2 * depth, 2 * experts, rows), BF16)],
        "layer": [
            pltpu.VMEM((2,) + stack, BF16), pltpu.VMEM(stack, F32), pltpu.VMEM((depth,) + stack, BF16),
            pltpu.SemaphoreType.DMA((2, depth)),
        ] + LineSum.scratch(depth, stack, BF16),
    }

    def kernel(own_ref, gates_ref, dots_ref, hidden_ref, shared_ref, router_ref, in_ref, out_ref, g_ref, after_ref,
               mixed_ref, scale_ref, gain_ref, back_ref, weighted_ref, second_ref,
               grad_ref, gain_grad_ref, router_grad_ref, layer_out_ref, low_out, scale_out, *scratch):
        work, cut = {}, 0
        for name, items in groups.items():
            work[name] = scratch[cut : cut + len(items)]
            cut += len(items)
        p = Place(reps, depth)
        slots, slot_sems, second_slots, second_sems = work["stream"]
        parts, own_part, pair, pair_sems = work["parts"]
        logits_all = work["logits"][0]
        layer_parts, layer_own, layer_pair, layer_pair_sems, layer_into, layer_sems = work["layer"]
        lower = p.z < depth // 2

        def goal_at(index):
            distance = lax.rem(depth - 1 - index + depth, depth)
            return jnp.where(lower, lax.rem(p.z + distance, depth), lax.rem(p.z - distance + depth, depth))

        def block_at(at):
            return goal_at(at // 2), jnp.where(lax.rem(at, 2) == 0, 1 - p.core, p.core)

        def load(source, at):
            goal, core = block_at(at)
            start = pl.multiple_of((2 * goal + core) * capacity, capacity)
            return pltpu.make_async_copy(
                source.at[:, pl.ds(start, capacity)], slots.at[lax.rem(at, 2)], slot_sems.at[lax.rem(at, 2)]
            )

        def swap(goal, slot, start):
            for at, piece in enumerate(halves):
                copy = pltpu.make_async_remote_copy(
                    src_ref=parts.at[slot, pl.ds(half_rows * at, half_rows)], dst_ref=pair.at[goal, at],
                    send_sem=pair_sems.at[0, goal] if at == 0 else pair_sems_late.at[0, goal],
                    recv_sem=pair_sems.at[1, goal] if at == 0 else pair_sems_late.at[1, goal],
                    device_id=p.sibling(), device_id_type=MESH_ID,
                )
                copy.start() if start else copy.wait_send()

        pair_sems_late = work["late"][0]
        load(back_ref, 0).start()
        p.barrier(plane=True, column=True)
        expert = lax.broadcasted_iota(jnp.int32, (experts, rows), 0)
        shard = 2 * p.z + p.core

        def matches(q):
            table = own_ref[q].astype(F32)
            return [slot_match(table[i : i + 1, :], capacity, rows) for i in range(local)]

        def visit(at, carry):
            goal, core = block_at(at)
            q = 2 * goal + core
            turn = lax.rem(at, 2)
            load(back_ref, at).wait()

            @pl.when(at + 1 < 2 * depth)
            def _():
                load(back_ref, at + 1).start()

            start = pl.multiple_of(q * rows, rows)
            gates = gates_ref[q]
            gate_grad = jnp.zeros_like(gates)
            total = mm_nt(shared_ref[pl.ds(start, rows), :], in_ref[...])
            for i, match in enumerate(matches(q)):
                total = total + mm_tn(match.astype(BF16), slots[turn, i])
                dot = dots_ref[i, pl.ds(pl.multiple_of(q * capacity, capacity), capacity), 0:1]
                row = jnp.sum(jnp.where(match, dot, 0.0), axis=0, keepdims=True)
                gate_grad = jnp.where(expert == local * shard + i, row, gate_grad)
            logit_grad = gates * (gate_grad - jnp.sum(gates * gate_grad, axis=0, keepdims=True))
            logit_pair = jnp.concatenate(split_two(logit_grad), axis=0)
            logits_all[q] = logit_pair
            total = total + mm_tn(logit_pair, jnp.concatenate([router_ref[...], router_ref[...]], axis=0))

            @pl.when(turn == 0)
            def _():
                slot = lax.rem(at // 2, 2)

                @pl.when(at >= 4)
                def _():
                    swap(goal_at(at // 2 - 2), slot, False)

                parts[slot] = total.astype(BF16)
                swap(goal, slot, True)

            @pl.when(turn == 1)
            def _():
                p.arrived(pair.at[goal, 0], pair_sems.at[1, goal])
                p.arrived(pair.at[goal, 1], pair_sems_late.at[1, goal])

                @pl.when(goal == p.z)
                def _():
                    for index, piece in enumerate(halves):
                        own_part[piece, :] = add_up(total[piece, :], pair[goal, index])

                @pl.when(goal != p.z)
                def _():
                    for index, piece in enumerate(halves):
                        pair[goal, index] = add_up(total[piece, :], pair[goal, index]).astype(BF16)

            return carry

        lines = []
        for index in range(2):
            view = pair.at[:, index]
            into, sems = work["line"][2 * index : 2 * index + 2]

            def terms(goal, view=view, index=index):
                return [view[goal]]

            lines.append(LineSum(p, terms, view, into, sems))

        for step in range(depth - 1):
            lax.fori_loop(2 * step, 2 * step + 2, visit, 0)
            lines[0].step(step)
        for step in range(depth - 1):
            lines[1].step(step)
        lax.fori_loop(2 * depth - 2, 2 * depth, visit, 0)

        low, scales = work["low"][:2]
        gather_sems = work["low"][2:]
        gain_grad_ref[...] = jnp.zeros_like(gain_grad_ref)
        row_dots = []

        def norm_back(index):
            piece = halves[index]
            into = lines[index].into
            grad_ref[piece, :] = own_part[piece, :]
            lines[index].gather(grad_ref.at[pl.ds(half_rows * index, half_rows)])
            second_grad = grad_ref[piece, :]
            after_rows = after_ref[piece, :]
            after_scale = rms_rows(after_rows)
            gain_grad_ref[...] += jnp.sum(after_rows * second_grad * after_scale, axis=0, keepdims=True)
            weighted = second_grad * gain_ref[...]
            after_grad = (
                g_ref[piece, :].astype(F32)
                + after_scale * weighted
                - after_rows * after_scale**3 * jnp.mean(after_rows * weighted, axis=1, keepdims=True)
            )
            grad_ref[piece, :] = after_grad
            after_low = after_grad.astype(BF16)
            low[index] = after_low
            row_dots.append(
                jnp.sum(after_low.astype(F32) * mixed_ref[piece, :].astype(F32), axis=1, keepdims=True)
            )
            return PlaneGather(p, low.at[index], low_out.at[:, :, pl.ds(half_rows * index, half_rows)],
                               *gather_sems[2 * index : 2 * index + 2])

        first_job = norm_back(0)

        def layer_load(at):
            q = block_at(at)
            start = pl.multiple_of((2 * q[0] + q[1]) * rows, rows)
            return pltpu.make_async_copy(
                second_ref.at[pl.ds(start, rows)], second_slots.at[lax.rem(at, 2)], second_sems.at[lax.rem(at, 2)]
            )

        def layer_swap(goal, slot):
            return pltpu.make_async_remote_copy(
                src_ref=layer_parts.at[slot], dst_ref=layer_pair.at[goal], send_sem=layer_pair_sems.at[0, goal],
                recv_sem=layer_pair_sems.at[1, goal], device_id=p.sibling(), device_id_type=MESH_ID,
            )

        def layer_visit(at, carry):
            goal, core = block_at(at)
            q = 2 * goal + core
            turn = lax.rem(at, 2)
            load(weighted_ref, at).wait()
            layer_load(at).wait()

            @pl.when(at + 1 < 2 * depth)
            def _():
                load(weighted_ref, at + 1).start()
                layer_load(at + 1).start()

            total = mm(hidden_ref[pl.ds(pl.multiple_of(q * rows, rows), rows), :], out_ref[...])
            for i, match in enumerate(matches(q)):
                total = total + mm_tn(match.astype(BF16), slots[turn, i])

            @pl.when(turn == 0)
            def _():
                slot = lax.rem(at // 2, 2)

                @pl.when(at >= 4)
                def _():
                    layer_swap(goal_at(at // 2 - 2), slot).wait_send()

                layer_parts[slot] = total.astype(BF16)
                layer_swap(goal, slot).start()

            @pl.when(turn == 1)
            def _():
                p.arrived(layer_pair.at[goal], layer_pair_sems.at[1, goal])

                @pl.when(goal == p.z)
                def _():
                    layer_own[...] = add_up(total, layer_pair[goal])

                @pl.when(goal != p.z)
                def _():
                    layer_pair[goal] = add_up(total, layer_pair[goal]).astype(BF16)

            both = mm(logits_all[q], second_slots[turn])
            router_grad_ref[...] += both[:experts, :] + both[experts:, :]
            return carry

        router_grad_ref[...] = jnp.zeros_like(router_grad_ref)
        load(weighted_ref, 0).start()
        layer_load(0).start()
        lax.fori_loop(0, 2 * depth, layer_visit, 0)
        first_job.relay()
        second_job = norm_back(1)
        layer_line = LineSum(p, lambda goal: [layer_pair[goal]], layer_pair, layer_into, layer_sems)
        layer_line.step(0)
        dot_row = row_of(jnp.concatenate(row_dots, axis=0), rows)
        scale_row = scale_ref[...]
        scales[0] = scale_row
        scales[1] = scale_row**2 * dot_row / inner
        scale_job = PlaneGather(p, scales, scale_out, *gather_sems[4:6], corner=False)
        for step in range(1, depth - 1):
            layer_line.step(step)
        scale_job.relay()
        second_job.relay()
        layer_line.gather(layer_own)
        layer_out_ref[...] = (layer_own[...] + after_ref[...]).astype(BF16)
        for job in (first_job, scale_job, second_job):
            job.finish()
        for at in range(max(depth - 2, 0), depth):
            swap(goal_at(at), at % 2, False)
            layer_swap(goal_at(at), at % 2).wait_send()
        layer_line.finish()
        for line in lines:
            line.finish()
        p.finish()

    groups["late"] = [pltpu.SemaphoreType.DMA((2, depth))]
    group = 2 * depth
    return pl.pallas_call(
        kernel,
        in_specs=in_vmem(13) + anywhere(3),
        out_specs=in_vmem(4) + anywhere(2),
        out_shape=[
            jax.ShapeDtypeStruct((rows, model), F32),
            jax.ShapeDtypeStruct((1, model), F32),
            jax.ShapeDtypeStruct((experts, model), F32),
            jax.ShapeDtypeStruct((rows, model), BF16),
            jax.ShapeDtypeStruct((reps, 2, rows, model), BF16),
            jax.ShapeDtypeStruct((reps, 2, 2, 8, rows), F32),
        ],
        scratch_shapes=[item for items in groups.values() for item in items],
        compiler_params=remote_params(2),
        name="join_experts",
    )(
        own, gates, dots, hidden, shared_grad, router_t, shared_in, shared_out, cotangent, after, mixed, scale,
        post_gain, back, weighted, second,
    )


def backward_mixer(
    scales, after_grad, tokens, in_gain, post_grad, router_parts, lengths, taps, head_rows, skip, norm, weight,
    out_weight, low, first, proj, gained, sizes,
):
    reps, depth, channels, width, state, sequences, inner, convolved = sizes
    rows, model = tokens.shape
    part = model // (2 * depth)
    wide = weight.shape[1]
    side = 2 * channels
    heads = channels // width
    per_shard = convolved // (2 * depth)
    quarter = channels // reps
    experts, router_width = router_parts.shape[2:]
    small_width = -(-max(per_shard, channels, router_width) // LANES) * LANES
    small_shape = (16 + experts, small_width)
    stack = (rows, model)
    corner = reps == 4 and rows % 32 == 0
    half_rows = rows // 2
    groups = {
        "early": [pltpu.VMEM((2, rows, channels), F32), pltpu.SemaphoreType.DMA((2,))],
        "stream": [
            pltpu.VMEM(stack, BF16), pltpu.VMEM((2, rows, wide), F32), pltpu.VMEM((2,) + stack, BF16),
            pltpu.SemaphoreType.DMA((3, 2)),
        ],
        "sum": [
            pltpu.VMEM((2,) + stack, BF16), pltpu.VMEM(stack, F32),
            pltpu.VMEM((reps,) + stack, BF16), pltpu.SemaphoreType.DMA((2, reps)),
            pltpu.VMEM((2 if corner else reps - 1,) + stack, BF16), pltpu.SemaphoreType.DMA((2, reps)),
            pltpu.VMEM((2, half_rows, model), BF16),
        ],
        "grads": [
            pltpu.VMEM((depth, 2, part, wide), F32), pltpu.VMEM((channels, model), F32),
            pltpu.VMEM((8, channels + 2 * state), F32), pltpu.VMEM((8, LANES), F32), pltpu.VMEM((8, channels), F32),
        ],
        "side": LineSum.scratch(depth, (2, part, channels), BF16) * 2
        + [pltpu.VMEM((2, 2, part, channels), BF16), pltpu.VMEM((2, part, channels), BF16),
           pltpu.SemaphoreType.DMA((2, 2))],
        "common": [pltpu.VMEM((depth, 2, part, wide - side), BF16)]
        + ColumnSum.scratch(depth, (part, wide - side), BF16)
        + [pltpu.VMEM((part, wide - side), F32), pltpu.VMEM((part, wide - side), BF16)],
        "out": [
            pltpu.VMEM((reps, quarter, model), BF16), pltpu.VMEM((reps, quarter, model), BF16),
            pltpu.SemaphoreType.DMA((2, reps)),
        ] + LineSum.scratch(depth, (quarter, model), BF16)
        + [pltpu.VMEM((quarter, model), BF16)],
        "small": [pltpu.VMEM((depth, 2) + small_shape, F32)] + ColumnSum.scratch(depth, small_shape, F32)
        + [pltpu.VMEM(small_shape, F32), pltpu.VMEM((reps,) + small_shape, F32)],
        "end": [pltpu.SemaphoreType.DMA((2, 5, reps)), pltpu.SemaphoreType.DMA((6,)), pltpu.VMEM((2, 32, model), F32)],
    }

    def kernel(scales_ref, grad_ref, x_ref, gain_ref, post_grad_ref, router_ref, lengths_ref, taps_ref,
               heads_ref, skip_ref, norm_ref, weight_ref, out_ref, low_ref, first_ref, proj_ref, gained_ref,
               tokens_grad_ref, side_out, common_out, out_out, small_out, *scratch):
        work, cut = {}, 0
        for name, items in groups.items():
            work[name] = scratch[cut : cut + len(items)]
            cut += len(items)
        p = Place(reps, depth)
        first_slot, proj_slots, low_slots, stream_sems = work["stream"]
        gained_slots, gained_sems = work["early"]

        def first_load(rep, core):
            return pltpu.make_async_copy(first_ref.at[rep, core], first_slot, stream_sems.at[0, 0])

        def proj_load(slot, rep, core):
            return pltpu.make_async_copy(proj_ref.at[rep, core], proj_slots.at[slot], stream_sems.at[1, slot])

        def low_load(slot, rep, core):
            return pltpu.make_async_copy(low_ref.at[rep, core], low_slots.at[slot], stream_sems.at[2, slot])

        def gained_load(slot, rep, core):
            return pltpu.make_async_copy(gained_ref.at[rep, core], gained_slots.at[slot], gained_sems.at[slot])

        def early_place(at):
            return at // 2, lax.rem(at, 2)

        for at in range(2):
            gained_load(at, *early_place(at)).start()
            low_load(at, *early_place(at)).start()
        def distance_at(index):
            if corner:
                return jnp.where(index == 0, 3, jnp.where(index == 3, 0, index))
            return lax.rem(index + 1, reps)

        opening = p.rep_at(distance_at(0))
        proj_load(0, opening, 1 - p.core).start()
        proj_load(1, opening, p.core).start()
        p.barrier(plane=True, column=True)
        in_total, out_total, taps_total, heads_total, wide_total = work["grads"]
        for total in work["grads"]:
            total[...] = jnp.zeros_like(total)

        def early(at, carry):
            rep, core = early_place(at)
            turn = lax.rem(at, 2)
            gained_load(turn, rep, core).wait()
            low_load(turn, rep, core).wait()
            scale = column_of(scales_ref[rep, core, 0][0:1, :], rows)
            out_total[...] += mm_tn((gained_slots[turn] * scale).astype(BF16), low_slots[turn])

            @pl.when(at + 2 < 2 * reps)
            def _():
                gained_load(turn, *early_place(at + 2)).start()
                low_load(turn, *early_place(at + 2)).start()

            return carry

        lax.fori_loop(0, 2 * reps, early, 0)
        low_load(0, opening, 1 - p.core).start()
        low_load(1, opening, p.core).start()
        out_parts, out_mid, out_sems, out_into, out_line_sems, out_low = work["out"]
        out_line_total = out_total.at[pl.ds(0, quarter)]
        out_parts[...] = out_total[...].astype(BF16).reshape(reps, quarter, model)
        for distance in range(1, reps):
            rep = p.rep_at(distance)
            p.send(out_parts.at[rep], out_mid.at[p.rep], out_sems.at[0, distance], out_sems.at[1, distance],
                   p.device(rep=rep))
        out_mid[p.rep] = out_parts[p.rep]
        out_job = LineSum(p, lambda at: [out_mid[at]], out_into, out_into, out_line_sems)

        parts, own_part, pair, pair_sems, into, into_sems, extra = work["sum"]

        def swap(index, start):
            rep = p.rep_at(distance_at(index))
            copy = pltpu.make_async_remote_copy(
                src_ref=parts.at[lax.rem(index, 2)], dst_ref=pair.at[rep], send_sem=pair_sems.at[0, rep],
                recv_sem=pair_sems.at[1, rep], device_id=p.sibling(), device_id_type=MESH_ID,
            )
            copy.start() if start else copy.wait_send()

        def onward(distance, rep, start):
            copy = pltpu.make_async_remote_copy(
                src_ref=pair.at[rep], dst_ref=into.at[distance - 1], send_sem=into_sems.at[0, distance],
                recv_sem=into_sems.at[1, distance], device_id=p.device(rep=rep), device_id_type=MESH_ID,
            )
            copy.start() if start else copy.wait_send()

        def to_corner(start):
            for half, index in ((0, 3), (1, 0)):
                copy = pltpu.make_async_remote_copy(
                    src_ref=pair.at[p.rep_at(3), pl.ds(half_rows * half, half_rows)], dst_ref=extra.at[half],
                    send_sem=into_sems.at[0, index], recv_sem=into_sems.at[1, index],
                    device_id=p.device(rep=p.rep_at(half + 1)), device_id_type=MESH_ID,
                )
                copy.start() if start else copy.wait_send()

        def add_corner(rep, half, index):
            piece = pl.ds(half_rows * half, half_rows)
            p.arrived(extra.at[half], into_sems.at[1, index])
            pair[rep, piece, :] = add_up(pair[rep, piece, :], extra[half]).astype(BF16)

        def visit(at, carry):
            distance, turn = distance_at(at // 2), lax.rem(at, 2)
            rep = p.rep_at(distance)
            core = jnp.where(turn == 0, 1 - p.core, p.core)
            first_load(rep, core).start()
            low_load(turn, rep, core).wait()
            proj_load(turn, rep, core).wait()
            scale = column_of(scales_ref[rep, core, 0][0:1, :], rows)
            pull = column_of(scales_ref[rep, core, 1][0:1, :], rows)
            seg_column, seg_line = segments(lengths_ref[rep, core][0:1, :], sequences, rows)
            block = Block(
                proj_slots[turn], seg_column, seg_line, taps_ref[...], heads_ref[...], channels, width, state
            )
            low_rows = low_slots[turn]
            proj_grad, tap_grads, head_grads, wide_grads = block_back(
                block, low_rows, scale, pull, taps_ref, skip_ref, norm_ref, weight_ref, out_ref[...]
            )
            taps_total[0:5, :] += tap_grads
            heads_total[0:1, :] += head_grads[0]
            heads_total[1:2, :] += head_grads[1]
            wide_total[0:2, :] += wide_grads
            part_rows = mm_nt(proj_grad, weight_ref[...])

            @pl.when(turn == 0)
            def _():
                @pl.when(at >= 4)
                def _():
                    swap(at // 2 - 2, False)

                parts[lax.rem(at // 2, 2)] = part_rows.astype(BF16)
                swap(at // 2, True)

            @pl.when((turn == 1) & (distance == 0))
            def _():
                own_part[...] = part_rows

            @pl.when((turn == 1) & (distance > 0))
            def _():
                p.arrived(pair.at[rep], pair_sems.at[1, rep])
                pair[rep] = add_up(part_rows, pair[rep]).astype(BF16)
                if corner:
                    pl.when(distance == 3)(functools.partial(to_corner, True))
                    pl.when(distance == 1)(functools.partial(add_corner, rep, 1, 0))
                    pl.when(distance == 2)(functools.partial(add_corner, rep, 0, 3))
                    pl.when(distance < 3)(functools.partial(onward, distance, rep, True))
                else:
                    onward(distance, rep, True)

            first_load(rep, core).wait()
            for z in range(depth):
                columns = first_slot[:, 2 * part * z : 2 * part * (z + 1)]
                for start in range(0, wide, 384):
                    piece = slice(start, min(start + 384, wide))
                    in_total[z, :, :, piece] += mm_tn(columns, proj_grad[:, piece]).reshape(2, part, -1)

            @pl.when(at < 2 * reps - 2)
            def _():
                later = p.rep_at(distance_at(at // 2 + 1))
                proj_load(turn, later, core).start()
                low_load(turn, later, core).start()

            def out_start():
                for distance in range(1, reps):
                    p.arrived(out_mid.at[p.rep_at(distance)], out_sems.at[1, distance])
                out_job.step(0)

            pl.when(at == 1)(out_start)
            for step in range(1, depth - 1):
                pl.when(at == 2 * step + 1)(functools.partial(out_job.step, step))
            return carry

        lax.fori_loop(0, 2 * reps, visit, 0)

        common_parts = work["common"][0]
        common_parts[...] = in_total[:, :, :, side:].astype(BF16)
        common_job = ColumnSum(p, common_parts, *work["common"][1:5])
        side_jobs = []
        for kind in range(2):
            columns = slice(kind * channels, (kind + 1) * channels)
            side_into, side_sems = work["side"][2 * kind : 2 * kind + 2]

            def terms(at, columns=columns):
                return [in_total[at, :, :, columns]]

            side_jobs.append(LineSum(p, terms, side_into, side_into, side_sems))
        side_pair, side_away, side_swap = work["side"][4:]
        side_total = gained_slots.at[:, pl.ds(0, part)]
        side_jobs[0].step(0)

        end_sems, keep_sems, late = work["end"]

        def late_load(source, chunk):
            return pltpu.make_async_copy(
                source.at[pl.ds(32 * chunk, 32)], late.at[chunk % 2], keep_sems.at[3 + chunk % 2]
            )

        late_load(grad_ref, 0).start()
        p.arrived(pair.at[p.rep], pair_sems.at[1, p.rep])
        common_job.ready()
        common_job.step(0)
        side_jobs[1].step(0)
        sources = 2 if corner else reps - 1
        for distance in range(1, sources + 1):
            p.arrived(into.at[distance - 1], into_sems.at[1, distance])
        gain_grad = jnp.zeros((1, model), F32)
        for start in range(0, rows, 32):
            piece = slice(start, start + 32)
            if start + 32 < rows:
                late_load(grad_ref, start // 32 + 1).start()
            late_load(grad_ref, start // 32).wait()
            first_grad = add_up(
                own_part[piece, :], pair[p.rep, piece, :], *[into[at, piece, :] for at in range(sources)]
            )
            x = x_ref[piece, :].astype(F32)
            x_scale = rms_rows(x)
            gain_grad = gain_grad + jnp.sum(x * first_grad * x_scale, axis=0, keepdims=True)
            weighted = first_grad * gain_ref[...]
            tokens_grad_ref[piece, :] = (
                late[start // 32 % 2]
                + x_scale * weighted
                - x * x_scale**3 * jnp.mean(x * weighted, axis=1, keepdims=True)
            ).astype(BF16)

        small = work["small"][0]
        small[...] = jnp.zeros_like(small)
        team = 2 * p.rep + p.core
        own_taps = taps_total[:, :channels]
        blank = jnp.zeros_like(own_taps)
        taps_full = jnp.concatenate(
            [jnp.where(team == member, own_taps, blank) for member in range(2 * reps)] + [taps_total[:, channels:]],
            axis=1,
        )
        for z in range(depth):
            for core in range(2):
                shard = 2 * z + core
                small[z, core, 0:8, 0:per_shard] = taps_full[:, per_shard * shard : per_shard * (shard + 1)]
                small[z, core, 12:13, 0:part] = post_grad_ref[:, part * shard : part * (shard + 1)]
                small[z, core, 13:14, 0:part] = gain_grad[:, part * shard : part * (shard + 1)]
                small[z, core, 16 : 16 + experts, 0:router_width] = router_ref[z, core]
        lane = lax.broadcasted_iota(jnp.int32, (1, LANES), 1)
        skip_row = jnp.zeros((1, LANES), F32)
        for head in range(heads):
            value = jnp.sum(wide_total[1:2, head * width : (head + 1) * width], axis=1, keepdims=True)
            skip_row = jnp.where(lane == head, value, skip_row)
        small[p.rep, p.core, 8:10, 0:LANES] = heads_total[0:2, :]
        small[p.rep, p.core, 10:11, 0:LANES] = skip_row
        small[p.rep, p.core, 11:12, 0:channels] = wide_total[0:1, :]
        small_job = ColumnSum(p, small, *work["small"][1:5])
        small_job.ready()
        small_job.step(0)
        for at in range(1, depth - 1):
            for job in (common_job, side_jobs[0], small_job):
                job.step(at)

        def to_reps(source, target, at):
            for distance in range(1, reps):
                p.send(source, target.at[p.rep], end_sems.at[0, at, distance], end_sems.at[1, at, distance],
                       p.device(rep=p.rep_at(distance)))

        def from_reps(target, at):
            for distance in range(1, reps):
                p.arrived(target.at[p.rep_at(distance)], end_sems.at[1, at, distance])

        def side_finish(kind):
            side_jobs[kind].total(side_total)
            side_pair[kind, p.core] = side_total[p.core].astype(BF16)
            side_away[kind] = side_total[1 - p.core].astype(BF16)
            p.send(side_away.at[kind], side_pair.at[kind, p.core], side_swap.at[0, kind], side_swap.at[1, kind],
                   p.sibling())
            p.arrived(side_pair.at[kind, 1 - p.core], side_swap.at[1, kind])
            to_reps(side_pair.at[kind], side_out.at[kind], kind)
            return p.local(side_pair.at[kind], side_out.at[kind, p.rep], keep_sems.at[kind])

        keeps = [side_finish(0)]
        common_total, common_low = work["common"][5:]
        common_job.total(common_total)
        common_low[...] = common_total[...].astype(BF16)
        to_reps(common_low, common_out, 2)
        keeps.append(p.local(common_low, common_out.at[p.rep], keep_sems.at[2]))
        out_job.total(out_line_total)
        out_low[...] = out_line_total[...].astype(BF16)
        to_reps(out_low, out_out, 3)
        keeps.append(p.local(out_low, out_out.at[p.rep], keep_sems.at[5]))
        small_total, small_all = work["small"][5:]
        small_job.total(small_total)
        small_all[p.rep] = small_total[...]
        to_reps(small_total, small_all, 4)
        for at in range(1, depth - 1):
            side_jobs[1].step(at)
        keeps.append(side_finish(1))

        from_reps(small_all, 4)
        small_out[...] = add_up(*[small_all[at] for at in range(reps)])
        for at, target in ((0, side_out.at[0]), (1, side_out.at[1]), (2, common_out), (3, out_out)):
            from_reps(target, at)
        for keep in keeps:
            keep.wait()
        for index in (reps - 2, reps - 1):
            swap(index, False)
        for distance in range(1, sources + 1):
            onward(distance, p.rep_at(distance), False)
        if corner:
            to_corner(False)
        p.finish()

    return pl.pallas_call(
        kernel,
        in_specs=in_vmem(1) + anywhere(1) + in_vmem(11) + anywhere(4),
        out_specs=in_vmem(1) + anywhere(3) + in_vmem(1),
        out_shape=[
            jax.ShapeDtypeStruct((rows, model), BF16),
            jax.ShapeDtypeStruct((2, reps, 2, part, channels), BF16),
            jax.ShapeDtypeStruct((reps, part, wide - side), BF16),
            jax.ShapeDtypeStruct((reps, quarter, model), BF16),
            jax.ShapeDtypeStruct(small_shape, F32),
        ],
        scratch_shapes=[item for items in groups.values() for item in items],
        compiler_params=remote_params(3, 63),
        name="backward_mixer",
    )(
        scales, after_grad, tokens, in_gain, post_grad, router_parts, lengths, taps, head_rows, skip, norm,
        weight, out_weight, low, first, proj, gained,
    )


def assemble_kernel(
    channels, state, heads, side_ref, common_ref, out_ref, small_ref, in_grad_ref, out_grad_ref, *small_refs
):
    reps = side_ref.shape[1]
    inner = 2 * reps * channels
    for kind in range(2):
        for rep in range(reps):
            for core in range(2):
                at = kind * inner + (2 * rep + core) * channels
                in_grad_ref[:, at : at + channels] = side_ref[kind, rep, core].astype(F32)
    in_grad_ref[:, 2 * inner : 2 * inner + 2 * state] = add_up(
        *[common_ref[rep, :, : 2 * state] for rep in range(reps)]
    )
    start = 2 * inner + 2 * state
    tail = []
    for rep in range(reps):
        pair = common_ref[rep, :, 2 * state :].astype(F32)
        tail += [pair[:, :heads], pair[:, LANES // 2 : LANES // 2 + heads]]
    in_grad_ref[:, start:] = jnp.concatenate(tail, axis=1)
    out_grad_ref[...] = out_ref[...].astype(F32).reshape(out_grad_ref.shape)
    router_grad_ref = small_refs[-1]
    for ref, row in zip(small_refs[:-1], (0, 4, 8, 9, 10, 11, 12, 13)):
        ref[...] = small_ref[row : row + ref.shape[0], : ref.shape[1]]
    part, experts = router_grad_ref.shape
    wide = -(-part // LANES) * LANES
    router = jnp.concatenate([small_ref[16:, :wide], jnp.zeros((LANES - experts, wide), F32)], axis=0)
    router_grad_ref[...] = router.T[:part, :experts]


def assemble(side, common, out_rows, small, small_shapes, channels, state, heads):
    reps, part = side.shape[1], side.shape[3]
    columns = 4 * reps * channels + 2 * state + 2 * reps * heads
    model = out_rows.shape[2]
    return pl.pallas_call(
        functools.partial(assemble_kernel, channels, state, heads),
        in_specs=in_vmem(4),
        out_specs=in_vmem(2 + len(small_shapes)),
        out_shape=[
            jax.ShapeDtypeStruct((part, columns), F32),
            jax.ShapeDtypeStruct((channels, model), F32),
        ] + [jax.ShapeDtypeStruct(shape, F32) for shape in small_shapes],
        compiler_params=pltpu.CompilerParams(vmem_limit_bytes=48 * 2**20),
        name="assemble",
    )(side, common, out_rows, small)


def slot_match(table_row, capacity, rows):
    slot = lax.broadcasted_iota(jnp.int32, (capacity, rows), 0).astype(F32) + 1.0
    return table_row == slot


def dispatch_kernel(
    local, capacity, half,
    table_ref, own_ref, second_ref, g_ref, router_ref, in_ref, out_ref,
    buffer_ref, slot_g_ref, gate_slot_ref, gates_ref, hidden_ref, grad_ref, in_grad_ref, out_grad_ref,
    in_total, out_total,
):
    at = pl.program_id(0)
    second, g = second_ref[...], g_ref[...]
    rows = second.shape[0]
    table = table_ref[...].astype(F32)
    used = table > 0.0
    logits = mm_nt(router_ref[...], second)
    top = jnp.max(jnp.where(used, logits, -jnp.inf), axis=0, keepdims=True)
    raw = jnp.where(used, jnp.exp(jnp.where(used, logits - top, 0.0)), 0.0)
    gates = raw / jnp.sum(raw, axis=0, keepdims=True)
    gates_ref[...] = gates
    expert = lax.broadcasted_iota(jnp.int32, gates.shape, 0)
    shard = 2 * lax.axis_index("z") + lax.axis_index("core")
    for i in range(local):
        match = slot_match(own_ref[i : i + 1, :].astype(F32), capacity, rows)
        onehot = match.astype(BF16)
        buffer_ref[i] = mm(onehot, second).astype(BF16)
        slot_g_ref[i] = mm(onehot, g).astype(BF16)
        gate_row = jnp.sum(jnp.where(expert == local * shard + i, gates, 0.0), axis=0, keepdims=True)
        gate_slot = jnp.sum(jnp.where(match, gate_row, 0.0), axis=1, keepdims=True)
        gate_slot_ref[i] = jnp.broadcast_to(gate_slot, (capacity, LANES))
    pre = mm(second, in_ref[...])
    a, b = pre[:, :half], pre[:, half:]
    sig = jax.nn.sigmoid(a)
    hidden = (a * sig * b).astype(BF16)
    hidden_ref[...] = hidden
    back = mm_nt(g, out_ref[...])
    grad = jnp.concatenate([back * b * silu_slope(a, sig), back * a * sig], axis=1).astype(BF16)
    grad_ref[...] = grad

    @pl.when(at == 0)
    def _():
        in_total[...] = jnp.zeros_like(in_total)
        out_total[...] = jnp.zeros_like(out_total)

    in_total[...] += mm_tn(second, grad)
    out_total[...] += mm_tn(hidden, g)

    @pl.when(at == pl.num_programs(0) - 1)
    def _():
        in_grad_ref[...] = in_total[...].astype(BF16)
        out_grad_ref[...] = out_total[...].astype(BF16)


def dispatch(table, own, second, g, router_t, shared_in, shared_out, capacity):
    group, experts, rows = table.shape
    local = own.shape[1]
    model = second.shape[1]
    half = shared_out.shape[0]
    slots = group * capacity

    def by_block(*shape):
        return pl.BlockSpec((None,) + shape, lambda q: (q,) + (0,) * len(shape))

    def by_slots(width):
        return pl.BlockSpec((local, capacity, width), lambda q: (0, q, 0))

    return pl.pallas_call(
        functools.partial(dispatch_kernel, local, capacity, half),
        grid=(group,),
        in_specs=[
            by_block(experts, rows), by_block(local, rows), by_rows((rows, model)), by_rows((rows, model)),
            whole((experts, model)), whole((model, 2 * half)), whole((half, model)),
        ],
        out_specs=[
            by_slots(model), by_slots(model), by_slots(LANES), by_block(experts, rows), by_rows((rows, half)),
            by_rows((rows, 2 * half)), whole((model, 2 * half)), whole((half, model)),
        ],
        out_shape=[
            jax.ShapeDtypeStruct((local, slots, model), BF16),
            jax.ShapeDtypeStruct((local, slots, model), BF16),
            jax.ShapeDtypeStruct((local, slots, LANES), F32),
            jax.ShapeDtypeStruct((group, experts, rows), F32),
            jax.ShapeDtypeStruct((group * rows, half), BF16),
            jax.ShapeDtypeStruct((group * rows, 2 * half), BF16),
            jax.ShapeDtypeStruct((model, 2 * half), BF16),
            jax.ShapeDtypeStruct((half, model), BF16),
        ],
        scratch_shapes=[pltpu.VMEM((model, 2 * half), F32), pltpu.VMEM((half, model), F32)],
        compiler_params=pltpu.CompilerParams(vmem_limit_bytes=56 * 2**20),
        name="dispatch",
    )(table, own, second, g, router_t, shared_in, shared_out)


def experts_kernel(
    buffer_ref, slot_g_ref, gate_ref, in_ref, out_ref,
    weighted_ref, back_ref, dot_ref, in_grad_ref, out_grad_ref, in_total, out_total,
):
    at = pl.program_id(1)
    buffer, weight_in, weight_out = buffer_ref[...], in_ref[...], out_ref[...]
    half = weight_out.shape[0]
    pre = mm(buffer, weight_in)
    a, b = pre[:, :half], pre[:, half:]
    sig = jax.nn.sigmoid(a)
    act = a * sig
    hidden = (act * b).astype(BF16)
    gate = gate_ref[:, 0:1]
    slot_g = slot_g_ref[...].astype(F32)
    result = mm(hidden, weight_out).astype(BF16).astype(F32)
    weighted_ref[...] = (gate * result).astype(BF16)
    dot_ref[...] = jnp.broadcast_to(jnp.sum(slot_g * result, axis=1, keepdims=True), dot_ref.shape)
    result_grad = (gate * slot_g).astype(BF16)
    hidden_grad = mm_nt(result_grad, weight_out)
    pre_grad = jnp.concatenate([hidden_grad * b * silu_slope(a, sig), hidden_grad * act], axis=1).astype(BF16)
    back_ref[...] = mm_nt(pre_grad, weight_in).astype(BF16)

    @pl.when(at == 0)
    def _():
        in_total[...] = mm_tn(buffer, pre_grad)
        out_total[...] = mm_tn(hidden, result_grad)

    @pl.when(at == 1)
    def _():
        in_grad_ref[...] = (in_total[...] + mm_tn(buffer, pre_grad)).astype(BF16)
        out_grad_ref[...] = (out_total[...] + mm_tn(hidden, result_grad)).astype(BF16)


def run_experts(buffer, slot_g, gate_slot, expert_in, expert_out):
    local, slots, model = buffer.shape
    step = slots // 2
    half = expert_out.shape[1]

    def by_step(width):
        return pl.BlockSpec((None, step, width), lambda i, m: (i, m, 0))

    def by_expert(*shape):
        return pl.BlockSpec((None,) + shape, lambda i, m: (i, 0, 0))

    return pl.pallas_call(
        experts_kernel,
        grid=(local, 2),
        in_specs=[
            by_step(model), by_step(model), by_step(LANES), by_expert(model, 2 * half), by_expert(half, model),
        ],
        out_specs=[
            by_step(model), by_step(model), by_step(LANES), by_expert(model, 2 * half), by_expert(half, model),
        ],
        out_shape=[
            jax.ShapeDtypeStruct((local, slots, model), BF16),
            jax.ShapeDtypeStruct((local, slots, model), BF16),
            jax.ShapeDtypeStruct((local, slots, LANES), F32),
            jax.ShapeDtypeStruct((local, model, 2 * half), BF16),
            jax.ShapeDtypeStruct((local, half, model), BF16),
        ],
        scratch_shapes=[pltpu.VMEM((model, 2 * half), F32), pltpu.VMEM((half, model), F32)],
        compiler_params=pltpu.CompilerParams(vmem_limit_bytes=62 * 2**20),
        name="run_experts",
    )(buffer, slot_g, gate_slot, expert_in, expert_out)


def widen_kernel(*refs):
    count = len(refs) // 2
    for source, target in zip(refs[:count], refs[count:]):
        target[...] = source[...].astype(F32)


def widen(streamed, kept, steps):
    specs = [by_rows((values.shape[0] // steps, values.shape[1])) for values in streamed]
    specs += [whole(values.shape) for values in kept]
    arrays = list(streamed) + list(kept)
    return pl.pallas_call(
        widen_kernel,
        grid=(steps,),
        in_specs=specs,
        out_specs=specs,
        out_shape=[jax.ShapeDtypeStruct(values.shape, F32) for values in arrays],
        compiler_params=pltpu.CompilerParams(vmem_limit_bytes=48 * 2**20),
        name="widen",
    )(*arrays)


def gather(values, axes, axis=0):
    return lax.all_gather(values, axes, axis=axis, tiled=True)


def scatter_sum(values, axes, axis=0):
    return lax.psum_scatter(values, axes, scatter_dimension=axis, tiled=True)


def columns_of(values, start, size, axis=1):
    return lax.dynamic_slice_in_dim(values, start, size, axis=axis)


def shards(
    tokens,
    cotangent,
    dealt_to,
    lengths,
    routes,
    slot_index,
    in_norm,
    in_proj,
    conv_weight,
    conv_bias,
    dt_bias,
    decay_log,
    skip_gain,
    mixer_norm,
    out_proj,
    post_norm,
    router,
    shared_in,
    shared_out,
    expert_in,
    expert_out,
):
    reps, depth = lax.axis_size("rep"), lax.axis_size("z")
    group = 2 * depth
    rep, z, core = lax.axis_index("rep"), lax.axis_index("z"), lax.axis_index("core")
    shard = 2 * z + core
    team = 2 * rep + core
    members = 2 * reps
    rows, model = tokens.shape
    top = routes.shape[1]
    local = expert_in.shape[0]
    experts = local * group
    capacity = rows * top * 4 // (3 * experts)
    inner = mixer_norm.shape[0] * group
    convolved = conv_bias.shape[0] * group
    head_count = dt_bias.shape[0] * group
    width = inner // head_count
    state = (convolved - inner) // 2
    channels = inner // members
    heads = head_count // members
    shared = shared_out.shape[0]
    part = in_norm.shape[0]

    expert_ids = jnp.arange(experts, dtype=jnp.int32)
    table = jnp.sum(
        jnp.where(routes[:, None, :] == expert_ids[None, :, None], slot_index[:, None, :] + 1, 0), axis=2
    ).astype(BF16)
    small = [in_norm[None], conv_weight, conv_bias[None], dt_bias[None], decay_log[None], skip_gain[None],
             mixer_norm[None], post_norm[None], lengths, dealt_to[None]]
    part_wide = -(-part // LANES) * LANES
    table_block = jnp.concatenate([table.T, jnp.pad(router.T, ((0, 0), (0, part_wide - part)))], axis=1)
    pair_heads = 2 * heads
    dt_pair = columns_of(in_proj, inner + convolved + pair_heads * rep, pair_heads)
    blank = jnp.zeros((part, LANES // 2 - heads), BF16)
    common = jnp.concatenate(
        [in_proj[:, 2 * inner : 2 * inner + 2 * state], dt_pair[:, :heads], blank, dt_pair[:, heads:], blank], axis=1
    )

    def pair_of(member):
        return jnp.concatenate(
            [columns_of(in_proj, channels * member, channels), columns_of(in_proj, inner + channels * member, channels)],
            axis=1,
        )

    shared_lanes = -(-shared // LANES) * LANES
    shared_padded = shared_in
    if shared_lanes != shared:
        shared_padded = jnp.pad(
            shared_in.reshape(part, 2 * group, shared), ((0, 0), (0, 0), (0, shared_lanes - shared))
        ).reshape(part, -1)
    sequences = lengths.shape[1]
    (after, mixer_result, scale, lengths_plane, in_gain, post_gain, taps_own, head_rows, skip_own, norm_own, table_all,
     second_column, g_column, first, weight, out_own, projected, gained, shared_in_own) = forward_mixer(
        tokens, cotangent, pair_of(team), pair_of(2 * rep + 1 - core), common, small, table_block,
        out_proj.reshape(reps, channels // reps, model), shared_padded,
        (reps, depth, channels, width, state, sequences, inner, convolved),
    )
    second_column = second_column.reshape(group * rows, model)
    g_column = g_column.reshape(group * rows, model)
    shared_in_own = shared_in_own.reshape(model, 2, shared_lanes)[:, :, :shared].reshape(model, 2 * shared)

    table_all = table_all.reshape(group, experts, -1)
    router_t = table_all[:, :, rows : rows + part].transpose(1, 0, 2).reshape(experts, model)
    dealt_column = shard ^ dealt_to[0] ^ jnp.arange(group, dtype=jnp.int32)
    table_dealt = jnp.take(table_all[:, :, :rows], dealt_column, axis=0)
    table_own = columns_of(table_dealt, local * shard, local)

    buffer, slot_g, gate_slot, gates, shared_hidden, shared_grad, shared_in_grad, shared_out_grad = dispatch(
        table_dealt, table_own, second_column, g_column, router_t, shared_in_own, shared_out, capacity
    )
    weighted, buffer_grad, dots, grad_expert_in, grad_expert_out = run_experts(
        buffer, slot_g, gate_slot, expert_in, expert_out
    )
    shared_in_rows = lax.all_to_all(shared_in_grad, COLUMN, split_axis=0, concat_axis=0, tiled=True)
    shared_in_rows = shared_in_rows.reshape(group, part, 2, shared).transpose(1, 2, 0, 3).reshape(part, -1)
    summed = lax.psum((grad_expert_in, grad_expert_out, shared_out_grad, shared_in_rows), "rep")
    wide_expert_in, wide_expert_out, grad_shared_out, grad_shared_in = widen(
        [summed[0].reshape(-1, summed[0].shape[2]), summed[1].reshape(-1, model)], summed[2:], 8
    )
    grad_expert_in = wide_expert_in.reshape(expert_in.shape)
    grad_expert_out = wide_expert_out.reshape(expert_out.shape)

    after_grad, post_grad, router_grad, layer_out, low_plane, scales = join_experts(
        table_own, gates, dots, shared_hidden, shared_grad, router_t, shared_in_own, shared_out, cotangent, after,
        mixer_result, scale, post_gain, buffer_grad, weighted, second_column, inner, reps, depth, capacity,
    )
    router_parts = jnp.pad(
        router_grad.reshape(experts, depth, 2, part).transpose(1, 2, 0, 3), ((0, 0), (0, 0), (0, 0), (0, part_wide - part))
    )
    grad_tokens, side_rows, common_rows, out_rows, small_sum = backward_mixer(
        scales, after_grad, tokens, in_gain, post_grad, router_parts, lengths_plane, taps_own, head_rows, skip_own, norm_own, weight.reshape(model, -1),
        out_own.reshape(channels, model), low_plane, first, projected, gained,
        (reps, depth, channels, width, state, sequences, inner, convolved),
    )
    per_shard = conv_bias.shape[0]
    small_shapes = [
        (4, per_shard), (1, per_shard), (1, heads), (1, heads), (1, heads), (1, channels), (1, part), (1, part),
        (part, experts),
    ]
    (grad_in_proj, grad_out_proj, grad_taps, grad_bias, grad_dt, grad_decay, grad_skip, grad_mixer_norm, grad_post,
     grad_in_norm, grad_router) = assemble(
        side_rows, common_rows, out_rows, small_sum, small_shapes, channels, state, heads
    )
    return (
        layer_out,
        grad_tokens,
        grad_in_norm[0],
        grad_in_proj,
        grad_taps,
        grad_bias[0],
        grad_dt[0],
        grad_decay[0],
        grad_skip[0],
        grad_mixer_norm[0],
        grad_out_proj,
        grad_post[0],
        grad_router,
        grad_shared_in,
        grad_shared_out,
        grad_expert_in,
        grad_expert_out,
    )


def solution(mesh):
    reps, group = mesh.shape["rep"], mesh.shape["shard"]
    split = Mesh(mesh.devices.reshape(reps, group // 2, 2), ALL)
    one, row = P(COLUMN), P(COLUMN, None)
    token = P(ALL, None)
    return jax.shard_map(
        shards,
        mesh=split,
        in_specs=(
            token, token, P(ALL), token, token, token, one, row, P(None, COLUMN), one, one, one, one, one, row,
            one, row, row, row, P(COLUMN, None, None), P(COLUMN, None, None),
        ),
        out_specs=(
            token, token, one, row, P(None, COLUMN), one, one, one, one, one, row, one, row, row, row,
            P(COLUMN, None, None), P(COLUMN, None, None),
        ),
        check_vma=False,
    )
```
